32 devices in a mesh: hash: 4 (over z), head: 4 (over y, x), seq: 2 (over core).
Axes of the slice: x: 2, y: 2, z: 4, core: 2. Of those that a mesh axis runs over, the one named last changes fastest.
Arguments:
- inputs: bfloat16 [2, 2048, 2, 768], P('seq', 'hash'), may hold values from -18 to 18
- w_qkv: bfloat16 [3, 768, 768], P(None, None, 'head'), may hold values from -0.21875 to 0.21875
- w_out: bfloat16 [768, 768], P('head'), may hold values from -2.5 to 2.5
- feedforward_up_weight: bfloat16 [768, 3072], P(None, 'head'), may hold values from -0.21875 to 0.21875
- feedforward_down_weight: bfloat16 [3072, 768], P('head'), may hold values from -0.109375 to 0.109375
- norm_gain: float32 [2, 768], replicated, may hold values from 0.1 to 1.9
- norm_bias: float32 [2, 768], replicated, may hold values from -3 to 3
- planes: int32 [32, 8, 64], P('hash'), may hold values from 0 to 1
- mask_pos: int32 [2, 1024], replicated, may hold values from 0 to 4096, as said below
- cot_rows: bfloat16 [2, 1024, 768], replicated, may hold values from -6 to 6
Outputs:
- layer_out: bfloat16 [2, 2048, 2, 768], P('seq', 'hash')
- grad_inputs: float32 [2, 2048, 2, 768], P('seq', 'hash')
- grad_w_qkv: float32 [3, 768, 768], P(None, None, 'head')
- grad_w_out: float32 [768, 768], P('head')
- grad_w_up: float32 [768, 3072], P(None, 'head')
- grad_w_down: float32 [3072, 768], P('head')
- grad_norm_gain: float32 [2, 768], P(None, 'head')
- grad_norm_bias: float32 [2, 768], P(None, 'head')
- stream_rms: float32 [3], replicated
The draws below stay inside these ranges and needn't reach their ends.
Inputs may be any that keep to these rules, and one draw needn't show every extreme that they name: `mask_pos`: each row lists between 204 and 1024 distinct positions in increasing order and fills its remaining slots with 4096; in every draw some sequence fills all 1024 slots.
All inputs are finite; a program needn't handle non-finite values.
Results may differ from the reference program's by a relative error of at most 0.012.
Values may be sent and summed in bfloat16 or wider, within the bound.
No kernel may reach another device: no remote copies, remote signals or barrier semaphores. Data moves between devices by JAX's collectives and lax.ppermute only.
A program may use at most 384 MiB of HBM per device.

```python
from functools import partial
import jax
import jax.numpy as jnp
from jax import lax

D = 768
HEADS = 12
HEAD_DIM = 64
FF = 3072
HASHES = 32
BITS = 8
LEN = 4096
SEQS = 2
HALF = 2048
MASKS = 1024
N_SEQ = 2


def draw_inputs(key, part):
    token_place = jnp.arange(N_SEQ, dtype=jnp.float32)[:, None, None, None] * HALF + jnp.arange(HALF, dtype=jnp.float32)[None, :, None, None] + jnp.arange(SEQS, dtype=jnp.float32)[None, None, :, None] * LEN
    fraction = token_place / (SEQS * LEN)
    draw_base = jnp.clip(jax.random.normal(key, (N_SEQ, HALF, SEQS, D), jnp.float32), -6.0, 6.0)
    row_scale = 1.0 + 2.0 * fraction
    return (draw_base * row_scale).astype(jnp.bfloat16)


def draw_mask_pos(key, part):
    key_count, key_order, key_full = jax.random.split(jax.random.fold_in(key, 7), 3)
    least_count = max(1, LEN // 20)
    counts_drawn = jax.random.randint(key_count, (SEQS,), least_count, MASKS + 1)
    full_seq = jax.random.randint(key_full, (), 0, SEQS)
    counts_drawn = jnp.where(jnp.arange(SEQS) == full_seq, MASKS, counts_drawn)
    seq_keys = jax.random.split(key_order, SEQS)

    def one_order(seq_key):
        return jax.random.permutation(seq_key, LEN)[:MASKS]
    orders = jax.vmap(one_order)(seq_keys).astype(jnp.int32)
    slot_ids = jnp.arange(MASKS)[None, :]
    chosen = jnp.where(slot_ids < counts_drawn[:, None], orders, LEN)
    return jnp.sort(chosen, axis=-1).astype(jnp.int32)


def set_ends(array, rng, low, largest):
    dims = array.shape
    place = [jax.random.randint(jax.random.fold_in(rng, axis), (), 0, dims[axis]) for axis in range(len(dims))]
    array = array.at[tuple(place)].set(low)
    longest = dims.index(max(dims))
    place[longest] = (place[longest] + 1) % dims[longest]
    return array.at[tuple(place)].set(largest)


def block_scale(stream_key, shape, pieces, smallest, largest):
    factor_of, own = 1.0, jax.random.fold_in(stream_key, 6)
    for position, parts in pieces:
        steps = jnp.exp(jax.random.uniform(jax.random.fold_in(own, position), (parts,), jnp.float32, smallest / len(pieces), largest / len(pieces)))
        factor_of = factor_of * jnp.repeat(steps, shape[position] // parts).reshape([-1 if axis == position else 1 for axis in range(len(shape))])
    return factor_of


def centred(own_key, extent, scale, reach, cuts=(), kind=jnp.bfloat16):
    drawn = jax.random.normal(own_key, extent, jnp.float32) * scale
    if len(cuts) > 0:
        drawn = block_scale(own_key, extent, cuts, -0.22, 0.18) * drawn
    return jnp.clip(drawn, min=-reach, max=reach).astype(kind)


def setup_inputs(seed: int = 0) -> dict:
    arg_keys = jax.random.split(jax.random.key(seed), 11)
    return {
        "inputs": draw_inputs(jax.random.fold_in(arg_keys[10], 71), 0),
        "w_qkv": centred(arg_keys[1], (3, D, HEADS * HEAD_DIM), D ** -0.5, 0.21875, ((2, 4),)),
        "w_out": centred(arg_keys[2], (HEADS * HEAD_DIM, D), (max(1, D // 128)) ** -0.5, 2.5, ((0, 4),)),
        "feedforward_up_weight": centred(arg_keys[3], (D, FF), D ** -0.5, 0.21875, ((1, 4),)),
        "feedforward_down_weight": centred(arg_keys[4], (FF, D), FF ** -0.5, 0.109375, ((0, 4),)),
        "norm_gain": jnp.clip(1.0 + 0.18 * jax.random.normal(arg_keys[5], (2, D), jnp.float32), 0.1, 1.9),
        "norm_bias": centred(arg_keys[6], (2, D), 0.5, 3.0, (), jnp.float32),
        "planes": set_ends(jax.random.randint(arg_keys[7], (HASHES, BITS, HEAD_DIM), 0, 2), jax.random.fold_in(arg_keys[7], 1), 0, 1).astype(jnp.int32),
        "mask_pos": draw_mask_pos(jax.random.fold_in(arg_keys[10], 71), 0),
        "cot_rows": centred(arg_keys[9], (SEQS, MASKS, D), 1.0, 6.0),
    }


highest_precision = lax.Precision.HIGHEST
sharpness = 3.0

@jax.custom_vjp
def low(v):
    return lax.optimization_barrier(v.astype(jnp.bfloat16)).astype(jnp.float32)

@jax.custom_vjp
def lower_backward(v):
    return v

def low_keep(v):
    return (low(v), None)

def low_pass(kept, grad):
    return (grad,)

def back_keep(v):
    return (v, None)

def back_low(kept, grad):
    return (low(grad),)
low.defvjp(low_keep, low_pass)
lower_backward.defvjp(back_keep, back_low)

def code_values(rows_in, signed):
    unit_rows = rows_in * lax.rsqrt(lax.optimization_barrier(jnp.sum(rows_in * rows_in, axis=-1, keepdims=True)) + 1e-06)
    project = jnp.einsum('lhe,tbe->lhtb', unit_rows, signed, precision=highest_precision) * sharpness
    upper = jax.nn.sigmoid(project)
    lower = jax.nn.sigmoid(-project)
    codes = jnp.ones(project.shape[:-1] + (1,), jnp.float32)
    for bit_index in range(project.shape[-1]):
        codes = jnp.concatenate([codes * lower[..., bit_index:bit_index + 1], codes * upper[..., bit_index:bit_index + 1]], axis=-1)
    return codes

def layer_norm(values_in, gain_row, bias_row):
    center = values_in - lax.optimization_barrier(jnp.mean(values_in, axis=-1, keepdims=True))
    spread = lax.optimization_barrier(jnp.mean(center * center, axis=-1, keepdims=True))
    return center * lax.rsqrt(spread + 1e-05) * gain_row + bias_row

def head_attention(operands, signed):
    head_q, head_k, head_v = operands
    code_q = low(code_values(head_q[:, None, :], signed)[:, 0])
    code_k = low(code_values(head_k[:, None, :], signed)[:, 0])
    tables = low(lower_backward(jnp.einsum('ltb,le->tbe', code_k, head_v, precision=highest_precision)))
    return jnp.einsum('ltb,tbe->le', code_q, tables, precision=highest_precision) / HASHES

def split_heads(block):
    return block.reshape(SEQS, LEN, HEADS, HEAD_DIM).transpose(0, 2, 1, 3).reshape(SEQS * HEADS, LEN, HEAD_DIM)

def to_layout(block):
    return block.reshape(SEQS, N_SEQ, HALF, D).transpose(1, 2, 0, 3)

def reference(inputs, w_qkv, w_out, feedforward_up_weight, feedforward_down_weight, norm_gain, norm_bias, planes, mask_pos, cot_rows):
    signed = (2 * planes - 1).astype(jnp.float32)
    seq_ids = jnp.broadcast_to(jnp.arange(SEQS, dtype=jnp.int32)[:, None], mask_pos.shape)
    grad_out = jnp.zeros((SEQS, LEN, D), jnp.float32).at[seq_ids, mask_pos.astype(jnp.int32)].add(cot_rows.astype(jnp.float32), mode='drop')
    attend = jax.checkpoint(partial(head_attention, signed=signed))

    def forward(input_matrix, query_key_value_weight, output_matrix, up_matrix, down_matrix, gains, biases):
        query_key_value_rows = jnp.einsum('bug,rgh->burh', input_matrix, query_key_value_weight, precision=highest_precision)
        query_key_value_rows = low(lower_backward(query_key_value_rows))
        query_rows = split_heads(query_key_value_rows[:, :, 0])
        key_rows = split_heads(query_key_value_rows[:, :, 1])
        value_rows = split_heads(query_key_value_rows[:, :, 2])
        mixed = lax.map(attend, (query_rows, key_rows, value_rows))
        mixed = mixed.reshape(SEQS, HEADS, LEN, HEAD_DIM).transpose(0, 2, 1, 3).reshape(SEQS, LEN, D)
        bucket_attention = low(lower_backward(mixed))
        attention_result = lower_backward(jnp.einsum('tzc,cq->tzq', bucket_attention, output_matrix, precision=highest_precision))
        first_sum = input_matrix + attention_result
        normalized_rows = low(layer_norm(first_sum, gains[0], biases[0]))
        preactivation = lower_backward(jnp.einsum('uio,og->uig', normalized_rows, up_matrix, precision=highest_precision))
        hidden_rows = low(jax.nn.gelu(preactivation, approximate=False))
        feedforward_result = lower_backward(jnp.einsum('png,ge->pne', hidden_rows, down_matrix, precision=highest_precision))
        layer_out = layer_norm(normalized_rows + feedforward_result, gains[1], biases[1])
        return (layer_out, attention_result, first_sum)
    input_matrix = inputs.astype(jnp.float32).transpose(2, 0, 1, 3).reshape(SEQS, LEN, D)
    outputs, pull = jax.vjp(forward, input_matrix, w_qkv.astype(jnp.float32), w_out.astype(jnp.float32), feedforward_up_weight.astype(jnp.float32), feedforward_down_weight.astype(jnp.float32), norm_gain, norm_bias)
    layer_out, attention_result, first_sum = outputs
    grads = pull((grad_out, jnp.zeros_like(attention_result), jnp.zeros_like(first_sum)))
    stream_rms = jnp.sqrt(jnp.stack([jnp.mean(input_matrix * input_matrix), jnp.mean(attention_result * attention_result), jnp.mean(first_sum * first_sum)]))
    return (to_layout(layer_out).astype(jnp.bfloat16), to_layout(grads[0]), grads[1], grads[2], grads[3], grads[4], grads[5], grads[6], stream_rms)
```

```python
from functools import partial

import jax
import jax.numpy as jnp
import numpy as np
from jax import lax
from jax.experimental import pallas as pl
from jax.experimental.pallas import tpu as pltpu
from jax.sharding import PartitionSpec as P

HEAD_DIM = 64
HASHES = 32
BITS = 8
SETS = 8
BUCKETS = 1 << BITS
ROWS = BUCKETS * SETS

bf16 = jnp.bfloat16
f32 = jnp.float32
NN = (((1,), (0,)), ((), ()))
NT = (((1,), (1,)), ((), ()))
TN = (((0,), (0,)), ((), ()))


def dot(a, b, dims):
    return lax.dot_general(a, b, dims, preferred_element_type=f32)


def sides(rows, planes):
    x = rows.astype(f32)
    inv = lax.rsqrt(jnp.sum(x * x, axis=0, keepdims=True) + 1e-6)
    proj = dot(planes, rows, NN) * (3.0 * inv)
    small = jnp.exp(-proj)
    upper = 1.0 / (1.0 + small)
    return inv, upper, small * upper


def products(upper, lower, first, count):
    out = None
    for i in range(first, first + count):
        lo, up = lower[SETS * i : SETS * (i + 1)], upper[SETS * i : SETS * (i + 1)]
        out = [lo, up] if out is None else [c * lo for c in out] + [c * up for c in out]
    return out


def half_codes(upper, lower):
    low = jnp.concatenate(products(upper, lower, 0, 4), axis=0).astype(bf16)
    high = [jnp.concatenate([a, a], axis=0).astype(bf16) for a in products(upper, lower, 4, 4)]
    return low, high


def code_chunk(low, high, first, count):
    return jnp.concatenate(
        [high[a] * low[16 * j : 16 * (j + 1)] for a in range(first, first + count) for j in range(8)],
        axis=0,
    )


def pull_back(rows, planes_t, inv, upper, sums):
    total = sums[BITS * SETS :][:SETS]
    grad_proj = sums[: BITS * SETS] - upper * jnp.concatenate([total] * BITS, axis=0)
    head = grad_proj.astype(bf16)
    tail = (grad_proj - head.astype(f32)).astype(bf16)
    grad_unit = dot(planes_t, jnp.concatenate([head, tail], axis=0), NN) * (3.0 * inv)
    x = rows.astype(f32)
    return grad_unit - x * (inv * inv * jnp.sum(x * grad_unit, axis=0, keepdims=True))


def both(a, b):
    return jnp.concatenate([a[...], b[...]], axis=1)


def key_kernel(planes, ka, va, kb, vb, *refs, chunk):
    start, out = (None, *refs) if len(refs) == 1 else refs
    _, upper, lower = sides(both(ka, kb), planes[...])
    low, high = half_codes(upper, lower)
    values = both(va, vb)
    for c in range(0, 16, chunk):
        at = slice(128 * c, 128 * (c + chunk))
        part = dot(code_chunk(low, high, c, chunk), values, NT)
        if start is not None:
            part = part + start[0, at, :]
        out[0, at, :] = part.astype(out.dtype)


def query_kernel(planes, qa, qb, tables, ea, eb, *, chunk):
    _, upper, lower = sides(both(qa, qb), planes[...])
    low, high = half_codes(upper, lower)
    width = qa.shape[1]
    acc = jnp.zeros((HEAD_DIM, 2 * width), f32)
    for c in range(0, 16, chunk):
        acc += dot(tables[0, 128 * c : 128 * (c + chunk), :], code_chunk(low, high, c, chunk), TN)
    acc = acc * (1.0 / HASHES)
    ea[...] = acc[:, :width].astype(ea.dtype)
    eb[...] = acc[:, width:].astype(eb.dtype)


def query_back_kernel(planes, planes_t, bits, qa, ga, qb, gb, tables, *refs, chunk):
    start, out, da, db = (None, *refs) if len(refs) == 3 else refs
    rows = both(qa, qb)
    inv, upper, lower = sides(rows, planes[...])
    low, high = half_codes(upper, lower)
    grad = both(ga, gb)
    width = qa.shape[1]
    sums = jnp.zeros((bits.shape[0], 2 * width), f32)
    for c in range(0, 16, chunk):
        at = slice(128 * c, 128 * (c + chunk))
        codes = code_chunk(low, high, c, chunk)
        part = dot(codes, grad, NT)
        if start is not None:
            part = (part + start[0, at, :]) * (1.0 / HASHES)
        out[0, at, :] = part.astype(out.dtype)
        weighted = dot(tables[0, at, :], grad, NN).astype(bf16) * codes
        sums += dot(bits[:, at], weighted, NN)
    back = pull_back(rows, planes_t[...], inv, upper, sums * (1.0 / HASHES))
    da[...] = back[:, :width].astype(da.dtype)
    db[...] = back[:, width:].astype(db.dtype)


def key_back_kernel(planes, planes_t, bits, ka, va, kb, vb, grad_tables, da, db, *, chunk):
    rows = both(ka, kb)
    inv, upper, lower = sides(rows, planes[...])
    low, high = half_codes(upper, lower)
    values = both(va, vb)
    width = ka.shape[1]
    sums = jnp.zeros((bits.shape[0], 2 * width), f32)
    grad_values = jnp.zeros((HEAD_DIM, 2 * width), f32)
    for c in range(0, 16, chunk):
        at = slice(128 * c, 128 * (c + chunk))
        codes = code_chunk(low, high, c, chunk)
        grad_values += dot(grad_tables[0, at, :], codes, TN)
        weighted = dot(grad_tables[0, at, :], values, NN).astype(bf16) * codes
        sums += dot(bits[:, at], weighted, NN)
    back = pull_back(rows, planes_t[...], inv, upper, sums)
    da[0] = back[:, :width].astype(da.dtype)
    db[0] = back[:, width:].astype(db.dtype)
    da[1] = grad_values[:, :width].astype(da.dtype)
    db[1] = grad_values[:, width:].astype(db.dtype)


def bit_rows():
    out = np.zeros((80, BUCKETS, SETS), np.float32)
    for t in range(SETS):
        for i in range(BITS):
            out[i * SETS + t, :, t] = (np.arange(BUCKETS) >> i) & 1
        out[BITS * SETS + t, :, t] = 1
    return jnp.asarray(out.reshape(80, ROWS), bf16)


def whole(*shape):
    return pl.BlockSpec(shape, lambda h: (0,) * len(shape))


def per_head(width, offset=0):
    return pl.BlockSpec((HEAD_DIM, width), lambda h: (h + offset, 0))


def table_spec():
    return pl.BlockSpec((1, ROWS, HEAD_DIM), lambda h: (h, 0, 0))


def call(kernel, heads, micros, name, in_specs, out_specs, out_shape):
    return pl.pallas_call(
        kernel,
        grid=(heads,),
        in_specs=in_specs,
        out_specs=out_specs,
        out_shape=out_shape,
        compiler_params=pltpu.CompilerParams(vmem_limit_bytes=48 << 20),
        cost_estimate=pl.CostEstimate(
            flops=int(micros * 1.1e9), bytes_accessed=4 << 20, transcendentals=0
        ),
        name=name,
    )


def key_tables(planes, kv_a, kv_b, start=None):
    heads, width = kv_a.shape[0] // (2 * HEAD_DIM), kv_a.shape[1]
    specs = [whole(64, 64)] + [per_head(width), per_head(width, heads)] * 2
    args = [planes, kv_a, kv_a, kv_b, kv_b]
    if start is not None:
        specs.append(table_spec())
        args.append(start)
    return call(
        partial(key_kernel, chunk=2),
        heads,
        10,
        "key_tables",
        specs,
        table_spec(),
        jax.ShapeDtypeStruct((heads, ROWS, HEAD_DIM), f32 if start is None else bf16),
    )(*args)


def query_estimates(planes, q_a, q_b, tables, kind_a, kind_b):
    heads, width = q_a.shape[0] // HEAD_DIM, q_a.shape[1]
    return call(
        partial(query_kernel, chunk=2),
        heads,
        7,
        "query_estimates",
        [whole(64, 64), per_head(width), per_head(width), table_spec()],
        [per_head(width), per_head(width)],
        [jax.ShapeDtypeStruct(q_a.shape, kind) for kind in (kind_a, kind_b)],
    )(planes, q_a, q_b, tables)


def query_backward(planes, planes_t, bits, q_a, g_a, q_b, g_b, tables, start, kind_a, kind_b):
    heads, width = q_a.shape[0] // HEAD_DIM, q_a.shape[1]
    specs = [whole(64, 64), whole(64, 128), whole(80, ROWS)] + [per_head(width)] * 4 + [table_spec()]
    args = [planes, planes_t, bits, q_a, g_a, q_b, g_b, tables]
    if start is not None:
        specs.append(table_spec())
        args.append(start)
    return call(
        partial(query_back_kernel, chunk=4),
        heads,
        20,
        "query_backward",
        specs,
        [table_spec(), per_head(width), per_head(width)],
        [jax.ShapeDtypeStruct((heads, ROWS, HEAD_DIM), f32 if start is None else bf16)]
        + [jax.ShapeDtypeStruct(q_a.shape, kind) for kind in (kind_a, kind_b)],
    )(*args)


def key_backward(planes, planes_t, bits, kv_a, kv_b, grad_tables, kind_a, kind_b):
    heads, width = kv_a.shape[0] // (2 * HEAD_DIM), kv_a.shape[1]
    pair = pl.BlockSpec((2, HEAD_DIM, width), lambda h: (0, h, 0))
    return call(
        partial(key_back_kernel, chunk=4),
        heads,
        18,
        "key_backward",
        [whole(64, 64), whole(64, 128), whole(80, ROWS)]
        + [per_head(width), per_head(width, heads)] * 2
        + [table_spec()],
        [pair, pair],
        [jax.ShapeDtypeStruct((2, heads * HEAD_DIM, width), kind) for kind in (kind_a, kind_b)],
    )(planes, planes_t, bits, kv_a, kv_a, kv_b, kv_b, grad_tables)


def layer_norm(values_in, gain_row, bias_row):
    center = values_in - jnp.mean(values_in, axis=-1, keepdims=True)
    spread = jnp.mean(center * center, axis=-1, keepdims=True)
    return center * lax.rsqrt(spread + 1e-05) * gain_row + bias_row


def gelu_exact(values_in):
    return jax.nn.gelu(values_in, approximate=False)


def shards(
    inputs,
    w_qkv,
    w_out,
    up_weight,
    down_weight,
    norm_gain,
    norm_bias,
    planes,
    mask_pos,
    cot_rows,
):
    own = inputs[0]
    piece, seqs, width = own.shape
    hash_count, head_count = lax.axis_size("hash"), lax.axis_size("head")
    groups, places = seqs, hash_count // seqs
    assert places == 2 and lax.axis_size("seq") == 2 and head_count == 4
    assert planes.shape[0] * hash_count == 4 * SETS
    quarter = piece // head_count
    rows = groups * quarter
    half_len = piece * hash_count
    hash_id, d, s = lax.axis_index("hash"), lax.axis_index("head"), lax.axis_index("seq")
    g, r = hash_id // places, hash_id % places

    def over_seq(x):
        return lax.ppermute(x, "seq", [(0, 1), (1, 0)])

    def over_place(x):
        return lax.ppermute(x, "hash", [(h, h ^ 1) for h in range(hash_count)])

    def over_group(x, k):
        moves = [(h, ((h // places + k) % groups) * places + h % places) for h in range(hash_count)]
        return lax.ppermute(x, "hash", moves)

    def over_head(x, j):
        return lax.ppermute(x, "head", [(h, h ^ j) for h in range(head_count)])

    def seq_rows(block, index):
        return lax.dynamic_index_in_dim(block, index % seqs, 1, keepdims=False)

    my_quarter = lax.dynamic_slice_in_dim(own, d * quarter, quarter, 0)
    arrived = [over_group(seq_rows(my_quarter, g + k), k) for k in range(1, groups)]
    dense_in = jnp.stack([seq_rows(my_quarter, g)] + arrived)
    blocks = [dense_in]
    for j in range(1, head_count):
        here = seq_rows(lax.dynamic_slice_in_dim(own, (d ^ j) * quarter, quarter, 0), g)
        blocks.append(jnp.concatenate([here[None], over_head(dense_in[1:], j)]))
    tokens = jnp.stack(blocks).reshape(head_count * rows, width)
    dense_in = dense_in.reshape(rows, width)

    signed = (2 * planes - 1).astype(bf16)
    signed = lax.all_gather(signed, "hash", axis=0, tiled=True)
    signed = lax.dynamic_slice_in_dim(signed, (r * 2 + s) * SETS, SETS, 0)
    signed = signed.transpose(1, 0, 2).reshape(BITS * SETS, HEAD_DIM)
    signed_t = jnp.concatenate([signed.T, signed.T], axis=1)
    bits = bit_rows()

    head_width = w_out.shape[0]
    n_tokens = head_count * rows

    def project(w):
        return jnp.einsum("cde,ld->cel", w, tokens, preferred_element_type=f32).astype(bf16)

    kv = project(w_qkv[1:]).reshape(2 * head_width, n_tokens)
    q = project(w_qkv[:1]).reshape(head_width, n_tokens)
    kv_o, q_o = over_seq(kv), over_seq(q)
    kv_z = over_place(kv)
    q_z = over_place(q)
    kv_zo, q_zo = over_seq(kv_z), over_seq(q_z)

    tables = key_tables(signed, kv, kv_o)
    tables = key_tables(signed, kv_z, kv_zo, tables)

    def to_owner(own_part, own_other, far_part, far_other):
        far = (far_part.astype(f32) + over_seq(far_other).astype(f32)).astype(bf16)
        far = over_place(far)
        return own_part + over_seq(own_other).astype(f32) + far.astype(f32)

    e_z, e_zo = query_estimates(signed, q_z, q_zo, tables, bf16, bf16)
    e, e_o = query_estimates(signed, q, q_o, tables, f32, bf16)
    attn = to_owner(e, e_o, e_z, e_zo).astype(bf16)

    def to_dense(block):
        parts = [block[:, j * rows : (j + 1) * rows] for j in range(head_count)]
        return jnp.concatenate([parts[0]] + [over_head(parts[j], j) for j in range(1, head_count)], 0)

    attn_t = to_dense(attn)

    packed = jnp.concatenate([up_weight.T, down_weight, w_out], axis=0)
    pack_half = packed.shape[0] // 2

    def halves(mine, other):
        first = jnp.where(s == 0, mine, other)
        second = jnp.where(s == 0, other, mine)
        return jnp.concatenate([first, second], axis=-2)

    my_half = lax.dynamic_slice_in_dim(packed, s * pack_half, pack_half, 0)
    fetched = jnp.stack([over_head(my_half, j) for j in range(1, head_count)])
    fetched = halves(fetched, over_seq(fetched))
    hidden_own = down_weight.shape[0]
    all_weights = jnp.concatenate([packed[None], fetched], axis=0)
    up_t = all_weights[:, :hidden_own].reshape(head_count * hidden_own, width)
    down = all_weights[:, hidden_own : 2 * hidden_own].reshape(head_count * hidden_own, width)
    out_w = all_weights[:, 2 * hidden_own :].reshape(head_count * head_width, width)
    qkv_w = [w_qkv] + [over_head(w_qkv, j) for j in range(1, head_count)]

    slot = jnp.arange(groups, dtype=jnp.int32)[:, None]
    place_of = ((g - slot) % groups) * places + r
    position = s * half_len + place_of * piece + d * quarter + jnp.arange(quarter, dtype=jnp.int32)[None]
    mask_row = lax.dynamic_index_in_dim(mask_pos, g, 0, keepdims=False)
    cot = lax.dynamic_index_in_dim(cot_rows, g, 0, keepdims=False)
    pick = (position.reshape(rows)[:, None] == mask_row[None]).astype(bf16)
    grad_out = jnp.dot(pick, cot, preferred_element_type=f32)

    attn_out = dot(attn_t, out_w, TN)
    resid = dense_in.astype(f32)
    first_sum = resid + attn_out
    normed_f, first_pull = jax.vjp(layer_norm, first_sum, norm_gain[0], norm_bias[0])
    normed = normed_f.astype(bf16)
    pre = dot(normed, up_t, NT)
    hidden_f, gelu_pull = jax.vjp(gelu_exact, pre)
    hidden = hidden_f.astype(bf16)
    second_sum = normed.astype(f32) + dot(hidden, down, NN)
    result, second_pull = jax.vjp(layer_norm, second_sum, norm_gain[1], norm_bias[1])

    grad_second, gain_second, bias_second = second_pull(grad_out)
    grad_ffn = grad_second.astype(bf16)
    grad_pre = gelu_pull(dot(grad_ffn, down, NT))[0].astype(bf16)
    grad_normed = grad_second + dot(grad_pre, up_t, NN)
    grad_first, gain_first, bias_first = first_pull(grad_normed)
    grad_attn = grad_first.astype(bf16)
    grad_est = dot(out_w, grad_attn, NT).astype(bf16)
    est_parts = [grad_est[j * head_width : (j + 1) * head_width] for j in range(head_count)]
    grad = jnp.concatenate(
        [est_parts[0]] + [over_head(est_parts[j], j) for j in range(1, head_count)], axis=1
    )

    grad_o = over_seq(grad)
    grad_z = over_place(grad)
    grad_zo = over_seq(grad_z)
    part, dq, dq_o = query_backward(
        signed, signed_t, bits, q, grad, q_o, grad_o, tables, None, f32, bf16
    )
    grad_tables, dq_z, dq_zo = query_backward(
        signed, signed_t, bits, q_z, grad_z, q_zo, grad_zo, tables, part, bf16, bf16
    )
    dkv_z, dkv_zo = key_backward(signed, signed_t, bits, kv_z, kv_zo, grad_tables, bf16, bf16)
    dkv, dkv_o = key_backward(signed, signed_t, bits, kv, kv_o, grad_tables, f32, bf16)
    grad_q = to_owner(dq, dq_o, dq_z, dq_zo).astype(bf16)
    grad_kv = to_owner(dkv, dkv_o, dkv_z, dkv_zo).astype(bf16)
    grad_qkv = jnp.concatenate([grad_q[None], grad_kv])

    grad_in = grad_first
    for j in range(head_count):
        block = grad_qkv[:, :, j * rows : (j + 1) * rows]
        if j:
            block = over_head(block, j)
        grad_in = grad_in + jnp.einsum("cel,cde->ld", block, qkv_w[j], preferred_element_type=f32)

    def home(dense):
        dense = dense.reshape(groups, quarter, width)
        parts = [dense[0]] + [over_group(dense[k], groups - k) for k in range(1, groups)]
        table = [jnp.stack(parts)]
        for j in range(1, head_count):
            table.append(jnp.stack([over_head(part, j) for part in parts]))
        table = jnp.stack(table)
        columns = []
        for q_at in range(head_count):
            block = lax.dynamic_index_in_dim(table, q_at ^ d, 0, keepdims=False)
            columns.append(
                jnp.stack(
                    [
                        lax.dynamic_index_in_dim(block, (at - g) % groups, 0, keepdims=False)
                        for at in range(seqs)
                    ],
                    axis=1,
                )
            )
        return jnp.concatenate(columns, axis=0)

    layer_out = home(result.astype(bf16))
    grad_inputs = home(grad_in.astype(bf16)).astype(f32)

    def over_hash_sum(x):
        half = x.shape[0] // 2
        mine = lax.dynamic_slice_in_dim(x, r * half, half, 0)
        other = over_place(lax.dynamic_slice_in_dim(x, (1 - r) * half, half, 0))
        total = mine.astype(f32) + other.astype(f32)
        total = sum(
            [total] + [over_group(total.astype(bf16), k).astype(f32) for k in range(1, groups)]
        ).astype(bf16)
        far = over_place(total)
        first, second = jnp.where(r == 0, total, far), jnp.where(r == 0, far, total)
        return jnp.concatenate([first, second], axis=0)

    def reduce_weights(parts):
        half = parts.shape[1] // 2
        parts = parts.astype(bf16)
        mine = lax.dynamic_slice_in_dim(parts, s * half, half, 1)
        other = over_seq(lax.dynamic_slice_in_dim(parts, (1 - s) * half, half, 1))
        chip = (mine.astype(f32) + other.astype(f32)).astype(bf16)
        total = sum([chip[0].astype(f32)] + [over_head(chip[j], j).astype(f32) for j in range(1, 4)])
        total = over_hash_sum(total.astype(bf16))
        return halves(total, over_seq(total)).astype(f32)

    grad_down = dot(hidden, grad_ffn, TN).reshape(head_count, hidden_own, width)
    grad_up = dot(grad_pre, normed, TN).reshape(head_count, hidden_own, width)
    grad_out_w = dot(attn_t, grad_attn, NN).reshape(head_count, head_width, width)
    down_total = reduce_weights(grad_down)
    up_total = reduce_weights(grad_up)
    out_total = reduce_weights(grad_out_w)

    grad_w_qkv = jnp.einsum("ld,cel->cde", tokens, grad_qkv, preferred_element_type=f32)
    grad_w_qkv = grad_w_qkv.reshape(3 * width, head_width).astype(bf16)
    half = grad_w_qkv.shape[0] // 2
    mine = lax.dynamic_slice_in_dim(grad_w_qkv, s * half, half, 0)
    other = over_seq(lax.dynamic_slice_in_dim(grad_w_qkv, (1 - s) * half, half, 0))
    total = over_hash_sum((mine.astype(f32) + other.astype(f32)).astype(bf16))
    grad_w_qkv = halves(total, over_seq(total)).reshape(3, width, head_width).astype(f32)

    squares = jnp.stack([jnp.sum(resid * resid), jnp.sum(attn_out * attn_out), jnp.sum(first_sum * first_sum)])
    small = jnp.concatenate(
        [gain_first, gain_second, bias_first, bias_second, jnp.pad(squares, (0, width - 3))]
    ).reshape(5, width)
    small = small + over_seq(small)
    small = small + over_head(small, 1)
    small = small + over_head(small, 2)
    small = small + over_place(small)
    small = sum([small] + [over_group(small, k) for k in range(1, groups)])
    count = piece * seqs * width * hash_count * 2
    stream_rms = jnp.sqrt(small[4, :3] / count)
    share = width // head_count
    mine = lax.dynamic_slice_in_dim(small, d * share, share, 1)
    return (
        layer_out[None],
        grad_inputs[None],
        grad_w_qkv,
        out_total,
        up_total.T,
        down_total,
        mine[0:2],
        mine[2:4],
        stream_rms,
    )


def solution(mesh):
    placed = (
        P("seq", "hash", None, None),
        P(None, None, "head"),
        P("head", None),
        P(None, "head"),
        P("head", None),
        P(),
        P(),
        P("hash", None, None),
        P(),
        P(),
    )
    return jax.shard_map(
        shards,
        mesh=mesh,
        in_specs=placed,
        out_specs=(
            P("seq", "hash", None, None),
            P("seq", "hash", None, None),
            P(None, None, "head"),
            P("head", None),
            P(None, "head"),
            P("head", None),
            P(None, "head"),
            P(None, "head"),
            P(),
        ),
        check_vma=False,
    )
```

```python
from functools import partial

import jax
import jax.numpy as jnp
import numpy as np
from jax import lax
from jax.experimental import pallas as pl
from jax.experimental.pallas import tpu as pltpu
from jax.sharding import PartitionSpec as P

HEAD_DIM = 64
HASHES = 32
BITS = 8
SETS = 8
BUCKETS = 1 << BITS
ROWS = BUCKETS * SETS

bf16 = jnp.bfloat16
f32 = jnp.float32
NN = (((1,), (0,)), ((), ()))
NT = (((1,), (1,)), ((), ()))
TN = (((0,), (0,)), ((), ()))


def dot(a, b, dims):
    return lax.dot_general(a, b, dims, preferred_element_type=f32)


def sides(rows, planes):
    x = rows.astype(f32)
    inv = lax.rsqrt(jnp.sum(x * x, axis=0, keepdims=True) + 1e-6)
    proj = dot(planes, rows, NN) * (3.0 * inv)
    small = jnp.exp(-proj)
    upper = 1.0 / (1.0 + small)
    return inv, upper, small * upper


def products(upper, lower, first, count):
    out = None
    for i in range(first, first + count):
        lo, up = lower[SETS * i : SETS * (i + 1)], upper[SETS * i : SETS * (i + 1)]
        out = [lo, up] if out is None else [c * lo for c in out] + [c * up for c in out]
    return out


def half_codes(upper, lower):
    low = jnp.concatenate(products(upper, lower, 0, 4), axis=0).astype(bf16)
    high = [jnp.concatenate([a, a], axis=0).astype(bf16) for a in products(upper, lower, 4, 4)]
    return low, high


def code_chunk(low, high, first, count):
    return jnp.concatenate(
        [high[a] * low[16 * j : 16 * (j + 1)] for a in range(first, first + count) for j in range(8)],
        axis=0,
    )


def pull_back(rows, planes_t, inv, upper, sums):
    total = sums[BITS * SETS :][:SETS]
    grad_proj = sums[: BITS * SETS] - upper * jnp.concatenate([total] * BITS, axis=0)
    head = grad_proj.astype(bf16)
    tail = (grad_proj - head.astype(f32)).astype(bf16)
    grad_unit = dot(planes_t, jnp.concatenate([head, tail], axis=0), NN) * (3.0 * inv)
    x = rows.astype(f32)
    return grad_unit - x * (inv * inv * jnp.sum(x * grad_unit, axis=0, keepdims=True))


def both(a, b):
    return jnp.concatenate([a[...], b[...]], axis=1)


def key_kernel(planes, ka, va, kb, vb, *refs, chunk):
    start, out = (None, *refs) if len(refs) == 1 else refs
    _, upper, lower = sides(both(ka, kb), planes[...])
    low, high = half_codes(upper, lower)
    values = both(va, vb)
    for c in range(0, 16, chunk):
        at = slice(128 * c, 128 * (c + chunk))
        part = dot(code_chunk(low, high, c, chunk), values, NT)
        if start is not None:
            part = part + start[0, at, :]
        out[0, at, :] = part.astype(out.dtype)


def query_kernel(planes, qa, qb, tables, ea, eb, *, chunk):
    _, upper, lower = sides(both(qa, qb), planes[...])
    low, high = half_codes(upper, lower)
    width = qa.shape[1]
    acc = jnp.zeros((HEAD_DIM, 2 * width), f32)
    for c in range(0, 16, chunk):
        acc += dot(tables[0, 128 * c : 128 * (c + chunk), :], code_chunk(low, high, c, chunk), TN)
    acc = acc * (1.0 / HASHES)
    ea[...] = acc[:, :width].astype(ea.dtype)
    eb[...] = acc[:, width:].astype(eb.dtype)


def query_back_kernel(planes, planes_t, bits, qa, ga, qb, gb, tables, *refs, chunk):
    start, out, da, db = (None, *refs) if len(refs) == 3 else refs
    rows = both(qa, qb)
    inv, upper, lower = sides(rows, planes[...])
    low, high = half_codes(upper, lower)
    grad = both(ga, gb)
    width = qa.shape[1]
    sums = jnp.zeros((bits.shape[0], 2 * width), f32)
    for c in range(0, 16, chunk):
        at = slice(128 * c, 128 * (c + chunk))
        codes = code_chunk(low, high, c, chunk)
        part = dot(codes, grad, NT)
        if start is not None:
            part = (part + start[0, at, :]) * (1.0 / HASHES)
        out[0, at, :] = part.astype(out.dtype)
        weighted = dot(tables[0, at, :], grad, NN).astype(bf16) * codes
        sums += dot(bits[:, at], weighted, NN)
    back = pull_back(rows, planes_t[...], inv, upper, sums * (1.0 / HASHES))
    da[...] = back[:, :width].astype(da.dtype)
    db[...] = back[:, width:].astype(db.dtype)


def key_back_kernel(planes, planes_t, bits, ka, va, kb, vb, grad_tables, da, db, *, chunk):
    rows = both(ka, kb)
    inv, upper, lower = sides(rows, planes[...])
    low, high = half_codes(upper, lower)
    values = both(va, vb)
    width = ka.shape[1]
    sums = jnp.zeros((bits.shape[0], 2 * width), f32)
    grad_values = jnp.zeros((HEAD_DIM, 2 * width), f32)
    for c in range(0, 16, chunk):
        at = slice(128 * c, 128 * (c + chunk))
        codes = code_chunk(low, high, c, chunk)
        grad_values += dot(grad_tables[0, at, :], codes, TN)
        weighted = dot(grad_tables[0, at, :], values, NN).astype(bf16) * codes
        sums += dot(bits[:, at], weighted, NN)
    back = pull_back(rows, planes_t[...], inv, upper, sums)
    da[0] = back[:, :width].astype(da.dtype)
    db[0] = back[:, width:].astype(db.dtype)
    da[1] = grad_values[:, :width].astype(da.dtype)
    db[1] = grad_values[:, width:].astype(db.dtype)


def bit_rows():
    out = np.zeros((80, BUCKETS, SETS), np.float32)
    for t in range(SETS):
        for i in range(BITS):
            out[i * SETS + t, :, t] = (np.arange(BUCKETS) >> i) & 1
        out[BITS * SETS + t, :, t] = 1
    return jnp.asarray(out.reshape(80, ROWS), bf16)


def whole(*shape):
    return pl.BlockSpec(shape, lambda h: (0,) * len(shape))


def per_head(width, offset=0):
    return pl.BlockSpec((HEAD_DIM, width), lambda h: (h + offset, 0))


def table_spec():
    return pl.BlockSpec((1, ROWS, HEAD_DIM), lambda h: (h, 0, 0))


def call(kernel, heads, micros, name, in_specs, out_specs, out_shape):
    return pl.pallas_call(
        kernel,
        grid=(heads,),
        in_specs=in_specs,
        out_specs=out_specs,
        out_shape=out_shape,
        compiler_params=pltpu.CompilerParams(vmem_limit_bytes=48 << 20),
        cost_estimate=pl.CostEstimate(
            flops=int(micros * 1.1e9), bytes_accessed=4 << 20, transcendentals=0
        ),
        name=name,
    )


def key_tables(planes, kv_a, kv_b, start=None):
    heads, width = kv_a.shape[0] // (2 * HEAD_DIM), kv_a.shape[1]
    specs = [whole(64, 64)] + [per_head(width), per_head(width, heads)] * 2
    args = [planes, kv_a, kv_a, kv_b, kv_b]
    if start is not None:
        specs.append(table_spec())
        args.append(start)
    return call(
        partial(key_kernel, chunk=2),
        heads,
        10,
        "key_tables",
        specs,
        table_spec(),
        jax.ShapeDtypeStruct((heads, ROWS, HEAD_DIM), f32 if start is None else bf16),
    )(*args)


def query_estimates(planes, q_a, q_b, tables, kind_a, kind_b):
    heads, width = q_a.shape[0] // HEAD_DIM, q_a.shape[1]
    return call(
        partial(query_kernel, chunk=2),
        heads,
        7,
        "query_estimates",
        [whole(64, 64), per_head(width), per_head(width), table_spec()],
        [per_head(width), per_head(width)],
        [jax.ShapeDtypeStruct(q_a.shape, kind) for kind in (kind_a, kind_b)],
    )(planes, q_a, q_b, tables)


def query_backward(planes, planes_t, bits, q_a, g_a, q_b, g_b, tables, start, kind_a, kind_b):
    heads, width = q_a.shape[0] // HEAD_DIM, q_a.shape[1]
    specs = [whole(64, 64), whole(64, 128), whole(80, ROWS)] + [per_head(width)] * 4 + [table_spec()]
    args = [planes, planes_t, bits, q_a, g_a, q_b, g_b, tables]
    if start is not None:
        specs.append(table_spec())
        args.append(start)
    return call(
        partial(query_back_kernel, chunk=4),
        heads,
        20,
        "query_backward",
        specs,
        [table_spec(), per_head(width), per_head(width)],
        [jax.ShapeDtypeStruct((heads, ROWS, HEAD_DIM), f32 if start is None else bf16)]
        + [jax.ShapeDtypeStruct(q_a.shape, kind) for kind in (kind_a, kind_b)],
    )(*args)


def key_backward(planes, planes_t, bits, kv_a, kv_b, grad_tables, kind_a, kind_b):
    heads, width = kv_a.shape[0] // (2 * HEAD_DIM), kv_a.shape[1]
    pair = pl.BlockSpec((2, HEAD_DIM, width), lambda h: (0, h, 0))
    return call(
        partial(key_back_kernel, chunk=4),
        heads,
        18,
        "key_backward",
        [whole(64, 64), whole(64, 128), whole(80, ROWS)]
        + [per_head(width), per_head(width, heads)] * 2
        + [table_spec()],
        [pair, pair],
        [jax.ShapeDtypeStruct((2, heads * HEAD_DIM, width), kind) for kind in (kind_a, kind_b)],
    )(planes, planes_t, bits, kv_a, kv_a, kv_b, kv_b, grad_tables)


def norm(x):
    center = x - jnp.mean(x, axis=-1, keepdims=True)
    inv = lax.rsqrt(jnp.mean(center * center, axis=-1, keepdims=True) + 1e-5)
    return center * inv, inv


def norm_back(grad, unit, inv):
    return inv * (
        grad
        - jnp.mean(grad, axis=-1, keepdims=True)
        - unit * jnp.mean(grad * unit, axis=-1, keepdims=True)
    )


def column_sum(x):
    return jnp.sum(x, axis=0, keepdims=True)


def core_rows(core, ref, which):
    half = ref.shape[0] // 2
    at = core[0] if which == 0 else 1 - core[0]
    return ref[pl.ds(pl.multiple_of(at * half, 16), half), :]


def dense_kernel(core, x_in, grad_out, gain, bias, *refs):
    attn, weights = refs[0:4], refs[4:12]
    layer_out, grad_first_out, normed_out, hidden, grad_pre, grad_ffn_out, grad_attn_out = refs[12:19]
    estimates, small, slope = refs[19:23], refs[23], refs[24]
    part = hidden.shape[2]
    blocks = range(8)
    heads = jnp.concatenate([core_rows(core, attn[b // 2], b % 2) for b in blocks], axis=0)
    out_w = jnp.concatenate([weights[b][2 * part :, :] for b in blocks], axis=0)
    attn_out = dot(heads, out_w, TN)
    resid = x_in[...].astype(f32)
    first = resid + attn_out
    small[4:5, :] = column_sum(resid * resid)
    small[5:6, :] = column_sum(attn_out * attn_out)
    small[6:7, :] = column_sum(first * first)
    small[7:8, :] = jnp.zeros_like(small[7:8, :])
    unit_1, inv_1 = norm(first)
    normed = (unit_1 * gain[0:1, :] + bias[0:1, :]).astype(bf16)
    normed_out[...] = normed
    second = normed.astype(f32)
    for b in blocks:
        pre = dot(normed, weights[b][0:part, :], NT)
        below = 0.5 * (1.0 + lax.erf(pre * 0.7071067811865476))
        rows = (pre * below).astype(bf16)
        hidden[b] = rows
        slope[b] = below + pre * (0.3989422804014327 * jnp.exp(-0.5 * pre * pre))
        second = second + dot(rows, weights[b][part : 2 * part, :], NN)
    unit_2, inv_2 = norm(second)
    layer_out[...] = (unit_2 * gain[1:2, :] + bias[1:2, :]).astype(layer_out.dtype)
    grad = grad_out[...]
    small[1:2, :] = column_sum(grad * unit_2)
    small[3:4, :] = column_sum(grad)
    grad_second = norm_back(grad * gain[1:2, :], unit_2, inv_2)
    grad_ffn = grad_second.astype(bf16)
    grad_ffn_out[...] = grad_ffn
    grad_normed = grad_second
    for b in blocks:
        rows = (dot(grad_ffn, weights[b][part : 2 * part, :], NT) * slope[b]).astype(bf16)
        grad_pre[b] = rows
        grad_normed = grad_normed + dot(rows, weights[b][0:part, :], NN)
    small[0:1, :] = column_sum(grad_normed * unit_1)
    small[2:3, :] = column_sum(grad_normed)
    grad_first = norm_back(grad_normed * gain[0:1, :], unit_1, inv_1)
    grad_first_out[...] = grad_first
    grad_attn = grad_first.astype(bf16)
    grad_attn_out[...] = grad_attn
    for b in blocks:
        half = estimates[0].shape[0] // 2
        at = core[0] if b % 2 == 0 else 1 - core[0]
        estimates[b // 2][pl.ds(pl.multiple_of(at * half, 16), half), :] = dot(
            weights[b][2 * part :, :], grad_attn, NT
        ).astype(bf16)


def weight_grad_kernel(core, normed, hidden, grad_pre, grad_ffn, grad_attn, *refs):
    attn, outs = refs[0:4], refs[4:8]
    part = hidden.shape[2]
    for b in range(8):
        down_out, up = outs[b % 2], outs[2 + b % 2]
        down_out[b // 2, 0:part, :] = dot(hidden[b], grad_ffn[...], TN).astype(bf16)
        down_out[b // 2, part:, :] = dot(core_rows(core, attn[b // 2], b % 2), grad_attn[...], NN).astype(bf16)
        up[b // 2] = dot(grad_pre[b], normed[...], TN).astype(bf16)


def vmem(count):
    return [pl.BlockSpec(memory_space=pltpu.VMEM)] * count


def dense(core, x_in, grad_out, gain, bias, attn, weights):
    rows, width = x_in.shape
    part = (weights[0].shape[0] - attn[0].shape[0] // 2) // 2
    shape = jax.ShapeDtypeStruct
    out_shape = [
        shape((rows, width), bf16),
        shape((rows, width), f32),
        shape((rows, width), bf16),
        shape((8, rows, part), bf16),
        shape((8, rows, part), bf16),
        shape((rows, width), bf16),
        shape((rows, width), bf16),
        *[shape(attn[0].shape, bf16)] * 4,
        shape((8, width), f32),
    ]
    return pl.pallas_call(
        dense_kernel,
        in_specs=[pl.BlockSpec(memory_space=pltpu.SMEM)] + vmem(16),
        out_specs=vmem(12),
        out_shape=out_shape,
        scratch_shapes=[pltpu.VMEM((8, rows, part), f32)],
        compiler_params=pltpu.CompilerParams(vmem_limit_bytes=56 << 20),
        cost_estimate=pl.CostEstimate(flops=18 * 10**9, bytes_accessed=4 << 20, transcendentals=0),
        name="dense",
    )(core, x_in, grad_out, gain, bias, *attn, *weights)


def weight_grads(core, normed, hidden, grad_pre, grad_ffn, grad_attn, attn):
    width, part = normed.shape[1], hidden.shape[2]
    shapes = [jax.ShapeDtypeStruct((4, part + attn[0].shape[0] // 2, width), bf16)] * 2
    shapes += [jax.ShapeDtypeStruct((4, part, width), bf16)] * 2
    return pl.pallas_call(
        weight_grad_kernel,
        in_specs=[pl.BlockSpec(memory_space=pltpu.SMEM)] + vmem(9),
        out_specs=vmem(4),
        out_shape=shapes,
        compiler_params=pltpu.CompilerParams(vmem_limit_bytes=56 << 20),
        cost_estimate=pl.CostEstimate(flops=7 * 10**9, bytes_accessed=4 << 20, transcendentals=0),
        name="weight_grads",
    )(core, normed, hidden, grad_pre, grad_ffn, grad_attn, *attn)


def after(x, *others):
    return lax.optimization_barrier((x, *others))[0]


def add(a, *others):
    return sum([b.astype(f32) for b in others], a.astype(f32))


def shards(
    inputs,
    w_qkv,
    w_out,
    up_weight,
    down_weight,
    norm_gain,
    norm_bias,
    planes,
    mask_pos,
    cot_rows,
):
    own = inputs[0]
    piece, seqs, width = own.shape
    hash_count, head_count = lax.axis_size("hash"), lax.axis_size("head")
    groups, places = seqs, hash_count // seqs
    assert places == 2 and lax.axis_size("seq") == 2 and head_count == 4
    assert planes.shape[0] * hash_count == 4 * SETS
    quarter = piece // head_count
    rows = groups * quarter
    half_len = piece * hash_count
    head_width = w_out.shape[0]
    hidden_own = down_weight.shape[0]
    n_tokens = head_count * rows
    hash_id, d, s = lax.axis_index("hash"), lax.axis_index("head"), lax.axis_index("seq")
    g, r = hash_id // places, hash_id % places

    def over_seq(x):
        return lax.ppermute(x, "seq", [(0, 1), (1, 0)])

    def over_place(x):
        return lax.ppermute(x, "hash", [(h, h ^ 1) for h in range(hash_count)])

    def over_group(x, k):
        moves = [(h, ((h // places + k) % groups) * places + h % places) for h in range(hash_count)]
        return lax.ppermute(x, "hash", moves)

    def over_head(x, j):
        return lax.ppermute(x, "head", [(h, h ^ j) for h in range(head_count)])

    def seq_rows(block, index):
        return lax.dynamic_index_in_dim(block, index % seqs, 1, keepdims=False)

    my_quarter = lax.dynamic_slice_in_dim(own, d * quarter, quarter, 0)
    arrived = [over_group(seq_rows(my_quarter, g + k), k) for k in range(1, groups)]

    signed = (2 * planes - 1).astype(bf16)
    if planes.shape[0] == SETS and groups == 2:
        moves = [
            ((2 * rr + ss) * 2 + gg, (gg * places + rr) * 2 + ss)
            for gg in range(2)
            for rr in range(2)
            for ss in range(2)
        ]
        signed = lax.ppermute(signed, ("hash", "seq"), moves)
    else:
        signed = lax.all_gather(signed, "hash", axis=0, tiled=True)
        signed = lax.dynamic_slice_in_dim(signed, (r * 2 + s) * SETS, SETS, 0)
    signed = signed.transpose(1, 0, 2).reshape(BITS * SETS, HEAD_DIM)
    signed_t = jnp.concatenate([signed.T, signed.T], axis=1)
    bits = bit_rows()

    dense_in = jnp.stack([seq_rows(my_quarter, g)] + arrived)
    blocks = [dense_in]
    for j in range(1, head_count):
        here = seq_rows(lax.dynamic_slice_in_dim(own, (d ^ j) * quarter, quarter, 0), g)
        blocks.append(jnp.concatenate([here[None], over_head(dense_in[1:], j)]))
    tokens = jnp.stack(blocks).reshape(n_tokens, width)
    dense_in = dense_in.reshape(rows, width)

    def project(w):
        return jnp.einsum("cde,ld->cel", w, tokens, preferred_element_type=f32).astype(bf16)

    kv = project(w_qkv[1:]).reshape(2 * head_width, n_tokens)
    q = project(w_qkv[:1]).reshape(head_width, n_tokens)
    kv_z = over_place(kv)
    kv_o = over_seq(kv)
    q_o = over_seq(q)
    q_z = over_place(after(q, kv_o))

    def core_half(at):
        cut = hidden_own // 2
        out_cut = head_width // 2
        return jnp.concatenate(
            [
                lax.dynamic_slice_in_dim(up_weight, at * cut, cut, 1).T,
                lax.dynamic_slice_in_dim(down_weight, at * cut, cut, 0),
                lax.dynamic_slice_in_dim(w_out, at * out_cut, out_cut, 0),
            ],
            axis=0,
        )

    weights = [core_half(s), core_half(1 - s)]
    my_half = after(weights[0], tokens)
    fetched = [over_head(my_half, j) for j in range(1, head_count)]
    for block in fetched:
        weights += [block, over_seq(block)]
    qkv_cut = width // 2
    qkv_half = lax.dynamic_slice_in_dim(w_qkv, s * qkv_cut, qkv_cut, 1)
    qkv_half = after(qkv_half, *weights)
    qkv_blocks = [over_head(qkv_half, j) for j in range(1, head_count)]
    qkv_far = [over_seq(block) for block in qkv_blocks]
    qkv_near = [lax.dynamic_slice_in_dim(w_qkv, s * qkv_cut, qkv_cut, 1)] + qkv_blocks
    qkv_far = [lax.dynamic_slice_in_dim(w_qkv, (1 - s) * qkv_cut, qkv_cut, 1)] + qkv_far

    slot = jnp.arange(groups, dtype=jnp.int32)[:, None]
    place_of = ((g - slot) % groups) * places + r
    position = s * half_len + place_of * piece + d * quarter + jnp.arange(quarter, dtype=jnp.int32)[None]
    mask_row = lax.dynamic_index_in_dim(mask_pos, g, 0, keepdims=False)
    cot = lax.dynamic_index_in_dim(cot_rows, g, 0, keepdims=False)
    pick = (position.reshape(rows)[:, None] == mask_row[None]).astype(bf16)
    grad_out = jnp.dot(pick, cot, preferred_element_type=f32)

    kv_zo = over_seq(kv_z)
    q_zo = over_seq(q_z)
    tables = key_tables(signed, kv, kv_o)
    tables = key_tables(signed, after(kv_z, grad_out), kv_zo, tables)

    e_z, e_zo = query_estimates(signed, q_z, q_zo, tables, bf16, bf16)
    e_far = add(e_z, over_seq(e_zo)).astype(bf16)
    e_far = over_place(e_far)
    e, e_o = query_estimates(signed, q, q_o, tables, f32, bf16)
    attn = add(e, over_seq(e_o), e_far).astype(bf16)

    def to_dense(block):
        parts = [block[..., j * rows : (j + 1) * rows] for j in range(head_count)]
        return [parts[0]] + [over_head(parts[j], j) for j in range(1, head_count)]

    attn_parts = to_dense(attn)

    core = s.astype(jnp.int32).reshape(1)
    (layer_rows, grad_first, normed, hidden, grad_pre, grad_ffn, grad_attn, *rest) = dense(
        core, dense_in, grad_out, norm_gain, norm_bias, attn_parts, weights
    )
    est_parts, small = rest[:4], rest[4]
    grad = jnp.concatenate(
        [est_parts[0]] + [over_head(est_parts[j], j) for j in range(1, head_count)], axis=1
    )
    mine_a, other_a, mine_b, other_b = weight_grads(
        core, normed, hidden, grad_pre, grad_ffn, grad_attn, attn_parts
    )

    grad_z = over_place(grad)
    grad_o = over_seq(grad)
    grad_zo = over_seq(grad_z)
    swap_a = over_seq(after(other_a, grad_o))
    swap_b = over_seq(after(other_b, grad_o))
    part, dq, dq_o = query_backward(
        signed, signed_t, bits, q, grad, q_o, grad_o, tables, None, f32, bf16
    )
    chip_a = add(mine_a, swap_a).astype(bf16)
    chip_b = add(mine_b, swap_b).astype(bf16)

    a_far = over_head(jnp.stack([chip_a[1], chip_a[3]]), 1)
    b_far = over_head(jnp.stack([chip_b[2], chip_b[3]]), 2)
    grad_tables, dq_z, dq_zo = query_backward(
        signed, signed_t, bits, after(q_z, chip_a, chip_b), grad_z, q_zo, grad_zo, tables, part, bf16, bf16
    )
    a_two = [add(chip_a[0], a_far[0]), add(chip_a[2], a_far[1]).astype(bf16)]
    b_two = [add(chip_b[0], b_far[0]), add(chip_b[1], b_far[1]).astype(bf16)]
    a_last = over_head(a_two[1], 2)
    b_last = over_head(b_two[1], 1)
    dkv_z, dkv_zo = key_backward(
        signed, signed_t, bits, after(kv_z, a_two[1], b_two[1]), kv_zo, grad_tables, bf16, bf16
    )
    dkv_far = add(dkv_z, over_seq(dkv_zo)).astype(bf16)
    dkv_far = over_place(dkv_far)
    a_sum = add(a_two[0], a_last).astype(bf16)
    b_sum = add(b_two[0], b_last).astype(bf16)
    dq_far = over_place(add(dq_z, over_seq(dq_zo)).astype(bf16))
    grad_q = add(dq, over_seq(dq_o), dq_far).astype(bf16)
    dkv, dkv_o = key_backward(
        signed, signed_t, bits, after(kv, a_sum, b_sum), kv_o, grad_tables, f32, bf16
    )
    grad_kv = add(dkv, over_seq(dkv_o), dkv_far).astype(bf16)
    q_parts, kv_parts = to_dense(grad_q), to_dense(grad_kv)

    near, far = 0.0, 0.0
    for j in range(head_count):
        block = jnp.concatenate([q_parts[j][None], kv_parts[j]])
        near = near + jnp.einsum("cel,cde->ld", block, qkv_near[j], preferred_element_type=f32)
        far = far + jnp.einsum("cel,cde->ld", block, qkv_far[j], preferred_element_type=f32)
    grad_in = grad_first + jnp.concatenate(
        [jnp.where(s == 0, near, far), jnp.where(s == 0, far, near)], axis=1
    )

    def home(dense_rows):
        dense_rows = dense_rows.reshape(groups, quarter, width)
        parts = [dense_rows[0]] + [over_group(dense_rows[k], groups - k) for k in range(1, groups)]
        parts = jnp.stack(parts)
        table = jnp.stack([parts] + [over_head(parts, j) for j in range(1, head_count)])
        columns = []
        for q_at in range(head_count):
            block = lax.dynamic_index_in_dim(table, q_at ^ d, 0, keepdims=False)
            columns.append(
                jnp.stack(
                    [
                        lax.dynamic_index_in_dim(block, (at - g) % groups, 0, keepdims=False)
                        for at in range(seqs)
                    ],
                    axis=1,
                )
            )
        return jnp.concatenate(columns, axis=0)

    layer_out = home(after(layer_rows, grad_tables))
    grad_inputs = home(grad_in.astype(bf16)).astype(f32)

    def in_halves(index, mine, other):
        first = jnp.where(index == 0, mine, other)
        second = jnp.where(index == 0, other, mine)
        return jnp.concatenate([first, second], axis=0)

    def over_hash_sum(x):
        half = x.shape[0] // 2
        mine = lax.dynamic_slice_in_dim(x, r * half, half, 0)
        total = add(mine, over_place(lax.dynamic_slice_in_dim(x, (1 - r) * half, half, 0)))
        sent = total.astype(bf16)
        total = add(total, *[over_group(sent, k) for k in range(1, groups)]).astype(bf16)
        return in_halves(r, total, over_place(total))

    a_sum, b_sum = over_hash_sum(a_sum), over_hash_sum(b_sum)
    a_other, b_other = over_seq(a_sum), over_seq(b_sum)
    cut = hidden_own // 2
    grad_w_down = in_halves(s, a_sum[:cut], a_other[:cut]).astype(f32)
    grad_w_out = in_halves(s, a_sum[cut:], a_other[cut:]).astype(f32)
    grad_w_up = in_halves(s, b_sum, b_other).T.astype(f32)

    grad_qkv = jnp.concatenate([grad_q[None], grad_kv])
    grad_w_qkv = jnp.einsum("ld,cel->cde", tokens, grad_qkv, preferred_element_type=f32)
    grad_w_qkv = grad_w_qkv.reshape(3 * width, head_width).astype(bf16)
    half = grad_w_qkv.shape[0] // 2
    mine = lax.dynamic_slice_in_dim(grad_w_qkv, s * half, half, 0)
    other = over_seq(lax.dynamic_slice_in_dim(grad_w_qkv, (1 - s) * half, half, 0))
    total = over_hash_sum(add(mine, other).astype(bf16))
    grad_w_qkv = in_halves(s, total, over_seq(total)).reshape(3, width, head_width).astype(f32)

    small = after(small, part)
    small = small + over_seq(small)
    small = small + over_head(small, 1)
    small = small + over_head(after(small, grad_tables), 2)
    small = small + over_place(small)
    small = after(small, dkv_z)
    small = sum([small] + [over_group(small, k) for k in range(1, groups)])
    count = piece * seqs * width * hash_count * 2
    stream_rms = jnp.sqrt(jnp.sum(small[4:7], axis=1) / count)
    share = width // head_count
    norm_grads = lax.dynamic_slice_in_dim(small, d * share, share, 1)
    return (
        layer_out[None],
        grad_inputs[None],
        grad_w_qkv,
        grad_w_out,
        grad_w_up,
        grad_w_down,
        norm_grads[0:2],
        norm_grads[2:4],
        stream_rms,
    )


def solution(mesh):
    placed = (
        P("seq", "hash", None, None),
        P(None, None, "head"),
        P("head", None),
        P(None, "head"),
        P("head", None),
        P(),
        P(),
        P("hash", None, None),
        P(),
        P(),
    )
    return jax.shard_map(
        shards,
        mesh=mesh,
        in_specs=placed,
        out_specs=(
            P("seq", "hash", None, None),
            P("seq", "hash", None, None),
            P(None, None, "head"),
            P("head", None),
            P(None, "head"),
            P("head", None),
            P(None, "head"),
            P(None, "head"),
            P(),
        ),
        check_vma=False,
    )
```

```python
from functools import partial

import jax
import jax.numpy as jnp
import numpy as np
from jax import lax
from jax.experimental import pallas as pl
from jax.experimental.pallas import tpu as pltpu
from jax.sharding import PartitionSpec as P

HEAD_DIM = 64
HASHES = 32
BITS = 8
SETS = 8
BUCKETS = 1 << BITS
ROWS = BUCKETS * SETS

bf16 = jnp.bfloat16
f32 = jnp.float32
NN = (((1,), (0,)), ((), ()))
NT = (((1,), (1,)), ((), ()))
TN = (((0,), (0,)), ((), ()))


def dot(a, b, dims):
    return lax.dot_general(a, b, dims, preferred_element_type=f32)


def sides(rows, planes):
    x = rows.astype(f32)
    inv = lax.rsqrt(jnp.sum(x * x, axis=0, keepdims=True) + 1e-6)
    proj = dot(planes, rows, NN) * (3.0 * inv)
    small = jnp.exp(-proj)
    upper = 1.0 / (1.0 + small)
    return inv, upper, small * upper


def products(upper, lower, first, count):
    out = None
    for i in range(first, first + count):
        lo, up = lower[SETS * i : SETS * (i + 1)], upper[SETS * i : SETS * (i + 1)]
        out = [lo, up] if out is None else [c * lo for c in out] + [c * up for c in out]
    return out


def half_codes(upper, lower):
    low = jnp.concatenate(products(upper, lower, 0, 4), axis=0).astype(bf16)
    high = [jnp.concatenate([a, a], axis=0).astype(bf16) for a in products(upper, lower, 4, 4)]
    return low, high


def code_chunk(low, high, first, count):
    return jnp.concatenate(
        [high[a] * low[16 * j : 16 * (j + 1)] for a in range(first, first + count) for j in range(8)],
        axis=0,
    )


def pull_back(rows, planes_t, inv, upper, sums):
    total = sums[BITS * SETS :][:SETS]
    grad_proj = sums[: BITS * SETS] - upper * jnp.concatenate([total] * BITS, axis=0)
    head = grad_proj.astype(bf16)
    tail = (grad_proj - head.astype(f32)).astype(bf16)
    grad_unit = dot(planes_t, jnp.concatenate([head, tail], axis=0), NN) * (3.0 * inv)
    x = rows.astype(f32)
    return grad_unit - x * (inv * inv * jnp.sum(x * grad_unit, axis=0, keepdims=True))


def both(a, b):
    return jnp.concatenate([a[...], b[...]], axis=1)


def key_kernel(planes, ka, va, kb, vb, *refs, chunk):
    start, out = (None, *refs) if len(refs) == 1 else refs
    _, upper, lower = sides(both(ka, kb), planes[...])
    low, high = half_codes(upper, lower)
    values = both(va, vb)
    for c in range(0, 16, chunk):
        at = slice(128 * c, 128 * (c + chunk))
        part = dot(code_chunk(low, high, c, chunk), values, NT)
        if start is not None:
            part = part + start[0, at, :]
        out[0, at, :] = part.astype(out.dtype)


def query_kernel(planes, q, tables, out, *, chunk):
    _, upper, lower = sides(q[...], planes[...])
    low, high = half_codes(upper, lower)
    acc = jnp.zeros((HEAD_DIM, q.shape[1]), f32)
    for c in range(0, 16, chunk):
        acc += dot(tables[0, 128 * c : 128 * (c + chunk), :], code_chunk(low, high, c, chunk), TN)
    out[...] = (acc * (1.0 / HASHES)).astype(out.dtype)


def query_back_kernel(planes, planes_t, bits, qa, ga, qb, gb, tables, *refs, chunk):
    start, out, da, db = (None, *refs) if len(refs) == 3 else refs
    rows = both(qa, qb)
    inv, upper, lower = sides(rows, planes[...])
    low, high = half_codes(upper, lower)
    grad = both(ga, gb)
    width = qa.shape[1]
    sums = jnp.zeros((bits.shape[0], 2 * width), f32)
    for c in range(0, 16, chunk):
        at = slice(128 * c, 128 * (c + chunk))
        codes = code_chunk(low, high, c, chunk)
        part = dot(codes, grad, NT)
        if start is not None:
            part = (part + start[0, at, :]) * (1.0 / HASHES)
        out[0, at, :] = part.astype(out.dtype)
        weighted = dot(tables[0, at, :], grad, NN).astype(bf16) * codes
        sums += dot(bits[:, at], weighted, NN)
    back = pull_back(rows, planes_t[...], inv, upper, sums * (1.0 / HASHES))
    da[...] = back[:, :width].astype(da.dtype)
    db[...] = back[:, width:].astype(db.dtype)


def key_back_kernel(planes, planes_t, bits, keys, vals, grad_tables, out, *, chunk):
    rows = keys[...]
    inv, upper, lower = sides(rows, planes[...])
    low, high = half_codes(upper, lower)
    values = vals[...]
    width = keys.shape[1]
    sums = jnp.zeros((bits.shape[0], width), f32)
    grad_values = jnp.zeros((HEAD_DIM, width), f32)
    for c in range(0, 16, chunk):
        at = slice(128 * c, 128 * (c + chunk))
        codes = code_chunk(low, high, c, chunk)
        grad_values += dot(grad_tables[0, at, :], codes, TN)
        weighted = dot(grad_tables[0, at, :], values, NN).astype(bf16) * codes
        sums += dot(bits[:, at], weighted, NN)
    out[0] = pull_back(rows, planes_t[...], inv, upper, sums).astype(out.dtype)
    out[1] = grad_values.astype(out.dtype)


def bit_rows():
    out = np.zeros((80, BUCKETS, SETS), np.float32)
    for t in range(SETS):
        for i in range(BITS):
            out[i * SETS + t, :, t] = (np.arange(BUCKETS) >> i) & 1
        out[BITS * SETS + t, :, t] = 1
    return jnp.asarray(out.reshape(80, ROWS), bf16)


def whole(*shape):
    return pl.BlockSpec(shape, lambda h: (0,) * len(shape))


def per_head(width, offset=0):
    return pl.BlockSpec((HEAD_DIM, width), lambda h: (h + offset, 0))


def table_spec():
    return pl.BlockSpec((1, ROWS, HEAD_DIM), lambda h: (h, 0, 0))


def call(kernel, heads, micros, name, in_specs, out_specs, out_shape):
    return pl.pallas_call(
        kernel,
        grid=(heads,),
        in_specs=in_specs,
        out_specs=out_specs,
        out_shape=out_shape,
        compiler_params=pltpu.CompilerParams(vmem_limit_bytes=48 << 20),
        cost_estimate=pl.CostEstimate(
            flops=int(micros * 1.1e9), bytes_accessed=1 << 20, transcendentals=0
        ),
        name=name,
    )


def key_tables(planes, kv_a, kv_b, start=None):
    heads, width = kv_a.shape[0] // (2 * HEAD_DIM), kv_a.shape[1]
    specs = [whole(64, 64)] + [per_head(width), per_head(width, heads)] * 2
    args = [planes, kv_a, kv_a, kv_b, kv_b]
    if start is not None:
        specs.append(table_spec())
        args.append(start)
    return call(
        partial(key_kernel, chunk=2),
        heads,
        10,
        "key_tables",
        specs,
        table_spec(),
        jax.ShapeDtypeStruct((heads, ROWS, HEAD_DIM), f32 if start is None else bf16),
    )(*args)


def query_estimates(planes, q, tables, kind):
    heads, width = q.shape[0] // HEAD_DIM, q.shape[1]
    return call(
        partial(query_kernel, chunk=2),
        heads,
        4,
        "query_estimates",
        [whole(64, 64), per_head(width), table_spec()],
        per_head(width),
        jax.ShapeDtypeStruct(q.shape, kind),
    )(planes, q, tables)


def query_backward(planes, planes_t, bits, q_a, g_a, q_b, g_b, tables, start, kind_a, kind_b):
    heads, width = q_a.shape[0] // HEAD_DIM, q_a.shape[1]
    specs = [whole(64, 64), whole(64, 128), whole(80, ROWS)] + [per_head(width)] * 4 + [table_spec()]
    args = [planes, planes_t, bits, q_a, g_a, q_b, g_b, tables]
    if start is not None:
        specs.append(table_spec())
        args.append(start)
    return call(
        partial(query_back_kernel, chunk=4),
        heads,
        20,
        "query_backward",
        specs,
        [table_spec(), per_head(width), per_head(width)],
        [jax.ShapeDtypeStruct((heads, ROWS, HEAD_DIM), f32 if start is None else bf16)]
        + [jax.ShapeDtypeStruct(q_a.shape, kind) for kind in (kind_a, kind_b)],
    )(*args)


def key_backward(planes, planes_t, bits, kv, grad_tables, kind):
    heads, width = kv.shape[0] // (2 * HEAD_DIM), kv.shape[1]
    return call(
        partial(key_back_kernel, chunk=4),
        heads,
        9,
        "key_backward",
        [whole(64, 64), whole(64, 128), whole(80, ROWS)]
        + [per_head(width), per_head(width, heads), table_spec()],
        pl.BlockSpec((2, HEAD_DIM, width), lambda h: (0, h, 0)),
        jax.ShapeDtypeStruct((2, heads * HEAD_DIM, width), kind),
    )(planes, planes_t, bits, kv, kv, grad_tables)


def norm(x):
    center = x - jnp.mean(x, axis=-1, keepdims=True)
    inv = lax.rsqrt(jnp.mean(center * center, axis=-1, keepdims=True) + 1e-5)
    return center * inv, inv


def norm_back(grad, unit, inv):
    return inv * (
        grad
        - jnp.mean(grad, axis=-1, keepdims=True)
        - unit * jnp.mean(grad * unit, axis=-1, keepdims=True)
    )


def column_sum(x):
    return jnp.sum(x, axis=0, keepdims=True)


def core_rows(core, ref, which):
    half = ref.shape[0] // 2
    at = core[0] if which == 0 else 1 - core[0]
    return ref[pl.ds(pl.multiple_of(at * half, 16), half), :]


def dense_kernel(core, x_in, grad_out, gain, bias, *refs):
    attn, weights = refs[0:4], refs[4:12]
    layer_out, grad_first_out, normed_out, hidden, grad_pre, grad_ffn_out, grad_attn_out = refs[12:19]
    estimates, small, slope = refs[19:23], refs[23], refs[24]
    part = hidden.shape[2]
    blocks = range(8)
    heads = jnp.concatenate([core_rows(core, attn[b // 2], b % 2) for b in blocks], axis=0)
    out_w = jnp.concatenate([weights[b][2 * part :, :] for b in blocks], axis=0)
    attn_out = dot(heads, out_w, TN)
    resid = x_in[...].astype(f32)
    first = resid + attn_out
    small[4:5, :] = column_sum(resid * resid)
    small[5:6, :] = column_sum(attn_out * attn_out)
    small[6:7, :] = column_sum(first * first)
    small[7:8, :] = jnp.zeros_like(small[7:8, :])
    unit_1, inv_1 = norm(first)
    normed = (unit_1 * gain[0:1, :] + bias[0:1, :]).astype(bf16)
    normed_out[...] = normed
    second = normed.astype(f32)
    for b in blocks:
        pre = dot(normed, weights[b][0:part, :], NT)
        below = 0.5 * (1.0 + lax.erf(pre * 0.7071067811865476))
        rows = (pre * below).astype(bf16)
        hidden[b] = rows
        slope[b] = below + pre * (0.3989422804014327 * jnp.exp(-0.5 * pre * pre))
        second = second + dot(rows, weights[b][part : 2 * part, :], NN)
    unit_2, inv_2 = norm(second)
    layer_out[...] = (unit_2 * gain[1:2, :] + bias[1:2, :]).astype(layer_out.dtype)
    grad = grad_out[...]
    small[1:2, :] = column_sum(grad * unit_2)
    small[3:4, :] = column_sum(grad)
    grad_second = norm_back(grad * gain[1:2, :], unit_2, inv_2)
    grad_ffn = grad_second.astype(bf16)
    grad_ffn_out[...] = grad_ffn
    grad_normed = grad_second
    for b in blocks:
        rows = (dot(grad_ffn, weights[b][part : 2 * part, :], NT) * slope[b]).astype(bf16)
        grad_pre[b] = rows
        grad_normed = grad_normed + dot(rows, weights[b][0:part, :], NN)
    small[0:1, :] = column_sum(grad_normed * unit_1)
    small[2:3, :] = column_sum(grad_normed)
    grad_first = norm_back(grad_normed * gain[0:1, :], unit_1, inv_1)
    grad_first_out[...] = grad_first
    grad_attn = grad_first.astype(bf16)
    grad_attn_out[...] = grad_attn
    for b in blocks:
        half = estimates[0].shape[0] // 2
        at = core[0] if b % 2 == 0 else 1 - core[0]
        estimates[b // 2][pl.ds(pl.multiple_of(at * half, 16), half), :] = dot(
            weights[b][2 * part :, :], grad_attn, NT
        ).astype(bf16)


def weight_grad_kernel(core, normed, hidden, grad_pre, grad_ffn, grad_attn, small, *refs):
    attn, outs = refs[0:4], refs[4:8]
    part = hidden.shape[2]
    sums = jnp.concatenate([small[...], jnp.zeros_like(small[...])], axis=0).astype(bf16)
    for b in range(8):
        down_out, up = outs[b % 2], outs[2 + b % 2]
        down_out[b // 2, 0:part, :] = dot(hidden[b], grad_ffn[...], TN).astype(bf16)
        heads = core_rows(core, attn[b // 2], b % 2)
        at = part + heads.shape[0]
        down_out[b // 2, part:at, :] = dot(heads, grad_attn[...], NN).astype(bf16)
        down_out[b // 2, at : at + 16, :] = sums
        down_out[b // 2, at + 16 :, :] = jnp.zeros_like(sums)
        up[b // 2] = dot(grad_pre[b], normed[...], TN).astype(bf16)


def vmem(count):
    return [pl.BlockSpec(memory_space=pltpu.VMEM)] * count


def dense(core, x_in, grad_out, gain, bias, attn, weights):
    rows, width = x_in.shape
    part = (weights[0].shape[0] - attn[0].shape[0] // 2) // 2
    shape = jax.ShapeDtypeStruct
    out_shape = [
        shape((rows, width), bf16),
        shape((rows, width), f32),
        shape((rows, width), bf16),
        shape((8, rows, part), bf16),
        shape((8, rows, part), bf16),
        shape((rows, width), bf16),
        shape((rows, width), bf16),
        *[shape(attn[0].shape, bf16)] * 4,
        shape((8, width), f32),
    ]
    return pl.pallas_call(
        dense_kernel,
        in_specs=[pl.BlockSpec(memory_space=pltpu.SMEM)] + vmem(16),
        out_specs=vmem(12),
        out_shape=out_shape,
        scratch_shapes=[pltpu.VMEM((8, rows, part), f32)],
        compiler_params=pltpu.CompilerParams(vmem_limit_bytes=56 << 20),
        cost_estimate=pl.CostEstimate(flops=18 * 10**9, bytes_accessed=1 << 20, transcendentals=0),
        name="dense",
    )(core, x_in, grad_out, gain, bias, *attn, *weights)


def weight_grads(core, normed, hidden, grad_pre, grad_ffn, grad_attn, small, attn):
    width, part = normed.shape[1], hidden.shape[2]
    shapes = [jax.ShapeDtypeStruct((4, part + attn[0].shape[0] // 2 + 32, width), bf16)] * 2
    shapes += [jax.ShapeDtypeStruct((4, part, width), bf16)] * 2
    return pl.pallas_call(
        weight_grad_kernel,
        in_specs=[pl.BlockSpec(memory_space=pltpu.SMEM)] + vmem(10),
        out_specs=vmem(4),
        out_shape=shapes,
        compiler_params=pltpu.CompilerParams(vmem_limit_bytes=56 << 20),
        cost_estimate=pl.CostEstimate(flops=9 * 10**9, bytes_accessed=1 << 20, transcendentals=0),
        name="weight_grads",
    )(core, normed, hidden, grad_pre, grad_ffn, grad_attn, small, *attn)


def after(x, *others):
    return lax.optimization_barrier((x, *others))[0]


def add(a, *others):
    return sum([b.astype(f32) for b in others], a.astype(f32))


def shards(
    inputs,
    w_qkv,
    w_out,
    up_weight,
    down_weight,
    norm_gain,
    norm_bias,
    planes,
    mask_pos,
    cot_rows,
):
    own = inputs[0]
    piece, seqs, width = own.shape
    hash_count, head_count = lax.axis_size("hash"), lax.axis_size("head")
    groups, places = seqs, hash_count // seqs
    assert places == 2 and lax.axis_size("seq") == 2 and head_count == 4
    assert planes.shape[0] * hash_count == 4 * SETS
    quarter = piece // head_count
    rows = groups * quarter
    half_len = piece * hash_count
    head_width = w_out.shape[0]
    hidden_own = down_weight.shape[0]
    n_tokens = head_count * rows
    hash_id, d, s = lax.axis_index("hash"), lax.axis_index("head"), lax.axis_index("seq")
    g, r = hash_id // places, hash_id % places

    def over_seq(x):
        return lax.ppermute(x, "seq", [(0, 1), (1, 0)])

    def over_place(x):
        return lax.ppermute(x, "hash", [(h, h ^ 1) for h in range(hash_count)])

    def over_group(x, k):
        moves = [(h, ((h // places + k) % groups) * places + h % places) for h in range(hash_count)]
        return lax.ppermute(x, "hash", moves)

    def over_head(x, j):
        return lax.ppermute(x, "head", [(h, h ^ j) for h in range(head_count)])

    def seq_rows(block, index):
        return lax.dynamic_index_in_dim(block, index % seqs, 1, keepdims=False)

    my_quarter = lax.dynamic_slice_in_dim(own, d * quarter, quarter, 0)
    arrived = [over_group(seq_rows(my_quarter, g + k), k) for k in range(1, groups)]

    signed = (2 * planes - 1).astype(bf16)
    if planes.shape[0] == SETS and groups == 2:
        moves = [
            ((2 * rr + ss) * 2 + gg, (gg * places + rr) * 2 + ss)
            for gg in range(2)
            for rr in range(2)
            for ss in range(2)
        ]
        signed = lax.ppermute(signed, ("hash", "seq"), moves)
    else:
        signed = lax.all_gather(signed, "hash", axis=0, tiled=True)
        signed = lax.dynamic_slice_in_dim(signed, (r * 2 + s) * SETS, SETS, 0)
    signed = signed.transpose(1, 0, 2).reshape(BITS * SETS, HEAD_DIM)
    signed_t = jnp.concatenate([signed.T, signed.T], axis=1)
    bits = bit_rows()

    dense_in = jnp.stack([seq_rows(my_quarter, g)] + arrived)
    blocks = [dense_in]
    for j in range(1, head_count):
        here = seq_rows(lax.dynamic_slice_in_dim(own, (d ^ j) * quarter, quarter, 0), g)
        blocks.append(jnp.concatenate([here[None], over_head(dense_in[1:], j)]))
    tokens = jnp.stack(blocks).reshape(n_tokens, width)
    dense_in = dense_in.reshape(rows, width)

    def project(w):
        return jnp.einsum("cde,ld->cel", w, tokens, preferred_element_type=f32).astype(bf16)

    kv = project(w_qkv[1:]).reshape(2 * head_width, n_tokens)
    q = project(w_qkv[:1]).reshape(head_width, n_tokens)
    kv_z = over_place(kv)
    kv_o = over_seq(kv)
    q_o = over_seq(q)
    q_z = over_place(after(q, kv_o))

    def core_half(at):
        cut = hidden_own // 2
        out_cut = head_width // 2
        return jnp.concatenate(
            [
                lax.dynamic_slice_in_dim(up_weight, at * cut, cut, 1).T,
                lax.dynamic_slice_in_dim(down_weight, at * cut, cut, 0),
                lax.dynamic_slice_in_dim(w_out, at * out_cut, out_cut, 0),
            ],
            axis=0,
        )

    weights = [core_half(s), core_half(1 - s)]
    my_half = after(weights[0], tokens)
    fetched = [over_head(my_half, j) for j in range(1, head_count)]

    slot = jnp.arange(groups, dtype=jnp.int32)[:, None]
    place_of = ((g - slot) % groups) * places + r
    position = s * half_len + place_of * piece + d * quarter + jnp.arange(quarter, dtype=jnp.int32)[None]
    mask_row = lax.dynamic_index_in_dim(mask_pos, g, 0, keepdims=False)
    cot = lax.dynamic_index_in_dim(cot_rows, g, 0, keepdims=False)
    pick = (position.reshape(rows)[:, None] == mask_row[None]).astype(bf16)
    grad_out = jnp.dot(pick, cot, preferred_element_type=f32)

    kv_zo = over_seq(kv_z)
    q_zo = over_seq(q_z)
    signed = after(signed, grad_out, weights[1])
    tables = key_tables(signed, kv, kv_o)
    tables = key_tables(signed, kv_z, kv_zo, tables)

    e_zo = query_estimates(signed, q_zo, tables, bf16)
    e_zo_moved = over_seq(e_zo)
    e_z = query_estimates(signed, after(q_z, e_zo), tables, bf16)
    e_far = add(e_z, after(e_zo_moved, e_z)).astype(bf16)
    e_o = query_estimates(signed, after(q_o, e_far), tables, bf16)
    e_far = over_place(e_far)
    e_o_moved = over_seq(e_o)
    fetched = [after(block, e_o) for block in fetched]
    e = query_estimates(signed, after(q, e_o, *fetched), tables, f32)
    for block in fetched:
        weights += [block, over_seq(block)]
    attn = add(e, after(e_o_moved, e), after(e_far, e)).astype(bf16)

    def to_dense(block):
        parts = [block[..., j * rows : (j + 1) * rows] for j in range(head_count)]
        return [parts[0]] + [over_head(parts[j], j) for j in range(1, head_count)]

    attn_parts = to_dense(attn)

    def away(dense_rows):
        dense_rows = dense_rows.reshape(groups, quarter, width)
        return jnp.stack(
            [dense_rows[0]] + [over_group(dense_rows[k], groups - k) for k in range(1, groups)]
        )

    core = s.astype(jnp.int32).reshape(1)
    (layer_rows, grad_first, normed, hidden, grad_pre, grad_ffn, grad_attn, *rest) = dense(
        core, dense_in, grad_out, norm_gain, norm_bias, attn_parts, weights
    )
    est_parts, small = rest[:4], rest[4]
    grad = jnp.concatenate(
        [est_parts[0]] + [over_head(est_parts[j], j) for j in range(1, head_count)], axis=1
    )
    mine_a, other_a, mine_b, other_b = weight_grads(
        core, normed, hidden, grad_pre, grad_ffn, grad_attn, small, attn_parts
    )

    grad_z = over_place(grad)
    grad_o = over_seq(grad)
    swap_a = over_seq(after(other_a, grad_o))
    swap_b = over_seq(after(other_b, grad_o))
    layer_moved = away(layer_rows)
    qkv_cut = width // 2
    qkv_near = [lax.dynamic_slice_in_dim(w_qkv, s * qkv_cut, qkv_cut, 1)]
    qkv_far = [lax.dynamic_slice_in_dim(w_qkv, (1 - s) * qkv_cut, qkv_cut, 1)]
    qkv_half = after(qkv_near[0], grad_o)
    qkv_near += [over_head(qkv_half, j) for j in range(1, head_count)]
    part, dq, dq_o = query_backward(
        signed, signed_t, bits, q, grad, q_o, after(grad_o, mine_a), tables, None, f32, bf16
    )

    grad_zo = over_seq(after(grad_z, part))
    chip_a = add(mine_a, after(swap_a, part)).astype(bf16)
    chip_b = add(mine_b, after(swap_b, part)).astype(bf16)
    qkv_near[1:] = [after(block, part) for block in qkv_near[1:]]
    layer_moved = after(layer_moved, part)
    a_out, b_out = jnp.stack([chip_a[1], chip_a[3]]), jnp.stack([chip_b[2], chip_b[3]])
    a_far, b_far = over_head(a_out, 1), over_head(b_out, 2)
    dq_o = over_seq(dq_o)
    q_gated = after(q_z, a_out, b_out, layer_moved, *qkv_near[1:])
    grad_tables, dq_z, dq_zo = query_backward(
        signed, signed_t, bits, q_gated, grad_z, q_zo, grad_zo, tables, part, bf16, bf16
    )

    dq_zo = over_seq(dq_zo)
    dq_own = add(dq, after(dq_o, dq_z))
    qkv_swaps = [over_seq(block) for block in qkv_near[1:]]
    dkv_zo = key_backward(signed, signed_t, bits, after(kv_zo, dq_own), grad_tables, bf16)

    dkv_zo_moved = over_seq(dkv_zo)
    qkv_far += [after(block, dkv_zo) for block in qkv_swaps]
    dq_far = add(dq_z, after(dq_zo, dkv_zo)).astype(bf16)
    a_far, b_far = after(a_far, dkv_zo), after(b_far, dkv_zo)
    a_two = [add(chip_a[0], a_far[0]), add(chip_a[2], a_far[1]).astype(bf16)]
    b_two = [add(chip_b[0], b_far[0]), add(chip_b[1], b_far[1]).astype(bf16)]
    kv_gated = after(kv_z, a_two[1], b_two[1], dq_far, *qkv_far)
    dkv_z = key_backward(signed, signed_t, bits, kv_gated, grad_tables, bf16)
    dq_far = over_place(dq_far)
    a_last, b_last = over_head(a_two[1], 2), over_head(b_two[1], 1)

    dkv_far = add(dkv_z, after(dkv_zo_moved, dkv_z)).astype(bf16)
    grad_q = add(dq_own, after(dq_far, dkv_z)).astype(bf16)
    dkv_o = key_backward(signed, signed_t, bits, after(kv_o, dkv_far, grad_q), grad_tables, bf16)
    dk_far, dv_far = over_place(dkv_far[0]), over_place(dkv_far[1])

    dkv_o_moved = over_seq(dkv_o)
    a_sum = add(a_two[0], after(a_last, dkv_o)).astype(bf16)
    b_sum = add(b_two[0], after(b_last, dkv_o)).astype(bf16)
    dk_far = after(dk_far, dkv_o)
    layer_moved = after(layer_moved, dkv_o)
    layer_moved = [layer_moved] + [over_head(layer_moved, j) for j in range(1, head_count)]
    dkv = key_backward(signed, signed_t, bits, after(kv, a_sum, b_sum, dk_far), grad_tables, f32)

    dkv_o_moved = after(dkv_o_moved, dkv)
    grad_k = add(dkv[0], dkv_o_moved[0], dk_far)
    grad_v = add(dkv[1], dkv_o_moved[1], after(dv_far, dkv))
    grad_qkv = jnp.stack([grad_q, grad_k.astype(bf16), grad_v.astype(bf16)])
    qkv_parts = to_dense(grad_qkv)

    near, far = 0.0, 0.0
    for j in range(head_count):
        block = qkv_parts[j]
        near = near + jnp.einsum("cel,cde->ld", block, qkv_near[j], preferred_element_type=f32)
        far = far + jnp.einsum("cel,cde->ld", block, qkv_far[j], preferred_element_type=f32)
    grad_in = grad_first + jnp.concatenate(
        [jnp.where(s == 0, near, far), jnp.where(s == 0, far, near)], axis=1
    )

    grad_moved = away(grad_in.astype(bf16))
    grad_moved = [grad_moved] + [over_head(grad_moved, j) for j in range(1, head_count)]

    def home(blocks):
        table = jnp.stack(blocks)
        columns = []
        for q_at in range(head_count):
            block = lax.dynamic_index_in_dim(table, q_at ^ d, 0, keepdims=False)
            columns.append(
                jnp.stack(
                    [
                        lax.dynamic_index_in_dim(block, (at - g) % groups, 0, keepdims=False)
                        for at in range(seqs)
                    ],
                    axis=1,
                )
            )
        return jnp.concatenate(columns, axis=0)

    layer_out = home([after(x, dkv) for x in layer_moved])
    grad_inputs = home(grad_moved).astype(f32)

    def in_halves(index, mine, other):
        first = jnp.where(index == 0, mine, other)
        second = jnp.where(index == 0, other, mine)
        return jnp.concatenate([first, second], axis=0)

    def over_hash_sum(x):
        half = x.shape[0] // 2
        mine = lax.dynamic_slice_in_dim(x, r * half, half, 0)
        total = add(mine, over_place(lax.dynamic_slice_in_dim(x, (1 - r) * half, half, 0)))
        sent = total.astype(bf16)
        total = add(total, *[over_group(sent, k) for k in range(1, groups)]).astype(bf16)
        return in_halves(r, total, over_place(total))

    a_sum, b_sum = over_hash_sum(a_sum), over_hash_sum(b_sum)
    a_other, b_other = over_seq(a_sum), over_seq(b_sum)
    cut = hidden_own // 2
    grad_w_down = in_halves(s, a_sum[:cut], a_other[:cut]).astype(f32)
    out_cut = cut + head_width // 2
    grad_w_out = in_halves(s, a_sum[cut:out_cut], a_other[cut:out_cut]).astype(f32)
    small = a_sum[out_cut : out_cut + 8].astype(f32)
    grad_w_up = in_halves(s, b_sum, b_other).T.astype(f32)

    grad_w_qkv = jnp.einsum("ld,cel->cde", tokens, grad_qkv, preferred_element_type=f32)
    grad_w_qkv = grad_w_qkv.reshape(3 * width, head_width).astype(bf16)
    half = grad_w_qkv.shape[0] // 2
    mine = lax.dynamic_slice_in_dim(grad_w_qkv, s * half, half, 0)
    other = over_seq(lax.dynamic_slice_in_dim(grad_w_qkv, (1 - s) * half, half, 0))
    total = over_hash_sum(add(mine, other).astype(bf16))
    grad_w_qkv = in_halves(s, total, over_seq(total)).reshape(3, width, head_width).astype(f32)

    count = piece * seqs * width * hash_count * 2
    stream_rms = jnp.sqrt(jnp.sum(small[4:7], axis=1) / count)
    share = width // head_count
    norm_grads = lax.dynamic_slice_in_dim(small, d * share, share, 1)
    return (
        layer_out[None],
        grad_inputs[None],
        grad_w_qkv,
        grad_w_out,
        grad_w_up,
        grad_w_down,
        norm_grads[0:2],
        norm_grads[2:4],
        stream_rms,
    )


def solution(mesh):
    placed = (
        P("seq", "hash", None, None),
        P(None, None, "head"),
        P("head", None),
        P(None, "head"),
        P("head", None),
        P(),
        P(),
        P("hash", None, None),
        P(),
        P(),
    )
    return jax.shard_map(
        shards,
        mesh=mesh,
        in_specs=placed,
        out_specs=(
            P("seq", "hash", None, None),
            P("seq", "hash", None, None),
            P(None, None, "head"),
            P("head", None),
            P(None, "head"),
            P("head", None),
            P(None, "head"),
            P(None, "head"),
            P(),
        ),
        check_vma=False,
    )
```

```python
from functools import partial

import jax
import jax.numpy as jnp
import numpy as np
from jax import lax
from jax.experimental import pallas as pl
from jax.experimental.pallas import tpu as pltpu
from jax.sharding import PartitionSpec as P

HEAD_DIM = 64
HASHES = 32
BITS = 8
SETS = 8
BUCKETS = 1 << BITS
ROWS = BUCKETS * SETS

bf16 = jnp.bfloat16
f32 = jnp.float32
NN = (((1,), (0,)), ((), ()))
NT = (((1,), (1,)), ((), ()))
TN = (((0,), (0,)), ((), ()))


def dot(a, b, dims):
    return lax.dot_general(a, b, dims, preferred_element_type=f32)


def sides(rows, planes):
    x = rows.astype(f32)
    inv = lax.rsqrt(jnp.sum(x * x, axis=0, keepdims=True) + 1e-6)
    proj = dot(planes, rows, NN) * (3.0 * inv)
    small = jnp.exp(-proj)
    upper = 1.0 / (1.0 + small)
    return inv, upper, small * upper


def products(upper, lower, first, count):
    out = None
    for i in range(first, first + count):
        lo, up = lower[SETS * i : SETS * (i + 1)], upper[SETS * i : SETS * (i + 1)]
        out = [lo, up] if out is None else [c * lo for c in out] + [c * up for c in out]
    return out


def half_codes(upper, lower):
    low = jnp.concatenate(products(upper, lower, 0, 4), axis=0).astype(bf16)
    high = [jnp.concatenate([a, a], axis=0).astype(bf16) for a in products(upper, lower, 4, 4)]
    return low, high


def code_chunk(low, high, first, count):
    return jnp.concatenate(
        [high[a] * low[16 * j : 16 * (j + 1)] for a in range(first, first + count) for j in range(8)],
        axis=0,
    )


def pull_back(rows, planes_t, inv, upper, sums):
    total = sums[BITS * SETS :][:SETS]
    grad_proj = sums[: BITS * SETS] - upper * jnp.concatenate([total] * BITS, axis=0)
    head = grad_proj.astype(bf16)
    tail = (grad_proj - head.astype(f32)).astype(bf16)
    grad_unit = dot(planes_t, jnp.concatenate([head, tail], axis=0), NN) * (3.0 * inv)
    x = rows.astype(f32)
    return grad_unit - x * (inv * inv * jnp.sum(x * grad_unit, axis=0, keepdims=True))


def both(*refs):
    return jnp.concatenate([ref[...] for ref in refs], axis=1)


def key_kernel(planes, *refs, chunk, blocks):
    keys, vals, out = refs[:blocks], refs[blocks : 2 * blocks], refs[-1]
    start = refs[2 * blocks] if len(refs) > 2 * blocks + 1 else None
    _, upper, lower = sides(both(*keys), planes[...])
    low, high = half_codes(upper, lower)
    values = both(*vals)
    for c in range(0, 16, chunk):
        at = slice(128 * c, 128 * (c + chunk))
        part = dot(code_chunk(low, high, c, chunk), values, NT)
        if start is not None:
            part = part + start[0, at, :]
        out[0, at, :] = part.astype(out.dtype)


def query_kernel(planes, q, tables, out, *, chunk):
    _, upper, lower = sides(q[...], planes[...])
    low, high = half_codes(upper, lower)
    acc = jnp.zeros((HEAD_DIM, q.shape[1]), f32)
    for c in range(0, 16, chunk):
        acc += dot(tables[0, 128 * c : 128 * (c + chunk), :], code_chunk(low, high, c, chunk), TN)
    out[...] = (acc * (1.0 / HASHES)).astype(out.dtype)


def query_back_kernel(planes, planes_t, bits, qa, ga, qb, gb, tables, *refs, chunk):
    start, out, da, db = (None, *refs) if len(refs) == 3 else refs
    rows = both(qa, qb)
    inv, upper, lower = sides(rows, planes[...])
    low, high = half_codes(upper, lower)
    grad = both(ga, gb)
    width = qa.shape[1]
    sums = jnp.zeros((bits.shape[0], 2 * width), f32)
    for c in range(0, 16, chunk):
        at = slice(128 * c, 128 * (c + chunk))
        codes = code_chunk(low, high, c, chunk)
        part = dot(codes, grad, NT)
        if start is not None:
            part = (part + start[0, at, :]) * (1.0 / HASHES)
        out[0, at, :] = part.astype(out.dtype)
        weighted = dot(tables[0, at, :], grad, NN).astype(bf16) * codes
        sums += dot(bits[:, at], weighted, NN)
    back = pull_back(rows, planes_t[...], inv, upper, sums * (1.0 / HASHES))
    da[...] = back[:, :width].astype(da.dtype)
    db[...] = back[:, width:].astype(db.dtype)


def key_back_kernel(planes, planes_t, bits, keys, vals, grad_tables, out, *, chunk):
    rows = keys[...]
    inv, upper, lower = sides(rows, planes[...])
    low, high = half_codes(upper, lower)
    values = vals[...]
    width = keys.shape[1]
    sums = jnp.zeros((bits.shape[0], width), f32)
    grad_values = jnp.zeros((HEAD_DIM, width), f32)
    for c in range(0, 16, chunk):
        at = slice(128 * c, 128 * (c + chunk))
        codes = code_chunk(low, high, c, chunk)
        grad_values += dot(grad_tables[0, at, :], codes, TN)
        weighted = dot(grad_tables[0, at, :], values, NN).astype(bf16) * codes
        sums += dot(bits[:, at], weighted, NN)
    out[0] = pull_back(rows, planes_t[...], inv, upper, sums).astype(out.dtype)
    out[1] = grad_values.astype(out.dtype)


def bit_rows():
    out = np.zeros((80, BUCKETS, SETS), np.float32)
    for t in range(SETS):
        for i in range(BITS):
            out[i * SETS + t, :, t] = (np.arange(BUCKETS) >> i) & 1
        out[BITS * SETS + t, :, t] = 1
    return jnp.asarray(out.reshape(80, ROWS), bf16)


def whole(*shape):
    return pl.BlockSpec(shape, lambda h: (0,) * len(shape))


def per_head(width, offset=0):
    return pl.BlockSpec((HEAD_DIM, width), lambda h: (h + offset, 0))


def table_spec():
    return pl.BlockSpec((1, ROWS, HEAD_DIM), lambda h: (h, 0, 0))


def call(kernel, heads, micros, name, in_specs, out_specs, out_shape):
    return pl.pallas_call(
        kernel,
        grid=(heads,),
        in_specs=in_specs,
        out_specs=out_specs,
        out_shape=out_shape,
        compiler_params=pltpu.CompilerParams(vmem_limit_bytes=48 << 20),
        cost_estimate=pl.CostEstimate(
            flops=int(micros * 1.1e9), bytes_accessed=1 << 20, transcendentals=0
        ),
        name=name,
    )


def key_tables(planes, blocks, start, kind):
    heads, width = blocks[0].shape[0] // (2 * HEAD_DIM), blocks[0].shape[1]
    specs = [whole(64, 64)] + [per_head(width)] * len(blocks) + [per_head(width, heads)] * len(blocks)
    args = [planes, *blocks, *blocks]
    if start is not None:
        specs.append(table_spec())
        args.append(start)
    return call(
        partial(key_kernel, chunk=2, blocks=len(blocks)),
        heads,
        5 * len(blocks),
        "key_tables",
        specs,
        table_spec(),
        jax.ShapeDtypeStruct((heads, ROWS, HEAD_DIM), kind),
    )(*args)


def query_estimates(planes, q, tables, kind):
    heads, width = q.shape[0] // HEAD_DIM, q.shape[1]
    return call(
        partial(query_kernel, chunk=2),
        heads,
        4,
        "query_estimates",
        [whole(64, 64), per_head(width), table_spec()],
        per_head(width),
        jax.ShapeDtypeStruct(q.shape, kind),
    )(planes, q, tables)


def query_backward(planes, planes_t, bits, q_a, g_a, q_b, g_b, tables, start, kind_a, kind_b):
    heads, width = q_a.shape[0] // HEAD_DIM, q_a.shape[1]
    specs = [whole(64, 64), whole(64, 128), whole(80, ROWS)] + [per_head(width)] * 4 + [table_spec()]
    args = [planes, planes_t, bits, q_a, g_a, q_b, g_b, tables]
    if start is not None:
        specs.append(table_spec())
        args.append(start)
    return call(
        partial(query_back_kernel, chunk=4),
        heads,
        20,
        "query_backward",
        specs,
        [table_spec(), per_head(width), per_head(width)],
        [jax.ShapeDtypeStruct((heads, ROWS, HEAD_DIM), f32 if start is None else bf16)]
        + [jax.ShapeDtypeStruct(q_a.shape, kind) for kind in (kind_a, kind_b)],
    )(*args)


def key_backward(planes, planes_t, bits, kv, grad_tables, kind):
    heads, width = kv.shape[0] // (2 * HEAD_DIM), kv.shape[1]
    return call(
        partial(key_back_kernel, chunk=4),
        heads,
        9,
        "key_backward",
        [whole(64, 64), whole(64, 128), whole(80, ROWS)]
        + [per_head(width), per_head(width, heads), table_spec()],
        pl.BlockSpec((2, HEAD_DIM, width), lambda h: (0, h, 0)),
        jax.ShapeDtypeStruct((2, heads * HEAD_DIM, width), kind),
    )(planes, planes_t, bits, kv, kv, grad_tables)


def norm(x):
    center = x - jnp.mean(x, axis=-1, keepdims=True)
    inv = lax.rsqrt(jnp.mean(center * center, axis=-1, keepdims=True) + 1e-5)
    return center * inv, inv


def norm_back(grad, unit, inv):
    return inv * (
        grad
        - jnp.mean(grad, axis=-1, keepdims=True)
        - unit * jnp.mean(grad * unit, axis=-1, keepdims=True)
    )


def column_sum(x):
    return jnp.sum(x, axis=0, keepdims=True)


def core_rows(core, ref, which):
    half = ref.shape[0] // 2
    at = core[0] if which == 0 else 1 - core[0]
    return ref[pl.ds(pl.multiple_of(at * half, 16), half), :]


def dense_kernel(core, x_in, grad_out, gain, bias, *refs):
    attn, ups, downs = refs[0:4], refs[4:12], refs[12:20]
    layer_out, grad_first_out, normed_out, hidden, grad_pre, grad_ffn_out, grad_attn_out = refs[20:27]
    estimates, small, slope = refs[27:31], refs[31], refs[32]
    part = hidden.shape[2]
    blocks = range(8)
    heads = jnp.concatenate([core_rows(core, attn[b // 2], b % 2) for b in blocks], axis=0)
    out_w = jnp.concatenate([downs[b][part:, :] for b in blocks], axis=0)
    attn_out = dot(heads, out_w, TN)
    resid = x_in[...].astype(f32)
    first = resid + attn_out
    small[4:5, :] = column_sum(resid * resid)
    small[5:6, :] = column_sum(attn_out * attn_out)
    small[6:7, :] = column_sum(first * first)
    small[7:8, :] = jnp.zeros_like(small[7:8, :])
    unit_1, inv_1 = norm(first)
    normed = (unit_1 * gain[0:1, :] + bias[0:1, :]).astype(bf16)
    normed_out[...] = normed
    second = normed.astype(f32)
    for b in blocks:
        pre = dot(normed, ups[b][...], NT)
        below = 0.5 * (1.0 + lax.erf(pre * 0.7071067811865476))
        rows = (pre * below).astype(bf16)
        hidden[b] = rows
        slope[b] = below + pre * (0.3989422804014327 * jnp.exp(-0.5 * pre * pre))
        second = second + dot(rows, downs[b][0:part, :], NN)
    unit_2, inv_2 = norm(second)
    layer_out[...] = (unit_2 * gain[1:2, :] + bias[1:2, :]).astype(layer_out.dtype)
    grad = grad_out[...]
    small[1:2, :] = column_sum(grad * unit_2)
    small[3:4, :] = column_sum(grad)
    grad_second = norm_back(grad * gain[1:2, :], unit_2, inv_2)
    grad_ffn = grad_second.astype(bf16)
    grad_ffn_out[...] = grad_ffn
    grad_normed = grad_second
    for b in blocks:
        rows = (dot(grad_ffn, downs[b][0:part, :], NT) * slope[b]).astype(bf16)
        grad_pre[b] = rows
        grad_normed = grad_normed + dot(rows, ups[b][...], NN)
    small[0:1, :] = column_sum(grad_normed * unit_1)
    small[2:3, :] = column_sum(grad_normed)
    grad_first = norm_back(grad_normed * gain[0:1, :], unit_1, inv_1)
    grad_first_out[...] = grad_first
    grad_attn = grad_first.astype(bf16)
    grad_attn_out[...] = grad_attn
    for b in blocks:
        half = estimates[0].shape[0] // 2
        at = core[0] if b % 2 == 0 else 1 - core[0]
        estimates[b // 2][pl.ds(pl.multiple_of(at * half, 16), half), :] = dot(
            downs[b][part:, :], grad_attn, NT
        ).astype(bf16)


def weight_grad_kernel(core, normed, hidden, grad_pre, grad_ffn, grad_attn, small, *refs):
    attn, down_out, ups = refs[0:4], refs[4], refs[5:7]
    part = hidden.shape[2]
    sums = jnp.concatenate([small[...], jnp.zeros_like(small[...])], axis=0).astype(bf16)
    for b in range(8):
        owner = (core[1] ^ (b // 2)) * 2 + (core[0] if b % 2 == 0 else 1 - core[0])
        heads = core_rows(core, attn[b // 2], b % 2)
        at = part + heads.shape[0]
        down_out[owner, 0:part, :] = dot(hidden[b], grad_ffn[...], TN).astype(bf16)
        down_out[owner, part:at, :] = dot(heads, grad_attn[...], NN).astype(bf16)
        down_out[owner, at : at + 16, :] = sums
        down_out[owner, at + 16 :, :] = jnp.zeros_like(sums)
        ups[b % 2][b // 2] = dot(grad_pre[b], normed[...], TN).astype(bf16)


def vmem(count):
    return [pl.BlockSpec(memory_space=pltpu.VMEM)] * count


def dense(core, x_in, grad_out, gain, bias, attn, ups, downs):
    rows, width = x_in.shape
    part = ups[0].shape[0]
    shape = jax.ShapeDtypeStruct
    out_shape = [
        shape((rows, width), bf16),
        shape((rows, width), f32),
        shape((rows, width), bf16),
        shape((8, rows, part), bf16),
        shape((8, rows, part), bf16),
        shape((rows, width), bf16),
        shape((rows, width), bf16),
        *[shape(attn[0].shape, bf16)] * 4,
        shape((8, width), f32),
    ]
    return pl.pallas_call(
        dense_kernel,
        in_specs=[pl.BlockSpec(memory_space=pltpu.SMEM)] + vmem(24),
        out_specs=vmem(12),
        out_shape=out_shape,
        scratch_shapes=[pltpu.VMEM((8, rows, part), f32)],
        compiler_params=pltpu.CompilerParams(vmem_limit_bytes=56 << 20),
        cost_estimate=pl.CostEstimate(flops=18 * 10**9, bytes_accessed=1 << 20, transcendentals=0),
        name="dense",
    )(core, x_in, grad_out, gain, bias, *attn, *ups, *downs)


def weight_grads(core, normed, hidden, grad_pre, grad_ffn, grad_attn, small, attn):
    width, part = normed.shape[1], hidden.shape[2]
    shapes = [jax.ShapeDtypeStruct((8, part + attn[0].shape[0] // 2 + 32, width), bf16)]
    shapes += [jax.ShapeDtypeStruct((4, part, width), bf16)] * 2
    return pl.pallas_call(
        weight_grad_kernel,
        in_specs=[pl.BlockSpec(memory_space=pltpu.SMEM)] + vmem(10),
        out_specs=vmem(3),
        out_shape=shapes,
        compiler_params=pltpu.CompilerParams(vmem_limit_bytes=56 << 20),
        cost_estimate=pl.CostEstimate(flops=9 * 10**9, bytes_accessed=1 << 20, transcendentals=0),
        name="weight_grads",
    )(core, normed, hidden, grad_pre, grad_ffn, grad_attn, small, *attn)


def after(x, *others):
    return lax.optimization_barrier((x, *others))[0]


def add(a, *others):
    return sum([b.astype(f32) for b in others], a.astype(f32))


def shards(
    inputs,
    w_qkv,
    w_out,
    up_weight,
    down_weight,
    norm_gain,
    norm_bias,
    planes,
    mask_pos,
    cot_rows,
):
    own = inputs[0]
    piece, seqs, width = own.shape
    hash_count, head_count = lax.axis_size("hash"), lax.axis_size("head")
    groups, places = seqs, hash_count // seqs
    assert places == 2 and lax.axis_size("seq") == 2 and head_count == 4
    assert planes.shape[0] * hash_count == 4 * SETS
    quarter = piece // head_count
    rows = groups * quarter
    half_len = piece * hash_count
    head_width = w_out.shape[0]
    hidden_own = down_weight.shape[0]
    n_tokens = head_count * rows
    hash_id, d, s = lax.axis_index("hash"), lax.axis_index("head"), lax.axis_index("seq")
    g, r = hash_id // places, hash_id % places

    def over_seq(x):
        return lax.ppermute(x, "seq", [(0, 1), (1, 0)])

    def over_place(x):
        return lax.ppermute(x, "hash", [(h, h ^ 1) for h in range(hash_count)])

    def over_group(x, k):
        moves = [(h, ((h // places + k) % groups) * places + h % places) for h in range(hash_count)]
        return lax.ppermute(x, "hash", moves)

    def over_head(x, j):
        return lax.ppermute(x, "head", [(h, h ^ j) for h in range(head_count)])

    def seq_rows(block, index):
        return lax.dynamic_index_in_dim(block, index % seqs, 1, keepdims=False)

    my_quarter = lax.dynamic_slice_in_dim(own, d * quarter, quarter, 0)
    arrived = [over_group(seq_rows(my_quarter, g + k), k) for k in range(1, groups)]

    signed = (2 * planes - 1).astype(bf16)
    if planes.shape[0] == SETS and groups == 2:
        moves = [
            ((2 * rr + ss) * 2 + gg, (gg * places + rr) * 2 + ss)
            for gg in range(2)
            for rr in range(2)
            for ss in range(2)
        ]
        signed = lax.ppermute(signed, ("hash", "seq"), moves)
    else:
        signed = lax.all_gather(signed, "hash", axis=0, tiled=True)
        signed = lax.dynamic_slice_in_dim(signed, (r * 2 + s) * SETS, SETS, 0)
    signed = signed.transpose(1, 0, 2).reshape(BITS * SETS, HEAD_DIM)
    signed_t = jnp.concatenate([signed.T, signed.T], axis=1)
    bits = bit_rows()

    dense_in = jnp.stack([seq_rows(my_quarter, g)] + arrived)

    def core_half(at):
        cut = hidden_own // 2
        out_cut = head_width // 2
        down = lax.dynamic_slice_in_dim(down_weight, at * cut, cut, 0)
        out = lax.dynamic_slice_in_dim(w_out, at * out_cut, out_cut, 0)
        return lax.dynamic_slice_in_dim(up_weight, at * cut, cut, 1).T, jnp.concatenate([down, out])

    up, down = core_half(s)
    ups, downs = [[x] for x in core_half(1 - s)]

    slot = jnp.arange(groups, dtype=jnp.int32)[:, None]
    place_of = ((g - slot) % groups) * places + r
    position = s * half_len + place_of * piece + d * quarter + jnp.arange(quarter, dtype=jnp.int32)[None]
    mask_row = lax.dynamic_index_in_dim(mask_pos, g, 0, keepdims=False)
    cot = lax.dynamic_index_in_dim(cot_rows, g, 0, keepdims=False)
    pick = (position.reshape(rows)[:, None] == mask_row[None]).astype(bf16)
    grad_out = jnp.dot(pick, cot, preferred_element_type=f32)

    blocks = [dense_in]
    for j in range(1, head_count):
        here = seq_rows(lax.dynamic_slice_in_dim(own, (d ^ j) * quarter, quarter, 0), g)
        there = after(over_head(dense_in[1:], j), up, down, *ups, *downs, grad_out, signed_t)
        blocks.append(jnp.concatenate([here[None], there]))
    tokens = jnp.stack(blocks).reshape(n_tokens, width)
    dense_in = dense_in.reshape(rows, width)

    def project(w):
        return jnp.einsum("cde,ld->cel", w, tokens, preferred_element_type=f32).astype(bf16)

    kv = project(w_qkv[1:]).reshape(2 * head_width, n_tokens)
    q = project(w_qkv[:1]).reshape(head_width, n_tokens)
    kv_z = over_place(kv)
    kv_o = over_seq(kv)
    q_o = over_seq(q)
    q_z = over_place(after(q, kv_o))

    up = after(up, tokens)
    ups, downs = [up] + ups, [down] + downs
    up_x, up_y = over_head(up, 1), over_head(up, 2)
    tables = key_tables(after(signed, up, q), [kv, kv_o], None, f32)

    kv_z = after(kv_z, tables)
    kv_zo = over_seq(kv_z)
    up_x, up_y = after(up_x, tables), after(up_y, tables)
    down = after(down, up_x, up_y)
    down_x, down_y = over_head(down, 1), over_head(down, 2)
    tables = key_tables(after(signed, down), [kv_z], tables, f32)

    up_xo, up_yo = over_seq(after(up_x, tables)), over_seq(after(up_y, tables))
    q_z = after(q_z, tables)
    q_zo = over_seq(q_z)
    kv_zo = after(kv_zo, tables)
    tables = key_tables(after(signed, q_z), [kv_zo], tables, bf16)

    q_zo = after(q_zo, tables)
    down_x, down_y = after(down_x, tables), after(down_y, tables)
    up_d, down_d = over_head(after(up_x, tables), 2), over_head(down_y, 1)
    down_xo, down_yo = over_seq(down_x), over_seq(down_y)
    q_zo = after(q_zo, down_x, down_y)
    e_zo = query_estimates(signed, q_zo, tables, bf16)
    e_zo_moved = over_seq(e_zo)
    e_z = query_estimates(signed, after(q_z, e_zo), tables, bf16)
    e_far = add(e_z, after(e_zo_moved, e_z)).astype(bf16)
    e_o = query_estimates(signed, after(q_o, e_far), tables, bf16)
    e_far = over_place(e_far)
    e_o_moved = over_seq(e_o)
    e = query_estimates(signed, after(q, e_o), tables, f32)
    e_far = after(e_far, e)
    up_d, down_d = after(up_d, e), after(down_d, e)
    up_xo, up_yo = after(up_xo, e_zo), after(up_yo, e_zo)
    down_xo, down_yo = after(down_xo, e_zo), after(down_yo, e_zo)
    ups += [up_x, up_xo, up_y, up_yo, up_d, over_seq(up_d)]
    downs += [down_x, down_xo, down_y, down_yo, down_d, over_seq(down_d)]
    attn = add(e, after(e_o_moved, e), e_far).astype(bf16)

    def to_dense(block):
        parts = [block[..., j * rows : (j + 1) * rows] for j in range(head_count)]
        moved = [over_head(parts[j], j) for j in range(1, head_count)]
        return [parts[0], *lax.optimization_barrier(moved)]

    attn_parts = to_dense(attn)

    def away(dense_rows):
        dense_rows = dense_rows.reshape(groups, quarter, width)
        return [dense_rows[0]] + [over_group(dense_rows[k], groups - k) for k in range(1, groups)]

    core = jnp.stack([s, d]).astype(jnp.int32)
    (layer_rows, grad_first, normed, hidden, grad_pre, grad_ffn, grad_attn, *rest) = dense(
        core, dense_in, grad_out, norm_gain, norm_bias, attn_parts, ups, downs
    )
    est_parts, small = rest[:4], rest[4]
    grad = jnp.concatenate(
        [est_parts[0]] + [over_head(est_parts[j], j) for j in range(1, head_count)], axis=1
    )
    a_grads, mine_b, other_b = weight_grads(
        core, normed, hidden, grad_pre, grad_ffn, grad_attn, small, attn_parts
    )

    a_sum = lax.psum_scatter(a_grads, ("head", "seq"), scatter_dimension=0, tiled=True)[0]
    grad_z = over_place(grad)
    grad_o = over_seq(grad)
    swap_b = over_seq(after(other_b, grad_o))
    layer_moved = away(layer_rows)
    part, dq, dq_o = query_backward(
        signed, signed_t, bits, q, grad, q_o, after(grad_o, mine_b), tables, None, f32, bf16
    )

    grad_zo = over_seq(after(grad_z, part))
    layer_moved = jnp.stack([after(x, part) for x in layer_moved])
    cut = mine_b.shape[1] // 2
    chip_b = add(mine_b, after(swap_b, part)).astype(bf16)
    x_out = jnp.stack([chip_b[1, :cut], chip_b[3, :cut]])
    y_out = jnp.stack([chip_b[2, cut:], chip_b[3, cut:]])
    x_far, y_far = over_head(x_out, 1), over_head(y_out, 2)
    dq_o = over_seq(dq_o)
    q_gated = after(q_z, x_out, y_out, layer_moved)
    grad_tables, dq_z, dq_zo = query_backward(
        signed, signed_t, bits, q_gated, grad_z, q_zo, grad_zo, tables, part, bf16, bf16
    )

    x_far, y_far = after(x_far, dq_z), after(y_far, dq_z)
    x_own = add(chip_b[0, :cut], x_far[0])
    y_own = add(chip_b[0, cut:], y_far[0])
    x_out = add(chip_b[2, :cut], x_far[1]).astype(bf16)
    y_out = add(chip_b[1, cut:], y_far[1]).astype(bf16)
    x_last, y_last = over_head(x_out, 2), over_head(y_out, 1)
    dq_zo = over_seq(dq_zo)
    dq_own = add(dq, after(dq_o, dq_z))
    dkv_zo = key_backward(
        signed, signed_t, bits, after(kv_zo, dq_own, x_out, y_out), grad_tables, bf16
    )

    dkv_zo_moved = over_seq(dkv_zo)
    dq_far = add(dq_z, after(dq_zo, dkv_zo)).astype(bf16)
    b_halves = jnp.stack(
        [add(x_own, after(x_last, dkv_zo)), add(y_own, after(y_last, dkv_zo))]
    ).astype(bf16)
    b_keep = lax.dynamic_index_in_dim(b_halves, r, 0, keepdims=False)
    b_send = lax.dynamic_index_in_dim(b_halves, 1 - r, 0, keepdims=False)
    dkv_z = key_backward(
        signed, signed_t, bits, after(kv_z, dq_far, b_keep, b_send), grad_tables, bf16
    )
    dq_far, b_far = over_place(dq_far), over_place(b_send)

    dkv_far = add(dkv_z, after(dkv_zo_moved, dkv_z)).astype(bf16)
    grad_q = add(dq_own, after(dq_far, dkv_z)).astype(bf16)
    b_keep = add(b_keep, after(b_far, dkv_z))
    b_send = b_keep.astype(bf16)
    dkv_o = key_backward(
        signed, signed_t, bits, after(kv_o, dkv_far, grad_q, b_send), grad_tables, bf16
    )
    dk_far, dv_far = over_place(dkv_far[0]), over_place(after(dkv_far[1], dkv_o))
    b_far = [over_group(b_send, k) for k in range(1, groups)]

    dkv_o_moved = over_seq(dkv_o)
    a_sum = after(a_sum, dkv_o)
    dk_far = after(dk_far, dkv_o)
    b_send = add(b_keep, *[after(x, dkv_o) for x in b_far]).astype(bf16)
    layer_moved = after(layer_moved, dkv_o)
    layer_moved = [layer_moved] + [over_head(layer_moved, j) for j in range(1, head_count)]
    qkv_cut = width // 2
    qkv_near = [lax.dynamic_slice_in_dim(w_qkv, s * qkv_cut, qkv_cut, 1)]
    qkv_far = [lax.dynamic_slice_in_dim(w_qkv, (1 - s) * qkv_cut, qkv_cut, 1)]
    qkv_half = after(qkv_near[0], dkv_z)
    qkv_near += [after(over_head(qkv_half, j), dkv_o) for j in range(1, head_count)]
    dkv = key_backward(
        signed, signed_t, bits, after(kv, dk_far, b_send, a_sum), grad_tables, f32
    )
    a_sum = lax.psum(a_sum, "hash")
    b_far = over_place(b_send)

    qkv_near[1:] = [after(x, dkv) for x in qkv_near[1:]]
    qkv_far += [over_seq(x) for x in qkv_near[1:]]
    dkv_o_moved = after(dkv_o_moved, dkv)
    grad_k = add(dkv[0], dkv_o_moved[0], dk_far)
    grad_v = add(dkv[1], dkv_o_moved[1], after(dv_far, dkv))
    grad_qkv = jnp.stack([grad_q, grad_k.astype(bf16), grad_v.astype(bf16)])
    qkv_parts = to_dense(grad_qkv)

    near, far = 0.0, 0.0
    for j in range(head_count):
        block = qkv_parts[j]
        near = near + jnp.einsum("cel,cde->ld", block, qkv_near[j], preferred_element_type=f32)
        far = far + jnp.einsum("cel,cde->ld", block, qkv_far[j], preferred_element_type=f32)
    grad_in = grad_first + jnp.concatenate(
        [jnp.where(s == 0, near, far), jnp.where(s == 0, far, near)], axis=1
    )

    grad_moved = jnp.stack(away(grad_in.astype(bf16)))
    grad_moved = [grad_moved] + [over_head(grad_moved, j) for j in range(1, head_count)]

    def home(blocks):
        table = jnp.stack(blocks)
        columns = []
        for q_at in range(head_count):
            block = lax.dynamic_index_in_dim(table, q_at ^ d, 0, keepdims=False)
            columns.append(
                jnp.stack(
                    [
                        lax.dynamic_index_in_dim(block, (at - g) % groups, 0, keepdims=False)
                        for at in range(seqs)
                    ],
                    axis=1,
                )
            )
        return jnp.concatenate(columns, axis=0)

    layer_out = home([after(x, grad_moved[0]) for x in layer_moved])
    grad_inputs = home(grad_moved).astype(f32)

    def in_halves(index, mine, other):
        first = jnp.where(index == 0, mine, other)
        second = jnp.where(index == 0, other, mine)
        return jnp.concatenate([first, second], axis=0)

    def over_hash_sum(x):
        half = x.shape[0] // 2
        mine = lax.dynamic_slice_in_dim(x, r * half, half, 0)
        total = add(mine, over_place(lax.dynamic_slice_in_dim(x, (1 - r) * half, half, 0)))
        sent = total.astype(bf16)
        total = add(total, *[over_group(sent, k) for k in range(1, groups)]).astype(bf16)
        return in_halves(r, total, over_place(total))

    b_sum = in_halves(r, b_send, after(b_far, dkv))
    b_other = over_seq(b_sum)
    grad_w_up = in_halves(s, b_sum, b_other).T.astype(f32)

    grad_w_qkv = jnp.einsum("ld,cel->cde", tokens, grad_qkv, preferred_element_type=f32)
    grad_w_qkv = grad_w_qkv.reshape(3 * width, head_width).astype(bf16)
    half = grad_w_qkv.shape[0] // 2
    mine = lax.dynamic_slice_in_dim(grad_w_qkv, s * half, half, 0)
    other = over_seq(lax.dynamic_slice_in_dim(grad_w_qkv, (1 - s) * half, half, 0))
    total = over_hash_sum(add(mine, other).astype(bf16))
    a_sum = after(a_sum, total)
    grad_w_qkv = in_halves(s, total, over_seq(total)).reshape(3, width, head_width).astype(f32)

    a_other = over_seq(a_sum)
    cut, out_cut = hidden_own // 2, (hidden_own + head_width) // 2
    grad_w_down = in_halves(s, a_sum[:cut], a_other[:cut]).astype(f32)
    grad_w_out = in_halves(s, a_sum[cut:out_cut], a_other[cut:out_cut]).astype(f32)
    small = a_sum[out_cut : out_cut + 8].astype(f32)

    count = piece * seqs * width * hash_count * 2
    stream_rms = jnp.sqrt(jnp.sum(small[4:7], axis=1) / count)
    share = width // head_count
    norm_grads = lax.dynamic_slice_in_dim(small, d * share, share, 1)
    return (
        layer_out[None],
        grad_inputs[None],
        grad_w_qkv,
        grad_w_out,
        grad_w_up,
        grad_w_down,
        norm_grads[0:2],
        norm_grads[2:4],
        stream_rms,
    )


def solution(mesh):
    placed = (
        P("seq", "hash", None, None),
        P(None, None, "head"),
        P("head", None),
        P(None, "head"),
        P("head", None),
        P(),
        P(),
        P("hash", None, None),
        P(),
        P(),
    )
    return jax.shard_map(
        shards,
        mesh=mesh,
        in_specs=placed,
        out_specs=(
            P("seq", "hash", None, None),
            P("seq", "hash", None, None),
            P(None, None, "head"),
            P("head", None),
            P(None, "head"),
            P("head", None),
            P(None, "head"),
            P(None, "head"),
            P(),
        ),
        check_vma=False,
    )
```

```python
from functools import partial

import jax
import jax.numpy as jnp
import numpy as np
from jax import lax
from jax.experimental import pallas as pl
from jax.experimental.pallas import tpu as pltpu
from jax.sharding import PartitionSpec as P

HEAD_DIM = 64
HASHES = 32
BITS = 8
SETS = 8
BUCKETS = 1 << BITS
ROWS = BUCKETS * SETS

bf16 = jnp.bfloat16
f32 = jnp.float32
NN = (((1,), (0,)), ((), ()))
NT = (((1,), (1,)), ((), ()))
TN = (((0,), (0,)), ((), ()))


def dot(a, b, dims):
    return lax.dot_general(a, b, dims, preferred_element_type=f32)


def sides(rows, planes):
    x = rows.astype(f32)
    inv = lax.rsqrt(jnp.sum(x * x, axis=0, keepdims=True) + 1e-6)
    proj = dot(planes, rows, NN) * (3.0 * inv)
    small = jnp.exp(-proj)
    upper = 1.0 / (1.0 + small)
    return inv, upper, small * upper


def products(upper, lower, first, count):
    out = None
    for i in range(first, first + count):
        lo, up = lower[SETS * i : SETS * (i + 1)], upper[SETS * i : SETS * (i + 1)]
        out = [lo, up] if out is None else [c * lo for c in out] + [c * up for c in out]
    return out


def half_codes(upper, lower):
    low = jnp.concatenate(products(upper, lower, 0, 4), axis=0).astype(bf16)
    high = [jnp.concatenate([a, a], axis=0).astype(bf16) for a in products(upper, lower, 4, 4)]
    return low, high


def code_chunk(low, high, first, count):
    return jnp.concatenate(
        [high[a] * low[16 * j : 16 * (j + 1)] for a in range(first, first + count) for j in range(8)],
        axis=0,
    )


def pull_back(rows, planes_t, inv, upper, sums):
    total = sums[BITS * SETS :][:SETS]
    grad_proj = sums[: BITS * SETS] - upper * jnp.concatenate([total] * BITS, axis=0)
    head = grad_proj.astype(bf16)
    tail = (grad_proj - head.astype(f32)).astype(bf16)
    grad_unit = dot(planes_t, jnp.concatenate([head, tail], axis=0), NN) * (3.0 * inv)
    x = rows.astype(f32)
    return grad_unit - x * (inv * inv * jnp.sum(x * grad_unit, axis=0, keepdims=True))


def both(*refs):
    return jnp.concatenate([ref[...] for ref in refs], axis=1)


def key_kernel(planes, *refs, chunk, blocks):
    keys, vals, out = refs[:blocks], refs[blocks : 2 * blocks], refs[-1]
    start = refs[2 * blocks] if len(refs) > 2 * blocks + 1 else None
    _, upper, lower = sides(both(*keys), planes[...])
    low, high = half_codes(upper, lower)
    values = both(*vals)
    for c in range(0, 16, chunk):
        at = slice(128 * c, 128 * (c + chunk))
        part = dot(code_chunk(low, high, c, chunk), values, NT)
        if start is not None:
            part = part + start[0, at, :]
        out[0, at, :] = part.astype(out.dtype)


def query_kernel(planes, q, tables, out, *, chunk):
    _, upper, lower = sides(q[...], planes[...])
    low, high = half_codes(upper, lower)
    acc = jnp.zeros((HEAD_DIM, q.shape[1]), f32)
    for c in range(0, 16, chunk):
        acc += dot(tables[0, 128 * c : 128 * (c + chunk), :], code_chunk(low, high, c, chunk), TN)
    out[...] = (acc * (1.0 / HASHES)).astype(out.dtype)


def query_back_kernel(planes, planes_t, bits, qa, ga, qb, gb, tables, *refs, chunk):
    start, out, da, db = (None, *refs) if len(refs) == 3 else refs
    rows = both(qa, qb)
    inv, upper, lower = sides(rows, planes[...])
    low, high = half_codes(upper, lower)
    grad = both(ga, gb)
    width = qa.shape[1]
    sums = jnp.zeros((bits.shape[0], 2 * width), f32)
    for c in range(0, 16, chunk):
        at = slice(128 * c, 128 * (c + chunk))
        codes = code_chunk(low, high, c, chunk)
        part = dot(codes, grad, NT)
        if start is not None:
            part = (part + start[0, at, :]) * (1.0 / HASHES)
        out[0, at, :] = part.astype(out.dtype)
        weighted = dot(tables[0, at, :], grad, NN).astype(bf16) * codes
        sums += dot(bits[:, at], weighted, NN)
    back = pull_back(rows, planes_t[...], inv, upper, sums * (1.0 / HASHES))
    da[...] = back[:, :width].astype(da.dtype)
    db[...] = back[:, width:].astype(db.dtype)


def key_back_kernel(planes, planes_t, bits, keys, vals, grad_tables, out, *, chunk):
    rows = keys[...]
    inv, upper, lower = sides(rows, planes[...])
    low, high = half_codes(upper, lower)
    values = vals[...]
    width = keys.shape[1]
    sums = jnp.zeros((bits.shape[0], width), f32)
    grad_values = jnp.zeros((HEAD_DIM, width), f32)
    for c in range(0, 16, chunk):
        at = slice(128 * c, 128 * (c + chunk))
        codes = code_chunk(low, high, c, chunk)
        grad_values += dot(grad_tables[0, at, :], codes, TN)
        weighted = dot(grad_tables[0, at, :], values, NN).astype(bf16) * codes
        sums += dot(bits[:, at], weighted, NN)
    out[0] = pull_back(rows, planes_t[...], inv, upper, sums).astype(out.dtype)
    out[1] = grad_values.astype(out.dtype)


def bit_rows():
    out = np.zeros((80, BUCKETS, SETS), np.float32)
    for t in range(SETS):
        for i in range(BITS):
            out[i * SETS + t, :, t] = (np.arange(BUCKETS) >> i) & 1
        out[BITS * SETS + t, :, t] = 1
    return jnp.asarray(out.reshape(80, ROWS), bf16)


def whole(*shape):
    return pl.BlockSpec(shape, lambda h: (0,) * len(shape))


def per_head(width, offset=0):
    return pl.BlockSpec((HEAD_DIM, width), lambda h: (h + offset, 0))


def table_spec():
    return pl.BlockSpec((1, ROWS, HEAD_DIM), lambda h: (h, 0, 0))


def call(kernel, heads, micros, name, in_specs, out_specs, out_shape):
    return pl.pallas_call(
        kernel,
        grid=(heads,),
        in_specs=in_specs,
        out_specs=out_specs,
        out_shape=out_shape,
        compiler_params=pltpu.CompilerParams(vmem_limit_bytes=48 << 20),
        cost_estimate=pl.CostEstimate(
            flops=int(micros * 1.1e9), bytes_accessed=1 << 20, transcendentals=0
        ),
        name=name,
    )


def key_tables(planes, blocks, start, kind):
    heads, width = blocks[0].shape[0] // (2 * HEAD_DIM), blocks[0].shape[1]
    specs = [whole(64, 64)] + [per_head(width)] * len(blocks) + [per_head(width, heads)] * len(blocks)
    args = [planes, *blocks, *blocks]
    if start is not None:
        specs.append(table_spec())
        args.append(start)
    return call(
        partial(key_kernel, chunk=2, blocks=len(blocks)),
        heads,
        5 * len(blocks),
        "key_tables",
        specs,
        table_spec(),
        jax.ShapeDtypeStruct((heads, ROWS, HEAD_DIM), kind),
    )(*args)


def query_estimates(planes, q, tables, kind):
    heads, width = q.shape[0] // HEAD_DIM, q.shape[1]
    return call(
        partial(query_kernel, chunk=2),
        heads,
        4,
        "query_estimates",
        [whole(64, 64), per_head(width), table_spec()],
        per_head(width),
        jax.ShapeDtypeStruct(q.shape, kind),
    )(planes, q, tables)


def query_backward(planes, planes_t, bits, q_a, g_a, q_b, g_b, tables, start, kind_a, kind_b):
    heads, width = q_a.shape[0] // HEAD_DIM, q_a.shape[1]
    specs = [whole(64, 64), whole(64, 128), whole(80, ROWS)] + [per_head(width)] * 4 + [table_spec()]
    args = [planes, planes_t, bits, q_a, g_a, q_b, g_b, tables]
    if start is not None:
        specs.append(table_spec())
        args.append(start)
    return call(
        partial(query_back_kernel, chunk=4),
        heads,
        20,
        "query_backward",
        specs,
        [table_spec(), per_head(width), per_head(width)],
        [jax.ShapeDtypeStruct((heads, ROWS, HEAD_DIM), f32 if start is None else bf16)]
        + [jax.ShapeDtypeStruct(q_a.shape, kind) for kind in (kind_a, kind_b)],
    )(*args)


def key_backward(planes, planes_t, bits, kv, grad_tables, kind):
    heads, width = kv.shape[0] // (2 * HEAD_DIM), kv.shape[1]
    return call(
        partial(key_back_kernel, chunk=4),
        heads,
        9,
        "key_backward",
        [whole(64, 64), whole(64, 128), whole(80, ROWS)]
        + [per_head(width), per_head(width, heads), table_spec()],
        pl.BlockSpec((2, HEAD_DIM, width), lambda h: (0, h, 0)),
        jax.ShapeDtypeStruct((2, heads * HEAD_DIM, width), kind),
    )(planes, planes_t, bits, kv, kv, grad_tables)


def norm(x):
    center = x - jnp.mean(x, axis=-1, keepdims=True)
    inv = lax.rsqrt(jnp.mean(center * center, axis=-1, keepdims=True) + 1e-5)
    return center * inv, inv


def norm_back(grad, unit, inv):
    return inv * (
        grad
        - jnp.mean(grad, axis=-1, keepdims=True)
        - unit * jnp.mean(grad * unit, axis=-1, keepdims=True)
    )


def column_sum(x):
    return jnp.sum(x, axis=0, keepdims=True)


def core_rows(core, ref, which):
    half = ref.shape[0] // 2
    at = core[0] if which == 0 else 1 - core[0]
    return ref[pl.ds(pl.multiple_of(at * half, 16), half), :]


def dense_kernel(core, x_in, grad_out, gain, bias, *refs):
    attn, ups, downs = refs[0:4], refs[4:12], refs[12:20]
    layer_out, first_out, normed_out, grad_second_out, slope, grad_down, small = refs[20:27]
    hidden = refs[27]
    part = hidden.shape[2]
    blocks = range(8)
    heads = jnp.concatenate([core_rows(core, attn[b // 2], b % 2) for b in blocks], axis=0)
    out_w = jnp.concatenate([downs[b][part:, :] for b in blocks], axis=0)
    attn_out = dot(heads, out_w, TN)
    resid = x_in[...].astype(f32)
    first = resid + attn_out
    first_out[...] = first
    small[0:1, :] = column_sum(resid * resid)
    small[1:2, :] = column_sum(attn_out * attn_out)
    small[2:3, :] = column_sum(first * first)
    unit_1, _ = norm(first)
    normed = (unit_1 * gain[0:1, :] + bias[0:1, :]).astype(bf16)
    normed_out[...] = normed
    second = normed.astype(f32)
    for b in blocks:
        pre = dot(normed, ups[b][...], NT)
        below = 0.5 * (1.0 + lax.erf(pre * 0.7071067811865476))
        rows = (pre * below).astype(bf16)
        hidden[b] = rows
        slope[b] = below + pre * (0.3989422804014327 * jnp.exp(-0.5 * pre * pre))
        second = second + dot(rows, downs[b][0:part, :], NN)
    unit_2, inv_2 = norm(second)
    layer_out[...] = (unit_2 * gain[1:2, :] + bias[1:2, :]).astype(layer_out.dtype)
    grad = grad_out[...]
    small[3:4, :] = column_sum(grad * unit_2)
    small[4:5, :] = column_sum(grad)
    small[5:8, :] = jnp.zeros_like(small[5:8, :])
    grad_second = norm_back(grad * gain[1:2, :], unit_2, inv_2)
    grad_second_out[...] = grad_second
    grad_ffn = grad_second.astype(bf16)
    for b in blocks:
        owner = (core[1] ^ (b // 2)) * 2 + (core[0] if b % 2 == 0 else 1 - core[0])
        grad_down[owner] = dot(hidden[b], grad_ffn, TN).astype(bf16)


def dense_back_kernel(core, first, grad_second, slope, gain, *refs):
    ups, downs = refs[0:8], refs[8:16]
    grad_first_out, grad_attn_out, grad_pre = refs[16:19]
    estimates, small = refs[19:23], refs[23]
    part = grad_pre.shape[2]
    blocks = range(8)
    grad_normed = grad_second[...]
    grad_ffn = grad_normed.astype(bf16)
    for b in blocks:
        rows = (dot(grad_ffn, downs[b][0:part, :], NT) * slope[b]).astype(bf16)
        grad_pre[b] = rows
        grad_normed = grad_normed + dot(rows, ups[b][...], NN)
    unit, inv = norm(first[...])
    small[0:1, :] = column_sum(grad_normed * unit)
    small[1:2, :] = column_sum(grad_normed)
    small[2:8, :] = jnp.zeros_like(small[2:8, :])
    grad_first = norm_back(grad_normed * gain[0:1, :], unit, inv)
    grad_first_out[...] = grad_first
    grad_attn = grad_first.astype(bf16)
    grad_attn_out[...] = grad_attn
    for b in blocks:
        half = estimates[0].shape[0] // 2
        at = core[0] if b % 2 == 0 else 1 - core[0]
        estimates[b // 2][pl.ds(pl.multiple_of(at * half, 16), half), :] = dot(
            downs[b][part:, :], grad_attn, NT
        ).astype(bf16)


def weight_grad_kernel(core, normed, grad_pre, grad_attn, small_a, small_b, *refs):
    attn, outs = refs[0:4], refs[4:6]
    part = grad_pre.shape[2]
    sums = jnp.concatenate([small_a[...], small_b[...]], axis=0).astype(bf16)
    for b in range(8):
        out = outs[b % 2]
        heads = core_rows(core, attn[b // 2], b % 2)
        at = part + heads.shape[0]
        out[b // 2, 0:part, :] = dot(grad_pre[b], normed[...], TN).astype(bf16)
        out[b // 2, part:at, :] = dot(heads, grad_attn[...], NN).astype(bf16)
        out[b // 2, at : at + 16, :] = sums
        out[b // 2, at + 16 :, :] = jnp.zeros_like(sums)


def input_grad_kernel(core, grad_first, *refs):
    blocks, near, far, out = refs[0:4], refs[4:8], refs[8:12], refs[12]
    half = near[0].shape[1]
    total = grad_first[...]
    for which, halves in enumerate((near, far)):
        at = core[0] if which == 0 else 1 - core[0]
        at = pl.ds(pl.multiple_of(at * half, 16), half)
        for j in range(4):
            rows = jnp.concatenate([blocks[j][c, at, :] for c in range(3)], axis=0)
            weights = jnp.concatenate([halves[j][c] for c in range(3)], axis=0)
            total = total + dot(rows, weights, TN)
    out[...] = total.astype(out.dtype)


def vmem(count):
    return [pl.BlockSpec(memory_space=pltpu.VMEM)] * count


def single(kernel, core, args, out_shape, micros, name, scratch=()):
    return pl.pallas_call(
        kernel,
        in_specs=[pl.BlockSpec(memory_space=pltpu.SMEM)] + vmem(len(args)),
        out_specs=vmem(len(out_shape)),
        out_shape=out_shape,
        scratch_shapes=scratch,
        compiler_params=pltpu.CompilerParams(vmem_limit_bytes=56 << 20),
        cost_estimate=pl.CostEstimate(
            flops=int(micros * 1.1e9), bytes_accessed=1 << 20, transcendentals=0
        ),
        name=name,
    )(core, *args)


shape = jax.ShapeDtypeStruct


def dense(core, x_in, grad_out, gain, bias, attn, ups, downs):
    rows, width = x_in.shape
    part = ups[0].shape[0]
    out_shape = [
        shape((rows, width), bf16),
        shape((rows, width), f32),
        shape((rows, width), bf16),
        shape((rows, width), f32),
        shape((8, rows, part), f32),
        shape((8, part, width), bf16),
        shape((8, width), f32),
    ]
    args = [x_in, grad_out, gain, bias, *attn, *ups, *downs]
    scratch = [pltpu.VMEM((8, rows, part), bf16)]
    return single(dense_kernel, core, args, out_shape, 14, "dense", scratch)


def dense_back(core, first, grad_second, slope, gain, attn, ups, downs):
    rows, width = first.shape
    out_shape = [
        shape((rows, width), f32),
        shape((rows, width), bf16),
        shape((8, rows, ups[0].shape[0]), bf16),
        *[shape(attn[0].shape, bf16)] * 4,
        shape((8, width), f32),
    ]
    args = [first, grad_second, slope, gain, *ups, *downs]
    return single(dense_back_kernel, core, args, out_shape, 8, "dense_back")


def weight_grads(core, normed, grad_pre, grad_attn, small_a, small_b, attn):
    width, part = normed.shape[1], grad_pre.shape[2]
    out_shape = [shape((4, part + attn[0].shape[0] // 2 + 32, width), bf16)] * 2
    args = [normed, grad_pre, grad_attn, small_a, small_b, *attn]
    return single(weight_grad_kernel, core, args, out_shape, 6, "weight_grads")


def input_grad(core, grad_first, blocks, near, far):
    out_shape = [shape(grad_first.shape, bf16)]
    args = [grad_first, *blocks, *near, *far]
    return single(input_grad_kernel, core, args, out_shape, 3, "input_grad")[0]


def after(x, *others):
    return lax.optimization_barrier((x, *others))[0]


def add(a, *others):
    return sum([b.astype(f32) for b in others], a.astype(f32))


def shards(
    inputs,
    w_qkv,
    w_out,
    up_weight,
    down_weight,
    norm_gain,
    norm_bias,
    planes,
    mask_pos,
    cot_rows,
):
    own = inputs[0]
    piece, seqs, width = own.shape
    hash_count, head_count = lax.axis_size("hash"), lax.axis_size("head")
    groups, places = seqs, hash_count // seqs
    assert places == 2 and lax.axis_size("seq") == 2 and head_count == 4
    assert planes.shape[0] * hash_count == 4 * SETS
    quarter = piece // head_count
    rows = groups * quarter
    half_len = piece * hash_count
    head_width = w_out.shape[0]
    hidden_own = down_weight.shape[0]
    n_tokens = head_count * rows
    hash_id, d, s = lax.axis_index("hash"), lax.axis_index("head"), lax.axis_index("seq")
    g, r = hash_id // places, hash_id % places

    def over_seq(x):
        return lax.ppermute(x, "seq", [(0, 1), (1, 0)])

    def over_place(x):
        return lax.ppermute(x, "hash", [(h, h ^ 1) for h in range(hash_count)])

    def over_group(x, k):
        moves = [(h, ((h // places + k) % groups) * places + h % places) for h in range(hash_count)]
        return lax.ppermute(x, "hash", moves)

    def over_head(x, j):
        return lax.ppermute(x, "head", [(h, h ^ j) for h in range(head_count)])

    def seq_rows(block, index):
        return lax.dynamic_index_in_dim(block, index % seqs, 1, keepdims=False)

    my_quarter = lax.dynamic_slice_in_dim(own, d * quarter, quarter, 0)
    arrived = [over_group(seq_rows(my_quarter, g + k), k) for k in range(1, groups)]

    signed = (2 * planes - 1).astype(bf16)
    if planes.shape[0] == SETS and groups == 2:
        moves = [
            ((2 * rr + ss) * 2 + gg, (gg * places + rr) * 2 + ss)
            for gg in range(2)
            for rr in range(2)
            for ss in range(2)
        ]
        signed = lax.ppermute(signed, ("hash", "seq"), moves)
    else:
        signed = lax.all_gather(signed, "hash", axis=0, tiled=True)
        signed = lax.dynamic_slice_in_dim(signed, (r * 2 + s) * SETS, SETS, 0)
    signed = signed.transpose(1, 0, 2).reshape(BITS * SETS, HEAD_DIM)
    signed_t = jnp.concatenate([signed.T, signed.T], axis=1)
    bits = bit_rows()

    dense_in = jnp.stack([seq_rows(my_quarter, g)] + arrived)

    def core_half(at):
        cut = hidden_own // 2
        out_cut = head_width // 2
        down = lax.dynamic_slice_in_dim(down_weight, at * cut, cut, 0)
        out = lax.dynamic_slice_in_dim(w_out, at * out_cut, out_cut, 0)
        return lax.dynamic_slice_in_dim(up_weight, at * cut, cut, 1).T, jnp.concatenate([down, out])

    up, down = core_half(s)
    ups, downs = [[x] for x in core_half(1 - s)]

    slot = jnp.arange(groups, dtype=jnp.int32)[:, None]
    place_of = ((g - slot) % groups) * places + r
    position = s * half_len + place_of * piece + d * quarter + jnp.arange(quarter, dtype=jnp.int32)[None]
    mask_row = lax.dynamic_index_in_dim(mask_pos, g, 0, keepdims=False)
    cot = lax.dynamic_index_in_dim(cot_rows, g, 0, keepdims=False)
    pick = (position.reshape(rows)[:, None] == mask_row[None]).astype(bf16)
    grad_out = jnp.dot(pick, cot, preferred_element_type=f32)

    blocks = [dense_in]
    for j in range(1, head_count):
        here = seq_rows(lax.dynamic_slice_in_dim(own, (d ^ j) * quarter, quarter, 0), g)
        there = after(over_head(dense_in[1:], j), up, down, *ups, *downs, grad_out, signed_t)
        blocks.append(jnp.concatenate([here[None], there]))
    tokens = jnp.stack(blocks).reshape(n_tokens, width)
    dense_in = dense_in.reshape(rows, width)

    def project(w):
        return jnp.einsum("cde,ld->cel", w, tokens, preferred_element_type=f32).astype(bf16)

    kv = project(w_qkv[1:]).reshape(2 * head_width, n_tokens)
    q = project(w_qkv[:1]).reshape(head_width, n_tokens)
    kv_z = over_place(kv)
    kv_o = over_seq(kv)
    q_o = over_seq(q)
    q_z = over_place(after(q, kv_o))

    up = after(up, q)
    ups, downs = [up] + ups, [down] + downs
    up_x, up_y = over_head(up, 1), over_head(up, 2)
    tables = key_tables(after(signed, up, q), [kv, kv_o], None, f32)

    kv_z = after(kv_z, tables)
    kv_zo = over_seq(kv_z)
    up_x, up_y = after(up_x, tables), after(up_y, tables)
    down = after(down, up_x, up_y)
    down_x, down_y = over_head(down, 1), over_head(down, 2)
    qkv_cut = head_width // 2
    w_qkv_t = w_qkv.transpose(0, 2, 1)
    qkv_near = [lax.dynamic_slice_in_dim(w_qkv_t, s * qkv_cut, qkv_cut, 1)]
    qkv_far = [lax.dynamic_slice_in_dim(w_qkv_t, (1 - s) * qkv_cut, qkv_cut, 1)]
    tables = key_tables(after(signed, down, qkv_near[0], qkv_far[0]), [kv_z], tables, f32)

    up_xo, up_yo = over_seq(after(up_x, tables)), over_seq(after(up_y, tables))
    q_z = after(q_z, tables)
    q_zo = over_seq(q_z)
    kv_zo = after(kv_zo, tables)
    tables = key_tables(after(signed, q_z), [kv_zo], tables, bf16)

    q_zo = after(q_zo, tables)
    down_x, down_y = after(down_x, tables), after(down_y, tables)
    up_d, down_d = over_head(after(up_x, tables), 2), over_head(down_y, 1)
    down_xo, down_yo = over_seq(down_x), over_seq(down_y)
    q_zo = after(q_zo, down_x, down_y)
    e_zo = query_estimates(signed, q_zo, tables, bf16)
    e_zo_moved = over_seq(e_zo)
    e_z = query_estimates(signed, after(q_z, e_zo), tables, bf16)
    e_far = add(e_z, after(e_zo_moved, e_z)).astype(bf16)
    e_o = query_estimates(signed, after(q_o, e_far), tables, bf16)
    e_far = over_place(e_far)
    e_o_moved = over_seq(e_o)
    e = query_estimates(signed, after(q, e_o), tables, f32)
    e_far = after(e_far, e)
    up_d, down_d = after(up_d, e_far), after(down_d, e_far)
    up_xo, up_yo = after(up_xo, e_zo), after(up_yo, e_zo)
    down_xo, down_yo = after(down_xo, e_zo), after(down_yo, e_zo)
    ups += [up_x, up_xo, up_y, up_yo, up_d, over_seq(up_d)]
    downs += [down_x, down_xo, down_y, down_yo, down_d, over_seq(down_d)]
    attn = add(e, after(e_o_moved, e), e_far).astype(bf16)

    def to_dense(block):
        parts = [block[..., j * rows : (j + 1) * rows] for j in range(head_count)]
        moved = [over_head(parts[j], j) for j in range(1, head_count)]
        return [parts[0], *lax.optimization_barrier(moved)]

    attn_parts = to_dense(attn)

    def away(dense_rows):
        dense_rows = dense_rows.reshape(groups, quarter, width)
        return [dense_rows[0]] + [over_group(dense_rows[k], groups - k) for k in range(1, groups)]

    core = jnp.stack([s, d]).astype(jnp.int32)
    layer_rows, first, normed, grad_second, slope, a_grads, small_a = dense(
        core, dense_in, grad_out, norm_gain, norm_bias, attn_parts, ups, downs
    )
    a_sum = lax.psum_scatter(a_grads, ("head", "seq"), scatter_dimension=0, tiled=True)[0]
    (grad_first, grad_attn, grad_pre, *est_parts, small_b) = dense_back(
        core, first, grad_second, slope, norm_gain, attn_parts, ups, downs
    )
    grad = jnp.concatenate(
        [est_parts[0]] + [over_head(est_parts[j], j) for j in range(1, head_count)], axis=1
    )
    mine_b, other_b = weight_grads(core, normed, grad_pre, grad_attn, small_a, small_b, attn_parts)

    grad_z = over_place(grad)
    grad_o = over_seq(grad)
    swap_b = over_seq(after(other_b, grad_o))
    layer_moved = away(layer_rows)
    part, dq, dq_o = query_backward(
        signed, signed_t, bits, q, grad, q_o, after(grad_o, mine_b), tables, None, f32, bf16
    )

    grad_zo = over_seq(after(grad_z, part))
    layer_moved = jnp.stack([after(x, part) for x in layer_moved])
    cut = mine_b.shape[1] // 2
    chip_b = add(mine_b, after(swap_b, part)).astype(bf16)
    x_out = jnp.stack([chip_b[1, :cut], chip_b[3, :cut]])
    y_out = jnp.stack([chip_b[2, cut:], chip_b[3, cut:]])
    x_far, y_far = over_head(x_out, 1), over_head(y_out, 2)
    dq_o = over_seq(dq_o)
    q_gated = after(q_z, x_out, y_out, layer_moved)
    grad_tables, dq_z, dq_zo = query_backward(
        signed, signed_t, bits, q_gated, grad_z, q_zo, grad_zo, tables, part, bf16, bf16
    )

    a_sum = after(a_sum, dq_z)
    x_far, y_far = after(x_far, dq_z), after(y_far, dq_z)
    x_own = add(chip_b[0, :cut], x_far[0])
    y_own = add(chip_b[0, cut:], y_far[0])
    x_out = add(chip_b[2, :cut], x_far[1]).astype(bf16)
    y_out = add(chip_b[1, cut:], y_far[1]).astype(bf16)
    x_last, y_last = over_head(x_out, 2), over_head(y_out, 1)
    dq_zo = over_seq(dq_zo)
    dq_own = add(dq, after(dq_o, dq_z))
    dkv_zo = key_backward(
        signed, signed_t, bits, after(kv_zo, dq_own, x_out, y_out, a_sum), grad_tables, bf16
    )
    a_sum = lax.psum(a_sum, "hash")

    dkv_zo_moved = over_seq(dkv_zo)
    dq_far = add(dq_z, after(dq_zo, dkv_zo)).astype(bf16)
    b_halves = jnp.stack(
        [add(x_own, after(x_last, dkv_zo)), add(y_own, after(y_last, dkv_zo))]
    ).astype(bf16)
    b_keep = lax.dynamic_index_in_dim(b_halves, r, 0, keepdims=False)
    b_send = lax.dynamic_index_in_dim(b_halves, 1 - r, 0, keepdims=False)
    dkv_z = key_backward(
        signed, signed_t, bits, after(kv_z, dq_far, b_keep, b_send), grad_tables, bf16
    )
    dq_far, b_far = over_place(dq_far), over_place(b_send)

    dkv_far = add(dkv_z, after(dkv_zo_moved, dkv_z)).astype(bf16)
    grad_q = add(dq_own, after(dq_far, dkv_z)).astype(bf16)
    b_keep = add(b_keep, after(b_far, dkv_z))
    b_send = b_keep.astype(bf16)
    dkv_o = key_backward(
        signed, signed_t, bits, after(kv_o, dkv_far, grad_q, b_send), grad_tables, bf16
    )
    dk_far, dv_far = over_place(dkv_far[0]), over_place(after(dkv_far[1], dkv_o))
    b_far = [over_group(b_send, k) for k in range(1, groups)]

    dkv_o_moved = over_seq(dkv_o)
    a_sum = after(a_sum, dkv_o)
    dk_far = after(dk_far, dkv_o)
    b_send = add(b_keep, *[after(x, dkv_o) for x in b_far]).astype(bf16)
    layer_moved = after(layer_moved, dkv_o)
    layer_moved = [layer_moved] + [over_head(layer_moved, j) for j in range(1, head_count)]
    qkv_half = after(qkv_near[0], dkv_z)
    qkv_near += [after(over_head(qkv_half, j), dkv_o) for j in range(1, head_count)]
    dkv = key_backward(
        signed, signed_t, bits, after(kv, dk_far, b_send, a_sum), grad_tables, f32
    )
    b_far = over_place(b_send)

    qkv_near[1:] = [after(x, dkv) for x in qkv_near[1:]]
    qkv_far += [over_seq(x) for x in qkv_near[1:]]
    dkv_o_moved = after(dkv_o_moved, dkv)
    grad_k = add(dkv[0], dkv_o_moved[0], dk_far)
    grad_v = add(dkv[1], dkv_o_moved[1], after(dv_far, dkv))
    grad_qkv = jnp.stack([grad_q, grad_k.astype(bf16), grad_v.astype(bf16)])
    qkv_parts = to_dense(grad_qkv)

    grad_in = input_grad(core, grad_first, qkv_parts, qkv_near, qkv_far)

    def in_halves(index, mine, other):
        first = jnp.where(index == 0, mine, other)
        second = jnp.where(index == 0, other, mine)
        return jnp.concatenate([first, second], axis=0)

    def split(x, index):
        half = x.shape[0] // 2
        return [lax.dynamic_slice_in_dim(x, at * half, half, 0) for at in (index, 1 - index)]

    w_grad = dot(grad_qkv.reshape(3 * head_width, n_tokens), tokens, NN).astype(bf16)
    w_keep, w_send = split(w_grad, s)
    w_keep, w_send = split(add(w_keep, over_seq(w_send)).astype(bf16), r)
    grad_moved = away(grad_in)
    w_keep = add(w_keep, over_place(w_send))
    w_send = w_keep.astype(bf16)
    grad_moved = after(jnp.stack(grad_moved), w_send)
    w_keep = add(w_keep, *[over_group(w_send, k) for k in range(1, groups)]).astype(bf16)
    grad_moved = [grad_moved] + [over_head(grad_moved, j) for j in range(1, head_count)]

    def home(blocks):
        table = jnp.stack(blocks)
        columns = []
        for q_at in range(head_count):
            block = lax.dynamic_index_in_dim(table, q_at ^ d, 0, keepdims=False)
            columns.append(
                jnp.stack(
                    [
                        lax.dynamic_index_in_dim(block, (at - g) % groups, 0, keepdims=False)
                        for at in range(seqs)
                    ],
                    axis=1,
                )
            )
        return jnp.concatenate(columns, axis=0)

    layer_out = home([after(x, grad_moved[0]) for x in layer_moved])
    grad_inputs = home(grad_moved).astype(f32)

    w_grad = in_halves(r, w_keep, over_place(w_keep))
    w_grad = in_halves(s, w_grad, over_seq(w_grad)).reshape(3, head_width, width)
    grad_w_qkv = w_grad.transpose(0, 2, 1).astype(f32)
    grad_w_down = in_halves(s, a_sum, over_seq(a_sum)).astype(f32)
    b_sum = in_halves(r, b_send, after(b_far, grad_moved[0]))
    b_other = over_seq(b_sum)
    cut, out_cut = hidden_own // 2, (hidden_own + head_width) // 2
    grad_w_up = in_halves(s, b_sum[:cut], b_other[:cut]).T.astype(f32)
    grad_w_out = in_halves(s, b_sum[cut:out_cut], b_other[cut:out_cut]).astype(f32)
    small = b_sum[out_cut : out_cut + 16].astype(f32)

    count = piece * seqs * width * hash_count * 2
    stream_rms = jnp.sqrt(jnp.sum(small[0:3], axis=1) / count)
    share = width // head_count
    norm_grads = lax.dynamic_slice_in_dim(small, d * share, share, 1)
    return (
        layer_out[None],
        grad_inputs[None],
        grad_w_qkv,
        grad_w_out,
        grad_w_up,
        grad_w_down,
        jnp.stack([norm_grads[8], norm_grads[3]]),
        jnp.stack([norm_grads[9], norm_grads[4]]),
        stream_rms,
    )


def solution(mesh):
    placed = (
        P("seq", "hash", None, None),
        P(None, None, "head"),
        P("head", None),
        P(None, "head"),
        P("head", None),
        P(),
        P(),
        P("hash", None, None),
        P(),
        P(),
    )
    return jax.shard_map(
        shards,
        mesh=mesh,
        in_specs=placed,
        out_specs=(
            P("seq", "hash", None, None),
            P("seq", "hash", None, None),
            P(None, None, "head"),
            P("head", None),
            P(None, "head"),
            P("head", None),
            P(None, "head"),
            P(None, "head"),
            P(),
        ),
        check_vma=False,
    )
```

```python
from functools import partial

import jax
import jax.numpy as jnp
import numpy as np
from jax import lax
from jax.experimental import pallas as pl
from jax.experimental.pallas import tpu as pltpu
from jax.sharding import PartitionSpec as P

HEAD_DIM = 64
HASHES = 32
BITS = 8
SETS = 8
BUCKETS = 1 << BITS
ROWS = BUCKETS * SETS

bf16 = jnp.bfloat16
f32 = jnp.float32
NN = (((1,), (0,)), ((), ()))
NT = (((1,), (1,)), ((), ()))
TN = (((0,), (0,)), ((), ()))


shape = jax.ShapeDtypeStruct


def dot(a, b, dims):
    return lax.dot_general(a, b, dims, preferred_element_type=f32)


def sides(rows, planes):
    x = rows.astype(f32)
    inv = lax.rsqrt(jnp.sum(x * x, axis=0, keepdims=True) + 1e-6)
    proj = dot(planes, rows, NN) * (3.0 * inv)
    small = jnp.exp(-proj)
    upper = 1.0 / (1.0 + small)
    return inv, upper, small * upper


def products(upper, lower, first, count):
    out = None
    for i in range(first, first + count):
        lo, up = lower[SETS * i : SETS * (i + 1)], upper[SETS * i : SETS * (i + 1)]
        out = [lo, up] if out is None else [c * lo for c in out] + [c * up for c in out]
    return out


def half_codes(upper, lower):
    low = jnp.concatenate(products(upper, lower, 0, 4), axis=0).astype(bf16)
    high = [jnp.concatenate([a, a], axis=0).astype(bf16) for a in products(upper, lower, 4, 4)]
    return low, high


def code_chunk(low, high, first, count):
    return jnp.concatenate(
        [high[a] * low[16 * j : 16 * (j + 1)] for a in range(first, first + count) for j in range(8)],
        axis=0,
    )


def pull_back(rows, planes_t, inv, upper, sums):
    total = sums[BITS * SETS :][:SETS]
    grad_proj = sums[: BITS * SETS] - upper * jnp.concatenate([total] * BITS, axis=0)
    head = grad_proj.astype(bf16)
    tail = (grad_proj - head.astype(f32)).astype(bf16)
    grad_unit = dot(planes_t, jnp.concatenate([head, tail], axis=0), NN) * (3.0 * inv)
    x = rows.astype(f32)
    return grad_unit - x * (inv * inv * jnp.sum(x * grad_unit, axis=0, keepdims=True))


def both(*refs):
    return jnp.concatenate([ref[...] for ref in refs], axis=1)


def key_kernel(planes, *refs, chunk, blocks):
    keys, vals, out = refs[:blocks], refs[blocks : 2 * blocks], refs[-1]
    start = refs[2 * blocks] if len(refs) > 2 * blocks + 1 else None
    _, upper, lower = sides(both(*keys), planes[...])
    low, high = half_codes(upper, lower)
    values = both(*vals)
    for c in range(0, 16, chunk):
        at = slice(128 * c, 128 * (c + chunk))
        part = dot(code_chunk(low, high, c, chunk), values, NT)
        if start is not None:
            part = part + start[0, at, :]
        out[0, at, :] = part.astype(out.dtype)


def query_kernel(planes, q, tables, out, *, chunk):
    _, upper, lower = sides(q[...], planes[...])
    low, high = half_codes(upper, lower)
    acc = jnp.zeros((HEAD_DIM, q.shape[1]), f32)
    for c in range(0, 16, chunk):
        acc += dot(tables[0, 128 * c : 128 * (c + chunk), :], code_chunk(low, high, c, chunk), TN)
    out[...] = (acc * (1.0 / HASHES)).astype(out.dtype)


def query_back_kernel(planes, planes_t, bits, tables, *refs, chunk, blocks, last):
    queries, grads = refs[:blocks], refs[blocks : 2 * blocks]
    start = refs[2 * blocks] if len(refs) > 3 * blocks + 1 else None
    out, back_out = refs[-1 - blocks], refs[-blocks:]
    rows = both(*queries)
    inv, upper, lower = sides(rows, planes[...])
    low, high = half_codes(upper, lower)
    grad = both(*grads)
    sums = jnp.zeros((bits.shape[0], rows.shape[1]), f32)
    for c in range(0, 16, chunk):
        at = slice(128 * c, 128 * (c + chunk))
        codes = code_chunk(low, high, c, chunk)
        part = dot(codes, grad, NT)
        if start is not None:
            part = part + start[0, at, :]
        if last:
            part = part * (1.0 / HASHES)
        out[0, at, :] = part.astype(out.dtype)
        weighted = dot(tables[0, at, :], grad, NN).astype(bf16) * codes
        sums += dot(bits[:, at], weighted, NN)
    back = pull_back(rows, planes_t[...], inv, upper, sums * (1.0 / HASHES))
    width = back_out[0].shape[1]
    for i in range(blocks):
        back_out[i][...] = back[:, i * width : (i + 1) * width].astype(back_out[i].dtype)


def key_back_kernel(planes, planes_t, bits, keys, vals, grad_tables, out, *, chunk):
    rows = keys[...]
    inv, upper, lower = sides(rows, planes[...])
    low, high = half_codes(upper, lower)
    values = vals[...]
    width = keys.shape[1]
    sums = jnp.zeros((bits.shape[0], width), f32)
    grad_values = jnp.zeros((HEAD_DIM, width), f32)
    for c in range(0, 16, chunk):
        at = slice(128 * c, 128 * (c + chunk))
        codes = code_chunk(low, high, c, chunk)
        grad_values += dot(grad_tables[0, at, :], codes, TN)
        weighted = dot(grad_tables[0, at, :], values, NN).astype(bf16) * codes
        sums += dot(bits[:, at], weighted, NN)
    out[0] = pull_back(rows, planes_t[...], inv, upper, sums).astype(out.dtype)
    out[1] = grad_values.astype(out.dtype)


def bit_rows():
    out = np.zeros((80, BUCKETS, SETS), np.float32)
    for t in range(SETS):
        for i in range(BITS):
            out[i * SETS + t, :, t] = (np.arange(BUCKETS) >> i) & 1
        out[BITS * SETS + t, :, t] = 1
    return jnp.asarray(out.reshape(80, ROWS), bf16)


def whole(*shape):
    return pl.BlockSpec(shape, lambda h: (0,) * len(shape))


def per_head(width, offset=0):
    return pl.BlockSpec((HEAD_DIM, width), lambda h: (h + offset, 0))


def table_spec():
    return pl.BlockSpec((1, ROWS, HEAD_DIM), lambda h: (h, 0, 0))


def call(kernel, heads, micros, name, in_specs, out_specs, out_shape):
    return pl.pallas_call(
        kernel,
        grid=(heads,),
        in_specs=in_specs,
        out_specs=out_specs,
        out_shape=out_shape,
        compiler_params=pltpu.CompilerParams(vmem_limit_bytes=48 << 20),
        cost_estimate=pl.CostEstimate(
            flops=int(micros * 1.1e9), bytes_accessed=1 << 20, transcendentals=0
        ),
        name=name,
    )


def key_tables(planes, blocks, start, kind):
    heads, width = blocks[0].shape[0] // (2 * HEAD_DIM), blocks[0].shape[1]
    specs = [whole(64, 64)] + [per_head(width)] * len(blocks) + [per_head(width, heads)] * len(blocks)
    args = [planes, *blocks, *blocks]
    if start is not None:
        specs.append(table_spec())
        args.append(start)
    return call(
        partial(key_kernel, chunk=2, blocks=len(blocks)),
        heads,
        15 * len(blocks),
        "key_tables",
        specs,
        table_spec(),
        jax.ShapeDtypeStruct((heads, ROWS, HEAD_DIM), kind),
    )(*args)


def query_estimates(planes, q, tables, kind):
    heads, width = q.shape[0] // HEAD_DIM, q.shape[1]
    return call(
        partial(query_kernel, chunk=2),
        heads,
        10,
        "query_estimates",
        [whole(64, 64), per_head(width), table_spec()],
        per_head(width),
        jax.ShapeDtypeStruct(q.shape, kind),
    )(planes, q, tables)


def query_backward(planes, planes_t, bits, tables, queries, grads, start, last, kinds):
    heads, width = queries[0].shape[0] // HEAD_DIM, queries[0].shape[1]
    blocks = len(queries)
    specs = [whole(64, 64), whole(64, 128), whole(80, ROWS), table_spec()] + [per_head(width)] * (2 * blocks)
    args = [planes, planes_t, bits, tables, *queries, *grads]
    if start is not None:
        specs.append(table_spec())
        args.append(start)
    return call(
        partial(query_back_kernel, chunk=4, blocks=blocks, last=last),
        heads,
        25 * blocks,
        "query_backward",
        specs,
        [table_spec()] + [per_head(width)] * blocks,
        [shape((heads, ROWS, HEAD_DIM), bf16 if last else f32)]
        + [shape(queries[0].shape, kind) for kind in kinds],
    )(*args)


def key_backward(planes, planes_t, bits, kv, grad_tables, kind):
    heads, width = kv.shape[0] // (2 * HEAD_DIM), kv.shape[1]
    return call(
        partial(key_back_kernel, chunk=4),
        heads,
        25,
        "key_backward",
        [whole(64, 64), whole(64, 128), whole(80, ROWS)]
        + [per_head(width), per_head(width, heads), table_spec()],
        pl.BlockSpec((2, HEAD_DIM, width), lambda h: (0, h, 0)),
        jax.ShapeDtypeStruct((2, heads * HEAD_DIM, width), kind),
    )(planes, planes_t, bits, kv, kv, grad_tables)


def norm(x):
    center = x - jnp.mean(x, axis=-1, keepdims=True)
    inv = lax.rsqrt(jnp.mean(center * center, axis=-1, keepdims=True) + 1e-5)
    return center * inv, inv


def norm_back(grad, unit, inv):
    return inv * (
        grad
        - jnp.mean(grad, axis=-1, keepdims=True)
        - unit * jnp.mean(grad * unit, axis=-1, keepdims=True)
    )


def column_sum(x):
    return jnp.sum(x, axis=0, keepdims=True)


def core_rows(core, ref, which):
    half = ref.shape[0] // 2
    at = core[0] if which == 0 else 1 - core[0]
    return ref[pl.ds(pl.multiple_of(at * half, 16), half), :]


def share_rows(keep, give, at, rows):
    part = keep.shape[2]
    for out in (keep, give):
        out[at] = rows[:, :part]
        out[at + 1] = rows[:, part:]


def dense_kernel(core, x_in, grad_out, gain, bias, *refs):
    attn, ups, downs = refs[0:4], refs[4:12], refs[12:20]
    layer_out, first_out, grad_second_out, slope, keep, give, heads_give, small = refs[20:28]
    for j in range(4):
        heads_give[j] = core_rows(core, attn[j], 1)
    part = slope.shape[2]
    blocks = range(8)
    heads = jnp.concatenate([core_rows(core, attn[b // 2], b % 2) for b in blocks], axis=0)
    out_w = jnp.concatenate([downs[b][part:, :] for b in blocks], axis=0)
    attn_out = dot(heads, out_w, TN)
    resid = x_in[...].astype(f32)
    first = resid + attn_out
    first_out[...] = first
    small[0:1, :] = column_sum(resid * resid)
    small[1:2, :] = column_sum(attn_out * attn_out)
    small[2:3, :] = column_sum(first * first)
    unit_1, _ = norm(first)
    normed = (unit_1 * gain[0:1, :] + bias[0:1, :]).astype(bf16)
    share_rows(keep, give, 4, normed)
    second = normed.astype(f32)
    for b in blocks:
        pre = dot(normed, ups[b][...], NT)
        below = 0.5 * (1.0 + lax.erf(pre * 0.7071067811865476))
        rows = (pre * below).astype(bf16)
        (keep, give)[b % 2][b // 2] = rows
        slope[b] = below + pre * (0.3989422804014327 * jnp.exp(-0.5 * pre * pre))
        second = second + dot(rows, downs[b][0:part, :], NN)
    unit_2, inv_2 = norm(second)
    layer_out[...] = (unit_2 * gain[1:2, :] + bias[1:2, :]).astype(layer_out.dtype)
    grad = grad_out[...]
    small[3:4, :] = column_sum(grad * unit_2)
    small[4:5, :] = column_sum(grad)
    small[5:8, :] = jnp.zeros_like(small[5:8, :])
    grad_second = norm_back(grad * gain[1:2, :], unit_2, inv_2)
    grad_second_out[...] = grad_second
    share_rows(keep, give, 6, grad_second.astype(bf16))


def dense_back_kernel(core, first, grad_second, slope, gain, *refs):
    ups, downs = refs[0:8], refs[8:16]
    grad_first_out, keep, give = refs[16:19]
    estimates, small = refs[19:23], refs[23]
    part = slope.shape[2]
    blocks = range(8)
    grad_normed = grad_second[...]
    grad_ffn = grad_normed.astype(bf16)
    for b in blocks:
        rows = (dot(grad_ffn, downs[b][0:part, :], NT) * slope[b]).astype(bf16)
        (keep, give)[b % 2][b // 2] = rows
        grad_normed = grad_normed + dot(rows, ups[b][...], NN)
    unit, inv = norm(first[...])
    small[0:1, :] = column_sum(grad_normed * unit)
    small[1:2, :] = column_sum(grad_normed)
    small[2:8, :] = jnp.zeros_like(small[2:8, :])
    grad_first = norm_back(grad_normed * gain[0:1, :], unit, inv)
    grad_first_out[...] = grad_first
    grad_attn = grad_first.astype(bf16)
    share_rows(keep, give, 4, grad_attn)
    for b in blocks:
        half = estimates[0].shape[0] // 2
        at = core[0] if b % 2 == 0 else 1 - core[0]
        estimates[b // 2][pl.ds(pl.multiple_of(at * half, 16), half), :] = dot(
            downs[b][part:, :], grad_attn, NT
        ).astype(bf16)


def weight_grad_kernel(core, small_a, small_b, *refs):
    near, far, near_back, far_back = refs[0:4]
    attn, attn_far, out = refs[4:8], refs[8], refs[9]
    part = near.shape[2]
    sums = jnp.concatenate([small_a[...], small_b[...]], axis=0).astype(bf16)

    def wide(ref, at):
        return jnp.concatenate([ref[at], ref[at + 1]], axis=1)

    def rows(ref, other, at):
        return jnp.concatenate([wide(ref, at), wide(other, at)], axis=0)

    normed, grad_ffn = rows(near, far, 4), rows(near, far, 6)
    grad_attn = rows(near_back, far_back, 4)
    for j in range(4):
        owner = core[1] ^ j
        hidden = jnp.concatenate([near[j], far[j]], axis=0)
        grad_pre = jnp.concatenate([near_back[j], far_back[j]], axis=0)
        out[owner, 0:part, :] = dot(grad_pre, normed, TN).astype(bf16)
        out[owner, part : 2 * part, :] = dot(hidden, grad_ffn, TN).astype(bf16)
        heads = jnp.concatenate([core_rows(core, attn[j], 0), attn_far[j]], axis=1)
        at = 2 * part + heads.shape[0]
        out[owner, 2 * part : at, :] = dot(heads, grad_attn, NN).astype(bf16)
        out[owner, at : at + 16, :] = sums
        out[owner, at + 16 :, :] = jnp.zeros_like(sums)


def input_grad_kernel(core, grad_first, *refs):
    blocks, near, far, out = refs[0:4], refs[4:8], refs[8:12], refs[12]
    half = near[0].shape[1]
    total = grad_first[...]
    for which, halves in enumerate((near, far)):
        at = core[0] if which == 0 else 1 - core[0]
        at = pl.ds(pl.multiple_of(at * half, 16), half)
        for j in range(4):
            rows = jnp.concatenate([blocks[j][c, at, :] for c in range(3)], axis=0)
            weights = jnp.concatenate([halves[j][c] for c in range(3)], axis=0)
            total = total + dot(rows, weights, TN)
    out[...] = total.astype(out.dtype)


def vmem(count):
    return [pl.BlockSpec(memory_space=pltpu.VMEM)] * count


def single(kernel, core, args, out_shape, micros, name, scratch=()):
    return pl.pallas_call(
        kernel,
        in_specs=[pl.BlockSpec(memory_space=pltpu.SMEM)] + vmem(len(args)),
        out_specs=vmem(len(out_shape)),
        out_shape=out_shape,
        scratch_shapes=scratch,
        compiler_params=pltpu.CompilerParams(vmem_limit_bytes=56 << 20),
        cost_estimate=pl.CostEstimate(
            flops=int(micros * 1.1e9), bytes_accessed=1 << 20, transcendentals=0
        ),
        name=name,
    )(core, *args)


def dense(core, x_in, grad_out, gain, bias, attn, ups, downs):
    rows, width = x_in.shape
    part = ups[0].shape[0]
    out_shape = [
        shape((rows, width), bf16),
        shape((rows, width), f32),
        shape((rows, width), f32),
        shape((8, rows, part), f32),
        shape((8, rows, part), bf16),
        shape((8, rows, part), bf16),
        shape((4, attn[0].shape[0] // 2, rows), bf16),
        shape((8, width), f32),
    ]
    args = [x_in, grad_out, gain, bias, *attn, *ups, *downs]
    return single(dense_kernel, core, args, out_shape, 14, "dense")


def dense_back(core, first, grad_second, slope, gain, attn, ups, downs):
    rows, width = first.shape
    part = ups[0].shape[0]
    out_shape = [
        shape((rows, width), f32),
        shape((6, rows, part), bf16),
        shape((6, rows, part), bf16),
        *[shape(attn[0].shape, bf16)] * 4,
        shape((8, width), f32),
    ]
    args = [first, grad_second, slope, gain, *ups, *downs]
    return single(dense_back_kernel, core, args, out_shape, 8, "dense_back")


def weight_grads(core, small_a, small_b, shared, attn, attn_far):
    part, width = shared[0].shape[2], small_a.shape[1]
    out_shape = [shape((4, 2 * part + attn[0].shape[0] // 2 + 32, width), bf16)]
    args = [small_a, small_b, *shared, *attn, attn_far]
    return single(weight_grad_kernel, core, args, out_shape, 7, "weight_grads")[0]


def input_grad(core, grad_first, blocks, near, far):
    out_shape = [shape(grad_first.shape, bf16)]
    args = [grad_first, *blocks, *near, *far]
    return single(input_grad_kernel, core, args, out_shape, 3, "input_grad")[0]


def after(x, *others):
    return lax.optimization_barrier((x, *others))[0]


def add(a, *others):
    return sum([b.astype(f32) for b in others], a.astype(f32))


def shards(
    inputs,
    w_qkv,
    w_out,
    up_weight,
    down_weight,
    norm_gain,
    norm_bias,
    planes,
    mask_pos,
    cot_rows,
):
    own = inputs[0]
    piece, seqs, width = own.shape
    hash_count, head_count = lax.axis_size("hash"), lax.axis_size("head")
    groups, places = seqs, hash_count // seqs
    assert places == 2 and lax.axis_size("seq") == 2 and head_count == 4
    assert planes.shape[0] * hash_count == 4 * SETS
    quarter = piece // head_count
    rows = groups * quarter
    half_len = piece * hash_count
    head_width = w_out.shape[0]
    hidden_own = down_weight.shape[0]
    n_tokens = head_count * rows
    hash_id, d, s = lax.axis_index("hash"), lax.axis_index("head"), lax.axis_index("seq")
    g, r = hash_id // places, hash_id % places

    def over_seq(x):
        return lax.ppermute(x, "seq", [(0, 1), (1, 0)])

    def over_place(x):
        return lax.ppermute(x, "hash", [(h, h ^ 1) for h in range(hash_count)])

    def over_group(x, k):
        moves = [(h, ((h // places + k) % groups) * places + h % places) for h in range(hash_count)]
        return lax.ppermute(x, "hash", moves)

    def over_head(x, j):
        return lax.ppermute(x, "head", [(h, h ^ j) for h in range(head_count)])

    def seq_rows(block, index):
        return lax.dynamic_index_in_dim(block, index % seqs, 1, keepdims=False)

    my_quarter = lax.dynamic_slice_in_dim(own, d * quarter, quarter, 0)
    arrived = [over_group(seq_rows(my_quarter, g + k), k) for k in range(1, groups)]

    signed = (2 * planes - 1).astype(bf16)
    if planes.shape[0] == SETS and groups == 2:
        moves = [
            ((2 * rr + ss) * 2 + gg, (gg * places + rr) * 2 + ss)
            for gg in range(2)
            for rr in range(2)
            for ss in range(2)
        ]
        signed = lax.ppermute(signed, ("hash", "seq"), moves)
    else:
        signed = lax.all_gather(signed, "hash", axis=0, tiled=True)
        signed = lax.dynamic_slice_in_dim(signed, (r * 2 + s) * SETS, SETS, 0)
    signed = signed.transpose(1, 0, 2).reshape(BITS * SETS, HEAD_DIM)
    signed_t = jnp.concatenate([signed.T, signed.T], axis=1)
    bits = bit_rows()

    dense_in = jnp.stack([seq_rows(my_quarter, g)] + arrived)

    def core_half(at):
        cut = hidden_own // 2
        out_cut = head_width // 2
        down = lax.dynamic_slice_in_dim(down_weight, at * cut, cut, 0)
        out = lax.dynamic_slice_in_dim(w_out, at * out_cut, out_cut, 0)
        return lax.dynamic_slice_in_dim(up_weight, at * cut, cut, 1).T, jnp.concatenate([down, out])

    up, down = core_half(s)
    ups, downs = [[x] for x in core_half(1 - s)]

    slot = jnp.arange(groups, dtype=jnp.int32)[:, None]
    place_of = ((g - slot) % groups) * places + r
    position = s * half_len + place_of * piece + d * quarter + jnp.arange(quarter, dtype=jnp.int32)[None]
    mask_row = lax.dynamic_index_in_dim(mask_pos, g, 0, keepdims=False)
    cot = lax.dynamic_index_in_dim(cot_rows, g, 0, keepdims=False)
    pick = (position.reshape(rows)[:, None] == mask_row[None]).astype(bf16)
    grad_out = jnp.dot(pick, cot, preferred_element_type=f32)

    blocks = [dense_in]
    for j in range(1, head_count):
        here = seq_rows(lax.dynamic_slice_in_dim(own, (d ^ j) * quarter, quarter, 0), g)
        there = after(over_head(dense_in[1:], j), up, down, *ups, *downs, grad_out, signed_t)
        blocks.append(jnp.concatenate([here[None], there]))
    tokens = jnp.stack(blocks).reshape(n_tokens, width)
    dense_in = dense_in.reshape(rows, width)

    def project(w):
        return jnp.einsum("cde,ld->cel", w, tokens, preferred_element_type=f32).astype(bf16)

    kv = project(w_qkv[1:]).reshape(2 * head_width, n_tokens)
    q = project(w_qkv[:1]).reshape(head_width, n_tokens)
    kv_z = over_place(kv)
    kv_o = over_seq(kv)
    q_o = over_seq(q)
    q_z = over_place(after(q, kv_o))

    up = after(up, q)
    ups, downs = [up] + ups, [down] + downs
    up_x, up_y = over_head(up, 1), over_head(up, 2)
    tables = key_tables(after(signed, up, q), [kv, kv_o], None, f32)

    kv_z = after(kv_z, tables)
    kv_zo = over_seq(kv_z)
    up_x, up_y = after(up_x, tables), after(up_y, tables)
    down = after(down, up_x, up_y)
    down_x, down_y = over_head(down, 1), over_head(down, 2)
    qkv_cut = head_width // 2
    w_qkv_t = w_qkv.transpose(0, 2, 1)
    qkv_near = [lax.dynamic_slice_in_dim(w_qkv_t, s * qkv_cut, qkv_cut, 1)]
    qkv_far = [lax.dynamic_slice_in_dim(w_qkv_t, (1 - s) * qkv_cut, qkv_cut, 1)]
    tables = key_tables(after(signed, down, qkv_near[0], qkv_far[0]), [kv_z], tables, f32)

    up_xo, up_yo = over_seq(after(up_x, tables)), over_seq(after(up_y, tables))
    q_z = after(q_z, tables)
    q_zo = over_seq(q_z)
    kv_zo = after(kv_zo, tables)
    tables = key_tables(after(signed, q_z), [kv_zo], tables, bf16)

    q_zo = after(q_zo, tables)
    down_x, down_y = after(down_x, tables), after(down_y, tables)
    up_xo, up_yo = after(up_xo, tables), after(up_yo, tables)
    up_d, down_d = over_head(after(up_x, tables), 2), over_head(down_y, 1)
    down_xo, down_yo = over_seq(down_x), over_seq(down_y)
    q_zo = after(q_zo, down_x, down_y, up_xo, up_yo)
    e_zo = query_estimates(signed, q_zo, tables, bf16)
    e_zo_moved = over_seq(e_zo)
    down_xo, down_yo = after(down_xo, e_zo), after(down_yo, e_zo)
    e_z = query_estimates(signed, after(q_z, e_zo, down_xo, down_yo), tables, bf16)
    e_far = add(e_z, after(e_zo_moved, e_z)).astype(bf16)
    e_o = query_estimates(signed, after(q_o, e_far), tables, bf16)
    e_far = over_place(e_far)
    e_o_moved = over_seq(e_o)
    e = query_estimates(signed, after(q, e_o), tables, f32)
    e_far = after(e_far, e)
    up_d, down_d = after(up_d, e_far), after(down_d, e_far)
    ups += [up_x, up_xo, up_y, up_yo, up_d, over_seq(up_d)]
    downs += [down_x, down_xo, down_y, down_yo, down_d, over_seq(down_d)]
    attn = add(e, after(e_o_moved, e), e_far).astype(bf16)

    def to_dense(block):
        parts = [block[..., j * rows : (j + 1) * rows] for j in range(head_count)]
        moved = [over_head(parts[j], j) for j in range(1, head_count)]
        return [parts[0], *lax.optimization_barrier(moved)]

    attn_parts = to_dense(attn)

    def away(dense_rows):
        dense_rows = dense_rows.reshape(groups, quarter, width)
        return [dense_rows[0]] + [over_group(dense_rows[k], groups - k) for k in range(1, groups)]

    core = jnp.stack([s, d]).astype(jnp.int32)
    layer_rows, first, grad_second, slope, near, give, heads_give, small_a = dense(
        core, dense_in, grad_out, norm_gain, norm_bias, attn_parts, ups, downs
    )
    far, heads_far = over_seq(give), over_seq(heads_give)
    grad_first, near_back, give_back, *est_parts, small_b = dense_back(
        core, first, grad_second, slope, norm_gain, attn_parts, ups, downs
    )
    far_back = over_seq(give_back)
    est_moved = [over_head(est_parts[j], j) for j in range(1, head_count)]
    grad = jnp.concatenate([est_parts[0], *lax.optimization_barrier(est_moved)], axis=1)
    layer_moved = away(layer_rows)
    weight_parts = weight_grads(
        core, after(small_a, grad), small_b, [near, far, near_back, far_back], attn_parts, heads_far
    )

    weight_sum = lax.psum_scatter(weight_parts, "head", scatter_dimension=0, tiled=True)[0]
    grad_z = over_place(grad)
    grad_o = after(over_seq(grad), weight_parts)
    layer_moved = jnp.stack([after(x, weight_parts) for x in layer_moved])
    part, dq, dq_o = query_backward(
        signed, signed_t, bits, tables, [after(q, layer_moved), q_o], [grad, grad_o], None, False, [f32, bf16]
    )

    grad_z = after(grad_z, part)
    grad_zo = over_seq(grad_z)
    dq_o = over_seq(dq_o)
    part, dq_z = query_backward(
        signed, signed_t, bits, tables, [q_z], [grad_z], part, False, [f32]
    )

    dq_own = add(dq, after(dq_o, dq_z))
    grad_zo = after(grad_zo, dq_z)
    grad_tables, dq_zo = query_backward(
        signed, signed_t, bits, tables, [after(q_zo, dq_own)], [grad_zo], part, True, [bf16]
    )

    dq_zo = over_seq(dq_zo)
    dkv_zo = key_backward(signed, signed_t, bits, kv_zo, grad_tables, bf16)

    dkv_zo_moved = over_seq(dkv_zo)
    dq_far = add(dq_z, after(dq_zo, dkv_zo)).astype(bf16)
    layer_moved = [layer_moved] + [over_head(layer_moved, j) for j in range(1, head_count)]
    dkv_z = key_backward(signed, signed_t, bits, after(kv_z, dq_far), grad_tables, bf16)
    dq_far = over_place(dq_far)

    dkv_far = add(dkv_z, after(dkv_zo_moved, dkv_z)).astype(bf16)
    grad_q = add(dq_own, after(dq_far, dkv_z)).astype(bf16)
    weight_sum = after(weight_sum, dkv_z)
    layer_moved = [after(x, dkv_z) for x in layer_moved]
    dkv_o = key_backward(
        signed, signed_t, bits, after(kv_o, dkv_far, grad_q, weight_sum, *layer_moved), grad_tables, bf16
    )
    weight_sum = lax.psum(weight_sum, "hash")
    dk_far, dv_far = over_place(dkv_far[0]), over_place(after(dkv_far[1], dkv_o))
    qkv_half = after(qkv_near[0], dkv_z)
    qkv_moved = [over_head(qkv_half, j) for j in range(1, head_count)]

    dkv_o_moved = over_seq(dkv_o)
    dk_far = after(dk_far, dkv_o)
    qkv_near += [after(x, dkv_o) for x in qkv_moved]
    dkv = key_backward(
        signed, signed_t, bits, after(kv, dk_far, *qkv_near[1:]), grad_tables, f32
    )
    qkv_far += [over_seq(x) for x in qkv_near[1:]]

    dkv_o_moved = after(dkv_o_moved, dkv)
    qkv_far[1:] = [after(x, dkv) for x in qkv_far[1:]]
    grad_k = add(dkv[0], dkv_o_moved[0], dk_far)
    grad_v = add(dkv[1], dkv_o_moved[1], after(dv_far, dkv))
    grad_qkv = jnp.stack([grad_q, grad_k.astype(bf16), grad_v.astype(bf16)])
    qkv_parts = to_dense(grad_qkv)

    grad_in = input_grad(core, grad_first, qkv_parts, qkv_near, qkv_far)

    def in_halves(index, mine, other):
        first = jnp.where(index == 0, mine, other)
        second = jnp.where(index == 0, other, mine)
        return jnp.concatenate([first, second], axis=0)

    def split(x, index):
        half = x.shape[0] // 2
        return [lax.dynamic_slice_in_dim(x, at * half, half, 0) for at in (index, 1 - index)]

    w_grad = dot(grad_qkv.reshape(3 * head_width, n_tokens), tokens, NN).astype(bf16)
    w_keep, w_send = split(w_grad, s)
    w_keep, w_send = split(add(w_keep, over_seq(w_send)).astype(bf16), r)
    grad_moved = away(grad_in)
    w_keep = add(w_keep, over_place(w_send))
    w_send = w_keep.astype(bf16)
    grad_moved = after(jnp.stack(grad_moved), w_send)
    w_keep = add(w_keep, *[over_group(w_send, k) for k in range(1, groups)]).astype(bf16)
    grad_moved = [grad_moved] + [over_head(grad_moved, j) for j in range(1, head_count)]

    def home(blocks):
        table = jnp.stack(blocks)
        columns = []
        for q_at in range(head_count):
            block = lax.dynamic_index_in_dim(table, q_at ^ d, 0, keepdims=False)
            columns.append(
                jnp.stack(
                    [
                        lax.dynamic_index_in_dim(block, (at - g) % groups, 0, keepdims=False)
                        for at in range(seqs)
                    ],
                    axis=1,
                )
            )
        return jnp.concatenate(columns, axis=0)

    layer_out = home([after(x, grad_moved[0]) for x in layer_moved])
    grad_inputs = home(grad_moved).astype(f32)

    w_grad = in_halves(r, w_keep, over_place(w_keep))
    w_grad = in_halves(s, w_grad, over_seq(w_grad)).reshape(3, head_width, width)
    grad_w_qkv = w_grad.transpose(0, 2, 1).astype(f32)
    weight_sum = after(weight_sum, w_keep)
    weight_far = over_seq(weight_sum)
    cut = hidden_own // 2
    ends = [0, cut, 2 * cut, 2 * cut + head_width // 2]
    grad_w_up, grad_w_down, grad_w_out = [
        in_halves(s, weight_sum[a:b], weight_far[a:b]) for a, b in zip(ends, ends[1:])
    ]
    grad_w_up = grad_w_up.T.astype(f32)
    grad_w_down, grad_w_out = grad_w_down.astype(f32), grad_w_out.astype(f32)
    at = slice(ends[3], ends[3] + 16)
    small = add(weight_sum[at], weight_far[at])

    count = piece * seqs * width * hash_count * 2
    stream_rms = jnp.sqrt(jnp.sum(small[0:3], axis=1) / count)
    share = width // head_count
    norm_grads = lax.dynamic_slice_in_dim(small, d * share, share, 1)
    return (
        layer_out[None],
        grad_inputs[None],
        grad_w_qkv,
        grad_w_out,
        grad_w_up,
        grad_w_down,
        jnp.stack([norm_grads[8], norm_grads[3]]),
        jnp.stack([norm_grads[9], norm_grads[4]]),
        stream_rms,
    )


def solution(mesh):
    placed = (
        P("seq", "hash", None, None),
        P(None, None, "head"),
        P("head", None),
        P(None, "head"),
        P("head", None),
        P(),
        P(),
        P("hash", None, None),
        P(),
        P(),
    )
    return jax.shard_map(
        shards,
        mesh=mesh,
        in_specs=placed,
        out_specs=(
            P("seq", "hash", None, None),
            P("seq", "hash", None, None),
            P(None, None, "head"),
            P("head", None),
            P(None, "head"),
            P("head", None),
            P(None, "head"),
            P(None, "head"),
            P(),
        ),
        check_vma=False,
    )
```

```python
from functools import partial

import jax
import jax.numpy as jnp
import numpy as np
from jax import lax
from jax.experimental import pallas as pl
from jax.experimental.pallas import tpu as pltpu
from jax.sharding import PartitionSpec as P

HEAD_DIM = 64
HASHES = 32
BITS = 8
SETS = 8
BUCKETS = 1 << BITS
ROWS = BUCKETS * SETS

bf16 = jnp.bfloat16
f32 = jnp.float32
NN = (((1,), (0,)), ((), ()))
NT = (((1,), (1,)), ((), ()))
TN = (((0,), (0,)), ((), ()))


shape = jax.ShapeDtypeStruct


def dot(a, b, dims):
    return lax.dot_general(a, b, dims, preferred_element_type=f32)


def sides(rows, planes):
    x = rows.astype(f32)
    inv = lax.rsqrt(jnp.sum(x * x, axis=0, keepdims=True) + 1e-6)
    proj = dot(planes, rows, NN) * (3.0 * inv)
    small = jnp.exp(-proj)
    upper = 1.0 / (1.0 + small)
    return inv, upper, small * upper


def products(upper, lower, first, count):
    out = None
    for i in range(first, first + count):
        lo, up = lower[SETS * i : SETS * (i + 1)], upper[SETS * i : SETS * (i + 1)]
        out = [lo, up] if out is None else [c * lo for c in out] + [c * up for c in out]
    return out


def half_codes(upper, lower):
    low = jnp.concatenate(products(upper, lower, 0, 4), axis=0).astype(bf16)
    high = [jnp.concatenate([a, a], axis=0).astype(bf16) for a in products(upper, lower, 4, 4)]
    return low, high


def code_chunk(low, high, first, count):
    return jnp.concatenate(
        [high[a] * low[16 * j : 16 * (j + 1)] for a in range(first, first + count) for j in range(8)],
        axis=0,
    )


def pull_back(rows, planes_t, inv, upper, sums):
    total = sums[BITS * SETS :][:SETS]
    grad_proj = sums[: BITS * SETS] - upper * jnp.concatenate([total] * BITS, axis=0)
    head = grad_proj.astype(bf16)
    tail = (grad_proj - head.astype(f32)).astype(bf16)
    grad_unit = dot(planes_t, jnp.concatenate([head, tail], axis=0), NN) * (3.0 * inv)
    x = rows.astype(f32)
    return grad_unit - x * (inv * inv * jnp.sum(x * grad_unit, axis=0, keepdims=True))


def both(*refs):
    return jnp.concatenate([ref[...] for ref in refs], axis=1)


def key_kernel(planes, *refs, chunk, blocks):
    keys, vals, out = refs[:blocks], refs[blocks : 2 * blocks], refs[-1]
    start = refs[2 * blocks] if len(refs) > 2 * blocks + 1 else None
    _, upper, lower = sides(both(*keys), planes[...])
    low, high = half_codes(upper, lower)
    values = both(*vals)
    for c in range(0, 16, chunk):
        at = slice(128 * c, 128 * (c + chunk))
        part = dot(code_chunk(low, high, c, chunk), values, NT)
        if start is not None:
            part = part + start[0, at, :]
        out[0, at, :] = part.astype(out.dtype)


def query_kernel(planes, q, tables, out, *, chunk):
    _, upper, lower = sides(q[...], planes[...])
    low, high = half_codes(upper, lower)
    acc = jnp.zeros((HEAD_DIM, q.shape[1]), f32)
    for c in range(0, 16, chunk):
        acc += dot(tables[0, 128 * c : 128 * (c + chunk), :], code_chunk(low, high, c, chunk), TN)
    out[...] = (acc * (1.0 / HASHES)).astype(out.dtype)


def query_back_kernel(planes, planes_t, bits, tables, *refs, chunk, blocks, last):
    queries, grads = refs[:blocks], refs[blocks : 2 * blocks]
    start = refs[2 * blocks] if len(refs) > 3 * blocks + 1 else None
    out, back_out = refs[-1 - blocks], refs[-blocks:]
    rows = both(*queries)
    inv, upper, lower = sides(rows, planes[...])
    low, high = half_codes(upper, lower)
    grad = both(*grads)
    sums = jnp.zeros((bits.shape[0], rows.shape[1]), f32)
    for c in range(0, 16, chunk):
        at = slice(128 * c, 128 * (c + chunk))
        codes = code_chunk(low, high, c, chunk)
        part = dot(codes, grad, NT)
        if start is not None:
            part = part + start[0, at, :]
        if last:
            part = part * (1.0 / HASHES)
        out[0, at, :] = part.astype(out.dtype)
        weighted = dot(tables[0, at, :], grad, NN).astype(bf16) * codes
        sums += dot(bits[:, at], weighted, NN)
    back = pull_back(rows, planes_t[...], inv, upper, sums * (1.0 / HASHES))
    width = back_out[0].shape[1]
    for i in range(blocks):
        back_out[i][...] = back[:, i * width : (i + 1) * width].astype(back_out[i].dtype)


def key_back_kernel(planes, planes_t, bits, keys, vals, grad_tables, out, *, chunk):
    rows = keys[...]
    inv, upper, lower = sides(rows, planes[...])
    low, high = half_codes(upper, lower)
    values = vals[...]
    width = keys.shape[1]
    sums = jnp.zeros((bits.shape[0], width), f32)
    grad_values = jnp.zeros((HEAD_DIM, width), f32)
    for c in range(0, 16, chunk):
        at = slice(128 * c, 128 * (c + chunk))
        codes = code_chunk(low, high, c, chunk)
        grad_values += dot(grad_tables[0, at, :], codes, TN)
        weighted = dot(grad_tables[0, at, :], values, NN).astype(bf16) * codes
        sums += dot(bits[:, at], weighted, NN)
    out[0] = pull_back(rows, planes_t[...], inv, upper, sums).astype(out.dtype)
    out[1] = grad_values.astype(out.dtype)


def bit_rows():
    out = np.zeros((80, BUCKETS, SETS), np.float32)
    for t in range(SETS):
        for i in range(BITS):
            out[i * SETS + t, :, t] = (np.arange(BUCKETS) >> i) & 1
        out[BITS * SETS + t, :, t] = 1
    return jnp.asarray(out.reshape(80, ROWS), bf16)


def whole(*shape):
    return pl.BlockSpec(shape, lambda h: (0,) * len(shape))


def per_head(width, offset=0):
    return pl.BlockSpec((HEAD_DIM, width), lambda h: (h + offset, 0))


def table_spec():
    return pl.BlockSpec((1, ROWS, HEAD_DIM), lambda h: (h, 0, 0))


def call(kernel, heads, micros, name, in_specs, out_specs, out_shape):
    return pl.pallas_call(
        kernel,
        grid=(heads,),
        in_specs=in_specs,
        out_specs=out_specs,
        out_shape=out_shape,
        compiler_params=pltpu.CompilerParams(vmem_limit_bytes=48 << 20),
        cost_estimate=pl.CostEstimate(
            flops=int(micros * 1.1e9), bytes_accessed=1 << 20, transcendentals=0
        ),
        name=name,
    )


def key_tables(planes, blocks, start, kind):
    heads, width = blocks[0].shape[0] // (2 * HEAD_DIM), blocks[0].shape[1]
    specs = [whole(64, 64)] + [per_head(width)] * len(blocks) + [per_head(width, heads)] * len(blocks)
    args = [planes, *blocks, *blocks]
    if start is not None:
        specs.append(table_spec())
        args.append(start)
    return call(
        partial(key_kernel, chunk=2, blocks=len(blocks)),
        heads,
        15 * len(blocks),
        "key_tables",
        specs,
        table_spec(),
        jax.ShapeDtypeStruct((heads, ROWS, HEAD_DIM), kind),
    )(*args)


def query_estimates(planes, q, tables, kind):
    heads, width = q.shape[0] // HEAD_DIM, q.shape[1]
    return call(
        partial(query_kernel, chunk=2),
        heads,
        10,
        "query_estimates",
        [whole(64, 64), per_head(width), table_spec()],
        per_head(width),
        jax.ShapeDtypeStruct(q.shape, kind),
    )(planes, q, tables)


def query_backward(planes, planes_t, bits, tables, queries, grads, start, last, kinds):
    heads, width = queries[0].shape[0] // HEAD_DIM, queries[0].shape[1]
    blocks = len(queries)
    specs = [whole(64, 64), whole(64, 128), whole(80, ROWS), table_spec()] + [per_head(width)] * (2 * blocks)
    args = [planes, planes_t, bits, tables, *queries, *grads]
    if start is not None:
        specs.append(table_spec())
        args.append(start)
    return call(
        partial(query_back_kernel, chunk=4, blocks=blocks, last=last),
        heads,
        25 * blocks,
        "query_backward",
        specs,
        [table_spec()] + [per_head(width)] * blocks,
        [shape((heads, ROWS, HEAD_DIM), bf16 if last else f32)]
        + [shape(queries[0].shape, kind) for kind in kinds],
    )(*args)


def key_backward(planes, planes_t, bits, kv, grad_tables, kind):
    heads, width = kv.shape[0] // (2 * HEAD_DIM), kv.shape[1]
    return call(
        partial(key_back_kernel, chunk=4),
        heads,
        25,
        "key_backward",
        [whole(64, 64), whole(64, 128), whole(80, ROWS)]
        + [per_head(width), per_head(width, heads), table_spec()],
        pl.BlockSpec((2, HEAD_DIM, width), lambda h: (0, h, 0)),
        jax.ShapeDtypeStruct((2, heads * HEAD_DIM, width), kind),
    )(planes, planes_t, bits, kv, kv, grad_tables)


def norm(x):
    center = x - jnp.mean(x, axis=-1, keepdims=True)
    inv = lax.rsqrt(jnp.mean(center * center, axis=-1, keepdims=True) + 1e-5)
    return center * inv, inv


def norm_back(grad, unit, inv):
    return inv * (
        grad
        - jnp.mean(grad, axis=-1, keepdims=True)
        - unit * jnp.mean(grad * unit, axis=-1, keepdims=True)
    )


def column_sum(x):
    return jnp.sum(x, axis=0, keepdims=True)


def core_rows(core, ref, which):
    half = ref.shape[0] // 2
    at = core[0] if which == 0 else 1 - core[0]
    return ref[pl.ds(pl.multiple_of(at * half, 16), half), :]


def share_rows(keep, give, at, rows):
    part = keep.shape[2]
    for out in (keep, give):
        out[at] = rows[:, :part]
        out[at + 1] = rows[:, part:]


def dense_kernel(core, x_in, grad_out, gain, bias, *refs):
    attn, ups, downs = refs[0:4], refs[4:12], refs[12:20]
    layer_out, first_out, grad_second_out, slope, keep, give, heads_give, small = refs[20:28]
    for j in range(4):
        heads_give[j] = core_rows(core, attn[j], 1)
    part = slope.shape[2]
    blocks = range(8)
    heads = jnp.concatenate([core_rows(core, attn[b // 2], b % 2) for b in blocks], axis=0)
    out_w = jnp.concatenate([downs[b][part:, :] for b in blocks], axis=0)
    attn_out = dot(heads, out_w, TN)
    resid = x_in[...].astype(f32)
    first = resid + attn_out
    first_out[...] = first
    small[0:1, :] = column_sum(resid * resid)
    small[1:2, :] = column_sum(attn_out * attn_out)
    small[2:3, :] = column_sum(first * first)
    unit_1, _ = norm(first)
    normed = (unit_1 * gain[0:1, :] + bias[0:1, :]).astype(bf16)
    share_rows(keep, give, 4, normed)
    second = normed.astype(f32)
    for b in blocks:
        pre = dot(normed, ups[b][...], NT)
        below = 0.5 * (1.0 + lax.erf(pre * 0.7071067811865476))
        rows = (pre * below).astype(bf16)
        (keep, give)[b % 2][b // 2] = rows
        slope[b] = below + pre * (0.3989422804014327 * jnp.exp(-0.5 * pre * pre))
        second = second + dot(rows, downs[b][0:part, :], NN)
    unit_2, inv_2 = norm(second)
    layer_out[...] = (unit_2 * gain[1:2, :] + bias[1:2, :]).astype(layer_out.dtype)
    grad = grad_out[...]
    small[3:4, :] = column_sum(grad * unit_2)
    small[4:5, :] = column_sum(grad)
    small[5:8, :] = jnp.zeros_like(small[5:8, :])
    grad_second = norm_back(grad * gain[1:2, :], unit_2, inv_2)
    grad_second_out[...] = grad_second
    share_rows(keep, give, 6, grad_second.astype(bf16))


def dense_back_kernel(core, first, grad_second, slope, gain, *refs):
    ups, downs = refs[0:8], refs[8:16]
    grad_first_out, keep, give = refs[16:19]
    estimates, small = refs[19:23], refs[23]
    part = slope.shape[2]
    blocks = range(8)
    grad_normed = grad_second[...]
    grad_ffn = grad_normed.astype(bf16)
    for b in blocks:
        rows = (dot(grad_ffn, downs[b][0:part, :], NT) * slope[b]).astype(bf16)
        (keep, give)[b % 2][b // 2] = rows
        grad_normed = grad_normed + dot(rows, ups[b][...], NN)
    unit, inv = norm(first[...])
    small[0:1, :] = column_sum(grad_normed * unit)
    small[1:2, :] = column_sum(grad_normed)
    small[2:8, :] = jnp.zeros_like(small[2:8, :])
    grad_first = norm_back(grad_normed * gain[0:1, :], unit, inv)
    grad_first_out[...] = grad_first
    grad_attn = grad_first.astype(bf16)
    share_rows(keep, give, 4, grad_attn)
    for b in blocks:
        half = estimates[0].shape[0] // 2
        at = core[0] if b % 2 == 0 else 1 - core[0]
        estimates[b // 2][pl.ds(pl.multiple_of(at * half, 16), half), :] = dot(
            downs[b][part:, :], grad_attn, NT
        ).astype(bf16)


def weight_grad_kernel(core, small_a, small_b, *refs):
    near, far, near_back, far_back = refs[0:4]
    attn, attn_far, out = refs[4:8], refs[8], refs[9]
    part = near.shape[2]
    sums = jnp.concatenate([small_a[...], small_b[...]], axis=0).astype(bf16)

    def wide(ref, at):
        return jnp.concatenate([ref[at], ref[at + 1]], axis=1)

    def rows(ref, other, at):
        return jnp.concatenate([wide(ref, at), wide(other, at)], axis=0)

    normed, grad_ffn = rows(near, far, 4), rows(near, far, 6)
    grad_attn = rows(near_back, far_back, 4)
    for j in range(4):
        owner = core[1] ^ j
        hidden = jnp.concatenate([near[j], far[j]], axis=0)
        grad_pre = jnp.concatenate([near_back[j], far_back[j]], axis=0)
        out[owner, 0:part, :] = dot(grad_pre, normed, TN).astype(bf16)
        out[owner, part : 2 * part, :] = dot(hidden, grad_ffn, TN).astype(bf16)
        heads = jnp.concatenate([core_rows(core, attn[j], 0), attn_far[j]], axis=1)
        at = 2 * part + heads.shape[0]
        out[owner, 2 * part : at, :] = dot(heads, grad_attn, NN).astype(bf16)
        out[owner, at : at + 16, :] = sums
        out[owner, at + 16 :, :] = jnp.zeros_like(sums)


def input_grad_kernel(core, grad_first, *refs):
    blocks, near, far, out = refs[0:4], refs[4:8], refs[8:12], refs[12]
    half = near[0].shape[1]
    total = grad_first[...]
    for which, halves in enumerate((near, far)):
        at = core[0] if which == 0 else 1 - core[0]
        at = pl.ds(pl.multiple_of(at * half, 16), half)
        for j in range(4):
            rows = jnp.concatenate([blocks[j][c, at, :] for c in range(3)], axis=0)
            weights = jnp.concatenate([halves[j][c] for c in range(3)], axis=0)
            total = total + dot(rows, weights, TN)
    out[...] = total.astype(out.dtype)


def vmem(count):
    return [pl.BlockSpec(memory_space=pltpu.VMEM)] * count


def single(kernel, core, args, out_shape, micros, name, scratch=()):
    return pl.pallas_call(
        kernel,
        in_specs=[pl.BlockSpec(memory_space=pltpu.SMEM)] + vmem(len(args)),
        out_specs=vmem(len(out_shape)),
        out_shape=out_shape,
        scratch_shapes=scratch,
        compiler_params=pltpu.CompilerParams(vmem_limit_bytes=56 << 20),
        cost_estimate=pl.CostEstimate(
            flops=int(micros * 1.1e9), bytes_accessed=1 << 20, transcendentals=0
        ),
        name=name,
    )(core, *args)


def dense(core, x_in, grad_out, gain, bias, attn, ups, downs):
    rows, width = x_in.shape
    part = ups[0].shape[0]
    out_shape = [
        shape((rows, width), bf16),
        shape((rows, width), f32),
        shape((rows, width), f32),
        shape((8, rows, part), f32),
        shape((8, rows, part), bf16),
        shape((8, rows, part), bf16),
        shape((4, attn[0].shape[0] // 2, rows), bf16),
        shape((8, width), f32),
    ]
    args = [x_in, grad_out, gain, bias, *attn, *ups, *downs]
    return single(dense_kernel, core, args, out_shape, 14, "dense")


def dense_back(core, first, grad_second, slope, gain, attn, ups, downs):
    rows, width = first.shape
    part = ups[0].shape[0]
    out_shape = [
        shape((rows, width), f32),
        shape((6, rows, part), bf16),
        shape((6, rows, part), bf16),
        *[shape(attn[0].shape, bf16)] * 4,
        shape((8, width), f32),
    ]
    args = [first, grad_second, slope, gain, *ups, *downs]
    return single(dense_back_kernel, core, args, out_shape, 8, "dense_back")


def weight_grads(core, small_a, small_b, shared, attn, attn_far):
    part, width = shared[0].shape[2], small_a.shape[1]
    out_shape = [shape((4, 2 * part + attn[0].shape[0] // 2 + 32, width), bf16)]
    args = [small_a, small_b, *shared, *attn, attn_far]
    return single(weight_grad_kernel, core, args, out_shape, 7, "weight_grads")[0]


def input_grad(core, grad_first, blocks, near, far):
    out_shape = [shape(grad_first.shape, bf16)]
    args = [grad_first, *blocks, *near, *far]
    return single(input_grad_kernel, core, args, out_shape, 3, "input_grad")[0]


def after(x, *others):
    return lax.optimization_barrier((x, *others))[0]


def add(a, *others):
    return sum([b.astype(f32) for b in others], a.astype(f32))


def shards(
    inputs,
    w_qkv,
    w_out,
    up_weight,
    down_weight,
    norm_gain,
    norm_bias,
    planes,
    mask_pos,
    cot_rows,
):
    own = inputs[0]
    piece, seqs, width = own.shape
    hash_count, head_count = lax.axis_size("hash"), lax.axis_size("head")
    groups, places = seqs, hash_count // seqs
    assert places == 2 and lax.axis_size("seq") == 2 and head_count == 4
    assert planes.shape[0] * hash_count == 4 * SETS
    quarter = piece // head_count
    rows = groups * quarter
    half_len = piece * hash_count
    head_width = w_out.shape[0]
    hidden_own = down_weight.shape[0]
    n_tokens = head_count * rows
    hash_id, d, s = lax.axis_index("hash"), lax.axis_index("head"), lax.axis_index("seq")
    g, r = hash_id // places, hash_id % places

    def over_seq(x):
        return lax.ppermute(x, "seq", [(0, 1), (1, 0)])

    def over_place(x):
        return lax.ppermute(x, "hash", [(h, h ^ 1) for h in range(hash_count)])

    def over_group(x, k):
        moves = [(h, ((h // places + k) % groups) * places + h % places) for h in range(hash_count)]
        return lax.ppermute(x, "hash", moves)

    def over_head(x, j):
        return lax.ppermute(x, "head", [(h, h ^ j) for h in range(head_count)])

    def seq_rows(block, index):
        return lax.dynamic_index_in_dim(block, index % seqs, 1, keepdims=False)

    my_quarter = lax.dynamic_slice_in_dim(own, d * quarter, quarter, 0)
    arrived = [over_group(seq_rows(my_quarter, g + k), k) for k in range(1, groups)]

    signed = (2 * planes - 1).astype(bf16)
    if planes.shape[0] == SETS and groups == 2:
        moves = [
            ((2 * rr + ss) * 2 + gg, (gg * places + rr) * 2 + ss)
            for gg in range(2)
            for rr in range(2)
            for ss in range(2)
        ]
        signed = lax.ppermute(signed, ("hash", "seq"), moves)
    else:
        signed = lax.all_gather(signed, "hash", axis=0, tiled=True)
        signed = lax.dynamic_slice_in_dim(signed, (r * 2 + s) * SETS, SETS, 0)
    signed = signed.transpose(1, 0, 2).reshape(BITS * SETS, HEAD_DIM)
    signed_t = jnp.concatenate([signed.T, signed.T], axis=1)
    bits = bit_rows()

    dense_in = jnp.stack([seq_rows(my_quarter, g)] + arrived)

    def core_half(at):
        cut = hidden_own // 2
        out_cut = head_width // 2
        down = lax.dynamic_slice_in_dim(down_weight, at * cut, cut, 0)
        out = lax.dynamic_slice_in_dim(w_out, at * out_cut, out_cut, 0)
        return lax.dynamic_slice_in_dim(up_weight, at * cut, cut, 1).T, jnp.concatenate([down, out])

    up, down = core_half(s)
    ups, downs = [[x] for x in core_half(1 - s)]

    slot = jnp.arange(groups, dtype=jnp.int32)[:, None]
    place_of = ((g - slot) % groups) * places + r
    position = s * half_len + place_of * piece + d * quarter + jnp.arange(quarter, dtype=jnp.int32)[None]
    mask_row = lax.dynamic_index_in_dim(mask_pos, g, 0, keepdims=False)
    cot = lax.dynamic_index_in_dim(cot_rows, g, 0, keepdims=False)
    pick = (position.reshape(rows)[:, None] == mask_row[None]).astype(bf16)
    grad_out = jnp.dot(pick, cot, preferred_element_type=f32)

    blocks = [dense_in]
    for j in range(1, head_count):
        here = seq_rows(lax.dynamic_slice_in_dim(own, (d ^ j) * quarter, quarter, 0), g)
        there = after(over_head(dense_in[1:], j), up, down, *ups, *downs, signed_t)
        blocks.append(jnp.concatenate([here[None], there]))
    tokens = jnp.stack(blocks).reshape(n_tokens, width)
    dense_in = dense_in.reshape(rows, width)

    def project(w):
        return jnp.einsum("cde,ld->cel", w, tokens, preferred_element_type=f32).astype(bf16)

    kv = project(w_qkv[1:]).reshape(2 * head_width, n_tokens)
    q = project(w_qkv[:1]).reshape(head_width, n_tokens)
    kv_z = over_place(kv)
    kv_o = over_seq(kv)
    q_o = over_seq(q)
    q_z = over_place(after(q, kv_o))

    up = after(up, q)
    ups, downs = [up] + ups, [down] + downs
    up_x, up_y = over_head(up, 1), over_head(up, 2)
    tables = key_tables(after(signed, up, q), [kv, kv_o], None, f32)

    kv_z = after(kv_z, tables)
    kv_zo = over_seq(kv_z)
    up_x, up_y = after(up_x, tables), after(up_y, tables)
    down = after(down, up_x, up_y)
    down_x, down_y = over_head(down, 1), over_head(down, 2)
    qkv_cut = head_width // 2
    w_qkv_t = w_qkv.transpose(0, 2, 1)
    qkv_near = [lax.dynamic_slice_in_dim(w_qkv_t, s * qkv_cut, qkv_cut, 1)]
    qkv_far = [lax.dynamic_slice_in_dim(w_qkv_t, (1 - s) * qkv_cut, qkv_cut, 1)]
    tables = key_tables(after(signed, down, qkv_near[0], qkv_far[0], grad_out), [kv_z], tables, f32)

    up_xo, up_yo = over_seq(after(up_x, tables)), over_seq(after(up_y, tables))
    q_z = after(q_z, tables)
    q_zo = over_seq(q_z)
    kv_zo = after(kv_zo, tables)
    tables = key_tables(after(signed, q_z), [kv_zo], tables, bf16)

    q_zo = after(q_zo, tables)
    down_x, down_y = after(down_x, tables), after(down_y, tables)
    up_xo, up_yo = after(up_xo, tables), after(up_yo, tables)
    up_d, down_d = over_head(after(up_x, tables), 2), over_head(down_y, 1)
    down_xo, down_yo = over_seq(down_x), over_seq(down_y)
    q_zo = after(q_zo, down_x, down_y, up_xo, up_yo)
    e_zo = query_estimates(signed, q_zo, tables, bf16)
    e_zo_moved = over_seq(e_zo)
    down_xo, down_yo = after(down_xo, e_zo), after(down_yo, e_zo)
    e_z = query_estimates(signed, after(q_z, e_zo, down_xo, down_yo), tables, bf16)
    e_far = add(e_z, after(e_zo_moved, e_z)).astype(bf16)
    e_o = query_estimates(signed, after(q_o, e_far), tables, bf16)
    e_far = over_place(e_far)
    e_o_moved = over_seq(e_o)
    e = query_estimates(signed, after(q, e_o), tables, f32)
    e_far = after(e_far, e)
    up_d, down_d = after(up_d, e_far), after(down_d, e_far)
    ups += [up_x, up_xo, up_y, up_yo, up_d, over_seq(up_d)]
    downs += [down_x, down_xo, down_y, down_yo, down_d, over_seq(down_d)]
    attn = add(e, after(e_o_moved, e), e_far).astype(bf16)

    def to_dense(block):
        parts = [block[..., j * rows : (j + 1) * rows] for j in range(head_count)]
        moved = [over_head(parts[j], j) for j in range(1, head_count)]
        return [parts[0], *lax.optimization_barrier(moved)]

    attn_parts = to_dense(attn)

    def away(dense_rows):
        dense_rows = dense_rows.reshape(groups, quarter, width)
        return [dense_rows[0]] + [over_group(dense_rows[k], groups - k) for k in range(1, groups)]

    core = jnp.stack([s, d]).astype(jnp.int32)
    layer_rows, first, grad_second, slope, near, give, heads_give, small_a = dense(
        core, dense_in, grad_out, norm_gain, norm_bias, attn_parts, ups, downs
    )
    far, heads_far = over_seq(give), over_seq(heads_give)
    grad_first, near_back, give_back, *est_parts, small_b = dense_back(
        core, first, grad_second, slope, norm_gain, attn_parts, ups, downs
    )
    far_back = over_seq(give_back)
    est_moved = [over_head(est_parts[j], j) for j in range(1, head_count)]
    layer_moved = away(layer_rows)
    weight_parts = weight_grads(
        core, small_a, small_b, [near, far, near_back, far_back], attn_parts, heads_far
    )

    weight_sum = lax.psum_scatter(weight_parts, "head", scatter_dimension=0, tiled=True)[0]
    est_moved = lax.optimization_barrier((*est_moved, weight_parts))[:-1]
    grad = jnp.concatenate([est_parts[0], *est_moved], axis=1)
    grad_z, grad_o = over_place(grad), over_seq(grad)
    layer_moved = [after(x, weight_parts) for x in layer_moved]
    part, dq, dq_o = query_backward(
        signed, signed_t, bits, tables, [after(q, *layer_moved), q_o], [grad, grad_o], None, False, [f32, bf16]
    )
    layer_moved = jnp.stack([after(x, part) for x in layer_moved])

    grad_z = after(grad_z, part)
    grad_zo = over_seq(grad_z)
    dq_o = over_seq(dq_o)
    part, dq_z = query_backward(
        signed, signed_t, bits, tables, [q_z], [grad_z], part, False, [f32]
    )

    dq_own = add(dq, after(dq_o, dq_z))
    grad_zo = after(grad_zo, dq_z)
    grad_tables, dq_zo = query_backward(
        signed, signed_t, bits, tables, [after(q_zo, dq_own)], [grad_zo], part, True, [bf16]
    )

    dq_zo = over_seq(dq_zo)
    dkv_zo = key_backward(signed, signed_t, bits, kv_zo, grad_tables, bf16)

    dkv_zo_moved = over_seq(dkv_zo)
    dq_far = add(dq_z, after(dq_zo, dkv_zo)).astype(bf16)
    layer_moved = [layer_moved] + [over_head(layer_moved, j) for j in range(1, head_count)]
    weight_sum = after(weight_sum, dkv_zo)
    dkv_z = key_backward(
        signed, signed_t, bits, after(kv_z, dq_far, weight_sum), grad_tables, bf16
    )
    weight_sum = lax.psum(weight_sum, "hash")
    dq_far = over_place(dq_far)

    dkv_far = add(dkv_z, after(dkv_zo_moved, dkv_z)).astype(bf16)
    grad_q = add(dq_own, after(dq_far, dkv_z)).astype(bf16)
    layer_moved = [after(x, dkv_z) for x in layer_moved]
    dkv_o = key_backward(
        signed, signed_t, bits, after(kv_o, dkv_far, grad_q, *layer_moved), grad_tables, bf16
    )
    dk_far, dv_far = over_place(dkv_far[0]), over_place(after(dkv_far[1], dkv_o))
    qkv_half = after(qkv_near[0], dkv_z)
    qkv_moved = [over_head(qkv_half, j) for j in range(1, head_count)]

    dkv_o_moved = over_seq(dkv_o)
    dk_far = after(dk_far, dkv_o)
    qkv_near += [after(x, dkv_o) for x in qkv_moved]
    dkv = key_backward(
        signed, signed_t, bits, after(kv, dk_far, *qkv_near[1:]), grad_tables, f32
    )
    qkv_far += [over_seq(x) for x in qkv_near[1:]]

    dkv_o_moved = after(dkv_o_moved, dkv)
    qkv_far[1:] = [after(x, dkv) for x in qkv_far[1:]]
    grad_k = add(dkv[0], dkv_o_moved[0], dk_far)
    grad_v = add(dkv[1], dkv_o_moved[1], after(dv_far, dkv))
    grad_qkv = jnp.stack([grad_q, grad_k.astype(bf16), grad_v.astype(bf16)])
    qkv_parts = to_dense(grad_qkv)

    grad_in = input_grad(core, grad_first, qkv_parts, qkv_near, qkv_far)

    def in_halves(index, mine, other):
        first = jnp.where(index == 0, mine, other)
        second = jnp.where(index == 0, other, mine)
        return jnp.concatenate([first, second], axis=0)

    def split(x, index):
        half = x.shape[0] // 2
        return [lax.dynamic_slice_in_dim(x, at * half, half, 0) for at in (index, 1 - index)]

    w_grad = dot(grad_qkv.reshape(3 * head_width, n_tokens), tokens, NN).astype(bf16)
    w_keep, w_send = split(w_grad, s)
    w_keep, w_send = split(add(w_keep, over_seq(w_send)).astype(bf16), r)
    grad_moved = away(grad_in)
    w_keep = add(w_keep, over_place(w_send))
    w_send = w_keep.astype(bf16)
    grad_moved = after(jnp.stack(grad_moved), w_send)
    w_keep = add(w_keep, *[over_group(w_send, k) for k in range(1, groups)]).astype(bf16)
    grad_moved = [grad_moved] + [over_head(grad_moved, j) for j in range(1, head_count)]

    def home(blocks):
        table = jnp.stack(blocks)
        columns = []
        for q_at in range(head_count):
            block = lax.dynamic_index_in_dim(table, q_at ^ d, 0, keepdims=False)
            columns.append(
                jnp.stack(
                    [
                        lax.dynamic_index_in_dim(block, (at - g) % groups, 0, keepdims=False)
                        for at in range(seqs)
                    ],
                    axis=1,
                )
            )
        return jnp.concatenate(columns, axis=0)

    layer_out = home([after(x, grad_moved[0]) for x in layer_moved])
    grad_inputs = home(grad_moved).astype(f32)

    w_grad = in_halves(r, w_keep, over_place(w_keep))
    w_grad = in_halves(s, w_grad, over_seq(w_grad)).reshape(3, head_width, width)
    grad_w_qkv = w_grad.transpose(0, 2, 1).astype(f32)
    weight_sum = after(weight_sum, w_keep)
    weight_far = over_seq(weight_sum)
    cut = hidden_own // 2
    ends = [0, cut, 2 * cut, 2 * cut + head_width // 2]
    grad_w_up, grad_w_down, grad_w_out = [
        in_halves(s, weight_sum[a:b], weight_far[a:b]) for a, b in zip(ends, ends[1:])
    ]
    grad_w_up = grad_w_up.T.astype(f32)
    grad_w_down, grad_w_out = grad_w_down.astype(f32), grad_w_out.astype(f32)
    at = slice(ends[3], ends[3] + 16)
    small = add(weight_sum[at], weight_far[at])

    count = piece * seqs * width * hash_count * 2
    stream_rms = jnp.sqrt(jnp.sum(small[0:3], axis=1) / count)
    share = width // head_count
    norm_grads = lax.dynamic_slice_in_dim(small, d * share, share, 1)
    return (
        layer_out[None],
        grad_inputs[None],
        grad_w_qkv,
        grad_w_out,
        grad_w_up,
        grad_w_down,
        jnp.stack([norm_grads[8], norm_grads[3]]),
        jnp.stack([norm_grads[9], norm_grads[4]]),
        stream_rms,
    )


def solution(mesh):
    placed = (
        P("seq", "hash", None, None),
        P(None, None, "head"),
        P("head", None),
        P(None, "head"),
        P("head", None),
        P(),
        P(),
        P("hash", None, None),
        P(),
        P(),
    )
    return jax.shard_map(
        shards,
        mesh=mesh,
        in_specs=placed,
        out_specs=(
            P("seq", "hash", None, None),
            P("seq", "hash", None, None),
            P(None, None, "head"),
            P("head", None),
            P(None, "head"),
            P("head", None),
            P(None, "head"),
            P(None, "head"),
            P(),
        ),
        check_vma=False,
    )
```

```python
from functools import partial

import jax
import jax.numpy as jnp
import numpy as np
from jax import lax
from jax.experimental import pallas as pl
from jax.experimental.pallas import tpu as pltpu
from jax.sharding import PartitionSpec as P

HEAD_DIM = 64
HASHES = 32
BITS = 8
SETS = 8
BUCKETS = 1 << BITS
ROWS = BUCKETS * SETS

bf16 = jnp.bfloat16
f32 = jnp.float32
NN = (((1,), (0,)), ((), ()))
NT = (((1,), (1,)), ((), ()))
TN = (((0,), (0,)), ((), ()))


shape = jax.ShapeDtypeStruct


def dot(a, b, dims):
    return lax.dot_general(a, b, dims, preferred_element_type=f32)


def sides(rows, planes):
    x = rows.astype(f32)
    inv = lax.rsqrt(jnp.sum(x * x, axis=0, keepdims=True) + 1e-6)
    proj = dot(planes, rows, NN) * (3.0 * inv)
    small = jnp.exp(-proj)
    upper = 1.0 / (1.0 + small)
    return inv, upper, small * upper


def products(upper, lower, first, count):
    out = None
    for i in range(first, first + count):
        lo, up = lower[SETS * i : SETS * (i + 1)], upper[SETS * i : SETS * (i + 1)]
        out = [lo, up] if out is None else [c * lo for c in out] + [c * up for c in out]
    return out


def half_codes(upper, lower):
    low = jnp.concatenate(products(upper, lower, 0, 4), axis=0).astype(bf16)
    high = [jnp.concatenate([a, a], axis=0).astype(bf16) for a in products(upper, lower, 4, 4)]
    return low, high


def code_chunk(low, high, first, count):
    return jnp.concatenate(
        [high[a] * low[16 * j : 16 * (j + 1)] for a in range(first, first + count) for j in range(8)],
        axis=0,
    )


def pull_back(rows, planes_t, inv, upper, sums):
    total = sums[BITS * SETS :][:SETS]
    grad_proj = sums[: BITS * SETS] - upper * jnp.concatenate([total] * BITS, axis=0)
    head = grad_proj.astype(bf16)
    tail = (grad_proj - head.astype(f32)).astype(bf16)
    grad_unit = dot(planes_t, jnp.concatenate([head, tail], axis=0), NN) * (3.0 * inv)
    x = rows.astype(f32)
    return grad_unit - x * (inv * inv * jnp.sum(x * grad_unit, axis=0, keepdims=True))


def both(*refs):
    return jnp.concatenate([ref[...] for ref in refs], axis=1)


def key_kernel(planes, *refs, chunk, blocks):
    keys, vals, out = refs[:blocks], refs[blocks : 2 * blocks], refs[-1]
    start = refs[2 * blocks] if len(refs) > 2 * blocks + 1 else None
    _, upper, lower = sides(both(*keys), planes[...])
    low, high = half_codes(upper, lower)
    values = both(*vals)
    for c in range(0, 16, chunk):
        at = slice(128 * c, 128 * (c + chunk))
        part = dot(code_chunk(low, high, c, chunk), values, NT)
        if start is not None:
            part = part + start[0, at, :]
        out[0, at, :] = part.astype(out.dtype)


def query_kernel(planes, tables, *refs, chunk):
    rows, out = both(*refs[:-1]), refs[-1]
    _, upper, lower = sides(rows, planes[...])
    low, high = half_codes(upper, lower)
    acc = jnp.zeros((HEAD_DIM, rows.shape[1]), f32)
    for c in range(0, 16, chunk):
        acc += dot(tables[0, 128 * c : 128 * (c + chunk), :], code_chunk(low, high, c, chunk), TN)
    out[...] = (acc * (1.0 / HASHES)).astype(out.dtype)


def query_back_kernel(planes, planes_t, bits, tables, *refs, chunk, blocks, last):
    queries, grads = refs[: 2 * blocks], refs[2 * blocks : 3 * blocks]
    start = refs[3 * blocks] if len(refs) > 4 * blocks + 1 else None
    out, back_out = refs[-1 - blocks], refs[-blocks:]
    rows = both(*queries)
    inv, upper, lower = sides(rows, planes[...])
    low, high = half_codes(upper, lower)
    grad = both(*grads)
    sums = jnp.zeros((bits.shape[0], rows.shape[1]), f32)
    for c in range(0, 16, chunk):
        at = slice(128 * c, 128 * (c + chunk))
        codes = code_chunk(low, high, c, chunk)
        part = dot(codes, grad, NT)
        if start is not None:
            part = part + start[0, at, :]
        if last:
            part = part * (1.0 / HASHES)
        out[0, at, :] = part.astype(out.dtype)
        weighted = dot(tables[0, at, :], grad, NN).astype(bf16) * codes
        sums += dot(bits[:, at], weighted, NN)
    back = pull_back(rows, planes_t[...], inv, upper, sums * (1.0 / HASHES))
    width = back_out[0].shape[1]
    for i in range(blocks):
        back_out[i][...] = back[:, i * width : (i + 1) * width].astype(back_out[i].dtype)


def key_back_kernel(planes, planes_t, bits, ka, kb, va, vb, grad_tables, out, *, chunk):
    rows = both(ka, kb)
    inv, upper, lower = sides(rows, planes[...])
    low, high = half_codes(upper, lower)
    values = both(va, vb)
    width = rows.shape[1]
    sums = jnp.zeros((bits.shape[0], width), f32)
    grad_values = jnp.zeros((HEAD_DIM, width), f32)
    for c in range(0, 16, chunk):
        at = slice(128 * c, 128 * (c + chunk))
        codes = code_chunk(low, high, c, chunk)
        grad_values += dot(grad_tables[0, at, :], codes, TN)
        weighted = dot(grad_tables[0, at, :], values, NN).astype(bf16) * codes
        sums += dot(bits[:, at], weighted, NN)
    out[0] = pull_back(rows, planes_t[...], inv, upper, sums).astype(out.dtype)
    out[1] = grad_values.astype(out.dtype)


def bit_rows():
    out = np.zeros((80, BUCKETS, SETS), np.float32)
    for t in range(SETS):
        for i in range(BITS):
            out[i * SETS + t, :, t] = (np.arange(BUCKETS) >> i) & 1
        out[BITS * SETS + t, :, t] = 1
    return jnp.asarray(out.reshape(80, ROWS), bf16)


def whole(*shape):
    return pl.BlockSpec(shape, lambda h: (0,) * len(shape))


def head_rows(array, heads, which):
    width = array.shape[1]
    offset = (which - 3) * heads + array.shape[0] // HEAD_DIM
    return pl.BlockSpec((HEAD_DIM, width), lambda h: (h + offset, 0))


def per_head(width):
    return pl.BlockSpec((HEAD_DIM, width), lambda h: (h, 0))


def table_spec():
    return pl.BlockSpec((1, ROWS, HEAD_DIM), lambda h: (h, 0, 0))


def call(kernel, heads, micros, name, in_specs, out_specs, out_shape):
    return pl.pallas_call(
        kernel,
        grid=(heads,),
        in_specs=in_specs,
        out_specs=out_specs,
        out_shape=out_shape,
        compiler_params=pltpu.CompilerParams(vmem_limit_bytes=48 << 20),
        cost_estimate=pl.CostEstimate(
            flops=int(micros * 1.1e9), bytes_accessed=1 << 20, transcendentals=0
        ),
        name=name,
    )


def key_tables(planes, heads, blocks, start, kind):
    args = [planes, *blocks, *blocks]
    specs = [whole(64, 64)] + [head_rows(x, heads, w) for w in (1, 2) for x in blocks]
    if start is not None:
        specs.append(table_spec())
        args.append(start)
    return call(
        partial(key_kernel, chunk=2, blocks=len(blocks)),
        heads,
        30 if len(blocks) > 1 else 1,
        "key_tables",
        specs,
        table_spec(),
        shape((heads, ROWS, HEAD_DIM), kind),
    )(*args)


def query_estimates(planes, heads, near, far, tables, kind):
    width = near.shape[1] + far.shape[1]
    return call(
        partial(query_kernel, chunk=2),
        heads,
        1,
        "query_estimates",
        [whole(64, 64), table_spec(), head_rows(near, heads, 0), per_head(far.shape[1])],
        per_head(width),
        shape((heads * HEAD_DIM, width), kind),
    )(planes, tables, near, far)


def query_backward(planes, planes_t, bits, heads, tables, queries, grads, start, last, kinds):
    width = grads[0].shape[1]
    blocks = len(grads)
    specs = [whole(64, 64), whole(64, 128), whole(80, ROWS), table_spec()]
    args = [planes, planes_t, bits, tables]
    for near, far in queries:
        specs += [head_rows(near, heads, 0), per_head(far.shape[1])]
        args += [near, far]
    specs += [per_head(width)] * blocks
    args += grads
    if start is not None:
        specs.append(table_spec())
        args.append(start)
    return call(
        partial(query_back_kernel, chunk=4, blocks=blocks, last=last),
        heads,
        25 * blocks,
        "query_backward",
        specs,
        [table_spec()] + [per_head(width)] * blocks,
        [shape((heads, ROWS, HEAD_DIM), bf16 if last else f32)]
        + [shape(grads[0].shape, kind) for kind in kinds],
    )(*args)


def key_backward(planes, planes_t, bits, heads, near, far, grad_tables, kind):
    width = near.shape[1] + far.shape[1]
    return call(
        partial(key_back_kernel, chunk=4),
        heads,
        25,
        "key_backward",
        [whole(64, 64), whole(64, 128), whole(80, ROWS)]
        + [head_rows(x, heads, w) for w in (1, 2) for x in (near, far)]
        + [table_spec()],
        pl.BlockSpec((2, HEAD_DIM, width), lambda h: (0, h, 0)),
        shape((2, heads * HEAD_DIM, width), kind),
    )(planes, planes_t, bits, near, far, near, far, grad_tables)


def norm(x):
    center = x - jnp.mean(x, axis=-1, keepdims=True)
    inv = lax.rsqrt(jnp.mean(center * center, axis=-1, keepdims=True) + 1e-5)
    return center * inv, inv


def norm_back(grad, unit, inv):
    return inv * (
        grad
        - jnp.mean(grad, axis=-1, keepdims=True)
        - unit * jnp.mean(grad * unit, axis=-1, keepdims=True)
    )


def column_sum(x):
    return jnp.sum(x, axis=0, keepdims=True)


def core_rows(core, ref, which):
    half = ref.shape[0] // 2
    at = core[0] if which == 0 else 1 - core[0]
    return ref[pl.ds(pl.multiple_of(at * half, 16), half), :]


def share_rows(keep, give, at, rows):
    part = keep.shape[2]
    for out in (keep, give):
        out[at] = rows[:, :part]
        out[at + 1] = rows[:, part:]


def dense_kernel(core, x_in, grad_out, gain, bias, *refs):
    attn, ups, downs = refs[0:4], refs[4:12], refs[12:20]
    layer_out, first_out, grad_second_out, slope, keep, give, heads_give, small = refs[20:28]
    for j in range(4):
        heads_give[j] = core_rows(core, attn[j], 1)
    part = slope.shape[2]
    blocks = range(8)
    heads = jnp.concatenate([core_rows(core, attn[b // 2], b % 2) for b in blocks], axis=0)
    out_w = jnp.concatenate([downs[b][part:, :] for b in blocks], axis=0)
    attn_out = dot(heads, out_w, TN)
    resid = x_in[...].astype(f32)
    first = resid + attn_out
    first_out[...] = first
    small[0:1, :] = column_sum(resid * resid)
    small[1:2, :] = column_sum(attn_out * attn_out)
    small[2:3, :] = column_sum(first * first)
    unit_1, _ = norm(first)
    normed = (unit_1 * gain[0:1, :] + bias[0:1, :]).astype(bf16)
    share_rows(keep, give, 4, normed)
    second = normed.astype(f32)
    for b in blocks:
        pre = dot(normed, ups[b][...], NN)
        below = 0.5 * (1.0 + lax.erf(pre * 0.7071067811865476))
        rows = (pre * below).astype(bf16)
        (keep, give)[b % 2][b // 2] = rows
        slope[b] = below + pre * (0.3989422804014327 * jnp.exp(-0.5 * pre * pre))
        second = second + dot(rows, downs[b][0:part, :], NN)
    unit_2, inv_2 = norm(second)
    layer_out[...] = (unit_2 * gain[1:2, :] + bias[1:2, :]).astype(layer_out.dtype)
    grad = grad_out[...]
    small[3:4, :] = column_sum(grad * unit_2)
    small[4:5, :] = column_sum(grad)
    small[5:8, :] = jnp.zeros_like(small[5:8, :])
    grad_second = norm_back(grad * gain[1:2, :], unit_2, inv_2)
    grad_second_out[...] = grad_second
    share_rows(keep, give, 6, grad_second.astype(bf16))


def dense_back_kernel(core, first, grad_second, slope, gain, *refs):
    ups, downs = refs[0:8], refs[8:16]
    grad_first_out, keep, give = refs[16:19]
    estimates, small = refs[19:23], refs[23]
    part = slope.shape[2]
    blocks = range(8)
    grad_normed = grad_second[...]
    grad_ffn = grad_normed.astype(bf16)
    for b in blocks:
        rows = (dot(grad_ffn, downs[b][0:part, :], NT) * slope[b]).astype(bf16)
        (keep, give)[b % 2][b // 2] = rows
        grad_normed = grad_normed + dot(rows, ups[b][...], NT)
    unit, inv = norm(first[...])
    small[0:1, :] = column_sum(grad_normed * unit)
    small[1:2, :] = column_sum(grad_normed)
    small[2:8, :] = jnp.zeros_like(small[2:8, :])
    grad_first = norm_back(grad_normed * gain[0:1, :], unit, inv)
    grad_first_out[...] = grad_first
    grad_attn = grad_first.astype(bf16)
    share_rows(keep, give, 4, grad_attn)
    for b in blocks:
        half = estimates[0].shape[0] // 2
        at = core[0] if b % 2 == 0 else 1 - core[0]
        estimates[b // 2][pl.ds(pl.multiple_of(at * half, 16), half), :] = dot(
            downs[b][part:, :], grad_attn, NT
        ).astype(bf16)


def weight_grad_kernel(core, small_a, small_b, *refs):
    near, far, near_back, far_back = refs[0:4]
    attn, attn_far, out = refs[4:8], refs[8], refs[9]
    part = near.shape[2]
    sums = jnp.concatenate([small_a[...], small_b[...]], axis=0).astype(bf16)

    def wide(ref, at):
        return jnp.concatenate([ref[at], ref[at + 1]], axis=1)

    def rows(ref, other, at):
        return jnp.concatenate([wide(ref, at), wide(other, at)], axis=0)

    normed, grad_ffn = rows(near, far, 4), rows(near, far, 6)
    grad_attn = rows(near_back, far_back, 4)
    for j in range(4):
        owner = core[1] ^ j
        hidden = jnp.concatenate([near[j], far[j]], axis=0)
        grad_pre = jnp.concatenate([near_back[j], far_back[j]], axis=0)
        out[owner, 0:part, :] = dot(grad_pre, normed, TN).astype(bf16)
        out[owner, part : 2 * part, :] = dot(hidden, grad_ffn, TN).astype(bf16)
        heads = jnp.concatenate([core_rows(core, attn[j], 0), attn_far[j]], axis=1)
        at = 2 * part + heads.shape[0]
        out[owner, 2 * part : at, :] = dot(heads, grad_attn, NN).astype(bf16)
        out[owner, at : at + 16, :] = sums
        out[owner, at + 16 :, :] = jnp.zeros_like(sums)


def input_grad_kernel(core, grad_first, *refs):
    blocks, near, far, out = refs[0:4], refs[4:8], refs[8:12], refs[12]
    half = near[0].shape[1]
    total = grad_first[...]
    for which, halves in enumerate((near, far)):
        at = core[0] if which == 0 else 1 - core[0]
        at = pl.ds(pl.multiple_of(at * half, 16), half)
        for j in range(4):
            rows = jnp.concatenate([blocks[j][c, at, :] for c in range(3)], axis=0)
            weights = jnp.concatenate([halves[j][c] for c in range(3)], axis=0)
            total = total + dot(rows, weights, TN)
    out[...] = total.astype(out.dtype)


def vmem(count):
    return [pl.BlockSpec(memory_space=pltpu.VMEM)] * count


def single(kernel, core, args, out_shape, micros, name, scratch=()):
    return pl.pallas_call(
        kernel,
        in_specs=[pl.BlockSpec(memory_space=pltpu.SMEM)] + vmem(len(args)),
        out_specs=vmem(len(out_shape)),
        out_shape=out_shape,
        scratch_shapes=scratch,
        compiler_params=pltpu.CompilerParams(vmem_limit_bytes=56 << 20),
        cost_estimate=pl.CostEstimate(
            flops=int(micros * 1.1e9), bytes_accessed=1 << 20, transcendentals=0
        ),
        name=name,
    )(core, *args)


def dense(core, x_in, grad_out, gain, bias, attn, ups, downs):
    rows, width = x_in.shape
    part = ups[0].shape[1]
    out_shape = [
        shape((rows, width), bf16),
        shape((rows, width), f32),
        shape((rows, width), f32),
        shape((8, rows, part), f32),
        shape((8, rows, part), bf16),
        shape((8, rows, part), bf16),
        shape((4, attn[0].shape[0] // 2, rows), bf16),
        shape((8, width), f32),
    ]
    args = [x_in, grad_out, gain, bias, *attn, *ups, *downs]
    return single(dense_kernel, core, args, out_shape, 14, "dense")


def dense_back(core, first, grad_second, slope, gain, attn, ups, downs):
    rows, width = first.shape
    part = ups[0].shape[1]
    out_shape = [
        shape((rows, width), f32),
        shape((6, rows, part), bf16),
        shape((6, rows, part), bf16),
        *[shape(attn[0].shape, bf16)] * 4,
        shape((8, width), f32),
    ]
    args = [first, grad_second, slope, gain, *ups, *downs]
    return single(dense_back_kernel, core, args, out_shape, 8, "dense_back")


def weight_grads(core, small_a, small_b, shared, attn, attn_far):
    part, width = shared[0].shape[2], small_a.shape[1]
    out_shape = [shape((4, 2 * part + attn[0].shape[0] // 2 + 32, width), bf16)]
    args = [small_a, small_b, *shared, *attn, attn_far]
    return single(weight_grad_kernel, core, args, out_shape, 7, "weight_grads")[0]


def input_grad(core, grad_first, blocks, near, far):
    out_shape = [shape(grad_first.shape, bf16)]
    args = [grad_first, *blocks, *near, *far]
    return single(input_grad_kernel, core, args, out_shape, 3, "input_grad")[0]


def after(x, *others):
    return lax.optimization_barrier((x, *others))[0]


def add(a, *others):
    return sum([b.astype(f32) for b in others], a.astype(f32))


def shards(
    inputs,
    w_qkv,
    w_out,
    up_weight,
    down_weight,
    norm_gain,
    norm_bias,
    planes,
    mask_pos,
    cot_rows,
):
    own = inputs[0]
    piece, seqs, width = own.shape
    hash_count, head_count = lax.axis_size("hash"), lax.axis_size("head")
    groups, places = seqs, hash_count // seqs
    assert places == 2 and lax.axis_size("seq") == 2 and head_count == 4
    assert planes.shape[0] * hash_count == 4 * SETS
    quarter = piece // head_count
    rows = groups * quarter
    half_len = piece * hash_count
    head_width = w_out.shape[0]
    hidden_own = down_weight.shape[0]
    n_tokens = head_count * rows
    hash_id, d, s = lax.axis_index("hash"), lax.axis_index("head"), lax.axis_index("seq")
    g, r = hash_id // places, hash_id % places

    def over_seq(x):
        return lax.ppermute(x, "seq", [(0, 1), (1, 0)])

    def over_place(x):
        return lax.ppermute(x, "hash", [(h, h ^ 1) for h in range(hash_count)])

    def over_group(x, k):
        moves = [(h, ((h // places + k) % groups) * places + h % places) for h in range(hash_count)]
        return lax.ppermute(x, "hash", moves)

    def over_head(x, j):
        return lax.ppermute(x, "head", [(h, h ^ j) for h in range(head_count)])

    def seq_rows(block, index):
        return lax.dynamic_index_in_dim(block, index % seqs, 1, keepdims=False)

    here = [
        seq_rows(lax.dynamic_slice_in_dim(own, (d ^ j) * quarter, quarter, 0), g)
        for j in range(head_count)
    ]
    near_tokens = jnp.concatenate(here)
    my_quarter = lax.dynamic_slice_in_dim(own, d * quarter, quarter, 0)
    arrived = [over_group(seq_rows(my_quarter, g + k), k) for k in range(1, groups)]

    signed = (2 * planes - 1).astype(bf16)
    if planes.shape[0] == SETS and groups == 2:
        moves = [
            ((2 * rr + ss) * 2 + gg, (gg * places + rr) * 2 + ss)
            for gg in range(2)
            for rr in range(2)
            for ss in range(2)
        ]
        signed = lax.ppermute(signed, ("hash", "seq"), moves)
    else:
        signed = lax.all_gather(signed, "hash", axis=0, tiled=True)
        signed = lax.dynamic_slice_in_dim(signed, (r * 2 + s) * SETS, SETS, 0)
    signed = signed.transpose(1, 0, 2).reshape(BITS * SETS, HEAD_DIM)
    signed_t = jnp.concatenate([signed.T, signed.T], axis=1)
    bits = bit_rows()

    def down_half(at):
        cut, out_cut = hidden_own // 2, head_width // 2
        rows_down = lax.dynamic_slice_in_dim(down_weight, at * cut, cut, 0)
        return jnp.concatenate([rows_down, lax.dynamic_slice_in_dim(w_out, at * out_cut, out_cut, 0)])

    down, downs = down_half(s), [down_half(1 - s)]

    head_n = head_width // HEAD_DIM

    def project(w, rows_in):
        out = jnp.einsum("cde,ld->cel", w, rows_in, preferred_element_type=f32)
        return out.astype(bf16).reshape(-1, rows_in.shape[0])

    near_tokens = after(near_tokens, *arrived)
    near = project(w_qkv, near_tokens)
    near_z, near_o = over_place(near), over_seq(near)
    far_quarter = jnp.stack(arrived)
    moved = [over_head(far_quarter, j) for j in range(1, head_count)]
    ready = after(signed, near_z)
    tables = key_tables(ready, head_n, [near, near_o], None, f32)
    moved = [after(x, tables) for x in moved]

    near_z = after(near_z, tables)
    near_zo = over_seq(near_z)

    up_weight, mask_pos = after(up_weight, tables), after(mask_pos, tables)
    up, up_other = [
        lax.dynamic_slice_in_dim(up_weight, at * (hidden_own // 2), hidden_own // 2, 1) for at in (s, 1 - s)
    ]
    ups = [up_other]
    slot = jnp.arange(groups, dtype=jnp.int32)[:, None]
    place_of = ((g - slot) % groups) * places + r
    position = s * half_len + place_of * piece + d * quarter + jnp.arange(quarter, dtype=jnp.int32)[None]
    mask_row = lax.dynamic_index_in_dim(mask_pos, g, 0, keepdims=False)
    cot = lax.dynamic_index_in_dim(cot_rows, g, 0, keepdims=False)
    pick = (position.reshape(rows)[:, None] == mask_row[None]).astype(bf16)
    grad_out = jnp.dot(pick, cot, preferred_element_type=f32)
    ready = after(signed, grad_out, up, down, *ups, *downs)
    tables = key_tables(ready, head_n, [near_z, near_zo], tables, f32)

    far_tokens = jnp.stack([far_quarter, *moved]).reshape(-1, width)
    kv = project(w_qkv[1:], far_tokens)
    q = project(after(w_qkv[:1], kv), far_tokens)
    tokens = jnp.concatenate([near_tokens, far_tokens])
    dense_in = jnp.concatenate([here[0], *arrived])
    kv_z, kv_o = over_place(kv), over_seq(kv)
    q_o, q_z = over_seq(q), over_place(q)
    n_near = near.shape[1]

    ups, downs = [up] + ups, [down] + downs
    up = after(up, kv)
    up_x, up_y = over_head(up, 1), over_head(up, 2)
    qkv_cut = head_width // 2
    w_qkv_t = w_qkv.transpose(0, 2, 1)
    qkv_near = [lax.dynamic_slice_in_dim(w_qkv_t, s * qkv_cut, qkv_cut, 1)]
    qkv_far = [lax.dynamic_slice_in_dim(w_qkv_t, (1 - s) * qkv_cut, qkv_cut, 1)]
    tables = key_tables(after(signed, q), head_n, [kv, kv_o], tables, f32)

    kv_z = after(kv_z, tables)
    kv_zo = over_seq(kv_z)
    up_x, up_y = after(up_x, tables), after(up_y, tables)
    down = after(down, up_x, up_y)
    down_x, down_y, up_d = over_head(down, 1), over_head(down, 2), over_head(up_x, 2)
    up_xo, up_yo = over_seq(up_x), over_seq(up_y)
    ready = after(signed, down, tokens, dense_in, qkv_near[0], qkv_far[0])
    tables = key_tables(ready, head_n, [kv_z], tables, f32)

    q_z = after(q_z, tables)
    q_zo = over_seq(q_z)
    kv_zo = after(kv_zo, tables)
    tables = key_tables(after(signed, q_z), head_n, [kv_zo], tables, bf16)

    q_zo = after(q_zo, tables)
    up_xo, up_yo = after(up_xo, tables), after(up_yo, tables)
    q_zo = after(q_zo, up_xo, up_yo)
    e_zo = query_estimates(signed, head_n, near_zo, q_zo, tables, bf16)
    down_x, down_y = after(down_x, e_zo), after(down_y, e_zo)
    down_d = over_head(down_y, 1)
    down_xo, down_yo = over_seq(down_x), over_seq(down_y)
    e_zo_moved = over_seq(e_zo)
    e_z = query_estimates(signed, head_n, near_z, after(q_z, e_zo, down_x, down_y), tables, bf16)
    e_far = add(e_z, after(e_zo_moved, e_z)).astype(bf16)
    down_xo, down_yo = after(down_xo, e_z), after(down_yo, e_z)
    ready = after(q_o, e_far, down_xo, down_yo)
    e_o = query_estimates(signed, head_n, near_o, ready, tables, bf16)
    e_far = over_place(e_far)
    e_o_moved = over_seq(e_o)
    e = query_estimates(signed, head_n, near, after(q, e_o), tables, f32)
    e_far = after(e_far, e)
    up_d, down_d = after(up_d, e_far), after(down_d, e_far)
    ups += [up_x, up_xo, up_y, up_yo, up_d, over_seq(up_d)]
    downs += [down_x, down_xo, down_y, down_yo, down_d, over_seq(down_d)]
    attn = add(e, after(e_o_moved, e), e_far).astype(bf16)

    def to_dense(block):
        parts = []
        for j in range(head_count):
            a, b = j * quarter, n_near + j * (rows - quarter)
            cut = [block[..., a : a + quarter], block[..., b : b + rows - quarter]]
            parts.append(jnp.concatenate(cut, axis=-1))
        moved = [over_head(parts[j], j) for j in range(1, head_count)]
        return [parts[0], *lax.optimization_barrier(moved)]

    attn_parts = to_dense(attn)

    def away(dense_rows):
        dense_rows = dense_rows.reshape(groups, quarter, width)
        return [dense_rows[0]] + [over_group(dense_rows[k], groups - k) for k in range(1, groups)]

    core = jnp.stack([s, d]).astype(jnp.int32)
    layer_rows, first, grad_second, slope, keep, give, heads_give, small_a = dense(
        core, dense_in, grad_out, norm_gain, norm_bias, attn_parts, ups, downs
    )
    taken, heads_far = over_seq(give), over_seq(heads_give)
    grad_first, keep_back, give_back, *est_parts, small_b = dense_back(
        core, first, grad_second, slope, norm_gain, attn_parts, ups, downs
    )
    taken_back = over_seq(give_back)
    est_moved = [over_head(est_parts[j], j) for j in range(1, head_count)]
    est_parts = [est_parts[0], *lax.optimization_barrier(est_moved)]
    grad = jnp.concatenate(
        [x[:, :quarter] for x in est_parts] + [x[:, quarter:] for x in est_parts], axis=1
    )
    layer_moved = away(layer_rows)
    weight_parts = weight_grads(
        core, after(small_a, grad), small_b, [keep, taken, keep_back, taken_back], attn_parts, heads_far
    )

    weight_sum = lax.psum_scatter(weight_parts, "head", scatter_dimension=0, tiled=True)[0]
    grad_z = over_place(grad)
    grad_o = after(over_seq(grad), weight_parts)
    layer_moved = jnp.stack([after(x, weight_parts) for x in layer_moved])
    part, dq, dq_o = query_backward(
        signed, signed_t, bits, head_n, tables, [(near, after(q, layer_moved)), (near_o, q_o)], [grad, grad_o],
        None, False, [f32, bf16],
    )

    grad_z = after(grad_z, part)
    grad_zo = over_seq(grad_z)
    dq_o = over_seq(dq_o)
    part, dq_z = query_backward(
        signed, signed_t, bits, head_n, tables, [(near_z, q_z)], [grad_z], part, False, [f32]
    )

    dq_own = add(dq, after(dq_o, dq_z))
    grad_zo = after(grad_zo, dq_z)
    grad_tables, dq_zo = query_backward(
        signed, signed_t, bits, head_n, tables, [(near_zo, after(q_zo, dq_own))], [grad_zo], part, True, [bf16]
    )

    dq_zo = over_seq(dq_zo)
    dkv_zo = key_backward(signed, signed_t, bits, head_n, near_zo, kv_zo, grad_tables, bf16)

    dkv_zo_moved = over_seq(dkv_zo)
    dq_far = add(dq_z, after(dq_zo, dkv_zo)).astype(bf16)
    layer_moved = [layer_moved] + [over_head(layer_moved, j) for j in range(1, head_count)]
    dkv_z = key_backward(signed, signed_t, bits, head_n, near_z, after(kv_z, dq_far), grad_tables, bf16)
    dq_far = over_place(dq_far)

    dkv_far = add(dkv_z, after(dkv_zo_moved, dkv_z)).astype(bf16)
    grad_q = add(dq_own, after(dq_far, dkv_z)).astype(bf16)
    weight_sum = after(weight_sum, dkv_z)
    layer_moved = [after(x, dkv_z) for x in layer_moved]
    dkv_o = key_backward(
        signed, signed_t, bits, head_n, near_o, after(kv_o, dkv_far, grad_q, weight_sum, *layer_moved),
        grad_tables, bf16,
    )
    weight_sum = lax.psum(weight_sum, "hash")
    dk_far, dv_far = over_place(dkv_far[0]), over_place(after(dkv_far[1], dkv_o))
    qkv_half = after(qkv_near[0], dkv_z)
    qkv_moved = [over_head(qkv_half, j) for j in range(1, head_count)]

    dkv_o_moved = over_seq(dkv_o)
    dk_far = after(dk_far, dkv_o)
    qkv_near += [after(x, dkv_o) for x in qkv_moved]
    dkv = key_backward(
        signed, signed_t, bits, head_n, near, after(kv, dk_far, *qkv_near[1:]), grad_tables, f32
    )
    qkv_far += [over_seq(x) for x in qkv_near[1:]]

    dkv_o_moved = after(dkv_o_moved, dkv)
    qkv_far[1:] = [after(x, dkv) for x in qkv_far[1:]]
    grad_k = add(dkv[0], dkv_o_moved[0], dk_far)
    grad_v = add(dkv[1], dkv_o_moved[1], after(dv_far, dkv))
    grad_qkv = jnp.stack([grad_q, grad_k.astype(bf16), grad_v.astype(bf16)])
    qkv_parts = to_dense(grad_qkv)

    grad_in = input_grad(core, grad_first, qkv_parts, qkv_near, qkv_far)

    def in_halves(index, mine, other):
        first = jnp.where(index == 0, mine, other)
        second = jnp.where(index == 0, other, mine)
        return jnp.concatenate([first, second], axis=0)

    def split(x, index):
        half = x.shape[0] // 2
        return [lax.dynamic_slice_in_dim(x, at * half, half, 0) for at in (index, 1 - index)]

    w_grad = dot(grad_qkv.reshape(3 * head_width, n_tokens), tokens, NN).astype(bf16)
    w_keep, w_send = split(w_grad, s)
    w_keep, w_send = split(add(w_keep, over_seq(w_send)).astype(bf16), r)
    grad_moved = away(grad_in)
    w_keep = add(w_keep, over_place(w_send))
    w_send = w_keep.astype(bf16)
    grad_moved = after(jnp.stack(grad_moved), w_send)
    w_keep = add(w_keep, *[over_group(w_send, k) for k in range(1, groups)]).astype(bf16)
    grad_moved = [grad_moved] + [over_head(grad_moved, j) for j in range(1, head_count)]

    def home(blocks):
        table = jnp.stack(blocks)
        columns = []
        for q_at in range(head_count):
            block = lax.dynamic_index_in_dim(table, q_at ^ d, 0, keepdims=False)
            columns.append(
                jnp.stack(
                    [
                        lax.dynamic_index_in_dim(block, (at - g) % groups, 0, keepdims=False)
                        for at in range(seqs)
                    ],
                    axis=1,
                )
            )
        return jnp.concatenate(columns, axis=0)

    layer_out = home([after(x, grad_moved[0]) for x in layer_moved])
    grad_inputs = home(grad_moved).astype(f32)

    w_grad = in_halves(r, w_keep, over_place(w_keep))
    w_grad = in_halves(s, w_grad, over_seq(w_grad)).reshape(3, head_width, width)
    grad_w_qkv = w_grad.transpose(0, 2, 1).astype(f32)
    weight_sum = after(weight_sum, grad_in)
    weight_far = over_seq(weight_sum)
    cut = hidden_own // 2
    ends = [0, cut, 2 * cut, 2 * cut + head_width // 2]
    grad_w_up, grad_w_down, grad_w_out = [
        in_halves(s, weight_sum[a:b], weight_far[a:b]) for a, b in zip(ends, ends[1:])
    ]
    grad_w_up = grad_w_up.T.astype(f32)
    grad_w_down, grad_w_out = grad_w_down.astype(f32), grad_w_out.astype(f32)
    at = slice(ends[3], ends[3] + 16)
    small = add(weight_sum[at], weight_far[at])

    count = piece * seqs * width * hash_count * 2
    stream_rms = jnp.sqrt(jnp.sum(small[0:3], axis=1) / count)
    share = width // head_count
    norm_grads = lax.dynamic_slice_in_dim(small, d * share, share, 1)
    return (
        layer_out[None],
        grad_inputs[None],
        grad_w_qkv,
        grad_w_out,
        grad_w_up,
        grad_w_down,
        jnp.stack([norm_grads[8], norm_grads[3]]),
        jnp.stack([norm_grads[9], norm_grads[4]]),
        stream_rms,
    )


def solution(mesh):
    placed = (
        P("seq", "hash", None, None),
        P(None, None, "head"),
        P("head", None),
        P(None, "head"),
        P("head", None),
        P(),
        P(),
        P("hash", None, None),
        P(),
        P(),
    )
    return jax.shard_map(
        shards,
        mesh=mesh,
        in_specs=placed,
        out_specs=(
            P("seq", "hash", None, None),
            P("seq", "hash", None, None),
            P(None, None, "head"),
            P("head", None),
            P(None, "head"),
            P("head", None),
            P(None, "head"),
            P(None, "head"),
            P(),
        ),
        check_vma=False,
    )
```

```python
from functools import partial

import jax
import jax.numpy as jnp
import numpy as np
from jax import lax
from jax.experimental import pallas as pl
from jax.experimental.pallas import tpu as pltpu
from jax.sharding import PartitionSpec as P

HEAD_DIM = 64
HASHES = 32
BITS = 8
SETS = 8
BUCKETS = 1 << BITS
ROWS = BUCKETS * SETS

bf16 = jnp.bfloat16
f32 = jnp.float32
NN = (((1,), (0,)), ((), ()))
NT = (((1,), (1,)), ((), ()))
TN = (((0,), (0,)), ((), ()))


shape = jax.ShapeDtypeStruct


def dot(a, b, dims):
    return lax.dot_general(a, b, dims, preferred_element_type=f32)


def sides(rows, planes):
    x = rows.astype(f32)
    inv = lax.rsqrt(jnp.sum(x * x, axis=0, keepdims=True) + 1e-6)
    proj = dot(planes, rows, NN) * (3.0 * inv)
    small = jnp.exp(-proj)
    upper = 1.0 / (1.0 + small)
    return inv, upper, small * upper


def products(upper, lower, first, count):
    out = None
    for i in range(first, first + count):
        lo, up = lower[SETS * i : SETS * (i + 1)], upper[SETS * i : SETS * (i + 1)]
        out = [lo, up] if out is None else [c * lo for c in out] + [c * up for c in out]
    return out


def half_codes(upper, lower):
    low = jnp.concatenate(products(upper, lower, 0, 4), axis=0).astype(bf16)
    high = [jnp.concatenate([a, a], axis=0).astype(bf16) for a in products(upper, lower, 4, 4)]
    return low, high


def code_chunk(low, high, first, count):
    return jnp.concatenate(
        [high[a] * low[16 * j : 16 * (j + 1)] for a in range(first, first + count) for j in range(8)],
        axis=0,
    )


def pull_back(rows, planes_t, inv, upper, sums):
    total = sums[BITS * SETS :][:SETS]
    grad_proj = sums[: BITS * SETS] - upper * jnp.concatenate([total] * BITS, axis=0)
    head = grad_proj.astype(bf16)
    tail = (grad_proj - head.astype(f32)).astype(bf16)
    grad_unit = dot(planes_t, jnp.concatenate([head, tail], axis=0), NN) * (3.0 * inv)
    x = rows.astype(f32)
    return grad_unit - x * (inv * inv * jnp.sum(x * grad_unit, axis=0, keepdims=True))


def both(*refs):
    return jnp.concatenate([ref[...] for ref in refs], axis=1)


def key_kernel(planes, *refs, chunk, blocks):
    keys, vals, out = refs[:blocks], refs[blocks : 2 * blocks], refs[-1]
    start = refs[2 * blocks] if len(refs) > 2 * blocks + 1 else None
    _, upper, lower = sides(both(*keys), planes[...])
    low, high = half_codes(upper, lower)
    values = both(*vals)
    for c in range(0, 16, chunk):
        at = slice(128 * c, 128 * (c + chunk))
        part = dot(code_chunk(low, high, c, chunk), values, NT)
        if start is not None:
            part = part + start[0, at, :]
        out[0, at, :] = part.astype(out.dtype)


def query_kernel(planes, tables, *refs, chunk):
    rows, out = both(*refs[:-1]), refs[-1]
    _, upper, lower = sides(rows, planes[...])
    low, high = half_codes(upper, lower)
    acc = jnp.zeros((HEAD_DIM, rows.shape[1]), f32)
    for c in range(0, 16, chunk):
        acc += dot(tables[0, 128 * c : 128 * (c + chunk), :], code_chunk(low, high, c, chunk), TN)
    out[...] = (acc * (1.0 / HASHES)).astype(out.dtype)


def query_back_kernel(planes, planes_t, bits, tables, *refs, chunk, blocks, last):
    queries, grads = refs[: 2 * blocks], refs[2 * blocks : 3 * blocks]
    start = refs[3 * blocks] if len(refs) > 4 * blocks + 1 else None
    out, back_out = refs[-1 - blocks], refs[-blocks:]
    rows = both(*queries)
    inv, upper, lower = sides(rows, planes[...])
    low, high = half_codes(upper, lower)
    grad = both(*grads)
    sums = jnp.zeros((bits.shape[0], rows.shape[1]), f32)
    for c in range(0, 16, chunk):
        at = slice(128 * c, 128 * (c + chunk))
        codes = code_chunk(low, high, c, chunk)
        part = dot(codes, grad, NT)
        if start is not None:
            part = part + start[0, at, :]
        if last:
            part = part * (1.0 / HASHES)
        out[0, at, :] = part.astype(out.dtype)
        weighted = dot(tables[0, at, :], grad, NN).astype(bf16) * codes
        sums += dot(bits[:, at], weighted, NN)
    back = pull_back(rows, planes_t[...], inv, upper, sums * (1.0 / HASHES))
    width = back_out[0].shape[1]
    for i in range(blocks):
        back_out[i][...] = back[:, i * width : (i + 1) * width].astype(back_out[i].dtype)


def key_back_kernel(planes, planes_t, bits, ka, kb, va, vb, grad_tables, out, *, chunk):
    rows = both(ka, kb)
    inv, upper, lower = sides(rows, planes[...])
    low, high = half_codes(upper, lower)
    values = both(va, vb)
    width = rows.shape[1]
    sums = jnp.zeros((bits.shape[0], width), f32)
    grad_values = jnp.zeros((HEAD_DIM, width), f32)
    for c in range(0, 16, chunk):
        at = slice(128 * c, 128 * (c + chunk))
        codes = code_chunk(low, high, c, chunk)
        grad_values += dot(grad_tables[0, at, :], codes, TN)
        weighted = dot(grad_tables[0, at, :], values, NN).astype(bf16) * codes
        sums += dot(bits[:, at], weighted, NN)
    out[0] = pull_back(rows, planes_t[...], inv, upper, sums).astype(out.dtype)
    out[1] = grad_values.astype(out.dtype)


def bit_rows():
    out = np.zeros((80, BUCKETS, SETS), np.float32)
    for t in range(SETS):
        for i in range(BITS):
            out[i * SETS + t, :, t] = (np.arange(BUCKETS) >> i) & 1
        out[BITS * SETS + t, :, t] = 1
    return jnp.asarray(out.reshape(80, ROWS), bf16)


def whole(*shape):
    return pl.BlockSpec(shape, lambda h: (0,) * len(shape))


def head_rows(array, heads, which):
    width = array.shape[1]
    offset = (which - 3) * heads + array.shape[0] // HEAD_DIM
    return pl.BlockSpec((HEAD_DIM, width), lambda h: (h + offset, 0))


def per_head(width):
    return pl.BlockSpec((HEAD_DIM, width), lambda h: (h, 0))


def table_spec():
    return pl.BlockSpec((1, ROWS, HEAD_DIM), lambda h: (h, 0, 0))


def call(kernel, heads, micros, name, in_specs, out_specs, out_shape):
    return pl.pallas_call(
        kernel,
        grid=(heads,),
        in_specs=in_specs,
        out_specs=out_specs,
        out_shape=out_shape,
        compiler_params=pltpu.CompilerParams(vmem_limit_bytes=48 << 20),
        cost_estimate=pl.CostEstimate(
            flops=int(micros * 1.1e9), bytes_accessed=1 << 20, transcendentals=0
        ),
        name=name,
    )


def key_tables(planes, heads, blocks, start, kind):
    args = [planes, *blocks, *blocks]
    specs = [whole(64, 64)] + [head_rows(x, heads, w) for w in (1, 2) for x in blocks]
    if start is not None:
        specs.append(table_spec())
        args.append(start)
    return call(
        partial(key_kernel, chunk=2, blocks=len(blocks)),
        heads,
        30 if len(blocks) > 1 and start is not None else 1,
        "key_tables",
        specs,
        table_spec(),
        shape((heads, ROWS, HEAD_DIM), kind),
    )(*args)


def query_estimates(planes, heads, near, far, tables, kind):
    width = near.shape[1] + far.shape[1]
    return call(
        partial(query_kernel, chunk=2),
        heads,
        1,
        "query_estimates",
        [whole(64, 64), table_spec(), head_rows(near, heads, 0), per_head(far.shape[1])],
        per_head(width),
        shape((heads * HEAD_DIM, width), kind),
    )(planes, tables, near, far)


def query_backward(planes, planes_t, bits, heads, tables, queries, grads, start, last, kinds):
    width = grads[0].shape[1]
    blocks = len(grads)
    specs = [whole(64, 64), whole(64, 128), whole(80, ROWS), table_spec()]
    args = [planes, planes_t, bits, tables]
    for near, far in queries:
        specs += [head_rows(near, heads, 0), per_head(far.shape[1])]
        args += [near, far]
    specs += [per_head(width)] * blocks
    args += grads
    if start is not None:
        specs.append(table_spec())
        args.append(start)
    return call(
        partial(query_back_kernel, chunk=4, blocks=blocks, last=last),
        heads,
        25 * blocks,
        "query_backward",
        specs,
        [table_spec()] + [per_head(width)] * blocks,
        [shape((heads, ROWS, HEAD_DIM), bf16 if last else f32)]
        + [shape(grads[0].shape, kind) for kind in kinds],
    )(*args)


def key_backward(planes, planes_t, bits, heads, near, far, grad_tables, kind):
    width = near.shape[1] + far.shape[1]
    return call(
        partial(key_back_kernel, chunk=4),
        heads,
        25,
        "key_backward",
        [whole(64, 64), whole(64, 128), whole(80, ROWS)]
        + [head_rows(x, heads, w) for w in (1, 2) for x in (near, far)]
        + [table_spec()],
        pl.BlockSpec((2, HEAD_DIM, width), lambda h: (0, h, 0)),
        shape((2, heads * HEAD_DIM, width), kind),
    )(planes, planes_t, bits, near, far, near, far, grad_tables)


def norm(x):
    center = x - jnp.mean(x, axis=-1, keepdims=True)
    inv = lax.rsqrt(jnp.mean(center * center, axis=-1, keepdims=True) + 1e-5)
    return center * inv, inv


def norm_back(grad, unit, inv):
    return inv * (
        grad
        - jnp.mean(grad, axis=-1, keepdims=True)
        - unit * jnp.mean(grad * unit, axis=-1, keepdims=True)
    )


def column_sum(x):
    return jnp.sum(x, axis=0, keepdims=True)


def core_rows(core, ref, which):
    half = ref.shape[0] // 2
    at = core[0] if which == 0 else 1 - core[0]
    return ref[pl.ds(pl.multiple_of(at * half, 16), half), :]


def share_rows(keep, give, at, rows):
    part = keep.shape[2]
    for out in (keep, give):
        out[at] = rows[:, :part]
        out[at + 1] = rows[:, part:]


def dense_kernel(core, x_in, grad_out, gain, bias, *refs):
    attn, ups, downs = refs[0:4], refs[4:12], refs[12:20]
    layer_out, first_out, grad_second_out, slope, keep, give, heads_give, small = refs[20:28]
    for j in range(4):
        heads_give[j] = core_rows(core, attn[j], 1)
    part = slope.shape[2]
    blocks = range(8)
    heads = jnp.concatenate([core_rows(core, attn[b // 2], b % 2) for b in blocks], axis=0)
    out_w = jnp.concatenate([downs[b][part:, :] for b in blocks], axis=0)
    attn_out = dot(heads, out_w, TN)
    resid = x_in[...].astype(f32)
    first = resid + attn_out
    first_out[...] = first
    small[0:1, :] = column_sum(resid * resid)
    small[1:2, :] = column_sum(attn_out * attn_out)
    small[2:3, :] = column_sum(first * first)
    unit_1, _ = norm(first)
    normed = (unit_1 * gain[0:1, :] + bias[0:1, :]).astype(bf16)
    share_rows(keep, give, 4, normed)
    second = normed.astype(f32)
    for b in blocks:
        pre = dot(normed, ups[b][...], NN)
        below = 0.5 * (1.0 + lax.erf(pre * 0.7071067811865476))
        rows = (pre * below).astype(bf16)
        (keep, give)[b % 2][b // 2] = rows
        slope[b] = below + pre * (0.3989422804014327 * jnp.exp(-0.5 * pre * pre))
        second = second + dot(rows, downs[b][0:part, :], NN)
    unit_2, inv_2 = norm(second)
    layer_out[...] = (unit_2 * gain[1:2, :] + bias[1:2, :]).astype(layer_out.dtype)
    grad = grad_out[...]
    small[3:4, :] = column_sum(grad * unit_2)
    small[4:5, :] = column_sum(grad)
    small[5:8, :] = jnp.zeros_like(small[5:8, :])
    grad_second = norm_back(grad * gain[1:2, :], unit_2, inv_2)
    grad_second_out[...] = grad_second
    share_rows(keep, give, 6, grad_second.astype(bf16))


def dense_back_kernel(core, first, grad_second, slope, gain, *refs):
    ups, downs = refs[0:8], refs[8:16]
    grad_first_out, keep, give = refs[16:19]
    estimates, small = refs[19:23], refs[23]
    part = slope.shape[2]
    blocks = range(8)
    grad_normed = grad_second[...]
    grad_ffn = grad_normed.astype(bf16)
    for b in blocks:
        rows = (dot(grad_ffn, downs[b][0:part, :], NT) * slope[b]).astype(bf16)
        (keep, give)[b % 2][b // 2] = rows
        grad_normed = grad_normed + dot(rows, ups[b][...], NT)
    unit, inv = norm(first[...])
    small[0:1, :] = column_sum(grad_normed * unit)
    small[1:2, :] = column_sum(grad_normed)
    small[2:8, :] = jnp.zeros_like(small[2:8, :])
    grad_first = norm_back(grad_normed * gain[0:1, :], unit, inv)
    grad_first_out[...] = grad_first
    grad_attn = grad_first.astype(bf16)
    share_rows(keep, give, 4, grad_attn)
    for b in blocks:
        half = estimates[0].shape[0] // 2
        at = core[0] if b % 2 == 0 else 1 - core[0]
        estimates[b // 2][pl.ds(pl.multiple_of(at * half, 16), half), :] = dot(
            downs[b][part:, :], grad_attn, NT
        ).astype(bf16)


def weight_grad_kernel(core, small_a, small_b, *refs):
    near, far, near_back, far_back = refs[0:4]
    attn, attn_far, out = refs[4:8], refs[8], refs[9]
    part = near.shape[2]
    sums = jnp.concatenate([small_a[...], small_b[...]], axis=0).astype(bf16)

    def wide(ref, at):
        return jnp.concatenate([ref[at], ref[at + 1]], axis=1)

    def rows(ref, other, at):
        return jnp.concatenate([wide(ref, at), wide(other, at)], axis=0)

    normed, grad_ffn = rows(near, far, 4), rows(near, far, 6)
    grad_attn = rows(near_back, far_back, 4)
    for j in range(4):
        owner = core[1] ^ j
        hidden = jnp.concatenate([near[j], far[j]], axis=0)
        grad_pre = jnp.concatenate([near_back[j], far_back[j]], axis=0)
        out[owner, 0:part, :] = dot(grad_pre, normed, TN).astype(bf16)
        out[owner, part : 2 * part, :] = dot(hidden, grad_ffn, TN).astype(bf16)
        heads = jnp.concatenate([core_rows(core, attn[j], 0), attn_far[j]], axis=1)
        at = 2 * part + heads.shape[0]
        out[owner, 2 * part : at, :] = dot(heads, grad_attn, NN).astype(bf16)
        out[owner, at : at + 16, :] = sums
        out[owner, at + 16 :, :] = jnp.zeros_like(sums)


def input_grad_kernel(core, grad_first, *refs):
    blocks, near, far, out = refs[0:4], refs[4:8], refs[8:12], refs[12]
    half = near[0].shape[1]
    total = grad_first[...]
    for which, halves in enumerate((near, far)):
        at = core[0] if which == 0 else 1 - core[0]
        at = pl.ds(pl.multiple_of(at * half, 16), half)
        for j in range(4):
            rows = jnp.concatenate([blocks[j][c, at, :] for c in range(3)], axis=0)
            weights = jnp.concatenate([halves[j][c] for c in range(3)], axis=0)
            total = total + dot(rows, weights, TN)
    out[...] = total.astype(out.dtype)


def vmem(count):
    return [pl.BlockSpec(memory_space=pltpu.VMEM)] * count


def single(kernel, core, args, out_shape, micros, name, scratch=()):
    return pl.pallas_call(
        kernel,
        in_specs=[pl.BlockSpec(memory_space=pltpu.SMEM)] + vmem(len(args)),
        out_specs=vmem(len(out_shape)),
        out_shape=out_shape,
        scratch_shapes=scratch,
        compiler_params=pltpu.CompilerParams(vmem_limit_bytes=56 << 20),
        cost_estimate=pl.CostEstimate(
            flops=int(micros * 1.1e9), bytes_accessed=1 << 20, transcendentals=0
        ),
        name=name,
    )(core, *args)


def dense(core, x_in, grad_out, gain, bias, attn, ups, downs):
    rows, width = x_in.shape
    part = ups[0].shape[1]
    out_shape = [
        shape((rows, width), bf16),
        shape((rows, width), f32),
        shape((rows, width), f32),
        shape((8, rows, part), f32),
        shape((8, rows, part), bf16),
        shape((8, rows, part), bf16),
        shape((4, attn[0].shape[0] // 2, rows), bf16),
        shape((8, width), f32),
    ]
    args = [x_in, grad_out, gain, bias, *attn, *ups, *downs]
    return single(dense_kernel, core, args, out_shape, 14, "dense")


def dense_back(core, first, grad_second, slope, gain, attn, ups, downs):
    rows, width = first.shape
    part = ups[0].shape[1]
    out_shape = [
        shape((rows, width), f32),
        shape((6, rows, part), bf16),
        shape((6, rows, part), bf16),
        *[shape(attn[0].shape, bf16)] * 4,
        shape((8, width), f32),
    ]
    args = [first, grad_second, slope, gain, *ups, *downs]
    return single(dense_back_kernel, core, args, out_shape, 8, "dense_back")


def weight_grads(core, small_a, small_b, shared, attn, attn_far):
    part, width = shared[0].shape[2], small_a.shape[1]
    out_shape = [shape((4, 2 * part + attn[0].shape[0] // 2 + 32, width), bf16)]
    args = [small_a, small_b, *shared, *attn, attn_far]
    return single(weight_grad_kernel, core, args, out_shape, 7, "weight_grads")[0]


def input_grad(core, grad_first, blocks, near, far):
    out_shape = [shape(grad_first.shape, bf16)]
    args = [grad_first, *blocks, *near, *far]
    return single(input_grad_kernel, core, args, out_shape, 3, "input_grad")[0]


def after(x, *others):
    return lax.optimization_barrier((x, *others))[0]


def add(a, *others):
    return sum([b.astype(f32) for b in others], a.astype(f32))


def shards(
    inputs,
    w_qkv,
    w_out,
    up_weight,
    down_weight,
    norm_gain,
    norm_bias,
    planes,
    mask_pos,
    cot_rows,
):
    own = inputs[0]
    piece, seqs, width = own.shape
    hash_count, head_count = lax.axis_size("hash"), lax.axis_size("head")
    groups, places = seqs, hash_count // seqs
    assert places == 2 and lax.axis_size("seq") == 2 and head_count == 4
    assert planes.shape[0] * hash_count == 4 * SETS
    quarter = piece // head_count
    rows = groups * quarter
    half_len = piece * hash_count
    head_width = w_out.shape[0]
    hidden_own = down_weight.shape[0]
    n_tokens = head_count * rows
    hash_id, d, s = lax.axis_index("hash"), lax.axis_index("head"), lax.axis_index("seq")
    g, r = hash_id // places, hash_id % places

    def over_seq(x):
        return lax.ppermute(x, "seq", [(0, 1), (1, 0)])

    def over_place(x):
        return lax.ppermute(x, "hash", [(h, h ^ 1) for h in range(hash_count)])

    def over_group(x, k):
        moves = [(h, ((h // places + k) % groups) * places + h % places) for h in range(hash_count)]
        return lax.ppermute(x, "hash", moves)

    def over_head(x, j):
        return lax.ppermute(x, "head", [(h, h ^ j) for h in range(head_count)])

    def seq_rows(block, index):
        return lax.dynamic_index_in_dim(block, index % seqs, 1, keepdims=False)

    here = [
        seq_rows(lax.dynamic_slice_in_dim(own, (d ^ j) * quarter, quarter, 0), g)
        for j in range(head_count)
    ]
    near_tokens = jnp.concatenate(here)
    my_quarter = lax.dynamic_slice_in_dim(own, d * quarter, quarter, 0)
    sent = [seq_rows(my_quarter, g + k) for k in range(1, groups)]
    arrived = [over_group(x, k + 1) for k, x in enumerate(sent)]

    signed = (2 * planes - 1).astype(bf16)
    if planes.shape[0] == SETS and groups == 2:
        moves = [
            ((2 * rr + ss) * 2 + gg, (gg * places + rr) * 2 + ss)
            for gg in range(2)
            for rr in range(2)
            for ss in range(2)
        ]
        signed = lax.ppermute(signed, ("hash", "seq"), moves)
    else:
        signed = lax.all_gather(signed, "hash", axis=0, tiled=True)
        signed = lax.dynamic_slice_in_dim(signed, (r * 2 + s) * SETS, SETS, 0)
    signed = signed.transpose(1, 0, 2).reshape(BITS * SETS, HEAD_DIM)
    signed_t = jnp.concatenate([signed.T, signed.T], axis=1)
    bits = bit_rows()

    def down_half(at):
        cut, out_cut = hidden_own // 2, head_width // 2
        rows_down = lax.dynamic_slice_in_dim(down_weight, at * cut, cut, 0)
        return jnp.concatenate([rows_down, lax.dynamic_slice_in_dim(w_out, at * out_cut, out_cut, 0)])

    down, downs = down_half(s), [down_half(1 - s)]
    up_weight = after(up_weight, *sent)
    up, up_other = [
        lax.dynamic_slice_in_dim(up_weight, at * (hidden_own // 2), hidden_own // 2, 1) for at in (s, 1 - s)
    ]
    ups = [up, up_other]
    up_x, up_y = over_head(up, 1), over_head(up, 2)

    head_n = head_width // HEAD_DIM

    def project(w, rows_in):
        out = jnp.einsum("cde,ld->cel", w, rows_in, preferred_element_type=f32)
        return out.astype(bf16).reshape(-1, rows_in.shape[0])

    near_tokens = after(near_tokens, *arrived)
    near = project(w_qkv, near_tokens)
    near_z, near_o = over_place(near), over_seq(near)
    far_quarter = jnp.stack(arrived)
    moved = [over_head(far_quarter, j) for j in range(1, head_count)]
    tables = key_tables(after(signed, up_x, up_y), head_n, [near, near_o], None, f32)
    moved = [after(x, tables) for x in moved]

    near_z = after(near_z, tables)
    near_zo = over_seq(near_z)

    mask_pos = after(mask_pos, tables)
    slot = jnp.arange(groups, dtype=jnp.int32)[:, None]
    place_of = ((g - slot) % groups) * places + r
    position = s * half_len + place_of * piece + d * quarter + jnp.arange(quarter, dtype=jnp.int32)[None]
    mask_row = lax.dynamic_index_in_dim(mask_pos, g, 0, keepdims=False)
    cot = lax.dynamic_index_in_dim(cot_rows, g, 0, keepdims=False)
    pick = (position.reshape(rows)[:, None] == mask_row[None]).astype(bf16)
    grad_out = jnp.dot(pick, cot, preferred_element_type=f32)
    ready = after(signed, grad_out, down, *ups, *downs)
    tables = key_tables(ready, head_n, [near_z, near_zo], tables, f32)

    far_tokens = jnp.stack([far_quarter, *moved]).reshape(-1, width)
    kv = project(w_qkv[1:], far_tokens)
    q = project(after(w_qkv[:1], kv), far_tokens)
    tokens = jnp.concatenate([near_tokens, far_tokens])
    dense_in = jnp.concatenate([here[0], *arrived])
    kv_z, kv_o = over_place(kv), over_seq(kv)
    q_o, q_z = over_seq(q), over_place(q)
    n_near = near.shape[1]

    downs = [down] + downs
    down = after(down, kv)
    down_x, down_y, up_d = over_head(down, 1), over_head(down, 2), over_head(after(up_x, kv), 2)
    up_xo, up_yo = over_seq(after(up_x, kv)), over_seq(after(up_y, kv))
    qkv_cut = head_width // 2
    w_qkv_t = w_qkv.transpose(0, 2, 1)
    qkv_near = [lax.dynamic_slice_in_dim(w_qkv_t, s * qkv_cut, qkv_cut, 1)]
    qkv_far = [lax.dynamic_slice_in_dim(w_qkv_t, (1 - s) * qkv_cut, qkv_cut, 1)]
    tables = key_tables(after(signed, q), head_n, [kv, kv_o], tables, f32)

    kv_z = after(kv_z, tables)
    kv_zo = over_seq(kv_z)
    up_xo, up_yo = after(up_xo, tables), after(up_yo, tables)
    ready = after(signed, up_xo, up_yo, tokens, dense_in, qkv_near[0], qkv_far[0])
    tables = key_tables(ready, head_n, [kv_z], tables, f32)

    q_z = after(q_z, tables)
    q_zo = over_seq(q_z)
    kv_zo = after(kv_zo, tables)
    down_x, down_y = after(down_x, tables), after(down_y, tables)
    down_d = over_head(down_y, 1)
    down_xo, down_yo = over_seq(down_x), over_seq(down_y)
    tables = key_tables(after(signed, q_z, down_x, down_y), head_n, [kv_zo], tables, bf16)

    q_zo = after(q_zo, tables)
    e_zo = query_estimates(signed, head_n, near_zo, q_zo, tables, bf16)
    e_zo_moved = over_seq(e_zo)
    e_z = query_estimates(signed, head_n, near_z, after(q_z, e_zo), tables, bf16)
    e_far = add(e_z, after(e_zo_moved, e_z)).astype(bf16)
    down_xo, down_yo = after(down_xo, e_z), after(down_yo, e_z)
    ready = after(q_o, e_far, down_xo, down_yo)
    e_o = query_estimates(signed, head_n, near_o, ready, tables, bf16)
    e_far = over_place(e_far)
    e_o_moved = over_seq(e_o)
    e = query_estimates(signed, head_n, near, after(q, e_o), tables, f32)
    e_far = after(e_far, e)
    up_d, down_d = after(up_d, e_far), after(down_d, e_far)
    ups += [up_x, up_xo, up_y, up_yo, up_d, over_seq(up_d)]
    downs += [down_x, down_xo, down_y, down_yo, down_d, over_seq(down_d)]
    attn = add(e, after(e_o_moved, e), e_far).astype(bf16)

    def to_dense(block):
        parts = []
        for j in range(head_count):
            a, b = j * quarter, n_near + j * (rows - quarter)
            cut = [block[..., a : a + quarter], block[..., b : b + rows - quarter]]
            parts.append(jnp.concatenate(cut, axis=-1))
        moved = [over_head(parts[j], j) for j in range(1, head_count)]
        return [parts[0], *lax.optimization_barrier(moved)]

    attn_parts = to_dense(attn)

    def away(dense_rows):
        dense_rows = dense_rows.reshape(groups, quarter, width)
        return [dense_rows[0]] + [over_group(dense_rows[k], groups - k) for k in range(1, groups)]

    core = jnp.stack([s, d]).astype(jnp.int32)
    layer_rows, first, grad_second, slope, keep, give, heads_give, small_a = dense(
        core, dense_in, grad_out, norm_gain, norm_bias, attn_parts, ups, downs
    )
    taken, heads_far = over_seq(give), over_seq(heads_give)
    grad_first, keep_back, give_back, *est_parts, small_b = dense_back(
        core, first, grad_second, slope, norm_gain, attn_parts, ups, downs
    )
    taken_back = over_seq(give_back)
    est_moved = [over_head(est_parts[j], j) for j in range(1, head_count)]
    est_parts = [est_parts[0], *lax.optimization_barrier(est_moved)]
    grad = jnp.concatenate(
        [x[:, :quarter] for x in est_parts] + [x[:, quarter:] for x in est_parts], axis=1
    )
    layer_moved = away(layer_rows)
    weight_parts = weight_grads(
        core, after(small_a, grad), small_b, [keep, taken, keep_back, taken_back], attn_parts, heads_far
    )

    weight_sum = lax.psum_scatter(weight_parts, "head", scatter_dimension=0, tiled=True)[0]
    grad_z = over_place(grad)
    grad_o = after(over_seq(grad), weight_parts)
    layer_moved = jnp.stack([after(x, weight_parts) for x in layer_moved])
    part, dq, dq_o = query_backward(
        signed, signed_t, bits, head_n, tables, [(near, after(q, layer_moved)), (near_o, q_o)], [grad, grad_o],
        None, False, [f32, bf16],
    )

    grad_z = after(grad_z, part)
    grad_zo = over_seq(grad_z)
    dq_o = over_seq(dq_o)
    part, dq_z = query_backward(
        signed, signed_t, bits, head_n, tables, [(near_z, q_z)], [grad_z], part, False, [f32]
    )

    dq_own = add(dq, after(dq_o, dq_z))
    grad_zo = after(grad_zo, dq_z)
    grad_tables, dq_zo = query_backward(
        signed, signed_t, bits, head_n, tables, [(near_zo, after(q_zo, dq_own))], [grad_zo], part, True, [bf16]
    )

    dq_zo = over_seq(dq_zo)
    dkv_zo = key_backward(signed, signed_t, bits, head_n, near_zo, kv_zo, grad_tables, bf16)

    dkv_zo_moved = over_seq(dkv_zo)
    dq_far = add(dq_z, after(dq_zo, dkv_zo)).astype(bf16)
    layer_moved = [layer_moved] + [over_head(layer_moved, j) for j in range(1, head_count)]
    dkv_z = key_backward(signed, signed_t, bits, head_n, near_z, after(kv_z, dq_far), grad_tables, bf16)
    dq_far = over_place(dq_far)

    dkv_far = add(dkv_z, after(dkv_zo_moved, dkv_z)).astype(bf16)
    grad_q = add(dq_own, after(dq_far, dkv_z)).astype(bf16)
    weight_sum = after(weight_sum, dkv_z)
    layer_moved = [after(x, dkv_z) for x in layer_moved]
    dkv_o = key_backward(
        signed, signed_t, bits, head_n, near_o, after(kv_o, dkv_far, grad_q, weight_sum, *layer_moved),
        grad_tables, bf16,
    )
    weight_sum = lax.psum(weight_sum, "hash")
    dk_far, dv_far = over_place(dkv_far[0]), over_place(after(dkv_far[1], dkv_o))
    qkv_half = after(qkv_near[0], dkv_z)
    qkv_moved = [over_head(qkv_half, j) for j in range(1, head_count)]

    dkv_o_moved = over_seq(dkv_o)
    dk_far = after(dk_far, dkv_o)
    qkv_near += [after(x, dkv_o) for x in qkv_moved]
    dkv = key_backward(
        signed, signed_t, bits, head_n, near, after(kv, dk_far, *qkv_near[1:]), grad_tables, f32
    )
    qkv_far += [over_seq(x) for x in qkv_near[1:]]

    dkv_o_moved = after(dkv_o_moved, dkv)
    qkv_far[1:] = [after(x, dkv) for x in qkv_far[1:]]
    grad_k = add(dkv[0], dkv_o_moved[0], dk_far)
    grad_v = add(dkv[1], dkv_o_moved[1], after(dv_far, dkv))
    grad_qkv = jnp.stack([grad_q, grad_k.astype(bf16), grad_v.astype(bf16)])
    qkv_parts = to_dense(grad_qkv)

    grad_in = input_grad(core, grad_first, qkv_parts, qkv_near, qkv_far)

    def in_halves(index, mine, other):
        first = jnp.where(index == 0, mine, other)
        second = jnp.where(index == 0, other, mine)
        return jnp.concatenate([first, second], axis=0)

    def split(x, index):
        half = x.shape[0] // 2
        return [lax.dynamic_slice_in_dim(x, at * half, half, 0) for at in (index, 1 - index)]

    w_grad = dot(grad_qkv.reshape(3 * head_width, n_tokens), tokens, NN).astype(bf16)
    w_keep, w_send = split(w_grad, s)
    w_keep, w_send = split(add(w_keep, over_seq(w_send)).astype(bf16), r)
    grad_moved = away(grad_in)
    w_keep = add(w_keep, over_place(w_send))
    w_send = w_keep.astype(bf16)
    grad_moved = after(jnp.stack(grad_moved), w_send)
    w_keep = add(w_keep, *[over_group(w_send, k) for k in range(1, groups)]).astype(bf16)
    grad_moved = [grad_moved] + [over_head(grad_moved, j) for j in range(1, head_count)]

    def home(blocks):
        table = jnp.stack(blocks)
        columns = []
        for q_at in range(head_count):
            block = lax.dynamic_index_in_dim(table, q_at ^ d, 0, keepdims=False)
            columns.append(
                jnp.stack(
                    [
                        lax.dynamic_index_in_dim(block, (at - g) % groups, 0, keepdims=False)
                        for at in range(seqs)
                    ],
                    axis=1,
                )
            )
        return jnp.concatenate(columns, axis=0)

    layer_out = home([after(x, grad_moved[0]) for x in layer_moved])
    grad_inputs = home(grad_moved).astype(f32)

    w_grad = in_halves(r, w_keep, over_place(w_keep))
    w_grad = in_halves(s, w_grad, over_seq(w_grad)).reshape(3, head_width, width)
    grad_w_qkv = w_grad.transpose(0, 2, 1).astype(f32)
    weight_sum = after(weight_sum, grad_in)
    weight_far = over_seq(weight_sum)
    cut = hidden_own // 2
    ends = [0, cut, 2 * cut, 2 * cut + head_width // 2]
    grad_w_up, grad_w_down, grad_w_out = [
        in_halves(s, weight_sum[a:b], weight_far[a:b]) for a, b in zip(ends, ends[1:])
    ]
    grad_w_up = grad_w_up.T.astype(f32)
    grad_w_down, grad_w_out = grad_w_down.astype(f32), grad_w_out.astype(f32)
    at = slice(ends[3], ends[3] + 16)
    small = add(weight_sum[at], weight_far[at])

    count = piece * seqs * width * hash_count * 2
    stream_rms = jnp.sqrt(jnp.sum(small[0:3], axis=1) / count)
    share = width // head_count
    norm_grads = lax.dynamic_slice_in_dim(small, d * share, share, 1)
    return (
        layer_out[None],
        grad_inputs[None],
        grad_w_qkv,
        grad_w_out,
        grad_w_up,
        grad_w_down,
        jnp.stack([norm_grads[8], norm_grads[3]]),
        jnp.stack([norm_grads[9], norm_grads[4]]),
        stream_rms,
    )


def solution(mesh):
    placed = (
        P("seq", "hash", None, None),
        P(None, None, "head"),
        P("head", None),
        P(None, "head"),
        P("head", None),
        P(),
        P(),
        P("hash", None, None),
        P(),
        P(),
    )
    return jax.shard_map(
        shards,
        mesh=mesh,
        in_specs=placed,
        out_specs=(
            P("seq", "hash", None, None),
            P("seq", "hash", None, None),
            P(None, None, "head"),
            P("head", None),
            P(None, "head"),
            P("head", None),
            P(None, "head"),
            P(None, "head"),
            P(),
        ),
        check_vma=False,
    )
```

```python
from functools import partial

import jax
import jax.numpy as jnp
import numpy as np
from jax import lax
from jax.experimental import pallas as pl
from jax.experimental.pallas import tpu as pltpu
from jax.sharding import PartitionSpec as P

HEAD_DIM = 64
HASHES = 32
BITS = 8
SETS = 8
BUCKETS = 1 << BITS
ROWS = BUCKETS * SETS

bf16 = jnp.bfloat16
f32 = jnp.float32
NN = (((1,), (0,)), ((), ()))
NT = (((1,), (1,)), ((), ()))
TN = (((0,), (0,)), ((), ()))


shape = jax.ShapeDtypeStruct


def dot(a, b, dims):
    return lax.dot_general(a, b, dims, preferred_element_type=f32)


def sides(rows, planes):
    x = rows.astype(f32)
    inv = lax.rsqrt(jnp.sum(x * x, axis=0, keepdims=True) + 1e-6)
    proj = dot(planes, rows, NN) * (3.0 * inv)
    small = jnp.exp(-proj)
    upper = 1.0 / (1.0 + small)
    return inv, upper, small * upper


def products(upper, lower, first, count):
    out = None
    for i in range(first, first + count):
        lo, up = lower[SETS * i : SETS * (i + 1)], upper[SETS * i : SETS * (i + 1)]
        out = [lo, up] if out is None else [c * lo for c in out] + [c * up for c in out]
    return out


def half_codes(upper, lower):
    low = jnp.concatenate(products(upper, lower, 0, 4), axis=0).astype(bf16)
    high = [jnp.concatenate([a, a], axis=0).astype(bf16) for a in products(upper, lower, 4, 4)]
    return low, high


def code_chunk(low, high, first, count):
    return jnp.concatenate(
        [high[a] * low[16 * j : 16 * (j + 1)] for a in range(first, first + count) for j in range(8)],
        axis=0,
    )


def pull_back(rows, planes_t, inv, upper, sums):
    total = sums[BITS * SETS :][:SETS]
    grad_proj = sums[: BITS * SETS] - upper * jnp.concatenate([total] * BITS, axis=0)
    head = grad_proj.astype(bf16)
    tail = (grad_proj - head.astype(f32)).astype(bf16)
    grad_unit = dot(planes_t, jnp.concatenate([head, tail], axis=0), NN) * (3.0 * inv)
    x = rows.astype(f32)
    return grad_unit - x * (inv * inv * jnp.sum(x * grad_unit, axis=0, keepdims=True))


def both(*refs):
    return jnp.concatenate([ref[...] for ref in refs], axis=1)


def key_kernel(planes, *refs, chunk, blocks):
    keys, vals, out = refs[:blocks], refs[blocks : 2 * blocks], refs[-1]
    start = refs[2 * blocks] if len(refs) > 2 * blocks + 1 else None
    _, upper, lower = sides(both(*keys), planes[...])
    low, high = half_codes(upper, lower)
    values = both(*vals)
    for c in range(0, 16, chunk):
        at = slice(128 * c, 128 * (c + chunk))
        part = dot(code_chunk(low, high, c, chunk), values, NT)
        if start is not None:
            part = part + start[0, at, :]
        out[0, at, :] = part.astype(out.dtype)


def query_kernel(planes, tables, *refs, chunk):
    rows, out = both(*refs[:-1]), refs[-1]
    _, upper, lower = sides(rows, planes[...])
    low, high = half_codes(upper, lower)
    acc = jnp.zeros((HEAD_DIM, rows.shape[1]), f32)
    for c in range(0, 16, chunk):
        acc += dot(tables[0, 128 * c : 128 * (c + chunk), :], code_chunk(low, high, c, chunk), TN)
    out[...] = (acc * (1.0 / HASHES)).astype(out.dtype)


def query_back_kernel(planes, planes_t, bits, tables, *refs, chunk, blocks, last):
    queries, grads = refs[: 2 * blocks], refs[2 * blocks : 3 * blocks]
    start = refs[3 * blocks] if len(refs) > 4 * blocks + 1 else None
    out, back_out = refs[-1 - blocks], refs[-blocks:]
    rows = both(*queries)
    inv, upper, lower = sides(rows, planes[...])
    low, high = half_codes(upper, lower)
    grad = both(*grads)
    sums = jnp.zeros((bits.shape[0], rows.shape[1]), f32)
    for c in range(0, 16, chunk):
        at = slice(128 * c, 128 * (c + chunk))
        codes = code_chunk(low, high, c, chunk)
        part = dot(codes, grad, NT)
        if start is not None:
            part = part + start[0, at, :]
        if last:
            part = part * (1.0 / HASHES)
        out[0, at, :] = part.astype(out.dtype)
        weighted = dot(tables[0, at, :], grad, NN).astype(bf16) * codes
        sums += dot(bits[:, at], weighted, NN)
    back = pull_back(rows, planes_t[...], inv, upper, sums * (1.0 / HASHES))
    width = back_out[0].shape[1]
    for i in range(blocks):
        back_out[i][...] = back[:, i * width : (i + 1) * width].astype(back_out[i].dtype)


def key_back_kernel(planes, planes_t, bits, ka, kb, va, vb, grad_tables, out, *, chunk):
    rows = both(ka, kb)
    inv, upper, lower = sides(rows, planes[...])
    low, high = half_codes(upper, lower)
    values = both(va, vb)
    width = rows.shape[1]
    sums = jnp.zeros((bits.shape[0], width), f32)
    grad_values = jnp.zeros((HEAD_DIM, width), f32)
    for c in range(0, 16, chunk):
        at = slice(128 * c, 128 * (c + chunk))
        codes = code_chunk(low, high, c, chunk)
        grad_values += dot(grad_tables[0, at, :], codes, TN)
        weighted = dot(grad_tables[0, at, :], values, NN).astype(bf16) * codes
        sums += dot(bits[:, at], weighted, NN)
    out[0] = pull_back(rows, planes_t[...], inv, upper, sums).astype(out.dtype)
    out[1] = grad_values.astype(out.dtype)


def bit_rows():
    out = np.zeros((80, BUCKETS, SETS), np.float32)
    for t in range(SETS):
        for i in range(BITS):
            out[i * SETS + t, :, t] = (np.arange(BUCKETS) >> i) & 1
        out[BITS * SETS + t, :, t] = 1
    return jnp.asarray(out.reshape(80, ROWS), bf16)


def whole(*shape):
    return pl.BlockSpec(shape, lambda h: (0,) * len(shape))


def head_rows(array, heads, which):
    width = array.shape[1]
    offset = (which - 3) * heads + array.shape[0] // HEAD_DIM
    return pl.BlockSpec((HEAD_DIM, width), lambda h: (h + offset, 0))


def per_head(width):
    return pl.BlockSpec((HEAD_DIM, width), lambda h: (h, 0))


def table_spec():
    return pl.BlockSpec((1, ROWS, HEAD_DIM), lambda h: (h, 0, 0))


def call(kernel, heads, micros, name, in_specs, out_specs, out_shape):
    return pl.pallas_call(
        kernel,
        grid=(heads,),
        in_specs=in_specs,
        out_specs=out_specs,
        out_shape=out_shape,
        compiler_params=pltpu.CompilerParams(vmem_limit_bytes=48 << 20),
        cost_estimate=pl.CostEstimate(
            flops=int(micros * 1.1e9), bytes_accessed=1 << 20, transcendentals=0
        ),
        name=name,
    )


def key_tables(planes, heads, blocks, start, kind):
    args = [planes, *blocks, *blocks]
    specs = [whole(64, 64)] + [head_rows(x, heads, w) for w in (1, 2) for x in blocks]
    if start is not None:
        specs.append(table_spec())
        args.append(start)
    return call(
        partial(key_kernel, chunk=2, blocks=len(blocks)),
        heads,
        30 if len(blocks) > 1 and start is not None else 1,
        "key_tables",
        specs,
        table_spec(),
        shape((heads, ROWS, HEAD_DIM), kind),
    )(*args)


def query_estimates(planes, heads, near, far, tables, kind):
    width = near.shape[1] + far.shape[1]
    return call(
        partial(query_kernel, chunk=2),
        heads,
        1,
        "query_estimates",
        [whole(64, 64), table_spec(), head_rows(near, heads, 0), per_head(far.shape[1])],
        per_head(width),
        shape((heads * HEAD_DIM, width), kind),
    )(planes, tables, near, far)


def query_backward(planes, planes_t, bits, heads, tables, queries, grads, start, last, kinds):
    width = grads[0].shape[1]
    blocks = len(grads)
    specs = [whole(64, 64), whole(64, 128), whole(80, ROWS), table_spec()]
    args = [planes, planes_t, bits, tables]
    for near, far in queries:
        specs += [head_rows(near, heads, 0), per_head(far.shape[1])]
        args += [near, far]
    specs += [per_head(width)] * blocks
    args += grads
    if start is not None:
        specs.append(table_spec())
        args.append(start)
    return call(
        partial(query_back_kernel, chunk=4, blocks=blocks, last=last),
        heads,
        25 * blocks,
        "query_backward",
        specs,
        [table_spec()] + [per_head(width)] * blocks,
        [shape((heads, ROWS, HEAD_DIM), bf16 if last else f32)]
        + [shape(grads[0].shape, kind) for kind in kinds],
    )(*args)


def key_backward(planes, planes_t, bits, heads, near, far, grad_tables, kind, micros=25):
    width = near.shape[1] + far.shape[1]
    return call(
        partial(key_back_kernel, chunk=4),
        heads,
        micros,
        "key_backward",
        [whole(64, 64), whole(64, 128), whole(80, ROWS)]
        + [head_rows(x, heads, w) for w in (1, 2) for x in (near, far)]
        + [table_spec()],
        pl.BlockSpec((2, HEAD_DIM, width), lambda h: (0, h, 0)),
        shape((2, heads * HEAD_DIM, width), kind),
    )(planes, planes_t, bits, near, far, near, far, grad_tables)


def norm(x):
    center = x - jnp.mean(x, axis=-1, keepdims=True)
    inv = lax.rsqrt(jnp.mean(center * center, axis=-1, keepdims=True) + 1e-5)
    return center * inv, inv


def norm_back(grad, unit, inv):
    return inv * (
        grad
        - jnp.mean(grad, axis=-1, keepdims=True)
        - unit * jnp.mean(grad * unit, axis=-1, keepdims=True)
    )


def column_sum(x):
    return jnp.sum(x, axis=0, keepdims=True)


def core_rows(core, ref, which):
    half = ref.shape[0] // 2
    at = core[0] if which == 0 else 1 - core[0]
    return ref[pl.ds(pl.multiple_of(at * half, 16), half), :]


def share_rows(keep, give, at, rows):
    part = keep.shape[2]
    for out in (keep, give):
        out[at] = rows[:, :part]
        out[at + 1] = rows[:, part:]


def dense_kernel(core, x_in, grad_out, gain, bias, *refs):
    attn, weights = refs[0:4], refs[4:6]
    layer_out, first_out, grad_second_out, slope, keep, give, heads_give, small = refs[6:14]
    owner = [core[1] ^ (b // 2) for b in range(8)]
    for j in range(4):
        heads_give[j] = core_rows(core, attn[j], 1)
    part = slope.shape[2]
    blocks = range(8)
    heads = jnp.concatenate([core_rows(core, attn[b // 2], b % 2) for b in blocks], axis=0)
    out_w = jnp.concatenate([weights[b % 2][owner[b], 2 * part :, :] for b in blocks], axis=0)
    attn_out = dot(heads, out_w, TN)
    resid = x_in[...].astype(f32)
    first = resid + attn_out
    first_out[...] = first
    small[0:1, :] = column_sum(resid * resid)
    small[1:2, :] = column_sum(attn_out * attn_out)
    small[2:3, :] = column_sum(first * first)
    unit_1, _ = norm(first)
    normed = (unit_1 * gain[0:1, :] + bias[0:1, :]).astype(bf16)
    share_rows(keep, give, 4, normed)
    second = normed.astype(f32)
    for b in blocks:
        pre = dot(normed, weights[b % 2][owner[b], 0:part, :], NT)
        below = 0.5 * (1.0 + lax.erf(pre * 0.7071067811865476))
        rows = (pre * below).astype(bf16)
        (keep, give)[b % 2][b // 2] = rows
        slope[b] = below + pre * (0.3989422804014327 * jnp.exp(-0.5 * pre * pre))
        second = second + dot(rows, weights[b % 2][owner[b], part : 2 * part, :], NN)
    unit_2, inv_2 = norm(second)
    layer_out[...] = (unit_2 * gain[1:2, :] + bias[1:2, :]).astype(layer_out.dtype)
    grad = grad_out[...]
    small[3:4, :] = column_sum(grad * unit_2)
    small[4:5, :] = column_sum(grad)
    small[5:8, :] = jnp.zeros_like(small[5:8, :])
    grad_second = norm_back(grad * gain[1:2, :], unit_2, inv_2)
    grad_second_out[...] = grad_second
    share_rows(keep, give, 6, grad_second.astype(bf16))


def dense_back_kernel(core, first, grad_second, slope, gain, *refs):
    weights = refs[0:2]
    grad_first_out, keep, give = refs[2:5]
    estimates, small = refs[5:9], refs[9]
    owner = [core[1] ^ (b // 2) for b in range(8)]
    part = slope.shape[2]
    blocks = range(8)
    grad_normed = grad_second[...]
    grad_ffn = grad_normed.astype(bf16)
    for b in blocks:
        rows = dot(grad_ffn, weights[b % 2][owner[b], part : 2 * part, :], NT)
        rows = (rows * slope[b]).astype(bf16)
        (keep, give)[b % 2][b // 2] = rows
        grad_normed = grad_normed + dot(rows, weights[b % 2][owner[b], 0:part, :], NN)
    unit, inv = norm(first[...])
    small[0:1, :] = column_sum(grad_normed * unit)
    small[1:2, :] = column_sum(grad_normed)
    small[2:8, :] = jnp.zeros_like(small[2:8, :])
    grad_first = norm_back(grad_normed * gain[0:1, :], unit, inv)
    grad_first_out[...] = grad_first
    grad_attn = grad_first.astype(bf16)
    share_rows(keep, give, 4, grad_attn)
    for b in blocks:
        half = estimates[0].shape[0] // 2
        at = core[0] if b % 2 == 0 else 1 - core[0]
        estimates[b // 2][pl.ds(pl.multiple_of(at * half, 16), half), :] = dot(
            weights[b % 2][owner[b], 2 * part :, :], grad_attn, NT
        ).astype(bf16)


def weight_grad_kernel(core, small_a, small_b, *refs):
    near, far, near_back, far_back = refs[0:4]
    attn, attn_far, out = refs[4:8], refs[8], refs[9]
    part = near.shape[2]
    sums = jnp.concatenate([small_a[...], small_b[...]], axis=0).astype(bf16)

    def wide(ref, at):
        return jnp.concatenate([ref[at], ref[at + 1]], axis=1)

    def rows(ref, other, at):
        return jnp.concatenate([wide(ref, at), wide(other, at)], axis=0)

    normed, grad_ffn = rows(near, far, 4), rows(near, far, 6)
    grad_attn = rows(near_back, far_back, 4)
    for j in range(4):
        owner = core[1] ^ j
        hidden = jnp.concatenate([near[j], far[j]], axis=0)
        grad_pre = jnp.concatenate([near_back[j], far_back[j]], axis=0)
        out[owner, 0:part, :] = dot(grad_pre, normed, TN).astype(bf16)
        out[owner, part : 2 * part, :] = dot(hidden, grad_ffn, TN).astype(bf16)
        heads = jnp.concatenate([core_rows(core, attn[j], 0), attn_far[j]], axis=1)
        at = 2 * part + heads.shape[0]
        out[owner, 2 * part : at, :] = dot(heads, grad_attn, NN).astype(bf16)
        out[owner, at : at + 16, :] = sums
        out[owner, at + 16 :, :] = jnp.zeros_like(sums)


def input_grad_kernel(core, grad_first, *refs):
    blocks, near, far, out = refs[0:4], refs[4], refs[5], refs[6]
    half = near.shape[2]
    total = grad_first[...]
    for which, halves in enumerate((near, far)):
        at = core[0] if which == 0 else 1 - core[0]
        at = pl.ds(pl.multiple_of(at * half, 16), half)
        for j in range(4):
            rows = jnp.concatenate([blocks[j][c, at, :] for c in range(3)], axis=0)
            weights = jnp.concatenate([halves[core[1] ^ j, c] for c in range(3)], axis=0)
            total = total + dot(rows, weights, TN)
    out[...] = total.astype(out.dtype)


def vmem(count):
    return [pl.BlockSpec(memory_space=pltpu.VMEM)] * count


def single(kernel, core, args, out_shape, micros, name, scratch=()):
    return pl.pallas_call(
        kernel,
        in_specs=[pl.BlockSpec(memory_space=pltpu.SMEM)] + vmem(len(args)),
        out_specs=vmem(len(out_shape)),
        out_shape=out_shape,
        scratch_shapes=scratch,
        compiler_params=pltpu.CompilerParams(vmem_limit_bytes=56 << 20),
        cost_estimate=pl.CostEstimate(
            flops=int(micros * 1.1e9), bytes_accessed=1 << 20, transcendentals=0
        ),
        name=name,
    )(core, *args)


def dense(core, x_in, grad_out, gain, bias, attn, weights):
    rows, width = x_in.shape
    part = (weights[0].shape[1] - attn[0].shape[0] // 2) // 2
    out_shape = [
        shape((rows, width), bf16),
        shape((rows, width), f32),
        shape((rows, width), f32),
        shape((8, rows, part), f32),
        shape((8, rows, part), bf16),
        shape((8, rows, part), bf16),
        shape((4, attn[0].shape[0] // 2, rows), bf16),
        shape((8, width), f32),
    ]
    args = [x_in, grad_out, gain, bias, *attn, *weights]
    return single(dense_kernel, core, args, out_shape, 14, "dense")


def dense_back(core, first, grad_second, slope, gain, attn, weights):
    rows, width = first.shape
    part = (weights[0].shape[1] - attn[0].shape[0] // 2) // 2
    out_shape = [
        shape((rows, width), f32),
        shape((6, rows, part), bf16),
        shape((6, rows, part), bf16),
        *[shape(attn[0].shape, bf16)] * 4,
        shape((8, width), f32),
    ]
    args = [first, grad_second, slope, gain, *weights]
    return single(dense_back_kernel, core, args, out_shape, 8, "dense_back")


def weight_grads(core, small_a, small_b, shared, attn, attn_far):
    part, width = shared[0].shape[2], small_a.shape[1]
    out_shape = [shape((4, 2 * part + attn[0].shape[0] // 2 + 32, width), bf16)]
    args = [small_a, small_b, *shared, *attn, attn_far]
    return single(weight_grad_kernel, core, args, out_shape, 7, "weight_grads")[0]


def input_grad(core, grad_first, blocks, near, far):
    out_shape = [shape(grad_first.shape, bf16)]
    args = [grad_first, *blocks, near, far]
    return single(input_grad_kernel, core, args, out_shape, 3, "input_grad")[0]


def after(x, *others):
    return lax.optimization_barrier((x, *others))[0]


def add(a, *others):
    return sum([b.astype(f32) for b in others], a.astype(f32))


def shards(
    inputs,
    w_qkv,
    w_out,
    up_weight,
    down_weight,
    norm_gain,
    norm_bias,
    planes,
    mask_pos,
    cot_rows,
):
    own = inputs[0]
    piece, seqs, width = own.shape
    hash_count, head_count = lax.axis_size("hash"), lax.axis_size("head")
    groups, places = seqs, hash_count // seqs
    assert places == 2 and lax.axis_size("seq") == 2 and head_count == 4
    assert planes.shape[0] * hash_count == 4 * SETS
    quarter = piece // head_count
    rows = groups * quarter
    half_len = piece * hash_count
    head_width = w_out.shape[0]
    hidden_own = down_weight.shape[0]
    n_tokens = head_count * rows
    hash_id, d, s = lax.axis_index("hash"), lax.axis_index("head"), lax.axis_index("seq")
    g, r = hash_id // places, hash_id % places

    def over_seq(x):
        return lax.ppermute(x, "seq", [(0, 1), (1, 0)])

    def over_place(x):
        return lax.ppermute(x, "hash", [(h, h ^ 1) for h in range(hash_count)])

    def over_group(x, k):
        moves = [(h, ((h // places + k) % groups) * places + h % places) for h in range(hash_count)]
        return lax.ppermute(x, "hash", moves)

    def over_head(x, j):
        return lax.ppermute(x, "head", [(h, h ^ j) for h in range(head_count)])

    def seq_rows(block, index):
        return lax.dynamic_index_in_dim(block, index % seqs, 1, keepdims=False)

    here = [
        seq_rows(lax.dynamic_slice_in_dim(own, (d ^ j) * quarter, quarter, 0), g)
        for j in range(head_count)
    ]
    near_tokens = jnp.concatenate(here)
    my_quarter = lax.dynamic_slice_in_dim(own, d * quarter, quarter, 0)
    sent = [seq_rows(my_quarter, g + k) for k in range(1, groups)]
    arrived = [over_group(x, k + 1) for k, x in enumerate(sent)]

    signed = (2 * planes - 1).astype(bf16)
    if planes.shape[0] == SETS and groups == 2:
        moves = [
            ((2 * rr + ss) * 2 + gg, (gg * places + rr) * 2 + ss)
            for gg in range(2)
            for rr in range(2)
            for ss in range(2)
        ]
        signed = lax.ppermute(signed, ("hash", "seq"), moves)
    else:
        signed = lax.all_gather(signed, "hash", axis=0, tiled=True)
        signed = lax.dynamic_slice_in_dim(signed, (r * 2 + s) * SETS, SETS, 0)
    signed = signed.transpose(1, 0, 2).reshape(BITS * SETS, HEAD_DIM)
    signed_t = jnp.concatenate([signed.T, signed.T], axis=1)
    bits = bit_rows()

    cut, out_cut = hidden_own // 2, head_width // 2
    weights = jnp.concatenate(
        [
            lax.dynamic_slice_in_dim(after(up_weight, *sent), s * cut, cut, 1).T,
            lax.dynamic_slice_in_dim(down_weight, s * cut, cut, 0),
            lax.dynamic_slice_in_dim(w_out, s * out_cut, out_cut, 0),
        ]
    )
    weights = lax.all_gather(weights, "head", axis=0)
    w_qkv_t = lax.dynamic_slice_in_dim(w_qkv.transpose(0, 2, 1), s * out_cut, out_cut, 1)

    head_n = head_width // HEAD_DIM

    def project(w, rows_in):
        out = jnp.einsum("cde,ld->cel", w, rows_in, preferred_element_type=f32)
        return out.astype(bf16).reshape(-1, rows_in.shape[0])

    near_tokens = after(near_tokens, *arrived)
    near = project(w_qkv, near_tokens)
    near_z, near_o = over_place(near), over_seq(near)
    far_quarter = jnp.stack(arrived)
    moved = [over_head(far_quarter, j) for j in range(1, head_count)]
    tables = key_tables(signed, head_n, [near, near_o], None, f32)
    moved = [after(x, tables) for x in moved]

    near_z = after(near_z, tables)
    near_zo = over_seq(near_z)

    mask_pos = after(mask_pos, tables)
    slot = jnp.arange(groups, dtype=jnp.int32)[:, None]
    place_of = ((g - slot) % groups) * places + r
    position = s * half_len + place_of * piece + d * quarter + jnp.arange(quarter, dtype=jnp.int32)[None]
    mask_row = lax.dynamic_index_in_dim(mask_pos, g, 0, keepdims=False)
    cot = lax.dynamic_index_in_dim(cot_rows, g, 0, keepdims=False)
    pick = (position.reshape(rows)[:, None] == mask_row[None]).astype(bf16)
    grad_out = jnp.dot(pick, cot, preferred_element_type=f32)
    ready = after(signed, grad_out)
    tables = key_tables(ready, head_n, [near_z, near_zo], tables, f32)

    far_tokens = jnp.stack([far_quarter, *moved]).reshape(-1, width)
    kv = project(w_qkv[1:], far_tokens)
    q = project(after(w_qkv[:1], kv), far_tokens)
    tokens = jnp.concatenate([near_tokens, far_tokens])
    dense_in = jnp.concatenate([here[0], *arrived])
    kv_z, kv_o = over_place(kv), over_seq(kv)
    q_o, q_z = over_seq(q), over_place(q)
    n_near = near.shape[1]

    tables = key_tables(after(signed, q), head_n, [kv, kv_o], tables, f32)

    kv_z = after(kv_z, tables)
    kv_zo = over_seq(kv_z)
    ready = after(signed, tokens, dense_in)
    tables = key_tables(ready, head_n, [kv_z], tables, f32)

    q_z = after(q_z, tables)
    q_zo = over_seq(q_z)
    kv_zo = after(kv_zo, tables)
    tables = key_tables(after(signed, q_z), head_n, [kv_zo], tables, bf16)

    q_zo = after(q_zo, tables)
    e_zo = query_estimates(signed, head_n, near_zo, q_zo, tables, bf16)
    e_zo_moved = over_seq(e_zo)
    e_z = query_estimates(signed, head_n, near_z, after(q_z, e_zo), tables, bf16)
    e_far = add(e_z, after(e_zo_moved, e_z)).astype(bf16)
    ready = after(q_o, e_far)
    e_o = query_estimates(signed, head_n, near_o, ready, tables, bf16)
    e_far = over_place(e_far)
    e_o_moved = over_seq(e_o)
    e = query_estimates(signed, head_n, near, after(q, e_o), tables, f32)
    e_far = after(e_far, e)
    weights = after(weights, e_o)
    weights = [weights, over_seq(weights)]
    w_qkv_t = lax.all_gather(after(w_qkv_t, weights[0]), "head", axis=0)
    attn = add(e, after(e_o_moved, e), e_far).astype(bf16)

    def to_dense(block):
        parts = []
        for j in range(head_count):
            a, b = j * quarter, n_near + j * (rows - quarter)
            cut = [block[..., a : a + quarter], block[..., b : b + rows - quarter]]
            parts.append(jnp.concatenate(cut, axis=-1))
        moved = [over_head(parts[j], j) for j in range(1, head_count)]
        return [parts[0], *lax.optimization_barrier(moved)]

    attn_parts = to_dense(attn)

    def away(dense_rows):
        dense_rows = dense_rows.reshape(groups, quarter, width)
        return [dense_rows[0]] + [over_group(dense_rows[k], groups - k) for k in range(1, groups)]

    core = jnp.stack([s, d]).astype(jnp.int32)
    layer_rows, first, grad_second, slope, keep, give, heads_give, small_a = dense(
        core, dense_in, grad_out, norm_gain, norm_bias, attn_parts, weights
    )
    taken, heads_far = over_seq(give), over_seq(heads_give)
    grad_first, keep_back, give_back, *est_parts, small_b = dense_back(
        core, first, grad_second, slope, norm_gain, attn_parts, weights
    )
    taken_back = over_seq(give_back)
    est_moved = [over_head(est_parts[j], j) for j in range(1, head_count)]
    est_parts = [est_parts[0], *lax.optimization_barrier(est_moved)]
    grad = jnp.concatenate(
        [x[:, :quarter] for x in est_parts] + [x[:, quarter:] for x in est_parts], axis=1
    )
    layer_moved = away(layer_rows)
    weight_parts = weight_grads(
        core, after(small_a, grad, w_qkv_t), small_b, [keep, taken, keep_back, taken_back], attn_parts, heads_far
    )

    weight_sum = lax.psum_scatter(weight_parts, "head", scatter_dimension=0, tiled=True)[0]
    grad_z = over_place(grad)
    grad_o = after(over_seq(grad), weight_parts)
    layer_moved = jnp.stack([after(x, weight_parts) for x in layer_moved])
    part, dq, dq_o = query_backward(
        signed, signed_t, bits, head_n, tables, [(near, after(q, layer_moved)), (near_o, q_o)], [grad, grad_o],
        None, False, [f32, bf16],
    )

    grad_z = after(grad_z, part)
    grad_zo = over_seq(grad_z)
    dq_o = over_seq(dq_o)
    part, dq_z = query_backward(
        signed, signed_t, bits, head_n, tables, [(near_z, q_z)], [grad_z], part, False, [f32]
    )

    dq_own = add(dq, after(dq_o, dq_z))
    grad_zo = after(grad_zo, dq_z)
    grad_tables, dq_zo = query_backward(
        signed, signed_t, bits, head_n, tables, [(near_zo, after(q_zo, dq_own))], [grad_zo], part, True, [bf16]
    )

    dq_zo = over_seq(dq_zo)
    w_qkv_t = after(w_qkv_t, grad_tables)
    w_qkv_far = over_seq(w_qkv_t)
    dkv_zo = key_backward(signed, signed_t, bits, head_n, near_zo, kv_zo, grad_tables, bf16)

    dkv_zo_moved = over_seq(dkv_zo)
    dq_far = add(dq_z, after(dq_zo, dkv_zo)).astype(bf16)
    layer_moved = [layer_moved] + [over_head(layer_moved, j) for j in range(1, head_count)]
    dkv_z = key_backward(signed, signed_t, bits, head_n, near_z, after(kv_z, dq_far), grad_tables, bf16)
    dq_far = over_place(dq_far)

    dkv_far = add(dkv_z, after(dkv_zo_moved, dkv_z)).astype(bf16)
    grad_q = add(dq_own, after(dq_far, dkv_z)).astype(bf16)
    weight_sum = after(weight_sum, dkv_z)
    layer_moved = [after(x, dkv_z) for x in layer_moved]
    dkv_o = key_backward(
        signed, signed_t, bits, head_n, near_o, after(kv_o, dkv_far, grad_q, weight_sum, *layer_moved),
        grad_tables, bf16, 2,
    )
    weight_sum = lax.psum(weight_sum, "hash")
    dkv_far = over_place(dkv_far)
    dkv_o_moved = over_seq(dkv_o)
    dkv = key_backward(
        signed, signed_t, bits, head_n, near, kv, grad_tables, f32, 2
    )

    dkv_o_moved = after(dkv_o_moved, dkv)
    grad_kv = add(dkv, dkv_o_moved, after(dkv_far, dkv)).astype(bf16)
    grad_qkv = jnp.concatenate([grad_q[None], grad_kv])
    qkv_parts = to_dense(grad_qkv)

    grad_in = input_grad(core, grad_first, qkv_parts, w_qkv_t, after(w_qkv_far, dkv))

    def in_halves(index, mine, other):
        first = jnp.where(index == 0, mine, other)
        second = jnp.where(index == 0, other, mine)
        return jnp.concatenate([first, second], axis=0)

    def split(x, index):
        half = x.shape[0] // 2
        return [lax.dynamic_slice_in_dim(x, at * half, half, 0) for at in (index, 1 - index)]

    w_grad = dot(grad_qkv.reshape(3 * head_width, n_tokens), tokens, NN).astype(bf16)
    w_keep, w_send = split(w_grad, s)
    w_keep, w_send = split(add(w_keep, over_seq(w_send)).astype(bf16), r)
    grad_moved = away(grad_in)
    w_keep = add(w_keep, over_place(w_send))
    w_send = w_keep.astype(bf16)
    grad_moved = after(jnp.stack(grad_moved), w_send)
    w_keep = add(w_keep, *[over_group(w_send, k) for k in range(1, groups)]).astype(bf16)
    grad_moved = [grad_moved] + [over_head(grad_moved, j) for j in range(1, head_count)]

    def home(blocks):
        table = jnp.stack(blocks)
        columns = []
        for q_at in range(head_count):
            block = lax.dynamic_index_in_dim(table, q_at ^ d, 0, keepdims=False)
            columns.append(
                jnp.stack(
                    [
                        lax.dynamic_index_in_dim(block, (at - g) % groups, 0, keepdims=False)
                        for at in range(seqs)
                    ],
                    axis=1,
                )
            )
        return jnp.concatenate(columns, axis=0)

    layer_out = home([after(x, grad_moved[0]) for x in layer_moved])
    grad_inputs = home(grad_moved).astype(f32)

    w_grad = in_halves(r, w_keep, over_place(w_keep))
    w_grad = in_halves(s, w_grad, over_seq(w_grad)).reshape(3, head_width, width)
    grad_w_qkv = w_grad.transpose(0, 2, 1).astype(f32)
    weight_sum = after(weight_sum, grad_in)
    weight_far = over_seq(weight_sum)
    ends = [0, cut, 2 * cut, 2 * cut + head_width // 2]
    grad_w_up, grad_w_down, grad_w_out = [
        in_halves(s, weight_sum[a:b], weight_far[a:b]) for a, b in zip(ends, ends[1:])
    ]
    grad_w_up = grad_w_up.T.astype(f32)
    grad_w_down, grad_w_out = grad_w_down.astype(f32), grad_w_out.astype(f32)
    at = slice(ends[3], ends[3] + 16)
    small = add(weight_sum[at], weight_far[at])

    count = piece * seqs * width * hash_count * 2
    stream_rms = jnp.sqrt(jnp.sum(small[0:3], axis=1) / count)
    share = width // head_count
    norm_grads = lax.dynamic_slice_in_dim(small, d * share, share, 1)
    return (
        layer_out[None],
        grad_inputs[None],
        grad_w_qkv,
        grad_w_out,
        grad_w_up,
        grad_w_down,
        jnp.stack([norm_grads[8], norm_grads[3]]),
        jnp.stack([norm_grads[9], norm_grads[4]]),
        stream_rms,
    )


def solution(mesh):
    placed = (
        P("seq", "hash", None, None),
        P(None, None, "head"),
        P("head", None),
        P(None, "head"),
        P("head", None),
        P(),
        P(),
        P("hash", None, None),
        P(),
        P(),
    )
    return jax.shard_map(
        shards,
        mesh=mesh,
        in_specs=placed,
        out_specs=(
            P("seq", "hash", None, None),
            P("seq", "hash", None, None),
            P(None, None, "head"),
            P("head", None),
            P(None, "head"),
            P("head", None),
            P(None, "head"),
            P(None, "head"),
            P(),
        ),
        check_vma=False,
    )
```

```python
from functools import partial

import jax
import jax.numpy as jnp
import numpy as np
from jax import lax
from jax.experimental import pallas as pl
from jax.experimental.pallas import tpu as pltpu
from jax.sharding import PartitionSpec as P

HEAD_DIM = 64
HASHES = 32
BITS = 8
SETS = 8
BUCKETS = 1 << BITS
ROWS = BUCKETS * SETS

bf16 = jnp.bfloat16
f32 = jnp.float32
NN = (((1,), (0,)), ((), ()))
NT = (((1,), (1,)), ((), ()))
TN = (((0,), (0,)), ((), ()))


shape = jax.ShapeDtypeStruct


def dot(a, b, dims):
    return lax.dot_general(a, b, dims, preferred_element_type=f32)


def sides(rows, planes):
    x = rows.astype(f32)
    inv = lax.rsqrt(jnp.sum(x * x, axis=0, keepdims=True) + 1e-6)
    proj = dot(planes, rows, NN) * (3.0 * inv)
    small = jnp.exp(-proj)
    upper = 1.0 / (1.0 + small)
    return inv, upper, small * upper


def products(upper, lower, first, count):
    out = None
    for i in range(first, first + count):
        lo, up = lower[SETS * i : SETS * (i + 1)], upper[SETS * i : SETS * (i + 1)]
        out = [lo, up] if out is None else [c * lo for c in out] + [c * up for c in out]
    return out


def half_codes(upper, lower):
    low = jnp.concatenate(products(upper, lower, 0, 4), axis=0).astype(bf16)
    high = [jnp.concatenate([a, a], axis=0).astype(bf16) for a in products(upper, lower, 4, 4)]
    return low, high


def code_chunk(low, high, first, count):
    return jnp.concatenate(
        [high[a] * low[16 * j : 16 * (j + 1)] for a in range(first, first + count) for j in range(8)],
        axis=0,
    )


def pull_back(rows, planes_t, inv, upper, sums):
    total = sums[BITS * SETS :][:SETS]
    grad_proj = sums[: BITS * SETS] - upper * jnp.concatenate([total] * BITS, axis=0)
    head = grad_proj.astype(bf16)
    tail = (grad_proj - head.astype(f32)).astype(bf16)
    grad_unit = dot(planes_t, jnp.concatenate([head, tail], axis=0), NN) * (3.0 * inv)
    x = rows.astype(f32)
    return grad_unit - x * (inv * inv * jnp.sum(x * grad_unit, axis=0, keepdims=True))


def both(*refs):
    return jnp.concatenate([ref[...] for ref in refs], axis=1)


def key_kernel(planes, *refs, chunk, blocks):
    keys, vals, out = refs[:blocks], refs[blocks : 2 * blocks], refs[-1]
    start = refs[2 * blocks] if len(refs) > 2 * blocks + 1 else None
    _, upper, lower = sides(both(*keys), planes[...])
    low, high = half_codes(upper, lower)
    values = both(*vals)
    for c in range(0, 16, chunk):
        at = slice(128 * c, 128 * (c + chunk))
        part = dot(code_chunk(low, high, c, chunk), values, NT)
        if start is not None:
            part = part + start[0, at, :]
        out[0, at, :] = part.astype(out.dtype)


def query_kernel(planes, tables, *refs, chunk):
    rows, out = both(*refs[:-1]), refs[-1]
    _, upper, lower = sides(rows, planes[...])
    low, high = half_codes(upper, lower)
    acc = jnp.zeros((HEAD_DIM, rows.shape[1]), f32)
    for c in range(0, 16, chunk):
        acc += dot(tables[0, 128 * c : 128 * (c + chunk), :], code_chunk(low, high, c, chunk), TN)
    out[...] = (acc * (1.0 / HASHES)).astype(out.dtype)


def query_back_kernel(planes, planes_t, bits, tables, *refs, chunk, blocks, last):
    queries, grads = refs[: 2 * blocks], refs[2 * blocks : 3 * blocks]
    start = refs[3 * blocks] if len(refs) > 4 * blocks + 1 else None
    out, back_out = refs[-1 - blocks], refs[-blocks:]
    rows = both(*queries)
    inv, upper, lower = sides(rows, planes[...])
    low, high = half_codes(upper, lower)
    grad = both(*grads)
    sums = jnp.zeros((bits.shape[0], rows.shape[1]), f32)
    for c in range(0, 16, chunk):
        at = slice(128 * c, 128 * (c + chunk))
        codes = code_chunk(low, high, c, chunk)
        part = dot(codes, grad, NT)
        if start is not None:
            part = part + start[0, at, :]
        if last:
            part = part * (1.0 / HASHES)
        out[0, at, :] = part.astype(out.dtype)
        weighted = dot(tables[0, at, :], grad, NN).astype(bf16) * codes
        sums += dot(bits[:, at], weighted, NN)
    back = pull_back(rows, planes_t[...], inv, upper, sums * (1.0 / HASHES))
    width = back_out[0].shape[1]
    for i in range(blocks):
        back_out[i][...] = back[:, i * width : (i + 1) * width].astype(back_out[i].dtype)


def key_back_kernel(planes, planes_t, bits, ka, kb, va, vb, grad_tables, out, *, chunk):
    rows = both(ka, kb)
    inv, upper, lower = sides(rows, planes[...])
    low, high = half_codes(upper, lower)
    values = both(va, vb)
    width = rows.shape[1]
    sums = jnp.zeros((bits.shape[0], width), f32)
    grad_values = jnp.zeros((HEAD_DIM, width), f32)
    for c in range(0, 16, chunk):
        at = slice(128 * c, 128 * (c + chunk))
        codes = code_chunk(low, high, c, chunk)
        grad_values += dot(grad_tables[0, at, :], codes, TN)
        weighted = dot(grad_tables[0, at, :], values, NN).astype(bf16) * codes
        sums += dot(bits[:, at], weighted, NN)
    out[0] = pull_back(rows, planes_t[...], inv, upper, sums).astype(out.dtype)
    out[1] = grad_values.astype(out.dtype)


def bit_rows():
    out = np.zeros((80, BUCKETS, SETS), np.float32)
    for t in range(SETS):
        for i in range(BITS):
            out[i * SETS + t, :, t] = (np.arange(BUCKETS) >> i) & 1
        out[BITS * SETS + t, :, t] = 1
    return jnp.asarray(out.reshape(80, ROWS), bf16)


def whole(*shape):
    return pl.BlockSpec(shape, lambda h: (0,) * len(shape))


def head_rows(array, heads, which):
    width = array.shape[1]
    offset = (which - 3) * heads + array.shape[0] // HEAD_DIM
    return pl.BlockSpec((HEAD_DIM, width), lambda h: (h + offset, 0))


def per_head(width):
    return pl.BlockSpec((HEAD_DIM, width), lambda h: (h, 0))


def table_spec():
    return pl.BlockSpec((1, ROWS, HEAD_DIM), lambda h: (h, 0, 0))


def call(kernel, heads, micros, name, in_specs, out_specs, out_shape):
    return pl.pallas_call(
        kernel,
        grid=(heads,),
        in_specs=in_specs,
        out_specs=out_specs,
        out_shape=out_shape,
        compiler_params=pltpu.CompilerParams(vmem_limit_bytes=48 << 20),
        cost_estimate=pl.CostEstimate(
            flops=int(micros * 1.1e9), bytes_accessed=1 << 20, transcendentals=0
        ),
        name=name,
    )


def key_tables(planes, heads, blocks, start, kind):
    args = [planes, *blocks, *blocks]
    specs = [whole(64, 64)] + [head_rows(x, heads, w) for w in (1, 2) for x in blocks]
    if start is not None:
        specs.append(table_spec())
        args.append(start)
    return call(
        partial(key_kernel, chunk=2, blocks=len(blocks)),
        heads,
        30 if len(blocks) > 1 and start is not None else 1,
        "key_tables",
        specs,
        table_spec(),
        shape((heads, ROWS, HEAD_DIM), kind),
    )(*args)


def query_estimates(planes, heads, near, far, tables, kind):
    width = near.shape[1] + far.shape[1]
    return call(
        partial(query_kernel, chunk=2),
        heads,
        1,
        "query_estimates",
        [whole(64, 64), table_spec(), head_rows(near, heads, 0), per_head(far.shape[1])],
        per_head(width),
        shape((heads * HEAD_DIM, width), kind),
    )(planes, tables, near, far)


def query_backward(planes, planes_t, bits, heads, tables, queries, grads, start, last, kinds):
    width = grads[0].shape[1]
    blocks = len(grads)
    specs = [whole(64, 64), whole(64, 128), whole(80, ROWS), table_spec()]
    args = [planes, planes_t, bits, tables]
    for near, far in queries:
        specs += [head_rows(near, heads, 0), per_head(far.shape[1])]
        args += [near, far]
    specs += [per_head(width)] * blocks
    args += grads
    if start is not None:
        specs.append(table_spec())
        args.append(start)
    return call(
        partial(query_back_kernel, chunk=4, blocks=blocks, last=last),
        heads,
        25 * blocks,
        "query_backward",
        specs,
        [table_spec()] + [per_head(width)] * blocks,
        [shape((heads, ROWS, HEAD_DIM), bf16 if last else f32)]
        + [shape(grads[0].shape, kind) for kind in kinds],
    )(*args)


def key_backward(planes, planes_t, bits, heads, near, far, grad_tables, kind, micros=25):
    width = near.shape[1] + far.shape[1]
    return call(
        partial(key_back_kernel, chunk=4),
        heads,
        micros,
        "key_backward",
        [whole(64, 64), whole(64, 128), whole(80, ROWS)]
        + [head_rows(x, heads, w) for w in (1, 2) for x in (near, far)]
        + [table_spec()],
        pl.BlockSpec((2, HEAD_DIM, width), lambda h: (0, h, 0)),
        shape((2, heads * HEAD_DIM, width), kind),
    )(planes, planes_t, bits, near, far, near, far, grad_tables)


def norm(x):
    center = x - jnp.mean(x, axis=-1, keepdims=True)
    inv = lax.rsqrt(jnp.mean(center * center, axis=-1, keepdims=True) + 1e-5)
    return center * inv, inv


def norm_back(grad, unit, inv):
    return inv * (
        grad
        - jnp.mean(grad, axis=-1, keepdims=True)
        - unit * jnp.mean(grad * unit, axis=-1, keepdims=True)
    )


def column_sum(x):
    return jnp.sum(x, axis=0, keepdims=True)


def core_rows(core, ref, which):
    half = ref.shape[0] // 2
    at = core[0] if which == 0 else 1 - core[0]
    return ref[pl.ds(pl.multiple_of(at * half, 16), half), :]


def share_rows(keep, give, at, rows):
    part = keep.shape[2]
    for out in (keep, give):
        out[at] = rows[:, :part]
        out[at + 1] = rows[:, part:]


def dense_kernel(core, x_in, grad_out, gain, bias, *refs):
    attn, weights = refs[0:4], refs[4:6]
    layer_out, first_out, grad_second_out, slope, keep, give, heads_give, small = refs[6:14]
    owner = [core[1] ^ (b // 2) for b in range(8)]
    for j in range(4):
        heads_give[j] = core_rows(core, attn[j], 1)
    part = slope.shape[2]
    blocks = range(8)
    heads = jnp.concatenate([core_rows(core, attn[b // 2], b % 2) for b in blocks], axis=0)
    out_w = jnp.concatenate([weights[b % 2][owner[b], 2 * part :, :] for b in blocks], axis=0)
    attn_out = dot(heads, out_w, TN)
    resid = x_in[...].astype(f32)
    first = resid + attn_out
    first_out[...] = first
    small[0:1, :] = column_sum(resid * resid)
    small[1:2, :] = column_sum(attn_out * attn_out)
    small[2:3, :] = column_sum(first * first)
    unit_1, _ = norm(first)
    normed = (unit_1 * gain[0:1, :] + bias[0:1, :]).astype(bf16)
    share_rows(keep, give, 4, normed)
    second = normed.astype(f32)
    for b in blocks:
        pre = dot(normed, weights[b % 2][owner[b], 0:part, :], NT)
        below = 0.5 * (1.0 + lax.erf(pre * 0.7071067811865476))
        rows = (pre * below).astype(bf16)
        (keep, give)[b % 2][b // 2] = rows
        slope[b] = below + pre * (0.3989422804014327 * jnp.exp(-0.5 * pre * pre))
        second = second + dot(rows, weights[b % 2][owner[b], part : 2 * part, :], NN)
    unit_2, inv_2 = norm(second)
    layer_out[...] = (unit_2 * gain[1:2, :] + bias[1:2, :]).astype(layer_out.dtype)
    grad = grad_out[...]
    small[3:4, :] = column_sum(grad * unit_2)
    small[4:5, :] = column_sum(grad)
    small[5:8, :] = jnp.zeros_like(small[5:8, :])
    grad_second = norm_back(grad * gain[1:2, :], unit_2, inv_2)
    grad_second_out[...] = grad_second
    share_rows(keep, give, 6, grad_second.astype(bf16))


def dense_back_kernel(core, first, grad_second, slope, gain, *refs):
    weights = refs[0:2]
    grad_first_out, keep, give = refs[2:5]
    estimates, small = refs[5:9], refs[9]
    owner = [core[1] ^ (b // 2) for b in range(8)]
    part = slope.shape[2]
    blocks = range(8)
    grad_normed = grad_second[...]
    grad_ffn = grad_normed.astype(bf16)
    for b in blocks:
        rows = dot(grad_ffn, weights[b % 2][owner[b], part : 2 * part, :], NT)
        rows = (rows * slope[b]).astype(bf16)
        (keep, give)[b % 2][b // 2] = rows
        grad_normed = grad_normed + dot(rows, weights[b % 2][owner[b], 0:part, :], NN)
    unit, inv = norm(first[...])
    small[0:1, :] = column_sum(grad_normed * unit)
    small[1:2, :] = column_sum(grad_normed)
    small[2:8, :] = jnp.zeros_like(small[2:8, :])
    grad_first = norm_back(grad_normed * gain[0:1, :], unit, inv)
    grad_first_out[...] = grad_first
    grad_attn = grad_first.astype(bf16)
    share_rows(keep, give, 4, grad_attn)
    for b in blocks:
        half = estimates[0].shape[0] // 2
        at = core[0] if b % 2 == 0 else 1 - core[0]
        estimates[b // 2][pl.ds(pl.multiple_of(at * half, 16), half), :] = dot(
            weights[b % 2][owner[b], 2 * part :, :], grad_attn, NT
        ).astype(bf16)


def weight_grad_kernel(core, small_a, small_b, *refs):
    near, far, near_back, far_back = refs[0:4]
    attn, attn_far, out = refs[4:8], refs[8], refs[9]
    part = near.shape[2]
    sums = jnp.concatenate([small_a[...], small_b[...]], axis=0).astype(bf16)

    def wide(ref, at):
        return jnp.concatenate([ref[at], ref[at + 1]], axis=1)

    def rows(ref, other, at):
        return jnp.concatenate([wide(ref, at), wide(other, at)], axis=0)

    normed, grad_ffn = rows(near, far, 4), rows(near, far, 6)
    grad_attn = rows(near_back, far_back, 4)
    for j in range(4):
        owner = core[1] ^ j
        hidden = jnp.concatenate([near[j], far[j]], axis=0)
        grad_pre = jnp.concatenate([near_back[j], far_back[j]], axis=0)
        out[owner, 0:part, :] = dot(grad_pre, normed, TN).astype(bf16)
        out[owner, part : 2 * part, :] = dot(hidden, grad_ffn, TN).astype(bf16)
        heads = jnp.concatenate([core_rows(core, attn[j], 0), attn_far[j]], axis=1)
        at = 2 * part + heads.shape[0]
        out[owner, 2 * part : at, :] = dot(heads, grad_attn, NN).astype(bf16)
        out[owner, at : at + 16, :] = sums
        out[owner, at + 16 :, :] = jnp.zeros_like(sums)


def input_grad_kernel(core, grad_first, *refs):
    blocks, near, far, out = refs[0:4], refs[4], refs[5], refs[6]
    half = near.shape[2]
    total = grad_first[...]
    for which, halves in enumerate((near, far)):
        at = core[0] if which == 0 else 1 - core[0]
        at = pl.ds(pl.multiple_of(at * half, 16), half)
        for j in range(4):
            rows = jnp.concatenate([blocks[j][c, at, :] for c in range(3)], axis=0)
            weights = jnp.concatenate([halves[core[1] ^ j, c] for c in range(3)], axis=0)
            total = total + dot(rows, weights, TN)
    out[...] = total.astype(out.dtype)


def vmem(count):
    return [pl.BlockSpec(memory_space=pltpu.VMEM)] * count


def single(kernel, core, args, out_shape, micros, name, scratch=()):
    return pl.pallas_call(
        kernel,
        in_specs=[pl.BlockSpec(memory_space=pltpu.SMEM)] + vmem(len(args)),
        out_specs=vmem(len(out_shape)),
        out_shape=out_shape,
        scratch_shapes=scratch,
        compiler_params=pltpu.CompilerParams(vmem_limit_bytes=56 << 20),
        cost_estimate=pl.CostEstimate(
            flops=int(micros * 1.1e9), bytes_accessed=1 << 20, transcendentals=0
        ),
        name=name,
    )(core, *args)


def dense(core, x_in, grad_out, gain, bias, attn, weights):
    rows, width = x_in.shape
    part = (weights[0].shape[1] - attn[0].shape[0] // 2) // 2
    out_shape = [
        shape((rows, width), bf16),
        shape((rows, width), f32),
        shape((rows, width), f32),
        shape((8, rows, part), f32),
        shape((8, rows, part), bf16),
        shape((8, rows, part), bf16),
        shape((4, attn[0].shape[0] // 2, rows), bf16),
        shape((8, width), f32),
    ]
    args = [x_in, grad_out, gain, bias, *attn, *weights]
    return single(dense_kernel, core, args, out_shape, 14, "dense")


def dense_back(core, first, grad_second, slope, gain, attn, weights):
    rows, width = first.shape
    part = (weights[0].shape[1] - attn[0].shape[0] // 2) // 2
    out_shape = [
        shape((rows, width), f32),
        shape((6, rows, part), bf16),
        shape((6, rows, part), bf16),
        *[shape(attn[0].shape, bf16)] * 4,
        shape((8, width), f32),
    ]
    args = [first, grad_second, slope, gain, *weights]
    return single(dense_back_kernel, core, args, out_shape, 8, "dense_back")


def weight_grads(core, small_a, small_b, shared, attn, attn_far):
    part, width = shared[0].shape[2], small_a.shape[1]
    out_shape = [shape((4, 2 * part + attn[0].shape[0] // 2 + 32, width), bf16)]
    args = [small_a, small_b, *shared, *attn, attn_far]
    return single(weight_grad_kernel, core, args, out_shape, 7, "weight_grads")[0]


def weight_results_kernel(core, near, far, up, down, out):
    part, rows = up.shape[1] // 2, out.shape[0] // 2
    for which, ref in enumerate((near, far)):
        at = core[0] if which == 0 else 1 - core[0]
        at_part = pl.ds(pl.multiple_of(at * part, 128), part)
        up[:, at_part] = ref[0:part, :].astype(f32).T
        down[at_part, :] = ref[part : 2 * part, :].astype(f32)
        at_rows = pl.ds(pl.multiple_of(at * rows, 16), rows)
        out[at_rows, :] = ref[2 * part : 2 * part + rows, :].astype(f32)


def weight_results(core, near, far, head_width):
    width = near.shape[1]
    part = (near.shape[0] - 32 - head_width // 2) // 2
    out_shape = [
        shape((width, 2 * part), f32), shape((2 * part, width), f32), shape((head_width, width), f32)
    ]
    return single(weight_results_kernel, core, [near, far], out_shape, 3, "weight_results")


def input_grad(core, grad_first, blocks, near, far):
    out_shape = [shape(grad_first.shape, bf16)]
    args = [grad_first, *blocks, near, far]
    return single(input_grad_kernel, core, args, out_shape, 40, "input_grad")[0]


def after(x, *others):
    return lax.optimization_barrier((x, *others))[0]


def add(a, *others):
    return sum([b.astype(f32) for b in others], a.astype(f32))


def shards(
    inputs,
    w_qkv,
    w_out,
    up_weight,
    down_weight,
    norm_gain,
    norm_bias,
    planes,
    mask_pos,
    cot_rows,
):
    own = inputs[0]
    piece, seqs, width = own.shape
    hash_count, head_count = lax.axis_size("hash"), lax.axis_size("head")
    groups, places = seqs, hash_count // seqs
    assert places == 2 and lax.axis_size("seq") == 2 and head_count == 4
    assert planes.shape[0] * hash_count == 4 * SETS
    quarter = piece // head_count
    rows = groups * quarter
    half_len = piece * hash_count
    head_width = w_out.shape[0]
    hidden_own = down_weight.shape[0]
    n_tokens = head_count * rows
    hash_id, d, s = lax.axis_index("hash"), lax.axis_index("head"), lax.axis_index("seq")
    g, r = hash_id // places, hash_id % places

    def over_seq(x):
        return lax.ppermute(x, "seq", [(0, 1), (1, 0)])

    def over_place(x):
        return lax.ppermute(x, "hash", [(h, h ^ 1) for h in range(hash_count)])

    def over_group(x, k):
        moves = [(h, ((h // places + k) % groups) * places + h % places) for h in range(hash_count)]
        return lax.ppermute(x, "hash", moves)

    def over_head(x, j):
        return lax.ppermute(x, "head", [(h, h ^ j) for h in range(head_count)])

    def seq_rows(block, index):
        return lax.dynamic_index_in_dim(block, index % seqs, 1, keepdims=False)

    here = [
        seq_rows(lax.dynamic_slice_in_dim(own, (d ^ j) * quarter, quarter, 0), g)
        for j in range(head_count)
    ]
    near_tokens = jnp.concatenate(here)
    my_quarter = lax.dynamic_slice_in_dim(own, d * quarter, quarter, 0)
    sent = [seq_rows(my_quarter, g + k) for k in range(1, groups)]
    arrived = [over_group(x, k + 1) for k, x in enumerate(sent)]

    signed = (2 * planes - 1).astype(bf16)
    if planes.shape[0] == SETS and groups == 2:
        moves = [
            ((2 * rr + ss) * 2 + gg, (gg * places + rr) * 2 + ss)
            for gg in range(2)
            for rr in range(2)
            for ss in range(2)
        ]
        signed = lax.ppermute(signed, ("hash", "seq"), moves)
    else:
        signed = lax.all_gather(signed, "hash", axis=0, tiled=True)
        signed = lax.dynamic_slice_in_dim(signed, (r * 2 + s) * SETS, SETS, 0)
    signed = signed.transpose(1, 0, 2).reshape(BITS * SETS, HEAD_DIM)
    signed_t = jnp.concatenate([signed.T, signed.T], axis=1)
    bits = bit_rows()

    cut, out_cut = hidden_own // 2, head_width // 2
    weights = jnp.concatenate(
        [
            lax.dynamic_slice_in_dim(after(up_weight, *sent), s * cut, cut, 1).T,
            lax.dynamic_slice_in_dim(down_weight, s * cut, cut, 0),
            lax.dynamic_slice_in_dim(w_out, s * out_cut, out_cut, 0),
        ]
    )
    weights = lax.all_gather(weights, "head", axis=0)
    w_qkv_t = lax.dynamic_slice_in_dim(w_qkv.transpose(0, 2, 1), s * out_cut, out_cut, 1)

    head_n = head_width // HEAD_DIM

    def project(w, rows_in):
        out = jnp.einsum("cde,ld->cel", w, rows_in, preferred_element_type=f32)
        return out.astype(bf16).reshape(-1, rows_in.shape[0])

    near_tokens = after(near_tokens, *arrived)
    near = project(w_qkv, near_tokens)
    near_z, near_o = over_place(near), over_seq(near)
    far_quarter = jnp.stack(arrived)
    moved = [over_head(far_quarter, j) for j in range(1, head_count)]
    tables = key_tables(signed, head_n, [near, near_o], None, f32)
    moved = [after(x, tables) for x in moved]

    near_z = after(near_z, tables)
    near_zo = over_seq(near_z)

    mask_pos = after(mask_pos, tables)
    slot = jnp.arange(groups, dtype=jnp.int32)[:, None]
    place_of = ((g - slot) % groups) * places + r
    position = s * half_len + place_of * piece + d * quarter + jnp.arange(quarter, dtype=jnp.int32)[None]
    mask_row = lax.dynamic_index_in_dim(mask_pos, g, 0, keepdims=False)
    cot = lax.dynamic_index_in_dim(cot_rows, g, 0, keepdims=False)
    pick = (position.reshape(rows)[:, None] == mask_row[None]).astype(bf16)
    grad_out = jnp.dot(pick, cot, preferred_element_type=f32)
    ready = after(signed, grad_out)
    tables = key_tables(ready, head_n, [near_z, near_zo], tables, f32)

    far_tokens = jnp.stack([far_quarter, *moved]).reshape(-1, width)
    kv = project(w_qkv[1:], far_tokens)
    q = project(after(w_qkv[:1], kv), far_tokens)
    tokens = jnp.concatenate([near_tokens, far_tokens])
    dense_in = jnp.concatenate([here[0], *arrived])
    kv_z, kv_o = over_place(kv), over_seq(kv)
    q_o, q_z = over_seq(q), over_place(q)
    n_near = near.shape[1]

    tables = key_tables(after(signed, q), head_n, [kv, kv_o], tables, f32)

    kv_z = after(kv_z, tables)
    kv_zo = over_seq(kv_z)
    ready = after(signed, tokens, dense_in)
    tables = key_tables(ready, head_n, [kv_z], tables, f32)

    q_z = after(q_z, tables)
    q_zo = over_seq(q_z)
    kv_zo = after(kv_zo, tables)
    tables = key_tables(after(signed, q_z), head_n, [kv_zo], tables, bf16)

    q_zo = after(q_zo, tables)
    e_zo = query_estimates(signed, head_n, near_zo, q_zo, tables, bf16)
    e_zo_moved = over_seq(e_zo)
    e_z = query_estimates(signed, head_n, near_z, after(q_z, e_zo), tables, bf16)
    e_far = add(e_z, after(e_zo_moved, e_z)).astype(bf16)
    ready = after(q_o, e_far)
    e_o = query_estimates(signed, head_n, near_o, ready, tables, bf16)
    e_far = over_place(e_far)
    e_o_moved = over_seq(e_o)
    e = query_estimates(signed, head_n, near, after(q, e_o), tables, f32)
    e_far = after(e_far, e)
    weights = after(weights, e_o)
    weights = [weights, over_seq(weights)]
    w_qkv_t = lax.all_gather(after(w_qkv_t, weights[0]), "head", axis=0)
    attn = add(e, after(e_o_moved, e), e_far).astype(bf16)

    def to_dense(block):
        parts = []
        for j in range(head_count):
            a, b = j * quarter, n_near + j * (rows - quarter)
            cut = [block[..., a : a + quarter], block[..., b : b + rows - quarter]]
            parts.append(jnp.concatenate(cut, axis=-1))
        moved = [over_head(parts[j], j) for j in range(1, head_count)]
        return [parts[0], *lax.optimization_barrier(moved)]

    attn_parts = to_dense(attn)

    def away(dense_rows):
        dense_rows = dense_rows.reshape(groups, quarter, width)
        return [dense_rows[0]] + [over_group(dense_rows[k], groups - k) for k in range(1, groups)]

    core = jnp.stack([s, d]).astype(jnp.int32)
    layer_rows, first, grad_second, slope, keep, give, heads_give, small_a = dense(
        core, dense_in, grad_out, norm_gain, norm_bias, attn_parts, weights
    )
    taken, heads_far = over_seq(give), over_seq(heads_give)
    grad_first, keep_back, give_back, *est_parts, small_b = dense_back(
        core, first, grad_second, slope, norm_gain, attn_parts, weights
    )
    taken_back = over_seq(give_back)
    est_moved = [over_head(est_parts[j], j) for j in range(1, head_count)]
    est_parts = [est_parts[0], *lax.optimization_barrier(est_moved)]
    grad = jnp.concatenate(
        [x[:, :quarter] for x in est_parts] + [x[:, quarter:] for x in est_parts], axis=1
    )
    layer_moved = away(layer_rows)
    weight_parts = weight_grads(
        core, after(small_a, grad, w_qkv_t), small_b, [keep, taken, keep_back, taken_back], attn_parts, heads_far
    )

    weight_sum = lax.psum_scatter(weight_parts, "head", scatter_dimension=0, tiled=True)[0]
    grad_z = over_place(grad)
    grad_o = after(over_seq(grad), weight_parts)
    layer_moved = jnp.stack([after(x, weight_parts) for x in layer_moved])
    part, dq, dq_o = query_backward(
        signed, signed_t, bits, head_n, tables, [(near, after(q, layer_moved)), (near_o, q_o)], [grad, grad_o],
        None, False, [f32, bf16],
    )

    grad_z = after(grad_z, part)
    grad_zo = over_seq(grad_z)
    dq_o = over_seq(dq_o)
    part, dq_z = query_backward(
        signed, signed_t, bits, head_n, tables, [(near_z, q_z)], [grad_z], part, False, [f32]
    )

    dq_own = add(dq, after(dq_o, dq_z))
    grad_zo = after(grad_zo, dq_z)
    grad_tables, dq_zo = query_backward(
        signed, signed_t, bits, head_n, tables, [(near_zo, after(q_zo, dq_own))], [grad_zo], part, True, [bf16]
    )

    dq_zo = over_seq(dq_zo)
    w_qkv_t = after(w_qkv_t, grad_tables)
    w_qkv_far = over_seq(w_qkv_t)
    dkv_zo = key_backward(signed, signed_t, bits, head_n, near_zo, kv_zo, grad_tables, bf16)

    dkv_zo_moved = over_seq(dkv_zo)
    dq_far = add(dq_z, after(dq_zo, dkv_zo)).astype(bf16)
    layer_moved = [layer_moved] + [over_head(layer_moved, j) for j in range(1, head_count)]
    dkv_z = key_backward(signed, signed_t, bits, head_n, near_z, after(kv_z, dq_far), grad_tables, bf16)
    dq_far = over_place(dq_far)

    dkv_far = add(dkv_z, after(dkv_zo_moved, dkv_z)).astype(bf16)
    grad_q = add(dq_own, after(dq_far, dkv_z)).astype(bf16)
    weight_sum = after(weight_sum, dkv_z)
    layer_moved = [after(x, dkv_z) for x in layer_moved]
    dkv_o = key_backward(
        signed, signed_t, bits, head_n, near_o, after(kv_o, dkv_far, grad_q, weight_sum, *layer_moved),
        grad_tables, bf16, 25,
    )
    weight_sum = lax.psum(weight_sum, "hash")
    dkv_far = over_place(dkv_far)
    dkv_o_moved = over_seq(dkv_o)
    dkv = key_backward(
        signed, signed_t, bits, head_n, near, kv, grad_tables, f32, 25
    )

    dkv_o_moved = after(dkv_o_moved, dkv)
    grad_kv = add(dkv, dkv_o_moved, after(dkv_far, dkv)).astype(bf16)
    grad_qkv = jnp.concatenate([grad_q[None], grad_kv])
    qkv_parts = to_dense(grad_qkv)

    grad_in = input_grad(core, grad_first, qkv_parts, w_qkv_t, after(w_qkv_far, dkv))

    def in_halves(index, mine, other):
        first = jnp.where(index == 0, mine, other)
        second = jnp.where(index == 0, other, mine)
        return jnp.concatenate([first, second], axis=0)

    def split(x, index):
        half = x.shape[0] // 2
        return [lax.dynamic_slice_in_dim(x, at * half, half, 0) for at in (index, 1 - index)]

    w_grad = dot(grad_qkv.reshape(3 * head_width, n_tokens), tokens, NN).astype(bf16)
    w_keep, w_send = split(w_grad, s)
    w_keep, w_send = split(add(w_keep, over_seq(w_send)).astype(bf16), r)
    grad_moved = away(grad_in)
    w_keep = add(w_keep, over_place(w_send))
    w_send = w_keep.astype(bf16)
    grad_moved = after(jnp.stack(grad_moved), w_send)
    w_keep = add(w_keep, *[over_group(w_send, k) for k in range(1, groups)]).astype(bf16)
    grad_moved = [grad_moved] + [over_head(grad_moved, j) for j in range(1, head_count)]

    def home(blocks):
        table = jnp.stack(blocks)
        columns = []
        for q_at in range(head_count):
            block = lax.dynamic_index_in_dim(table, q_at ^ d, 0, keepdims=False)
            columns.append(
                jnp.stack(
                    [
                        lax.dynamic_index_in_dim(block, (at - g) % groups, 0, keepdims=False)
                        for at in range(seqs)
                    ],
                    axis=1,
                )
            )
        return jnp.concatenate(columns, axis=0)

    layer_out = home([after(x, grad_moved[0]) for x in layer_moved])
    grad_inputs = home(grad_moved).astype(f32)

    w_grad = in_halves(r, w_keep, over_place(w_keep))
    w_grad = in_halves(s, w_grad, over_seq(w_grad)).reshape(3, head_width, width)
    grad_w_qkv = w_grad.transpose(0, 2, 1).astype(f32)
    weight_sum = after(weight_sum, *grad_moved)
    weight_far = over_seq(weight_sum)
    grad_w_up, grad_w_down, grad_w_out = weight_results(core, weight_sum, weight_far, head_width)
    at = slice(2 * cut + out_cut, 2 * cut + out_cut + 16)
    small = add(weight_sum[at], weight_far[at])

    count = piece * seqs * width * hash_count * 2
    stream_rms = jnp.sqrt(jnp.sum(small[0:3], axis=1) / count)
    share = width // head_count
    norm_grads = lax.dynamic_slice_in_dim(small, d * share, share, 1)
    return (
        layer_out[None],
        grad_inputs[None],
        grad_w_qkv,
        grad_w_out,
        grad_w_up,
        grad_w_down,
        jnp.stack([norm_grads[8], norm_grads[3]]),
        jnp.stack([norm_grads[9], norm_grads[4]]),
        stream_rms,
    )


def solution(mesh):
    placed = (
        P("seq", "hash", None, None),
        P(None, None, "head"),
        P("head", None),
        P(None, "head"),
        P("head", None),
        P(),
        P(),
        P("hash", None, None),
        P(),
        P(),
    )
    return jax.shard_map(
        shards,
        mesh=mesh,
        in_specs=placed,
        out_specs=(
            P("seq", "hash", None, None),
            P("seq", "hash", None, None),
            P(None, None, "head"),
            P("head", None),
            P(None, "head"),
            P("head", None),
            P(None, "head"),
            P(None, "head"),
            P(),
        ),
        check_vma=False,
    )
```

```python
from functools import partial

import jax
import jax.numpy as jnp
import numpy as np
from jax import lax
from jax.experimental import pallas as pl
from jax.experimental.pallas import tpu as pltpu
from jax.sharding import PartitionSpec as P

HEAD_DIM = 64
HASHES = 32
BITS = 8
SETS = 8
BUCKETS = 1 << BITS
ROWS = BUCKETS * SETS

bf16 = jnp.bfloat16
f32 = jnp.float32
NN = (((1,), (0,)), ((), ()))
NT = (((1,), (1,)), ((), ()))
TN = (((0,), (0,)), ((), ()))


shape = jax.ShapeDtypeStruct


def dot(a, b, dims):
    return lax.dot_general(a, b, dims, preferred_element_type=f32)


def sides(rows, planes):
    x = rows.astype(f32)
    inv = lax.rsqrt(jnp.sum(x * x, axis=0, keepdims=True) + 1e-6)
    proj = dot(planes, rows, NN) * (3.0 * inv)
    small = jnp.exp(-proj)
    upper = 1.0 / (1.0 + small)
    return inv, upper, small * upper


def products(upper, lower, first, count):
    out = None
    for i in range(first, first + count):
        lo, up = lower[SETS * i : SETS * (i + 1)], upper[SETS * i : SETS * (i + 1)]
        out = [lo, up] if out is None else [c * lo for c in out] + [c * up for c in out]
    return out


def half_codes(upper, lower):
    low = jnp.concatenate(products(upper, lower, 0, 4), axis=0).astype(bf16)
    high = [jnp.concatenate([a, a], axis=0).astype(bf16) for a in products(upper, lower, 4, 4)]
    return low, high


def code_chunk(low, high, first, count):
    return jnp.concatenate(
        [high[a] * low[16 * j : 16 * (j + 1)] for a in range(first, first + count) for j in range(8)],
        axis=0,
    )


def pull_back(rows, planes_t, inv, upper, sums):
    total = sums[BITS * SETS :][:SETS]
    grad_proj = sums[: BITS * SETS] - upper * jnp.concatenate([total] * BITS, axis=0)
    head = grad_proj.astype(bf16)
    tail = (grad_proj - head.astype(f32)).astype(bf16)
    grad_unit = dot(planes_t, jnp.concatenate([head, tail], axis=0), NN) * (3.0 * inv)
    x = rows.astype(f32)
    return grad_unit - x * (inv * inv * jnp.sum(x * grad_unit, axis=0, keepdims=True))


def both(*refs):
    return jnp.concatenate([ref[...] for ref in refs], axis=1)


def key_kernel(planes, *refs, chunk, blocks):
    keys, vals, out = refs[:blocks], refs[blocks : 2 * blocks], refs[-1]
    start = refs[2 * blocks] if len(refs) > 2 * blocks + 1 else None
    _, upper, lower = sides(both(*keys), planes[...])
    low, high = half_codes(upper, lower)
    values = both(*vals)
    for c in range(0, 16, chunk):
        at = slice(128 * c, 128 * (c + chunk))
        part = dot(code_chunk(low, high, c, chunk), values, NT)
        if start is not None:
            part = part + start[0, at, :]
        out[0, at, :] = part.astype(out.dtype)


def query_kernel(planes, tables, *refs, chunk):
    rows, out = both(*refs[:-1]), refs[-1]
    _, upper, lower = sides(rows, planes[...])
    low, high = half_codes(upper, lower)
    acc = jnp.zeros((HEAD_DIM, rows.shape[1]), f32)
    for c in range(0, 16, chunk):
        acc += dot(tables[0, 128 * c : 128 * (c + chunk), :], code_chunk(low, high, c, chunk), TN)
    out[...] = (acc * (1.0 / HASHES)).astype(out.dtype)


def query_back_kernel(planes, planes_t, bits, tables, *refs, chunk, blocks, last):
    queries, grads = refs[: 2 * blocks], refs[2 * blocks : 3 * blocks]
    start = refs[3 * blocks] if len(refs) > 4 * blocks + 1 else None
    out, back_out = refs[-1 - blocks], refs[-blocks:]
    rows = both(*queries)
    inv, upper, lower = sides(rows, planes[...])
    low, high = half_codes(upper, lower)
    grad = both(*grads)
    sums = jnp.zeros((bits.shape[0], rows.shape[1]), f32)
    for c in range(0, 16, chunk):
        at = slice(128 * c, 128 * (c + chunk))
        codes = code_chunk(low, high, c, chunk)
        part = dot(codes, grad, NT)
        if start is not None:
            part = part + start[0, at, :]
        if last:
            part = part * (1.0 / HASHES)
        out[0, at, :] = part.astype(out.dtype)
        weighted = dot(tables[0, at, :], grad, NN).astype(bf16) * codes
        sums += dot(bits[:, at], weighted, NN)
    back = pull_back(rows, planes_t[...], inv, upper, sums * (1.0 / HASHES))
    width = back_out[0].shape[1]
    for i in range(blocks):
        back_out[i][...] = back[:, i * width : (i + 1) * width].astype(back_out[i].dtype)


def key_back_kernel(planes, planes_t, bits, ka, kb, va, vb, grad_tables, out, *, chunk):
    rows = both(ka, kb)
    inv, upper, lower = sides(rows, planes[...])
    low, high = half_codes(upper, lower)
    values = both(va, vb)
    width = rows.shape[1]
    sums = jnp.zeros((bits.shape[0], width), f32)
    grad_values = jnp.zeros((HEAD_DIM, width), f32)
    for c in range(0, 16, chunk):
        at = slice(128 * c, 128 * (c + chunk))
        codes = code_chunk(low, high, c, chunk)
        grad_values += dot(grad_tables[0, at, :], codes, TN)
        weighted = dot(grad_tables[0, at, :], values, NN).astype(bf16) * codes
        sums += dot(bits[:, at], weighted, NN)
    out[0] = pull_back(rows, planes_t[...], inv, upper, sums).astype(out.dtype)
    out[1] = grad_values.astype(out.dtype)


def bit_rows():
    out = np.zeros((80, BUCKETS, SETS), np.float32)
    for t in range(SETS):
        for i in range(BITS):
            out[i * SETS + t, :, t] = (np.arange(BUCKETS) >> i) & 1
        out[BITS * SETS + t, :, t] = 1
    return jnp.asarray(out.reshape(80, ROWS), bf16)


def whole(*shape):
    return pl.BlockSpec(shape, lambda h: (0,) * len(shape))


def head_rows(array, heads, which):
    width = array.shape[1]
    offset = (which - 3) * heads + array.shape[0] // HEAD_DIM
    return pl.BlockSpec((HEAD_DIM, width), lambda h: (h + offset, 0))


def per_head(width):
    return pl.BlockSpec((HEAD_DIM, width), lambda h: (h, 0))


def table_spec():
    return pl.BlockSpec((1, ROWS, HEAD_DIM), lambda h: (h, 0, 0))


def call(kernel, heads, micros, name, in_specs, out_specs, out_shape):
    return pl.pallas_call(
        kernel,
        grid=(heads,),
        in_specs=in_specs,
        out_specs=out_specs,
        out_shape=out_shape,
        compiler_params=pltpu.CompilerParams(vmem_limit_bytes=48 << 20),
        cost_estimate=pl.CostEstimate(
            flops=int(micros * 1.1e9), bytes_accessed=1 << 20, transcendentals=0
        ),
        name=name,
    )


def key_tables(planes, heads, blocks, start, kind):
    args = [planes, *blocks, *blocks]
    specs = [whole(64, 64)] + [head_rows(x, heads, w) for w in (1, 2) for x in blocks]
    if start is not None:
        specs.append(table_spec())
        args.append(start)
    return call(
        partial(key_kernel, chunk=2, blocks=len(blocks)),
        heads,
        30 if len(blocks) > 1 and start is not None else 1,
        "key_tables",
        specs,
        table_spec(),
        shape((heads, ROWS, HEAD_DIM), kind),
    )(*args)


def query_estimates(planes, heads, near, far, tables, kind):
    width = near.shape[1] + far.shape[1]
    return call(
        partial(query_kernel, chunk=2),
        heads,
        1,
        "query_estimates",
        [whole(64, 64), table_spec(), head_rows(near, heads, 0), per_head(far.shape[1])],
        per_head(width),
        shape((heads * HEAD_DIM, width), kind),
    )(planes, tables, near, far)


def query_backward(planes, planes_t, bits, heads, tables, queries, grads, start, last, kinds):
    width = grads[0].shape[1]
    blocks = len(grads)
    specs = [whole(64, 64), whole(64, 128), whole(80, ROWS), table_spec()]
    args = [planes, planes_t, bits, tables]
    for near, far in queries:
        specs += [head_rows(near, heads, 0), per_head(far.shape[1])]
        args += [near, far]
    specs += [per_head(width)] * blocks
    args += grads
    if start is not None:
        specs.append(table_spec())
        args.append(start)
    return call(
        partial(query_back_kernel, chunk=4, blocks=blocks, last=last),
        heads,
        25 * blocks,
        "query_backward",
        specs,
        [table_spec()] + [per_head(width)] * blocks,
        [shape((heads, ROWS, HEAD_DIM), bf16 if last else f32)]
        + [shape(grads[0].shape, kind) for kind in kinds],
    )(*args)


def key_backward(planes, planes_t, bits, heads, near, far, grad_tables, kind, micros=25):
    width = near.shape[1] + far.shape[1]
    return call(
        partial(key_back_kernel, chunk=4),
        heads,
        micros,
        "key_backward",
        [whole(64, 64), whole(64, 128), whole(80, ROWS)]
        + [head_rows(x, heads, w) for w in (1, 2) for x in (near, far)]
        + [table_spec()],
        pl.BlockSpec((2, HEAD_DIM, width), lambda h: (0, h, 0)),
        shape((2, heads * HEAD_DIM, width), kind),
    )(planes, planes_t, bits, near, far, near, far, grad_tables)


def norm(x):
    center = x - jnp.mean(x, axis=-1, keepdims=True)
    inv = lax.rsqrt(jnp.mean(center * center, axis=-1, keepdims=True) + 1e-5)
    return center * inv, inv


def norm_back(grad, unit, inv):
    return inv * (
        grad
        - jnp.mean(grad, axis=-1, keepdims=True)
        - unit * jnp.mean(grad * unit, axis=-1, keepdims=True)
    )


def column_sum(x):
    return jnp.sum(x, axis=0, keepdims=True)


def core_rows(core, ref, which):
    half = ref.shape[0] // 2
    at = core[0] if which == 0 else 1 - core[0]
    return ref[pl.ds(pl.multiple_of(at * half, 16), half), :]


def share_rows(keep, give, at, rows):
    part = keep.shape[2]
    for out in (keep, give):
        out[at] = rows[:, :part]
        out[at + 1] = rows[:, part:]


def dense_kernel(core, x_in, grad_out, gain, bias, *refs):
    attn, weights = refs[0:4], refs[4:6]
    layer_out, first_out, grad_second_out, slope, keep, give, heads_give, small = refs[6:14]
    owner = [core[1] ^ (b // 2) for b in range(8)]
    for j in range(4):
        heads_give[j] = core_rows(core, attn[j], 1)
    part = slope.shape[2]
    blocks = range(8)
    heads = jnp.concatenate([core_rows(core, attn[b // 2], b % 2) for b in blocks], axis=0)
    out_w = jnp.concatenate([weights[b % 2][owner[b], 2 * part :, :] for b in blocks], axis=0)
    attn_out = dot(heads, out_w, TN)
    resid = x_in[...].astype(f32)
    first = resid + attn_out
    first_out[...] = first
    small[0:1, :] = column_sum(resid * resid)
    small[1:2, :] = column_sum(attn_out * attn_out)
    small[2:3, :] = column_sum(first * first)
    unit_1, _ = norm(first)
    normed = (unit_1 * gain[0:1, :] + bias[0:1, :]).astype(bf16)
    share_rows(keep, give, 4, normed)
    second = normed.astype(f32)
    for b in blocks:
        pre = dot(normed, weights[b % 2][owner[b], 0:part, :], NT)
        below = 0.5 * (1.0 + lax.erf(pre * 0.7071067811865476))
        rows = (pre * below).astype(bf16)
        (keep, give)[b % 2][b // 2] = rows
        slope[b] = below + pre * (0.3989422804014327 * jnp.exp(-0.5 * pre * pre))
        second = second + dot(rows, weights[b % 2][owner[b], part : 2 * part, :], NN)
    unit_2, inv_2 = norm(second)
    layer_out[...] = (unit_2 * gain[1:2, :] + bias[1:2, :]).astype(layer_out.dtype)
    grad = grad_out[...]
    small[3:4, :] = column_sum(grad * unit_2)
    small[4:5, :] = column_sum(grad)
    small[5:8, :] = jnp.zeros_like(small[5:8, :])
    grad_second = norm_back(grad * gain[1:2, :], unit_2, inv_2)
    grad_second_out[...] = grad_second
    share_rows(keep, give, 6, grad_second.astype(bf16))


def dense_back_kernel(core, first, grad_second, slope, gain, *refs):
    weights = refs[0:2]
    grad_first_out, keep, give = refs[2:5]
    estimates, small = refs[5:9], refs[9]
    owner = [core[1] ^ (b // 2) for b in range(8)]
    part = slope.shape[2]
    blocks = range(8)
    grad_normed = grad_second[...]
    grad_ffn = grad_normed.astype(bf16)
    for b in blocks:
        rows = dot(grad_ffn, weights[b % 2][owner[b], part : 2 * part, :], NT)
        rows = (rows * slope[b]).astype(bf16)
        (keep, give)[b % 2][b // 2] = rows
        grad_normed = grad_normed + dot(rows, weights[b % 2][owner[b], 0:part, :], NN)
    unit, inv = norm(first[...])
    small[0:1, :] = column_sum(grad_normed * unit)
    small[1:2, :] = column_sum(grad_normed)
    small[2:8, :] = jnp.zeros_like(small[2:8, :])
    grad_first = norm_back(grad_normed * gain[0:1, :], unit, inv)
    grad_first_out[...] = grad_first
    grad_attn = grad_first.astype(bf16)
    share_rows(keep, give, 4, grad_attn)
    for b in blocks:
        half = estimates[0].shape[0] // 2
        at = core[0] if b % 2 == 0 else 1 - core[0]
        estimates[b // 2][pl.ds(pl.multiple_of(at * half, 16), half), :] = dot(
            weights[b % 2][owner[b], 2 * part :, :], grad_attn, NT
        ).astype(bf16)


def weight_grad_kernel(core, small_a, small_b, *refs):
    near, far, near_back, far_back = refs[0:4]
    attn, attn_far, out = refs[4:8], refs[8], refs[9]
    part = near.shape[2]
    sums = jnp.concatenate([small_a[...], small_b[...]], axis=0).astype(bf16)

    def wide(ref, at):
        return jnp.concatenate([ref[at], ref[at + 1]], axis=1)

    def rows(ref, other, at):
        return jnp.concatenate([wide(ref, at), wide(other, at)], axis=0)

    normed, grad_ffn = rows(near, far, 4), rows(near, far, 6)
    grad_attn = rows(near_back, far_back, 4)
    for j in range(4):
        owner = core[1] ^ j
        hidden = jnp.concatenate([near[j], far[j]], axis=0)
        grad_pre = jnp.concatenate([near_back[j], far_back[j]], axis=0)
        out[owner, 0:part, :] = dot(grad_pre, normed, TN).astype(bf16)
        out[owner, part : 2 * part, :] = dot(hidden, grad_ffn, TN).astype(bf16)
        heads = jnp.concatenate([core_rows(core, attn[j], 0), attn_far[j]], axis=1)
        at = 2 * part + heads.shape[0]
        out[owner, 2 * part : at, :] = dot(heads, grad_attn, NN).astype(bf16)
        out[owner, at : at + 16, :] = sums
        out[owner, at + 16 :, :] = jnp.zeros_like(sums)


def input_grad_kernel(core, grad_first, *refs):
    blocks, near, far, out = refs[0:4], refs[4], refs[5], refs[6]
    half = near.shape[2]
    total = grad_first[...]
    for which, halves in enumerate((near, far)):
        at = core[0] if which == 0 else 1 - core[0]
        at = pl.ds(pl.multiple_of(at * half, 16), half)
        for j in range(4):
            rows = jnp.concatenate([blocks[j][c, at, :] for c in range(3)], axis=0)
            weights = jnp.concatenate([halves[core[1] ^ j, c] for c in range(3)], axis=0)
            total = total + dot(rows, weights, TN)
    out[...] = total.astype(out.dtype)


def vmem(count):
    return [pl.BlockSpec(memory_space=pltpu.VMEM)] * count


def single(kernel, core, args, out_shape, micros, name, scratch=()):
    return pl.pallas_call(
        kernel,
        in_specs=[pl.BlockSpec(memory_space=pltpu.SMEM)] + vmem(len(args)),
        out_specs=vmem(len(out_shape)),
        out_shape=out_shape,
        scratch_shapes=scratch,
        compiler_params=pltpu.CompilerParams(vmem_limit_bytes=56 << 20),
        cost_estimate=pl.CostEstimate(
            flops=int(micros * 1.1e9), bytes_accessed=1 << 20, transcendentals=0
        ),
        name=name,
    )(core, *args)


def dense(core, x_in, grad_out, gain, bias, attn, weights):
    rows, width = x_in.shape
    part = (weights[0].shape[1] - attn[0].shape[0] // 2) // 2
    out_shape = [
        shape((rows, width), bf16),
        shape((rows, width), f32),
        shape((rows, width), f32),
        shape((8, rows, part), f32),
        shape((8, rows, part), bf16),
        shape((8, rows, part), bf16),
        shape((4, attn[0].shape[0] // 2, rows), bf16),
        shape((8, width), f32),
    ]
    args = [x_in, grad_out, gain, bias, *attn, *weights]
    return single(dense_kernel, core, args, out_shape, 14, "dense")


def dense_back(core, first, grad_second, slope, gain, attn, weights):
    rows, width = first.shape
    part = (weights[0].shape[1] - attn[0].shape[0] // 2) // 2
    out_shape = [
        shape((rows, width), f32),
        shape((6, rows, part), bf16),
        shape((6, rows, part), bf16),
        *[shape(attn[0].shape, bf16)] * 4,
        shape((8, width), f32),
    ]
    args = [first, grad_second, slope, gain, *weights]
    return single(dense_back_kernel, core, args, out_shape, 8, "dense_back")


def weight_grads(core, small_a, small_b, shared, attn, attn_far):
    part, width = shared[0].shape[2], small_a.shape[1]
    out_shape = [shape((4, 2 * part + attn[0].shape[0] // 2 + 32, width), bf16)]
    args = [small_a, small_b, *shared, *attn, attn_far]
    return single(weight_grad_kernel, core, args, out_shape, 7, "weight_grads")[0]


def weight_results_kernel(core, near, far, up, down, out):
    part, rows = up.shape[1] // 2, out.shape[0] // 2
    for which, ref in enumerate((near, far)):
        at = core[0] if which == 0 else 1 - core[0]
        at_part = pl.ds(pl.multiple_of(at * part, 128), part)
        up[:, at_part] = ref[0:part, :].astype(f32).T
        down[at_part, :] = ref[part : 2 * part, :].astype(f32)
        at_rows = pl.ds(pl.multiple_of(at * rows, 16), rows)
        out[at_rows, :] = ref[2 * part : 2 * part + rows, :].astype(f32)


def weight_results(core, near, far, head_width):
    width = near.shape[1]
    part = (near.shape[0] - 32 - head_width // 2) // 2
    out_shape = [
        shape((width, 2 * part), f32), shape((2 * part, width), f32), shape((head_width, width), f32)
    ]
    return single(weight_results_kernel, core, [near, far], out_shape, 3, "weight_results")


def input_grad(core, grad_first, blocks, near, far):
    out_shape = [shape(grad_first.shape, bf16)]
    args = [grad_first, *blocks, near, far]
    return single(input_grad_kernel, core, args, out_shape, 40, "input_grad")[0]


def after(x, *others):
    return lax.optimization_barrier((x, *others))[0]


def add(a, *others):
    return sum([b.astype(f32) for b in others], a.astype(f32))


def shards(
    inputs,
    w_qkv,
    w_out,
    up_weight,
    down_weight,
    norm_gain,
    norm_bias,
    planes,
    mask_pos,
    cot_rows,
):
    own = inputs[0]
    piece, seqs, width = own.shape
    hash_count, head_count = lax.axis_size("hash"), lax.axis_size("head")
    groups, places = seqs, hash_count // seqs
    assert places == 2 and lax.axis_size("seq") == 2 and head_count == 4
    assert planes.shape[0] * hash_count == 4 * SETS
    quarter = piece // head_count
    rows = groups * quarter
    half_len = piece * hash_count
    head_width = w_out.shape[0]
    hidden_own = down_weight.shape[0]
    n_tokens = head_count * rows
    hash_id, d, s = lax.axis_index("hash"), lax.axis_index("head"), lax.axis_index("seq")
    g, r = hash_id // places, hash_id % places

    def in_halves(index, mine, other):
        first = jnp.where(index == 0, mine, other)
        second = jnp.where(index == 0, other, mine)
        return jnp.concatenate([first, second], axis=0)

    def split(x, index):
        half = x.shape[0] // 2
        return [lax.dynamic_slice_in_dim(x, at * half, half, 0) for at in (index, 1 - index)]

    def over_seq(x):
        return lax.ppermute(x, "seq", [(0, 1), (1, 0)])

    def over_place(x):
        return lax.ppermute(x, "hash", [(h, h ^ 1) for h in range(hash_count)])

    def over_group(x, k):
        moves = [(h, ((h // places + k) % groups) * places + h % places) for h in range(hash_count)]
        return lax.ppermute(x, "hash", moves)

    def over_head(x, j):
        return lax.ppermute(x, "head", [(h, h ^ j) for h in range(head_count)])

    def seq_rows(block, index):
        return lax.dynamic_index_in_dim(block, index % seqs, 1, keepdims=False)

    here = [
        seq_rows(lax.dynamic_slice_in_dim(own, (d ^ j) * quarter, quarter, 0), g)
        for j in range(head_count)
    ]
    near_tokens = jnp.concatenate(here)
    my_quarter = lax.dynamic_slice_in_dim(own, d * quarter, quarter, 0)
    sent = [seq_rows(my_quarter, g + k) for k in range(1, groups)]
    arrived = [over_group(x, k + 1) for k, x in enumerate(sent)]

    signed = (2 * planes - 1).astype(bf16)
    if planes.shape[0] == SETS and groups == 2:
        moves = [
            ((2 * rr + ss) * 2 + gg, (gg * places + rr) * 2 + ss)
            for gg in range(2)
            for rr in range(2)
            for ss in range(2)
        ]
        signed = lax.ppermute(signed, ("hash", "seq"), moves)
    else:
        signed = lax.all_gather(signed, "hash", axis=0, tiled=True)
        signed = lax.dynamic_slice_in_dim(signed, (r * 2 + s) * SETS, SETS, 0)
    signed = signed.transpose(1, 0, 2).reshape(BITS * SETS, HEAD_DIM)
    signed_t = jnp.concatenate([signed.T, signed.T], axis=1)
    bits = bit_rows()

    cut, out_cut = hidden_own // 2, head_width // 2
    weights = jnp.concatenate(
        [
            lax.dynamic_slice_in_dim(after(up_weight, *sent), s * cut, cut, 1).T,
            lax.dynamic_slice_in_dim(down_weight, s * cut, cut, 0),
            lax.dynamic_slice_in_dim(w_out, s * out_cut, out_cut, 0),
        ]
    )
    weights = lax.all_gather(weights, "head", axis=0)
    w_qkv_t = lax.dynamic_slice_in_dim(w_qkv.transpose(0, 2, 1), s * out_cut, out_cut, 1)

    head_n = head_width // HEAD_DIM

    def project(w, rows_in):
        out = jnp.einsum("cde,ld->cel", w, rows_in, preferred_element_type=f32)
        return out.astype(bf16).reshape(-1, rows_in.shape[0])

    near_tokens = after(near_tokens, *arrived)
    near = project(w_qkv, near_tokens)
    near_z, near_o = over_place(near), over_seq(near)
    far_quarter = jnp.stack(arrived)
    moved = [over_head(far_quarter, j) for j in range(1, head_count)]
    tables = key_tables(signed, head_n, [near, near_o], None, f32)
    moved = [after(x, tables) for x in moved]

    near_z = after(near_z, tables)
    near_zo = over_seq(near_z)

    mask_pos = after(mask_pos, tables)
    slot = jnp.arange(groups, dtype=jnp.int32)[:, None]
    place_of = ((g - slot) % groups) * places + r
    position = s * half_len + place_of * piece + d * quarter + jnp.arange(quarter, dtype=jnp.int32)[None]
    mask_row = lax.dynamic_index_in_dim(mask_pos, g, 0, keepdims=False)
    cot = lax.dynamic_index_in_dim(cot_rows, g, 0, keepdims=False)
    pick = (position.reshape(rows)[:, None] == mask_row[None]).astype(bf16)
    grad_out = jnp.dot(pick, cot, preferred_element_type=f32)
    ready = after(signed, grad_out)
    tables = key_tables(ready, head_n, [near_z, near_zo], tables, f32)

    far_tokens = jnp.stack([far_quarter, *moved]).reshape(-1, width)
    kv = project(w_qkv[1:], far_tokens)
    q = project(after(w_qkv[:1], kv), far_tokens)
    tokens = jnp.concatenate([near_tokens, far_tokens])
    dense_in = jnp.concatenate([here[0], *arrived])
    kv_z, kv_o = over_place(kv), over_seq(kv)
    q_o, q_z = over_seq(q), over_place(q)
    n_near = near.shape[1]

    tables = key_tables(after(signed, q), head_n, [kv, kv_o], tables, f32)

    kv_z = after(kv_z, tables)
    kv_zo = over_seq(kv_z)
    ready = after(signed, tokens, dense_in)
    tables = key_tables(ready, head_n, [kv_z], tables, f32)

    q_z = after(q_z, tables)
    q_zo = over_seq(q_z)
    kv_zo = after(kv_zo, tables)
    tables = key_tables(after(signed, q_z), head_n, [kv_zo], tables, bf16)

    q_zo = after(q_zo, tables)
    e_zo = query_estimates(signed, head_n, near_zo, q_zo, tables, bf16)
    e_zo_moved = over_seq(e_zo)
    e_z = query_estimates(signed, head_n, near_z, after(q_z, e_zo), tables, bf16)
    e_far = add(e_z, after(e_zo_moved, e_z)).astype(bf16)
    ready = after(q_o, e_far)
    e_o = query_estimates(signed, head_n, near_o, ready, tables, bf16)
    e_far = over_place(e_far)
    e_o_moved = over_seq(e_o)
    e = query_estimates(signed, head_n, near, after(q, e_o), tables, f32)
    e_far = after(e_far, e)
    weights = after(weights, e_o)
    weights = [weights, over_seq(weights)]
    w_qkv_t = lax.all_gather(after(w_qkv_t, weights[0]), "head", axis=0)
    attn = add(e, after(e_o_moved, e), e_far).astype(bf16)

    def to_dense(block):
        parts = []
        for j in range(head_count):
            a, b = j * quarter, n_near + j * (rows - quarter)
            cut = [block[..., a : a + quarter], block[..., b : b + rows - quarter]]
            parts.append(jnp.concatenate(cut, axis=-1))
        moved = [over_head(parts[j], j) for j in range(1, head_count)]
        return [parts[0], *lax.optimization_barrier(moved)]

    attn_parts = to_dense(attn)

    def away(dense_rows):
        dense_rows = dense_rows.reshape(groups, quarter, width)
        return [dense_rows[0]] + [over_group(dense_rows[k], groups - k) for k in range(1, groups)]

    core = jnp.stack([s, d]).astype(jnp.int32)
    layer_rows, first, grad_second, slope, keep, give, heads_give, small_a = dense(
        core, dense_in, grad_out, norm_gain, norm_bias, attn_parts, weights
    )
    taken, heads_far = over_seq(give), over_seq(heads_give)
    grad_first, keep_back, give_back, *est_parts, small_b = dense_back(
        core, first, grad_second, slope, norm_gain, attn_parts, weights
    )
    taken_back = over_seq(give_back)
    est_moved = [over_head(est_parts[j], j) for j in range(1, head_count)]
    est_parts = [est_parts[0], *lax.optimization_barrier(est_moved)]
    grad = jnp.concatenate(
        [x[:, :quarter] for x in est_parts] + [x[:, quarter:] for x in est_parts], axis=1
    )
    layer_moved = away(layer_rows)
    weight_parts = weight_grads(
        core, after(small_a, grad, w_qkv_t), small_b, [keep, taken, keep_back, taken_back], attn_parts, heads_far
    )

    weight_sum = lax.psum_scatter(weight_parts, "head", scatter_dimension=0, tiled=True)[0]
    grad_z = over_place(grad)
    grad_o = after(over_seq(grad), weight_parts)
    layer_moved = jnp.stack([after(x, weight_parts) for x in layer_moved])
    part, dq, dq_o = query_backward(
        signed, signed_t, bits, head_n, tables, [(near, after(q, layer_moved)), (near_o, q_o)], [grad, grad_o],
        None, False, [f32, bf16],
    )

    grad_z = after(grad_z, part)
    grad_zo = over_seq(grad_z)
    dq_o = over_seq(dq_o)
    part, dq_z = query_backward(
        signed, signed_t, bits, head_n, tables, [(near_z, q_z)], [grad_z], part, False, [f32]
    )

    dq_own = add(dq, after(dq_o, dq_z))
    grad_zo = after(grad_zo, dq_z)
    grad_tables, dq_zo = query_backward(
        signed, signed_t, bits, head_n, tables, [(near_zo, after(q_zo, dq_own))], [grad_zo], part, True, [bf16]
    )

    dq_zo = over_seq(dq_zo)
    w_qkv_t = after(w_qkv_t, grad_tables)
    w_qkv_far = over_seq(w_qkv_t)
    dkv_zo = key_backward(signed, signed_t, bits, head_n, near_zo, kv_zo, grad_tables, bf16)

    dkv_zo_moved = over_seq(dkv_zo)
    dq_far = add(dq_z, after(dq_zo, dkv_zo)).astype(bf16)
    layer_moved = [layer_moved] + [over_head(layer_moved, j) for j in range(1, head_count)]
    dkv_z = key_backward(signed, signed_t, bits, head_n, near_z, after(kv_z, dq_far), grad_tables, bf16)
    dq_far = over_place(dq_far)

    dkv_far = add(dkv_z, after(dkv_zo_moved, dkv_z)).astype(bf16)
    grad_q = add(dq_own, after(dq_far, dkv_z)).astype(bf16)
    weight_sum = after(weight_sum, dkv_z)
    layer_moved = [after(x, dkv_z) for x in layer_moved]
    dkv_o = key_backward(
        signed, signed_t, bits, head_n, near_o, after(kv_o, dkv_far, grad_q, weight_sum, *layer_moved),
        grad_tables, bf16, 25,
    )
    half = weight_sum.shape[0] // 2
    low_keep, low_send = split(weight_sum[:half], r)
    low_far = over_place(low_send)
    high_sum = lax.psum(weight_sum[half:], "hash")
    dkv_far = over_place(dkv_far)
    dkv_o_moved = over_seq(dkv_o)
    low_keep = add(low_keep, after(low_far, dkv_o))
    low_send = low_keep.astype(bf16)
    low_far = [over_group(low_send, k) for k in range(1, groups)]
    dkv = key_backward(
        signed, signed_t, bits, head_n, near, after(kv, low_send), grad_tables, f32, 25
    )

    dkv_o_moved = after(dkv_o_moved, dkv)
    grad_kv = add(dkv, dkv_o_moved, after(dkv_far, dkv)).astype(bf16)
    grad_qkv = jnp.concatenate([grad_q[None], grad_kv])
    qkv_parts = to_dense(grad_qkv)
    low_keep = add(low_keep, *[after(x, qkv_parts[1]) for x in low_far]).astype(bf16)
    low_far = over_place(low_keep)

    grad_in = input_grad(core, grad_first, qkv_parts, w_qkv_t, after(w_qkv_far, dkv))

    w_grad = dot(grad_qkv.reshape(3 * head_width, n_tokens), tokens, NN).astype(bf16)
    w_keep, w_send = split(w_grad, s)
    w_keep, w_send = split(add(w_keep, over_seq(w_send)).astype(bf16), r)
    grad_moved = away(grad_in)
    w_keep = add(w_keep, over_place(w_send))
    w_send = w_keep.astype(bf16)
    grad_moved = after(jnp.stack(grad_moved), w_send)
    w_keep = add(w_keep, *[over_group(w_send, k) for k in range(1, groups)]).astype(bf16)
    grad_moved = [grad_moved] + [over_head(grad_moved, j) for j in range(1, head_count)]

    def home(blocks):
        table = jnp.stack(blocks)
        columns = []
        for q_at in range(head_count):
            block = lax.dynamic_index_in_dim(table, q_at ^ d, 0, keepdims=False)
            columns.append(
                jnp.stack(
                    [
                        lax.dynamic_index_in_dim(block, (at - g) % groups, 0, keepdims=False)
                        for at in range(seqs)
                    ],
                    axis=1,
                )
            )
        return jnp.concatenate(columns, axis=0)

    layer_out = home([after(x, grad_moved[0]) for x in layer_moved])
    grad_inputs = home(grad_moved).astype(f32)

    w_grad = in_halves(r, w_keep, over_place(w_keep))
    w_grad = in_halves(s, w_grad, over_seq(w_grad)).reshape(3, head_width, width)
    grad_w_qkv = w_grad.transpose(0, 2, 1).astype(f32)
    low_keep = in_halves(r, low_keep, after(low_far, *grad_moved))
    weight_sum = jnp.concatenate([low_keep, after(high_sum, *grad_moved)])
    weight_far = over_seq(weight_sum)
    grad_w_up, grad_w_down, grad_w_out = weight_results(core, weight_sum, weight_far, head_width)
    at = slice(2 * cut + out_cut, 2 * cut + out_cut + 16)
    small = add(weight_sum[at], weight_far[at])

    count = piece * seqs * width * hash_count * 2
    stream_rms = jnp.sqrt(jnp.sum(small[0:3], axis=1) / count)
    share = width // head_count
    norm_grads = lax.dynamic_slice_in_dim(small, d * share, share, 1)
    return (
        layer_out[None],
        grad_inputs[None],
        grad_w_qkv,
        grad_w_out,
        grad_w_up,
        grad_w_down,
        jnp.stack([norm_grads[8], norm_grads[3]]),
        jnp.stack([norm_grads[9], norm_grads[4]]),
        stream_rms,
    )


def solution(mesh):
    placed = (
        P("seq", "hash", None, None),
        P(None, None, "head"),
        P("head", None),
        P(None, "head"),
        P("head", None),
        P(),
        P(),
        P("hash", None, None),
        P(),
        P(),
    )
    return jax.shard_map(
        shards,
        mesh=mesh,
        in_specs=placed,
        out_specs=(
            P("seq", "hash", None, None),
            P("seq", "hash", None, None),
            P(None, None, "head"),
            P("head", None),
            P(None, "head"),
            P("head", None),
            P(None, "head"),
            P(None, "head"),
            P(),
        ),
        check_vma=False,
    )
```

```python
from functools import partial

import jax
import jax.numpy as jnp
import numpy as np
from jax import lax
from jax.experimental import pallas as pl
from jax.experimental.pallas import tpu as pltpu
from jax.sharding import PartitionSpec as P

HEAD_DIM = 64
HASHES = 32
BITS = 8
SETS = 8
BUCKETS = 1 << BITS
ROWS = BUCKETS * SETS

bf16 = jnp.bfloat16
f32 = jnp.float32
NN = (((1,), (0,)), ((), ()))
NT = (((1,), (1,)), ((), ()))
TN = (((0,), (0,)), ((), ()))


shape = jax.ShapeDtypeStruct


def dot(a, b, dims):
    return lax.dot_general(a, b, dims, preferred_element_type=f32)


def sides(rows, planes):
    x = rows.astype(f32)
    inv = lax.rsqrt(jnp.sum(x * x, axis=0, keepdims=True) + 1e-6)
    proj = dot(planes, rows, NN) * (3.0 * inv)
    small = jnp.exp(-proj)
    upper = 1.0 / (1.0 + small)
    return inv, upper, small * upper


def products(upper, lower, first, count):
    out = None
    for i in range(first, first + count):
        lo, up = lower[SETS * i : SETS * (i + 1)], upper[SETS * i : SETS * (i + 1)]
        out = [lo, up] if out is None else [c * lo for c in out] + [c * up for c in out]
    return out


def half_codes(upper, lower):
    low = jnp.concatenate(products(upper, lower, 0, 4), axis=0).astype(bf16)
    high = [jnp.concatenate([a, a], axis=0).astype(bf16) for a in products(upper, lower, 4, 4)]
    return low, high


def code_chunk(low, high, first, count):
    return jnp.concatenate(
        [high[a] * low[16 * j : 16 * (j + 1)] for a in range(first, first + count) for j in range(8)],
        axis=0,
    )


def pull_back(rows, planes_t, inv, upper, sums):
    total = sums[BITS * SETS :][:SETS]
    grad_proj = sums[: BITS * SETS] - upper * jnp.concatenate([total] * BITS, axis=0)
    head = grad_proj.astype(bf16)
    tail = (grad_proj - head.astype(f32)).astype(bf16)
    grad_unit = dot(planes_t, jnp.concatenate([head, tail], axis=0), NN) * (3.0 * inv)
    x = rows.astype(f32)
    return grad_unit - x * (inv * inv * jnp.sum(x * grad_unit, axis=0, keepdims=True))


def both(*refs):
    return jnp.concatenate([ref[...] for ref in refs], axis=1)


def key_kernel(planes, *refs, chunk, blocks):
    keys, vals, out = refs[:blocks], refs[blocks : 2 * blocks], refs[-1]
    start = refs[2 * blocks] if len(refs) > 2 * blocks + 1 else None
    _, upper, lower = sides(both(*keys), planes[...])
    low, high = half_codes(upper, lower)
    values = both(*vals)
    for c in range(0, 16, chunk):
        at = slice(128 * c, 128 * (c + chunk))
        part = dot(code_chunk(low, high, c, chunk), values, NT)
        if start is not None:
            part = part + start[0, at, :]
        out[0, at, :] = part.astype(out.dtype)


def query_kernel(planes, tables, *refs, chunk):
    rows, out = both(*refs[:-1]), refs[-1]
    _, upper, lower = sides(rows, planes[...])
    low, high = half_codes(upper, lower)
    acc = jnp.zeros((HEAD_DIM, rows.shape[1]), f32)
    for c in range(0, 16, chunk):
        acc += dot(tables[0, 128 * c : 128 * (c + chunk), :], code_chunk(low, high, c, chunk), TN)
    out[...] = (acc * (1.0 / HASHES)).astype(out.dtype)


def query_back_kernel(planes, planes_t, bits, tables, *refs, chunk, blocks, last):
    queries, grads = refs[: 2 * blocks], refs[2 * blocks : 3 * blocks]
    start = refs[3 * blocks] if len(refs) > 4 * blocks + 1 else None
    out, back_out = refs[-1 - blocks], refs[-blocks:]
    rows = both(*queries)
    inv, upper, lower = sides(rows, planes[...])
    low, high = half_codes(upper, lower)
    grad = both(*grads)
    sums = jnp.zeros((bits.shape[0], rows.shape[1]), f32)
    for c in range(0, 16, chunk):
        at = slice(128 * c, 128 * (c + chunk))
        codes = code_chunk(low, high, c, chunk)
        part = dot(codes, grad, NT)
        if start is not None:
            part = part + start[0, at, :]
        if last:
            part = part * (1.0 / HASHES)
        out[0, at, :] = part.astype(out.dtype)
        weighted = dot(tables[0, at, :], grad, NN).astype(bf16) * codes
        sums += dot(bits[:, at], weighted, NN)
    back = pull_back(rows, planes_t[...], inv, upper, sums * (1.0 / HASHES))
    width = back_out[0].shape[1]
    for i in range(blocks):
        back_out[i][...] = back[:, i * width : (i + 1) * width].astype(back_out[i].dtype)


def key_back_kernel(planes, planes_t, bits, ka, kb, va, vb, grad_tables, out, *, chunk):
    rows = both(ka, kb)
    inv, upper, lower = sides(rows, planes[...])
    low, high = half_codes(upper, lower)
    values = both(va, vb)
    width = rows.shape[1]
    sums = jnp.zeros((bits.shape[0], width), f32)
    grad_values = jnp.zeros((HEAD_DIM, width), f32)
    for c in range(0, 16, chunk):
        at = slice(128 * c, 128 * (c + chunk))
        codes = code_chunk(low, high, c, chunk)
        grad_values += dot(grad_tables[0, at, :], codes, TN)
        weighted = dot(grad_tables[0, at, :], values, NN).astype(bf16) * codes
        sums += dot(bits[:, at], weighted, NN)
    out[0] = pull_back(rows, planes_t[...], inv, upper, sums).astype(out.dtype)
    out[1] = grad_values.astype(out.dtype)


def bit_rows():
    out = np.zeros((80, BUCKETS, SETS), np.float32)
    for t in range(SETS):
        for i in range(BITS):
            out[i * SETS + t, :, t] = (np.arange(BUCKETS) >> i) & 1
        out[BITS * SETS + t, :, t] = 1
    return jnp.asarray(out.reshape(80, ROWS), bf16)


def whole(*shape):
    return pl.BlockSpec(shape, lambda h: (0,) * len(shape))


def head_rows(array, heads, which):
    width = array.shape[1]
    offset = (which - 3) * heads + array.shape[0] // HEAD_DIM
    return pl.BlockSpec((HEAD_DIM, width), lambda h: (h + offset, 0))


def per_head(width):
    return pl.BlockSpec((HEAD_DIM, width), lambda h: (h, 0))


def table_spec():
    return pl.BlockSpec((1, ROWS, HEAD_DIM), lambda h: (h, 0, 0))


def call(kernel, heads, micros, name, in_specs, out_specs, out_shape):
    return pl.pallas_call(
        kernel,
        grid=(heads,),
        in_specs=in_specs,
        out_specs=out_specs,
        out_shape=out_shape,
        compiler_params=pltpu.CompilerParams(vmem_limit_bytes=48 << 20),
        cost_estimate=pl.CostEstimate(
            flops=int(micros * 1.1e9), bytes_accessed=1 << 20, transcendentals=0
        ),
        name=name,
    )


def key_tables(planes, heads, blocks, start, kind):
    args = [planes, *blocks, *blocks]
    specs = [whole(64, 64)] + [head_rows(x, heads, w) for w in (1, 2) for x in blocks]
    if start is not None:
        specs.append(table_spec())
        args.append(start)
    return call(
        partial(key_kernel, chunk=2, blocks=len(blocks)),
        heads,
        30 if len(blocks) > 1 and start is not None else 1,
        "key_tables",
        specs,
        table_spec(),
        shape((heads, ROWS, HEAD_DIM), kind),
    )(*args)


def query_estimates(planes, heads, near, far, tables, kind):
    width = near.shape[1] + far.shape[1]
    return call(
        partial(query_kernel, chunk=2),
        heads,
        1,
        "query_estimates",
        [whole(64, 64), table_spec(), head_rows(near, heads, 0), per_head(far.shape[1])],
        per_head(width),
        shape((heads * HEAD_DIM, width), kind),
    )(planes, tables, near, far)


def query_backward(planes, planes_t, bits, heads, tables, queries, grads, start, last, kinds):
    width = grads[0].shape[1]
    blocks = len(grads)
    specs = [whole(64, 64), whole(64, 128), whole(80, ROWS), table_spec()]
    args = [planes, planes_t, bits, tables]
    for near, far in queries:
        specs += [head_rows(near, heads, 0), per_head(far.shape[1])]
        args += [near, far]
    specs += [per_head(width)] * blocks
    args += grads
    if start is not None:
        specs.append(table_spec())
        args.append(start)
    return call(
        partial(query_back_kernel, chunk=4, blocks=blocks, last=last),
        heads,
        25 * blocks,
        "query_backward",
        specs,
        [table_spec()] + [per_head(width)] * blocks,
        [shape((heads, ROWS, HEAD_DIM), bf16 if last else f32)]
        + [shape(grads[0].shape, kind) for kind in kinds],
    )(*args)


def key_backward(planes, planes_t, bits, heads, near, far, grad_tables, kind, micros=25):
    width = near.shape[1] + far.shape[1]
    return call(
        partial(key_back_kernel, chunk=4),
        heads,
        micros,
        "key_backward",
        [whole(64, 64), whole(64, 128), whole(80, ROWS)]
        + [head_rows(x, heads, w) for w in (1, 2) for x in (near, far)]
        + [table_spec()],
        pl.BlockSpec((2, HEAD_DIM, width), lambda h: (0, h, 0)),
        shape((2, heads * HEAD_DIM, width), kind),
    )(planes, planes_t, bits, near, far, near, far, grad_tables)


def norm(x):
    center = x - jnp.mean(x, axis=-1, keepdims=True)
    inv = lax.rsqrt(jnp.mean(center * center, axis=-1, keepdims=True) + 1e-5)
    return center * inv, inv


def norm_back(grad, unit, inv):
    return inv * (
        grad
        - jnp.mean(grad, axis=-1, keepdims=True)
        - unit * jnp.mean(grad * unit, axis=-1, keepdims=True)
    )


def column_sum(x):
    return jnp.sum(x, axis=0, keepdims=True)


def core_rows(core, ref, which):
    half = ref.shape[0] // 2
    at = core[0] if which == 0 else 1 - core[0]
    return ref[pl.ds(pl.multiple_of(at * half, 16), half), :]


def share_rows(keep, give, at, rows):
    part = keep.shape[2]
    for out in (keep, give):
        out[at] = rows[:, :part]
        out[at + 1] = rows[:, part:]


def dense_kernel(core, x_in, grad_out, gain, bias, *refs):
    attn, weights = refs[0:4], refs[4:6]
    layer_out, first_out, grad_second_out, slope, keep, give, heads_give, small = refs[6:14]
    owner = [core[1] ^ (b // 2) for b in range(8)]
    for j in range(4):
        heads_give[j] = core_rows(core, attn[j], 1)
    part = slope.shape[2]
    blocks = range(8)
    heads = jnp.concatenate([core_rows(core, attn[b // 2], b % 2) for b in blocks], axis=0)
    out_w = jnp.concatenate([weights[b % 2][owner[b], 2 * part :, :] for b in blocks], axis=0)
    attn_out = dot(heads, out_w, TN)
    resid = x_in[...].astype(f32)
    first = resid + attn_out
    first_out[...] = first
    small[0:1, :] = column_sum(resid * resid)
    small[1:2, :] = column_sum(attn_out * attn_out)
    small[2:3, :] = column_sum(first * first)
    unit_1, _ = norm(first)
    normed = (unit_1 * gain[0:1, :] + bias[0:1, :]).astype(bf16)
    share_rows(keep, give, 4, normed)
    second = normed.astype(f32)
    for b in blocks:
        pre = dot(normed, weights[b % 2][owner[b], 0:part, :], NT)
        below = 0.5 * (1.0 + lax.erf(pre * 0.7071067811865476))
        rows = (pre * below).astype(bf16)
        (keep, give)[b % 2][b // 2] = rows
        slope[b] = below + pre * (0.3989422804014327 * jnp.exp(-0.5 * pre * pre))
        second = second + dot(rows, weights[b % 2][owner[b], part : 2 * part, :], NN)
    unit_2, inv_2 = norm(second)
    layer_out[...] = (unit_2 * gain[1:2, :] + bias[1:2, :]).astype(layer_out.dtype)
    grad = grad_out[...]
    small[3:4, :] = column_sum(grad * unit_2)
    small[4:5, :] = column_sum(grad)
    small[5:8, :] = jnp.zeros_like(small[5:8, :])
    grad_second = norm_back(grad * gain[1:2, :], unit_2, inv_2)
    grad_second_out[...] = grad_second
    share_rows(keep, give, 6, grad_second.astype(bf16))


def dense_back_kernel(core, first, grad_second, slope, gain, *refs):
    weights = refs[0:2]
    grad_first_out, keep, give = refs[2:5]
    estimates, small = refs[5:9], refs[9]
    owner = [core[1] ^ (b // 2) for b in range(8)]
    part = slope.shape[2]
    blocks = range(8)
    grad_normed = grad_second[...]
    grad_ffn = grad_normed.astype(bf16)
    for b in blocks:
        rows = dot(grad_ffn, weights[b % 2][owner[b], part : 2 * part, :], NT)
        rows = (rows * slope[b]).astype(bf16)
        (keep, give)[b % 2][b // 2] = rows
        grad_normed = grad_normed + dot(rows, weights[b % 2][owner[b], 0:part, :], NN)
    unit, inv = norm(first[...])
    small[0:1, :] = column_sum(grad_normed * unit)
    small[1:2, :] = column_sum(grad_normed)
    small[2:8, :] = jnp.zeros_like(small[2:8, :])
    grad_first = norm_back(grad_normed * gain[0:1, :], unit, inv)
    grad_first_out[...] = grad_first
    grad_attn = grad_first.astype(bf16)
    share_rows(keep, give, 4, grad_attn)
    for b in blocks:
        half = estimates[0].shape[0] // 2
        at = core[0] if b % 2 == 0 else 1 - core[0]
        estimates[b // 2][pl.ds(pl.multiple_of(at * half, 16), half), :] = dot(
            weights[b % 2][owner[b], 2 * part :, :], grad_attn, NT
        ).astype(bf16)


def weight_grad_kernel(core, small_a, small_b, *refs):
    near, far, near_back, far_back = refs[0:4]
    attn, attn_far, out = refs[4:8], refs[8], refs[9]
    part = near.shape[2]
    sums = jnp.concatenate([small_a[...], small_b[...]], axis=0).astype(bf16)

    def wide(ref, at):
        return jnp.concatenate([ref[at], ref[at + 1]], axis=1)

    def rows(ref, other, at):
        return jnp.concatenate([wide(ref, at), wide(other, at)], axis=0)

    normed, grad_ffn = rows(near, far, 4), rows(near, far, 6)
    grad_attn = rows(near_back, far_back, 4)
    for j in range(4):
        owner = core[1] ^ j
        hidden = jnp.concatenate([near[j], far[j]], axis=0)
        grad_pre = jnp.concatenate([near_back[j], far_back[j]], axis=0)
        out[owner, 0:part, :] = dot(grad_pre, normed, TN).astype(bf16)
        out[owner, part : 2 * part, :] = dot(hidden, grad_ffn, TN).astype(bf16)
        heads = jnp.concatenate([core_rows(core, attn[j], 0), attn_far[j]], axis=1)
        at = 2 * part + heads.shape[0]
        out[owner, 2 * part : at, :] = dot(heads, grad_attn, NN).astype(bf16)
        out[owner, at : at + 16, :] = sums
        out[owner, at + 16 :, :] = jnp.zeros_like(sums)


def input_grad_kernel(core, grad_first, *refs):
    blocks, near, far, out = refs[0:4], refs[4], refs[5], refs[6]
    half = near.shape[2]
    total = grad_first[...]
    for which, halves in enumerate((near, far)):
        at = core[0] if which == 0 else 1 - core[0]
        at = pl.ds(pl.multiple_of(at * half, 16), half)
        for j in range(4):
            rows = jnp.concatenate([blocks[j][c, at, :] for c in range(3)], axis=0)
            weights = jnp.concatenate([halves[core[1] ^ j, c] for c in range(3)], axis=0)
            total = total + dot(rows, weights, TN)
    out[...] = total.astype(out.dtype)


def vmem(count):
    return [pl.BlockSpec(memory_space=pltpu.VMEM)] * count


def single(kernel, core, args, out_shape, micros, name, scratch=()):
    return pl.pallas_call(
        kernel,
        in_specs=[pl.BlockSpec(memory_space=pltpu.SMEM)] + vmem(len(args)),
        out_specs=vmem(len(out_shape)),
        out_shape=out_shape,
        scratch_shapes=scratch,
        compiler_params=pltpu.CompilerParams(vmem_limit_bytes=56 << 20),
        cost_estimate=pl.CostEstimate(
            flops=int(micros * 1.1e9), bytes_accessed=1 << 20, transcendentals=0
        ),
        name=name,
    )(core, *args)


def dense(core, x_in, grad_out, gain, bias, attn, weights):
    rows, width = x_in.shape
    part = (weights[0].shape[1] - attn[0].shape[0] // 2) // 2
    out_shape = [
        shape((rows, width), bf16),
        shape((rows, width), f32),
        shape((rows, width), f32),
        shape((8, rows, part), f32),
        shape((8, rows, part), bf16),
        shape((8, rows, part), bf16),
        shape((4, attn[0].shape[0] // 2, rows), bf16),
        shape((8, width), f32),
    ]
    args = [x_in, grad_out, gain, bias, *attn, *weights]
    return single(dense_kernel, core, args, out_shape, 14, "dense")


def dense_back(core, first, grad_second, slope, gain, attn, weights):
    rows, width = first.shape
    part = (weights[0].shape[1] - attn[0].shape[0] // 2) // 2
    out_shape = [
        shape((rows, width), f32),
        shape((6, rows, part), bf16),
        shape((6, rows, part), bf16),
        *[shape(attn[0].shape, bf16)] * 4,
        shape((8, width), f32),
    ]
    args = [first, grad_second, slope, gain, *weights]
    return single(dense_back_kernel, core, args, out_shape, 8, "dense_back")


def weight_grads(core, small_a, small_b, shared, attn, attn_far):
    part, width = shared[0].shape[2], small_a.shape[1]
    out_shape = [shape((4, 2 * part + attn[0].shape[0] // 2 + 32, width), bf16)]
    args = [small_a, small_b, *shared, *attn, attn_far]
    return single(weight_grad_kernel, core, args, out_shape, 7, "weight_grads")[0]


def weight_results_kernel(core, near, far, up, down, out):
    part, rows = up.shape[1] // 2, out.shape[0] // 2
    for which, ref in enumerate((near, far)):
        at = core[0] if which == 0 else 1 - core[0]
        at_part = pl.ds(pl.multiple_of(at * part, 128), part)
        up[:, at_part] = ref[0:part, :].astype(f32).T
        down[at_part, :] = ref[part : 2 * part, :].astype(f32)
        at_rows = pl.ds(pl.multiple_of(at * rows, 16), rows)
        out[at_rows, :] = ref[2 * part : 2 * part + rows, :].astype(f32)


def weight_results(core, near, far, head_width):
    width = near.shape[1]
    part = (near.shape[0] - 32 - head_width // 2) // 2
    out_shape = [
        shape((width, 2 * part), f32), shape((2 * part, width), f32), shape((head_width, width), f32)
    ]
    return single(weight_results_kernel, core, [near, far], out_shape, 3, "weight_results")


def input_grad(core, grad_first, blocks, near, far):
    out_shape = [shape(grad_first.shape, bf16)]
    args = [grad_first, *blocks, near, far]
    return single(input_grad_kernel, core, args, out_shape, 40, "input_grad")[0]


def after(x, *others):
    return lax.optimization_barrier((x, *others))[0]


def add(a, *others):
    return sum([b.astype(f32) for b in others], a.astype(f32))


def shards(
    inputs,
    w_qkv,
    w_out,
    up_weight,
    down_weight,
    norm_gain,
    norm_bias,
    planes,
    mask_pos,
    cot_rows,
):
    own = inputs[0]
    piece, seqs, width = own.shape
    hash_count, head_count = lax.axis_size("hash"), lax.axis_size("head")
    groups, places = seqs, hash_count // seqs
    assert places == 2 and lax.axis_size("seq") == 2 and head_count == 4
    assert planes.shape[0] * hash_count == 4 * SETS
    quarter = piece // head_count
    rows = groups * quarter
    half_len = piece * hash_count
    head_width = w_out.shape[0]
    hidden_own = down_weight.shape[0]
    n_tokens = head_count * rows
    hash_id, d, s = lax.axis_index("hash"), lax.axis_index("head"), lax.axis_index("seq")
    g, r = hash_id // places, hash_id % places

    def in_halves(index, mine, other):
        first = jnp.where(index == 0, mine, other)
        second = jnp.where(index == 0, other, mine)
        return jnp.concatenate([first, second], axis=0)

    def split(x, index):
        half = x.shape[0] // 2
        return [lax.dynamic_slice_in_dim(x, at * half, half, 0) for at in (index, 1 - index)]

    def over_seq(x):
        return lax.ppermute(x, "seq", [(0, 1), (1, 0)])

    def over_place(x):
        return lax.ppermute(x, "hash", [(h, h ^ 1) for h in range(hash_count)])

    def over_group(x, k):
        moves = [(h, ((h // places + k) % groups) * places + h % places) for h in range(hash_count)]
        return lax.ppermute(x, "hash", moves)

    def over_head(x, j):
        return lax.ppermute(x, "head", [(h, h ^ j) for h in range(head_count)])

    def seq_rows(block, index):
        return lax.dynamic_index_in_dim(block, index % seqs, 1, keepdims=False)

    here = [
        seq_rows(lax.dynamic_slice_in_dim(own, (d ^ j) * quarter, quarter, 0), g)
        for j in range(head_count)
    ]
    near_tokens = jnp.concatenate(here)
    my_quarter = lax.dynamic_slice_in_dim(own, d * quarter, quarter, 0)
    sent = [seq_rows(my_quarter, g + k) for k in range(1, groups)]
    arrived = [over_group(x, k + 1) for k, x in enumerate(sent)]

    signed = (2 * planes - 1).astype(bf16)
    if planes.shape[0] == SETS and groups == 2:
        moves = [
            ((2 * rr + ss) * 2 + gg, (gg * places + rr) * 2 + ss)
            for gg in range(2)
            for rr in range(2)
            for ss in range(2)
        ]
        signed = lax.ppermute(signed, ("hash", "seq"), moves)
    else:
        signed = lax.all_gather(signed, "hash", axis=0, tiled=True)
        signed = lax.dynamic_slice_in_dim(signed, (r * 2 + s) * SETS, SETS, 0)
    signed = signed.transpose(1, 0, 2).reshape(BITS * SETS, HEAD_DIM)
    signed_t = jnp.concatenate([signed.T, signed.T], axis=1)
    bits = bit_rows()

    cut, out_cut = hidden_own // 2, head_width // 2
    weights = jnp.concatenate(
        [
            lax.dynamic_slice_in_dim(after(up_weight, *sent), s * cut, cut, 1).T,
            lax.dynamic_slice_in_dim(down_weight, s * cut, cut, 0),
            lax.dynamic_slice_in_dim(w_out, s * out_cut, out_cut, 0),
        ]
    )
    weights = lax.all_gather(weights, "head", axis=0)
    w_qkv_t = lax.dynamic_slice_in_dim(w_qkv.transpose(0, 2, 1), s * out_cut, out_cut, 1)

    head_n = head_width // HEAD_DIM

    def project(w, rows_in):
        out = jnp.einsum("cde,ld->cel", w, rows_in, preferred_element_type=f32)
        return out.astype(bf16).reshape(-1, rows_in.shape[0])

    near_tokens = after(near_tokens, *arrived)
    near = project(w_qkv, near_tokens)
    near_z, near_o = over_place(near), over_seq(near)
    far_quarter = jnp.stack(arrived)
    moved = [over_head(far_quarter, j) for j in range(1, head_count)]
    tables = key_tables(signed, head_n, [near, near_o], None, f32)
    moved = [after(x, tables) for x in moved]

    near_z = after(near_z, tables)
    near_zo = over_seq(near_z)

    mask_pos = after(mask_pos, tables)
    slot = jnp.arange(groups, dtype=jnp.int32)[:, None]
    place_of = ((g - slot) % groups) * places + r
    position = s * half_len + place_of * piece + d * quarter + jnp.arange(quarter, dtype=jnp.int32)[None]
    mask_row = lax.dynamic_index_in_dim(mask_pos, g, 0, keepdims=False)
    cot = lax.dynamic_index_in_dim(cot_rows, g, 0, keepdims=False)
    pick = (position.reshape(rows)[:, None] == mask_row[None]).astype(bf16)
    grad_out = jnp.dot(pick, cot, preferred_element_type=f32)
    ready = after(signed, grad_out)
    tables = key_tables(ready, head_n, [near_z, near_zo], tables, f32)

    far_tokens = jnp.stack([far_quarter, *moved]).reshape(-1, width)
    kv = project(w_qkv[1:], far_tokens)
    q = project(after(w_qkv[:1], kv), far_tokens)
    tokens = jnp.concatenate([near_tokens, far_tokens])
    dense_in = jnp.concatenate([here[0], *arrived])
    kv_z, kv_o = over_place(kv), over_seq(kv)
    q_o, q_z = over_seq(q), over_place(q)
    n_near = near.shape[1]

    tables = key_tables(after(signed, q), head_n, [kv, kv_o], tables, f32)

    kv_z = after(kv_z, tables)
    kv_zo = over_seq(kv_z)
    ready = after(signed, tokens, dense_in)
    tables = key_tables(ready, head_n, [kv_z], tables, f32)

    q_z = after(q_z, tables)
    q_zo = over_seq(q_z)
    kv_zo = after(kv_zo, tables)
    tables = key_tables(after(signed, q_z), head_n, [kv_zo], tables, bf16)

    q_zo = after(q_zo, tables)
    e_zo = query_estimates(signed, head_n, near_zo, q_zo, tables, bf16)
    e_zo_moved = over_seq(e_zo)
    e_z = query_estimates(signed, head_n, near_z, after(q_z, e_zo), tables, bf16)
    e_far = add(e_z, after(e_zo_moved, e_z)).astype(bf16)
    ready = after(q_o, e_far)
    e_o = query_estimates(signed, head_n, near_o, ready, tables, bf16)
    e_far = over_place(e_far)
    e_o_moved = over_seq(e_o)
    e = query_estimates(signed, head_n, near, after(q, e_o), tables, f32)
    e_far = after(e_far, e)
    weights = after(weights, e_o)
    weights = [weights, over_seq(weights)]
    w_qkv_t = lax.all_gather(after(w_qkv_t, weights[0]), "head", axis=0)
    attn = add(e, after(e_o_moved, e), e_far).astype(bf16)

    def to_dense(block):
        parts = []
        for j in range(head_count):
            a, b = j * quarter, n_near + j * (rows - quarter)
            cut = [block[..., a : a + quarter], block[..., b : b + rows - quarter]]
            parts.append(jnp.concatenate(cut, axis=-1))
        moved = [over_head(parts[j], j) for j in range(1, head_count)]
        return [parts[0], *lax.optimization_barrier(moved)]

    attn_parts = to_dense(attn)

    def away(dense_rows):
        dense_rows = dense_rows.reshape(groups, quarter, width)
        return [dense_rows[0]] + [over_group(dense_rows[k], groups - k) for k in range(1, groups)]

    core = jnp.stack([s, d]).astype(jnp.int32)
    layer_rows, first, grad_second, slope, keep, give, heads_give, small_a = dense(
        core, dense_in, grad_out, norm_gain, norm_bias, attn_parts, weights
    )
    taken, heads_far = over_seq(give), over_seq(heads_give)
    grad_first, keep_back, give_back, *est_parts, small_b = dense_back(
        core, first, grad_second, slope, norm_gain, attn_parts, weights
    )
    taken_back = over_seq(give_back)
    est_moved = [over_head(est_parts[j], j) for j in range(1, head_count)]
    est_parts = [est_parts[0], *lax.optimization_barrier(est_moved)]
    grad = jnp.concatenate(
        [x[:, :quarter] for x in est_parts] + [x[:, quarter:] for x in est_parts], axis=1
    )
    layer_moved = away(layer_rows)
    weight_parts = weight_grads(
        core, after(small_a, grad, w_qkv_t), small_b, [keep, taken, keep_back, taken_back], attn_parts, heads_far
    )

    weight_sum = lax.psum_scatter(weight_parts, "head", scatter_dimension=0, tiled=True)[0]
    grad_z = over_place(grad)
    grad_o = after(over_seq(grad), weight_parts)
    layer_moved = jnp.stack([after(x, weight_parts) for x in layer_moved])
    part, dq, dq_o = query_backward(
        signed, signed_t, bits, head_n, tables, [(near, after(q, layer_moved)), (near_o, q_o)], [grad, grad_o],
        None, False, [f32, bf16],
    )

    grad_z = after(grad_z, part)
    grad_zo = over_seq(grad_z)
    dq_o = over_seq(dq_o)
    part, dq_z = query_backward(
        signed, signed_t, bits, head_n, tables, [(near_z, q_z)], [grad_z], part, False, [f32]
    )

    dq_own = add(dq, after(dq_o, dq_z))
    grad_zo = after(grad_zo, dq_z)
    grad_tables, dq_zo = query_backward(
        signed, signed_t, bits, head_n, tables, [(near_zo, after(q_zo, dq_own))], [grad_zo], part, True, [bf16]
    )

    dq_zo = over_seq(dq_zo)
    w_qkv_t = after(w_qkv_t, grad_tables)
    w_qkv_far = over_seq(w_qkv_t)
    dkv_zo = key_backward(signed, signed_t, bits, head_n, near_zo, kv_zo, grad_tables, bf16)

    dkv_zo_moved = over_seq(dkv_zo)
    dq_far = add(dq_z, after(dq_zo, dkv_zo)).astype(bf16)
    layer_moved = [layer_moved] + [over_head(layer_moved, j) for j in range(1, head_count)]
    dkv_z = key_backward(signed, signed_t, bits, head_n, near_z, after(kv_z, dq_far), grad_tables, bf16)
    dq_far = over_place(dq_far)

    dkv_far = add(dkv_z, after(dkv_zo_moved, dkv_z)).astype(bf16)
    grad_q = add(dq_own, after(dq_far, dkv_z)).astype(bf16)
    weight_sum = after(weight_sum, dkv_z)
    layer_moved = [after(x, dkv_z) for x in layer_moved]
    dkv_o = key_backward(
        signed, signed_t, bits, head_n, near_o, after(kv_o, dkv_far, grad_q, weight_sum, *layer_moved),
        grad_tables, bf16, 25,
    )
    low = weight_sum.shape[0] // 4
    low_keep, low_send = split(weight_sum[:low], r)
    low_far = over_place(low_send)
    high_sum = lax.psum(weight_sum[low:], "hash")
    dkv_far = over_place(dkv_far)
    dkv_o_moved = over_seq(dkv_o)
    dkv = key_backward(
        signed, signed_t, bits, head_n, near, kv, grad_tables, f32, 25
    )

    dkv_o_moved = after(dkv_o_moved, dkv)
    grad_kv = add(dkv, dkv_o_moved, after(dkv_far, dkv)).astype(bf16)
    grad_qkv = jnp.concatenate([grad_q[None], grad_kv])
    qkv_parts = to_dense(grad_qkv)
    low_keep = add(low_keep, after(low_far, qkv_parts[1]))
    low_send = low_keep.astype(bf16)
    low_far = [over_group(low_send, k) for k in range(1, groups)]

    grad_in = input_grad(core, grad_first, qkv_parts, w_qkv_t, after(w_qkv_far, dkv))

    w_grad = dot(grad_qkv.reshape(3 * head_width, n_tokens), tokens, NN).astype(bf16)
    w_keep, w_send = split(w_grad, s)
    w_keep, w_send = split(add(w_keep, over_seq(w_send)).astype(bf16), r)
    grad_moved = away(grad_in)
    w_keep = add(w_keep, over_place(w_send))
    w_send = w_keep.astype(bf16)
    grad_moved = after(jnp.stack(grad_moved), w_send)
    w_keep = add(w_keep, *[over_group(w_send, k) for k in range(1, groups)]).astype(bf16)
    low_keep = add(low_keep, *[after(x, grad_moved) for x in low_far]).astype(bf16)
    low_far = over_place(low_keep)
    grad_moved = [grad_moved] + [over_head(grad_moved, j) for j in range(1, head_count)]

    def home(blocks):
        table = jnp.stack(blocks)
        columns = []
        for q_at in range(head_count):
            block = lax.dynamic_index_in_dim(table, q_at ^ d, 0, keepdims=False)
            columns.append(
                jnp.stack(
                    [
                        lax.dynamic_index_in_dim(block, (at - g) % groups, 0, keepdims=False)
                        for at in range(seqs)
                    ],
                    axis=1,
                )
            )
        return jnp.concatenate(columns, axis=0)

    layer_out = home([after(x, grad_moved[0]) for x in layer_moved])
    grad_inputs = home(grad_moved).astype(f32)

    w_grad = in_halves(r, w_keep, over_place(w_keep))
    w_grad = in_halves(s, w_grad, over_seq(w_grad)).reshape(3, head_width, width)
    grad_w_qkv = w_grad.transpose(0, 2, 1).astype(f32)
    low_keep = in_halves(r, low_keep, low_far)
    weight_sum = jnp.concatenate([low_keep, after(high_sum, *grad_moved)])
    weight_far = over_seq(weight_sum)
    grad_w_up, grad_w_down, grad_w_out = weight_results(core, weight_sum, weight_far, head_width)
    at = slice(2 * cut + out_cut, 2 * cut + out_cut + 16)
    small = add(weight_sum[at], weight_far[at])

    count = piece * seqs * width * hash_count * 2
    stream_rms = jnp.sqrt(jnp.sum(small[0:3], axis=1) / count)
    share = width // head_count
    norm_grads = lax.dynamic_slice_in_dim(small, d * share, share, 1)
    return (
        layer_out[None],
        grad_inputs[None],
        grad_w_qkv,
        grad_w_out,
        grad_w_up,
        grad_w_down,
        jnp.stack([norm_grads[8], norm_grads[3]]),
        jnp.stack([norm_grads[9], norm_grads[4]]),
        stream_rms,
    )


def solution(mesh):
    placed = (
        P("seq", "hash", None, None),
        P(None, None, "head"),
        P("head", None),
        P(None, "head"),
        P("head", None),
        P(),
        P(),
        P("hash", None, None),
        P(),
        P(),
    )
    return jax.shard_map(
        shards,
        mesh=mesh,
        in_specs=placed,
        out_specs=(
            P("seq", "hash", None, None),
            P("seq", "hash", None, None),
            P(None, None, "head"),
            P("head", None),
            P(None, "head"),
            P("head", None),
            P(None, "head"),
            P(None, "head"),
            P(),
        ),
        check_vma=False,
    )
```

```python
from functools import partial

import jax
import jax.numpy as jnp
import numpy as np
from jax import lax
from jax.experimental import pallas as pl
from jax.experimental.pallas import tpu as pltpu
from jax.sharding import PartitionSpec as P

HEAD_DIM = 64
HASHES = 32
BITS = 8
SETS = 8
BUCKETS = 1 << BITS
ROWS = BUCKETS * SETS

bf16 = jnp.bfloat16
f32 = jnp.float32
NN = (((1,), (0,)), ((), ()))
NT = (((1,), (1,)), ((), ()))
TN = (((0,), (0,)), ((), ()))


shape = jax.ShapeDtypeStruct


def dot(a, b, dims):
    return lax.dot_general(a, b, dims, preferred_element_type=f32)


def sides(rows, planes):
    x = rows.astype(f32)
    inv = lax.rsqrt(jnp.sum(x * x, axis=0, keepdims=True) + 1e-6)
    proj = dot(planes, rows, NN) * (3.0 * inv)
    small = jnp.exp(-proj)
    upper = 1.0 / (1.0 + small)
    return inv, upper, small * upper


def products(upper, lower, first, count):
    out = None
    for i in range(first, first + count):
        lo, up = lower[SETS * i : SETS * (i + 1)], upper[SETS * i : SETS * (i + 1)]
        out = [lo, up] if out is None else [c * lo for c in out] + [c * up for c in out]
    return out


def half_codes(upper, lower):
    low = jnp.concatenate(products(upper, lower, 0, 4), axis=0).astype(bf16)
    high = [jnp.concatenate([a, a], axis=0).astype(bf16) for a in products(upper, lower, 4, 4)]
    return low, high


def code_chunk(low, high, first, count):
    return jnp.concatenate(
        [high[a] * low[16 * j : 16 * (j + 1)] for a in range(first, first + count) for j in range(8)],
        axis=0,
    )


def pull_back(rows, planes_t, inv, upper, sums):
    total = sums[BITS * SETS :][:SETS]
    grad_proj = sums[: BITS * SETS] - upper * jnp.concatenate([total] * BITS, axis=0)
    head = grad_proj.astype(bf16)
    tail = (grad_proj - head.astype(f32)).astype(bf16)
    grad_unit = dot(planes_t, jnp.concatenate([head, tail], axis=0), NN) * (3.0 * inv)
    x = rows.astype(f32)
    return grad_unit - x * (inv * inv * jnp.sum(x * grad_unit, axis=0, keepdims=True))


def both(*refs):
    return jnp.concatenate([ref[...] for ref in refs], axis=1)


def key_kernel(planes, *refs, chunk, blocks):
    keys, vals, out = refs[:blocks], refs[blocks : 2 * blocks], refs[-1]
    start = refs[2 * blocks] if len(refs) > 2 * blocks + 1 else None
    _, upper, lower = sides(both(*keys), planes[...])
    low, high = half_codes(upper, lower)
    values = both(*vals)
    for c in range(0, 16, chunk):
        at = slice(128 * c, 128 * (c + chunk))
        part = dot(code_chunk(low, high, c, chunk), values, NT)
        if start is not None:
            part = part + start[0, at, :]
        out[0, at, :] = part.astype(out.dtype)


def query_kernel(planes, tables, *refs, chunk):
    rows, out = both(*refs[:-1]), refs[-1]
    _, upper, lower = sides(rows, planes[...])
    low, high = half_codes(upper, lower)
    acc = jnp.zeros((HEAD_DIM, rows.shape[1]), f32)
    for c in range(0, 16, chunk):
        acc += dot(tables[0, 128 * c : 128 * (c + chunk), :], code_chunk(low, high, c, chunk), TN)
    out[...] = (acc * (1.0 / HASHES)).astype(out.dtype)


def query_back_kernel(planes, planes_t, bits, tables, *refs, chunk, blocks, last):
    queries, grads = refs[: 2 * blocks], refs[2 * blocks : 3 * blocks]
    start = refs[3 * blocks] if len(refs) > 4 * blocks + 1 else None
    out, back_out = refs[-1 - blocks], refs[-blocks:]
    rows = both(*queries)
    inv, upper, lower = sides(rows, planes[...])
    low, high = half_codes(upper, lower)
    grad = both(*grads)
    sums = jnp.zeros((bits.shape[0], rows.shape[1]), f32)
    for c in range(0, 16, chunk):
        at = slice(128 * c, 128 * (c + chunk))
        codes = code_chunk(low, high, c, chunk)
        part = dot(codes, grad, NT)
        if start is not None:
            part = part + start[0, at, :]
        if last:
            part = part * (1.0 / HASHES)
        out[0, at, :] = part.astype(out.dtype)
        weighted = dot(tables[0, at, :], grad, NN).astype(bf16) * codes
        sums += dot(bits[:, at], weighted, NN)
    back = pull_back(rows, planes_t[...], inv, upper, sums * (1.0 / HASHES))
    width = back_out[0].shape[1]
    for i in range(blocks):
        back_out[i][...] = back[:, i * width : (i + 1) * width].astype(back_out[i].dtype)


def key_back_kernel(planes, planes_t, bits, ka, kb, va, vb, grad_tables, out, *, chunk):
    rows = both(ka, kb)
    inv, upper, lower = sides(rows, planes[...])
    low, high = half_codes(upper, lower)
    values = both(va, vb)
    width = rows.shape[1]
    sums = jnp.zeros((bits.shape[0], width), f32)
    grad_values = jnp.zeros((HEAD_DIM, width), f32)
    for c in range(0, 16, chunk):
        at = slice(128 * c, 128 * (c + chunk))
        codes = code_chunk(low, high, c, chunk)
        grad_values += dot(grad_tables[0, at, :], codes, TN)
        weighted = dot(grad_tables[0, at, :], values, NN).astype(bf16) * codes
        sums += dot(bits[:, at], weighted, NN)
    out[0] = pull_back(rows, planes_t[...], inv, upper, sums).astype(out.dtype)
    out[1] = grad_values.astype(out.dtype)


def bit_rows():
    out = np.zeros((80, BUCKETS, SETS), np.float32)
    for t in range(SETS):
        for i in range(BITS):
            out[i * SETS + t, :, t] = (np.arange(BUCKETS) >> i) & 1
        out[BITS * SETS + t, :, t] = 1
    return jnp.asarray(out.reshape(80, ROWS), bf16)


def whole(*shape):
    return pl.BlockSpec(shape, lambda h: (0,) * len(shape))


def head_rows(array, heads, which):
    width = array.shape[1]
    offset = (which - 3) * heads + array.shape[0] // HEAD_DIM
    return pl.BlockSpec((HEAD_DIM, width), lambda h: (h + offset, 0))


def per_head(width):
    return pl.BlockSpec((HEAD_DIM, width), lambda h: (h, 0))


def table_spec():
    return pl.BlockSpec((1, ROWS, HEAD_DIM), lambda h: (h, 0, 0))


def call(kernel, heads, micros, name, in_specs, out_specs, out_shape):
    return pl.pallas_call(
        kernel,
        grid=(heads,),
        in_specs=in_specs,
        out_specs=out_specs,
        out_shape=out_shape,
        compiler_params=pltpu.CompilerParams(vmem_limit_bytes=48 << 20),
        cost_estimate=pl.CostEstimate(
            flops=int(micros * 1.1e9), bytes_accessed=1 << 20, transcendentals=0
        ),
        name=name,
    )


def key_tables(planes, heads, blocks, start, kind):
    args = [planes, *blocks, *blocks]
    specs = [whole(64, 64)] + [head_rows(x, heads, w) for w in (1, 2) for x in blocks]
    if start is not None:
        specs.append(table_spec())
        args.append(start)
    return call(
        partial(key_kernel, chunk=2, blocks=len(blocks)),
        heads,
        30 if len(blocks) > 1 and start is not None else 1,
        "key_tables",
        specs,
        table_spec(),
        shape((heads, ROWS, HEAD_DIM), kind),
    )(*args)


def query_estimates(planes, heads, near, far, tables, kind):
    width = near.shape[1] + far.shape[1]
    return call(
        partial(query_kernel, chunk=2),
        heads,
        1,
        "query_estimates",
        [whole(64, 64), table_spec(), head_rows(near, heads, 0), per_head(far.shape[1])],
        per_head(width),
        shape((heads * HEAD_DIM, width), kind),
    )(planes, tables, near, far)


def query_backward(planes, planes_t, bits, heads, tables, queries, grads, start, last, kinds):
    width = grads[0].shape[1]
    blocks = len(grads)
    specs = [whole(64, 64), whole(64, 128), whole(80, ROWS), table_spec()]
    args = [planes, planes_t, bits, tables]
    for near, far in queries:
        specs += [head_rows(near, heads, 0), per_head(far.shape[1])]
        args += [near, far]
    specs += [per_head(width)] * blocks
    args += grads
    if start is not None:
        specs.append(table_spec())
        args.append(start)
    return call(
        partial(query_back_kernel, chunk=4, blocks=blocks, last=last),
        heads,
        25 * blocks,
        "query_backward",
        specs,
        [table_spec()] + [per_head(width)] * blocks,
        [shape((heads, ROWS, HEAD_DIM), bf16 if last else f32)]
        + [shape(grads[0].shape, kind) for kind in kinds],
    )(*args)


def key_backward(planes, planes_t, bits, heads, near, far, grad_tables, kind, micros=25):
    width = near.shape[1] + far.shape[1]
    return call(
        partial(key_back_kernel, chunk=4),
        heads,
        micros,
        "key_backward",
        [whole(64, 64), whole(64, 128), whole(80, ROWS)]
        + [head_rows(x, heads, w) for w in (1, 2) for x in (near, far)]
        + [table_spec()],
        pl.BlockSpec((2, HEAD_DIM, width), lambda h: (0, h, 0)),
        shape((2, heads * HEAD_DIM, width), kind),
    )(planes, planes_t, bits, near, far, near, far, grad_tables)


def norm(x):
    center = x - jnp.mean(x, axis=-1, keepdims=True)
    inv = lax.rsqrt(jnp.mean(center * center, axis=-1, keepdims=True) + 1e-5)
    return center * inv, inv


def norm_back(grad, unit, inv):
    return inv * (
        grad
        - jnp.mean(grad, axis=-1, keepdims=True)
        - unit * jnp.mean(grad * unit, axis=-1, keepdims=True)
    )


def column_sum(x):
    return jnp.sum(x, axis=0, keepdims=True)


def core_rows(core, ref, which):
    half = ref.shape[0] // 2
    at = core[0] if which == 0 else 1 - core[0]
    return ref[pl.ds(pl.multiple_of(at * half, 16), half), :]


def share_rows(keep, give, at, rows):
    part = keep.shape[2]
    for out in (keep, give):
        out[at] = rows[:, :part]
        out[at + 1] = rows[:, part:]


def dense_kernel(core, x_in, grad_out, gain, bias, *refs):
    attn, weights = refs[0:4], refs[4:6]
    layer_out, first_out, grad_second_out, slope, keep, give, heads_give, small = refs[6:14]
    owner = [core[1] ^ (b // 2) for b in range(8)]
    for j in range(4):
        heads_give[j] = core_rows(core, attn[j], 1)
    part = slope.shape[2]
    blocks = range(8)
    heads = jnp.concatenate([core_rows(core, attn[b // 2], b % 2) for b in blocks], axis=0)
    out_w = jnp.concatenate([weights[b % 2][owner[b], 2 * part :, :] for b in blocks], axis=0)
    attn_out = dot(heads, out_w, TN)
    resid = x_in[...].astype(f32)
    first = resid + attn_out
    first_out[...] = first
    small[0:1, :] = column_sum(resid * resid)
    small[1:2, :] = column_sum(attn_out * attn_out)
    small[2:3, :] = column_sum(first * first)
    unit_1, _ = norm(first)
    normed = (unit_1 * gain[0:1, :] + bias[0:1, :]).astype(bf16)
    share_rows(keep, give, 4, normed)
    second = normed.astype(f32)
    for b in blocks:
        pre = dot(normed, weights[b % 2][owner[b], 0:part, :], NT)
        below = 0.5 * (1.0 + lax.erf(pre * 0.7071067811865476))
        rows = (pre * below).astype(bf16)
        (keep, give)[b % 2][b // 2] = rows
        slope[b] = below + pre * (0.3989422804014327 * jnp.exp(-0.5 * pre * pre))
        second = second + dot(rows, weights[b % 2][owner[b], part : 2 * part, :], NN)
    unit_2, inv_2 = norm(second)
    layer_out[...] = (unit_2 * gain[1:2, :] + bias[1:2, :]).astype(layer_out.dtype)
    grad = grad_out[...]
    small[3:4, :] = column_sum(grad * unit_2)
    small[4:5, :] = column_sum(grad)
    small[5:8, :] = jnp.zeros_like(small[5:8, :])
    grad_second = norm_back(grad * gain[1:2, :], unit_2, inv_2)
    grad_second_out[...] = grad_second
    share_rows(keep, give, 6, grad_second.astype(bf16))


def dense_back_kernel(core, first, grad_second, slope, gain, *refs):
    weights = refs[0:2]
    grad_first_out, keep, give = refs[2:5]
    estimates, small = refs[5:9], refs[9]
    owner = [core[1] ^ (b // 2) for b in range(8)]
    part = slope.shape[2]
    blocks = range(8)
    grad_normed = grad_second[...]
    grad_ffn = grad_normed.astype(bf16)
    for b in blocks:
        rows = dot(grad_ffn, weights[b % 2][owner[b], part : 2 * part, :], NT)
        rows = (rows * slope[b]).astype(bf16)
        (keep, give)[b % 2][b // 2] = rows
        grad_normed = grad_normed + dot(rows, weights[b % 2][owner[b], 0:part, :], NN)
    unit, inv = norm(first[...])
    small[0:1, :] = column_sum(grad_normed * unit)
    small[1:2, :] = column_sum(grad_normed)
    small[2:8, :] = jnp.zeros_like(small[2:8, :])
    grad_first = norm_back(grad_normed * gain[0:1, :], unit, inv)
    grad_first_out[...] = grad_first
    grad_attn = grad_first.astype(bf16)
    share_rows(keep, give, 4, grad_attn)
    for b in blocks:
        half = estimates[0].shape[0] // 2
        at = core[0] if b % 2 == 0 else 1 - core[0]
        estimates[b // 2][pl.ds(pl.multiple_of(at * half, 16), half), :] = dot(
            weights[b % 2][owner[b], 2 * part :, :], grad_attn, NT
        ).astype(bf16)


def weight_grad_kernel(core, small_a, small_b, *refs):
    near, far, near_back, far_back = refs[0:4]
    attn, attn_far, out = refs[4:8], refs[8], refs[9]
    part = near.shape[2]
    sums = jnp.concatenate([small_a[...], small_b[...]], axis=0).astype(bf16)

    def wide(ref, at):
        return jnp.concatenate([ref[at], ref[at + 1]], axis=1)

    def rows(ref, other, at):
        return jnp.concatenate([wide(ref, at), wide(other, at)], axis=0)

    normed, grad_ffn = rows(near, far, 4), rows(near, far, 6)
    grad_attn = rows(near_back, far_back, 4)
    for j in range(4):
        owner = core[1] ^ j
        hidden = jnp.concatenate([near[j], far[j]], axis=0)
        grad_pre = jnp.concatenate([near_back[j], far_back[j]], axis=0)
        out[owner, 0:part, :] = dot(grad_pre, normed, TN).astype(bf16)
        out[owner, part : 2 * part, :] = dot(hidden, grad_ffn, TN).astype(bf16)
        heads = jnp.concatenate([core_rows(core, attn[j], 0), attn_far[j]], axis=1)
        at = 2 * part + heads.shape[0]
        out[owner, 2 * part : at, :] = dot(heads, grad_attn, NN).astype(bf16)
        out[owner, at : at + 16, :] = sums
        out[owner, at + 16 :, :] = jnp.zeros_like(sums)


def input_grad_kernel(core, grad_first, *refs):
    blocks, near, far, out = refs[0:4], refs[4], refs[5], refs[6]
    half = near.shape[2]
    total = grad_first[...]
    for which, halves in enumerate((near, far)):
        at = core[0] if which == 0 else 1 - core[0]
        at = pl.ds(pl.multiple_of(at * half, 16), half)
        for j in range(4):
            rows = jnp.concatenate([blocks[j][c, at, :] for c in range(3)], axis=0)
            weights = jnp.concatenate([halves[core[1] ^ j, c] for c in range(3)], axis=0)
            total = total + dot(rows, weights, TN)
    out[...] = total.astype(out.dtype)


def vmem(count):
    return [pl.BlockSpec(memory_space=pltpu.VMEM)] * count


def single(kernel, core, args, out_shape, micros, name, scratch=()):
    return pl.pallas_call(
        kernel,
        in_specs=[pl.BlockSpec(memory_space=pltpu.SMEM)] + vmem(len(args)),
        out_specs=vmem(len(out_shape)),
        out_shape=out_shape,
        scratch_shapes=scratch,
        compiler_params=pltpu.CompilerParams(vmem_limit_bytes=56 << 20),
        cost_estimate=pl.CostEstimate(
            flops=int(micros * 1.1e9), bytes_accessed=1 << 20, transcendentals=0
        ),
        name=name,
    )(core, *args)


def dense(core, x_in, grad_out, gain, bias, attn, weights):
    rows, width = x_in.shape
    part = (weights[0].shape[1] - attn[0].shape[0] // 2) // 2
    out_shape = [
        shape((rows, width), bf16),
        shape((rows, width), f32),
        shape((rows, width), f32),
        shape((8, rows, part), f32),
        shape((8, rows, part), bf16),
        shape((8, rows, part), bf16),
        shape((4, attn[0].shape[0] // 2, rows), bf16),
        shape((8, width), f32),
    ]
    args = [x_in, grad_out, gain, bias, *attn, *weights]
    return single(dense_kernel, core, args, out_shape, 14, "dense")


def dense_back(core, first, grad_second, slope, gain, attn, weights):
    rows, width = first.shape
    part = (weights[0].shape[1] - attn[0].shape[0] // 2) // 2
    out_shape = [
        shape((rows, width), f32),
        shape((6, rows, part), bf16),
        shape((6, rows, part), bf16),
        *[shape(attn[0].shape, bf16)] * 4,
        shape((8, width), f32),
    ]
    args = [first, grad_second, slope, gain, *weights]
    return single(dense_back_kernel, core, args, out_shape, 8, "dense_back")


def weight_grads(core, small_a, small_b, shared, attn, attn_far):
    part, width = shared[0].shape[2], small_a.shape[1]
    out_shape = [shape((4, 2 * part + attn[0].shape[0] // 2 + 32, width), bf16)]
    args = [small_a, small_b, *shared, *attn, attn_far]
    return single(weight_grad_kernel, core, args, out_shape, 7, "weight_grads")[0]


def weight_results_kernel(core, near, far, up, down, out):
    part, rows = up.shape[1] // 2, out.shape[0] // 2
    for which, ref in enumerate((near, far)):
        at = core[0] if which == 0 else 1 - core[0]
        at_part = pl.ds(pl.multiple_of(at * part, 128), part)
        up[:, at_part] = ref[0:part, :].astype(f32).T
        down[at_part, :] = ref[part : 2 * part, :].astype(f32)
        at_rows = pl.ds(pl.multiple_of(at * rows, 16), rows)
        out[at_rows, :] = ref[2 * part : 2 * part + rows, :].astype(f32)


def weight_results(core, near, far, head_width):
    width = near.shape[1]
    part = (near.shape[0] - 32 - head_width // 2) // 2
    out_shape = [
        shape((width, 2 * part), f32), shape((2 * part, width), f32), shape((head_width, width), f32)
    ]
    return single(weight_results_kernel, core, [near, far], out_shape, 3, "weight_results")


def input_grad(core, grad_first, blocks, near, far):
    out_shape = [shape(grad_first.shape, bf16)]
    args = [grad_first, *blocks, near, far]
    return single(input_grad_kernel, core, args, out_shape, 40, "input_grad")[0]


def after(x, *others):
    return lax.optimization_barrier((x, *others))[0]


def add(a, *others):
    return sum([b.astype(f32) for b in others], a.astype(f32))


def shards(
    inputs,
    w_qkv,
    w_out,
    up_weight,
    down_weight,
    norm_gain,
    norm_bias,
    planes,
    mask_pos,
    cot_rows,
):
    own = inputs[0]
    piece, seqs, width = own.shape
    hash_count, head_count = lax.axis_size("hash"), lax.axis_size("head")
    groups, places = seqs, hash_count // seqs
    assert places == 2 and lax.axis_size("seq") == 2 and head_count == 4
    assert planes.shape[0] * hash_count == 4 * SETS
    quarter = piece // head_count
    rows = groups * quarter
    half_len = piece * hash_count
    head_width = w_out.shape[0]
    hidden_own = down_weight.shape[0]
    n_tokens = head_count * rows
    hash_id, d, s = lax.axis_index("hash"), lax.axis_index("head"), lax.axis_index("seq")
    g, r = hash_id // places, hash_id % places

    def over_seq(x):
        return lax.ppermute(x, "seq", [(0, 1), (1, 0)])

    def over_place(x):
        return lax.ppermute(x, "hash", [(h, h ^ 1) for h in range(hash_count)])

    def over_group(x, k):
        moves = [(h, ((h // places + k) % groups) * places + h % places) for h in range(hash_count)]
        return lax.ppermute(x, "hash", moves)

    def over_head(x, j):
        return lax.ppermute(x, "head", [(h, h ^ j) for h in range(head_count)])

    def seq_rows(block, index):
        return lax.dynamic_index_in_dim(block, index % seqs, 1, keepdims=False)

    here = [
        seq_rows(lax.dynamic_slice_in_dim(own, (d ^ j) * quarter, quarter, 0), g)
        for j in range(head_count)
    ]
    near_tokens = jnp.concatenate(here)
    my_quarter = lax.dynamic_slice_in_dim(own, d * quarter, quarter, 0)
    sent = [seq_rows(my_quarter, g + k) for k in range(1, groups)]
    arrived = [over_group(x, k + 1) for k, x in enumerate(sent)]

    signed = (2 * planes - 1).astype(bf16)
    if planes.shape[0] == SETS and groups == 2:
        moves = [
            ((2 * rr + ss) * 2 + gg, (gg * places + rr) * 2 + ss)
            for gg in range(2)
            for rr in range(2)
            for ss in range(2)
        ]
        signed = lax.ppermute(signed, ("hash", "seq"), moves)
    else:
        signed = lax.all_gather(signed, "hash", axis=0, tiled=True)
        signed = lax.dynamic_slice_in_dim(signed, (r * 2 + s) * SETS, SETS, 0)
    signed = signed.transpose(1, 0, 2).reshape(BITS * SETS, HEAD_DIM)
    signed_t = jnp.concatenate([signed.T, signed.T], axis=1)
    bits = bit_rows()

    cut, out_cut = hidden_own // 2, head_width // 2
    weights = jnp.concatenate(
        [
            lax.dynamic_slice_in_dim(after(up_weight, *sent), s * cut, cut, 1).T,
            lax.dynamic_slice_in_dim(down_weight, s * cut, cut, 0),
            lax.dynamic_slice_in_dim(w_out, s * out_cut, out_cut, 0),
        ]
    )
    weights = lax.all_gather(weights, "head", axis=0)
    w_qkv_t = lax.dynamic_slice_in_dim(w_qkv.transpose(0, 2, 1), s * out_cut, out_cut, 1)

    head_n = head_width // HEAD_DIM

    def project(w, rows_in):
        out = jnp.einsum("cde,ld->cel", w, rows_in, preferred_element_type=f32)
        return out.astype(bf16).reshape(-1, rows_in.shape[0])

    near_tokens = after(near_tokens, *arrived)
    near = project(w_qkv, near_tokens)
    near_z, near_o = over_place(near), over_seq(near)
    far_quarter = jnp.stack(arrived)
    moved = [over_head(far_quarter, j) for j in range(1, head_count)]
    tables = key_tables(signed, head_n, [near, near_o], None, f32)
    moved = [after(x, tables) for x in moved]

    near_z = after(near_z, tables)
    near_zo = over_seq(near_z)

    mask_pos = after(mask_pos, tables)
    slot = jnp.arange(groups, dtype=jnp.int32)[:, None]
    place_of = ((g - slot) % groups) * places + r
    position = s * half_len + place_of * piece + d * quarter + jnp.arange(quarter, dtype=jnp.int32)[None]
    mask_row = lax.dynamic_index_in_dim(mask_pos, g, 0, keepdims=False)
    cot = lax.dynamic_index_in_dim(cot_rows, g, 0, keepdims=False)
    pick = (position.reshape(rows)[:, None] == mask_row[None]).astype(bf16)
    grad_out = jnp.dot(pick, cot, preferred_element_type=f32)
    ready = after(signed, grad_out)
    tables = key_tables(ready, head_n, [near_z, near_zo], tables, f32)

    far_tokens = jnp.stack([far_quarter, *moved]).reshape(-1, width)
    kv = project(w_qkv[1:], far_tokens)
    q = project(after(w_qkv[:1], kv), far_tokens)
    tokens = jnp.concatenate([near_tokens, far_tokens])
    dense_in = jnp.concatenate([here[0], *arrived])
    kv_z, kv_o = over_place(kv), over_seq(kv)
    q_o, q_z = over_seq(q), over_place(q)
    n_near = near.shape[1]

    tables = key_tables(after(signed, q), head_n, [kv, kv_o], tables, f32)

    kv_z = after(kv_z, tables)
    kv_zo = over_seq(kv_z)
    ready = after(signed, tokens, dense_in)
    tables = key_tables(ready, head_n, [kv_z], tables, f32)

    q_z = after(q_z, tables)
    q_zo = over_seq(q_z)
    kv_zo = after(kv_zo, tables)
    tables = key_tables(after(signed, q_z), head_n, [kv_zo], tables, bf16)

    q_zo = after(q_zo, tables)
    e_zo = query_estimates(signed, head_n, near_zo, q_zo, tables, bf16)
    e_zo_moved = over_seq(e_zo)
    e_z = query_estimates(signed, head_n, near_z, after(q_z, e_zo), tables, bf16)
    e_far = add(e_z, after(e_zo_moved, e_z)).astype(bf16)
    ready = after(q_o, e_far)
    e_o = query_estimates(signed, head_n, near_o, ready, tables, bf16)
    e_far = over_place(e_far)
    e_o_moved = over_seq(e_o)
    e = query_estimates(signed, head_n, near, after(q, e_o), tables, f32)
    e_far = after(e_far, e)
    weights = after(weights, e_o)
    weights = [weights, over_seq(weights)]
    w_qkv_t = lax.all_gather(after(w_qkv_t, weights[0]), "head", axis=0)
    attn = add(e, after(e_o_moved, e), e_far).astype(bf16)

    def to_dense(block):
        parts = []
        for j in range(head_count):
            a, b = j * quarter, n_near + j * (rows - quarter)
            cut = [block[..., a : a + quarter], block[..., b : b + rows - quarter]]
            parts.append(jnp.concatenate(cut, axis=-1))
        moved = [over_head(parts[j], j) for j in range(1, head_count)]
        return [parts[0], *lax.optimization_barrier(moved)]

    attn_parts = to_dense(attn)

    def away(dense_rows):
        dense_rows = dense_rows.reshape(groups, quarter, width)
        return [dense_rows[0]] + [over_group(dense_rows[k], groups - k) for k in range(1, groups)]

    core = jnp.stack([s, d]).astype(jnp.int32)
    layer_rows, first, grad_second, slope, keep, give, heads_give, small_a = dense(
        core, dense_in, grad_out, norm_gain, norm_bias, attn_parts, weights
    )
    taken, heads_far = over_seq(give), over_seq(heads_give)
    grad_first, keep_back, give_back, *est_parts, small_b = dense_back(
        core, first, grad_second, slope, norm_gain, attn_parts, weights
    )
    taken_back = over_seq(give_back)
    est_moved = [over_head(est_parts[j], j) for j in range(1, head_count)]
    est_parts = [est_parts[0], *lax.optimization_barrier(est_moved)]
    grad = jnp.concatenate(
        [x[:, :quarter] for x in est_parts] + [x[:, quarter:] for x in est_parts], axis=1
    )
    layer_moved = away(layer_rows)
    weight_parts = weight_grads(
        core, after(small_a, grad, w_qkv_t), small_b, [keep, taken, keep_back, taken_back], attn_parts, heads_far
    )

    weight_sum = lax.psum_scatter(weight_parts, "head", scatter_dimension=0, tiled=True)[0]
    grad_z = over_place(grad)
    grad_o = after(over_seq(grad), weight_parts)
    layer_moved = jnp.stack([after(x, weight_parts) for x in layer_moved])
    part, dq, dq_o = query_backward(
        signed, signed_t, bits, head_n, tables, [(near, after(q, layer_moved)), (near_o, q_o)], [grad, grad_o],
        None, False, [f32, bf16],
    )

    grad_z = after(grad_z, part)
    grad_zo = over_seq(grad_z)
    dq_o = over_seq(dq_o)
    part, dq_z = query_backward(
        signed, signed_t, bits, head_n, tables, [(near_z, q_z)], [grad_z], part, False, [f32]
    )

    dq_own = add(dq, after(dq_o, dq_z))
    grad_zo = after(grad_zo, dq_z)
    grad_tables, dq_zo = query_backward(
        signed, signed_t, bits, head_n, tables, [(near_zo, after(q_zo, dq_own))], [grad_zo], part, True, [bf16]
    )

    dq_zo = over_seq(dq_zo)
    w_qkv_t = after(w_qkv_t, grad_tables)
    w_qkv_far = over_seq(w_qkv_t)
    dkv_zo = key_backward(signed, signed_t, bits, head_n, near_zo, kv_zo, grad_tables, bf16)

    dkv_zo_moved = over_seq(dkv_zo)
    dq_far = add(dq_z, after(dq_zo, dkv_zo)).astype(bf16)
    layer_moved = [layer_moved] + [over_head(layer_moved, j) for j in range(1, head_count)]
    dkv_z = key_backward(signed, signed_t, bits, head_n, near_z, after(kv_z, dq_far), grad_tables, bf16)
    dq_far = over_place(dq_far)

    dkv_far = add(dkv_z, after(dkv_zo_moved, dkv_z)).astype(bf16)
    grad_q = add(dq_own, after(dq_far, dkv_z)).astype(bf16)
    weight_sum = after(weight_sum, dkv_z)
    layer_moved = [after(x, dkv_z) for x in layer_moved]
    dkv_o = key_backward(
        signed, signed_t, bits, head_n, near_o, after(kv_o, dkv_far, grad_q, weight_sum, *layer_moved),
        grad_tables, bf16, 25,
    )
    weight_sum = lax.psum_scatter(weight_sum, "hash", scatter_dimension=0, tiled=True)
    dkv_far = over_place(dkv_far)
    dkv_o_moved = over_seq(dkv_o)
    dkv = key_backward(
        signed, signed_t, bits, head_n, near, kv, grad_tables, f32, 25
    )

    dkv_o_moved = after(dkv_o_moved, dkv)
    grad_kv = add(dkv, dkv_o_moved, after(dkv_far, dkv)).astype(bf16)
    grad_qkv = jnp.concatenate([grad_q[None], grad_kv])
    qkv_parts = to_dense(grad_qkv)

    grad_in = input_grad(core, after(grad_first, weight_sum), qkv_parts, w_qkv_t, after(w_qkv_far, dkv))

    def in_halves(index, mine, other):
        first = jnp.where(index == 0, mine, other)
        second = jnp.where(index == 0, other, mine)
        return jnp.concatenate([first, second], axis=0)

    def split(x, index):
        half = x.shape[0] // 2
        return [lax.dynamic_slice_in_dim(x, at * half, half, 0) for at in (index, 1 - index)]

    w_grad = dot(grad_qkv.reshape(3 * head_width, n_tokens), tokens, NN).astype(bf16)
    w_keep, w_send = split(w_grad, s)
    w_keep, w_send = split(add(w_keep, over_seq(w_send)).astype(bf16), r)
    grad_moved = away(grad_in)
    w_keep = add(w_keep, over_place(w_send))
    w_send = w_keep.astype(bf16)
    grad_moved = after(jnp.stack(grad_moved), w_send)
    w_keep = add(w_keep, *[over_group(w_send, k) for k in range(1, groups)]).astype(bf16)
    grad_moved = [grad_moved] + [over_head(grad_moved, j) for j in range(1, head_count)]

    def home(blocks):
        table = jnp.stack(blocks)
        columns = []
        for q_at in range(head_count):
            block = lax.dynamic_index_in_dim(table, q_at ^ d, 0, keepdims=False)
            columns.append(
                jnp.stack(
                    [
                        lax.dynamic_index_in_dim(block, (at - g) % groups, 0, keepdims=False)
                        for at in range(seqs)
                    ],
                    axis=1,
                )
            )
        return jnp.concatenate(columns, axis=0)

    layer_out = home([after(x, grad_moved[0]) for x in layer_moved])
    grad_inputs = home(grad_moved).astype(f32)

    w_grad = in_halves(r, w_keep, over_place(w_keep))
    w_grad = in_halves(s, w_grad, over_seq(w_grad)).reshape(3, head_width, width)
    grad_w_qkv = w_grad.transpose(0, 2, 1).astype(f32)
    weight_sum = after(weight_sum, grad_in)
    weight_sum = lax.all_gather(weight_sum, "hash", axis=0, tiled=True)
    weight_sum = after(weight_sum, *grad_moved)
    weight_far = over_seq(weight_sum)
    grad_w_up, grad_w_down, grad_w_out = weight_results(core, weight_sum, weight_far, head_width)
    at = slice(2 * cut + out_cut, 2 * cut + out_cut + 16)
    small = add(weight_sum[at], weight_far[at])

    count = piece * seqs * width * hash_count * 2
    stream_rms = jnp.sqrt(jnp.sum(small[0:3], axis=1) / count)
    share = width // head_count
    norm_grads = lax.dynamic_slice_in_dim(small, d * share, share, 1)
    return (
        layer_out[None],
        grad_inputs[None],
        grad_w_qkv,
        grad_w_out,
        grad_w_up,
        grad_w_down,
        jnp.stack([norm_grads[8], norm_grads[3]]),
        jnp.stack([norm_grads[9], norm_grads[4]]),
        stream_rms,
    )


def solution(mesh):
    placed = (
        P("seq", "hash", None, None),
        P(None, None, "head"),
        P("head", None),
        P(None, "head"),
        P("head", None),
        P(),
        P(),
        P("hash", None, None),
        P(),
        P(),
    )
    return jax.shard_map(
        shards,
        mesh=mesh,
        in_specs=placed,
        out_specs=(
            P("seq", "hash", None, None),
            P("seq", "hash", None, None),
            P(None, None, "head"),
            P("head", None),
            P(None, "head"),
            P("head", None),
            P(None, "head"),
            P(None, "head"),
            P(),
        ),
        check_vma=False,
    )
```

```python
from functools import partial

import jax
import jax.numpy as jnp
import numpy as np
from jax import lax
from jax.experimental import pallas as pl
from jax.experimental.pallas import tpu as pltpu
from jax.sharding import PartitionSpec as P

HEAD_DIM = 64
HASHES = 32
BITS = 8
SETS = 8
BUCKETS = 1 << BITS
ROWS = BUCKETS * SETS

bf16 = jnp.bfloat16
f32 = jnp.float32
NN = (((1,), (0,)), ((), ()))
NT = (((1,), (1,)), ((), ()))
TN = (((0,), (0,)), ((), ()))


shape = jax.ShapeDtypeStruct


def dot(a, b, dims):
    return lax.dot_general(a, b, dims, preferred_element_type=f32)


def sides(rows, planes):
    x = rows.astype(f32)
    inv = lax.rsqrt(jnp.sum(x * x, axis=0, keepdims=True) + 1e-6)
    proj = dot(planes, rows, NN) * (3.0 * inv)
    small = jnp.exp(-proj)
    upper = 1.0 / (1.0 + small)
    return inv, upper, small * upper


def products(upper, lower, first, count):
    out = None
    for i in range(first, first + count):
        lo, up = lower[SETS * i : SETS * (i + 1)], upper[SETS * i : SETS * (i + 1)]
        out = [lo, up] if out is None else [c * lo for c in out] + [c * up for c in out]
    return out


def half_codes(upper, lower):
    low = jnp.concatenate(products(upper, lower, 0, 4), axis=0).astype(bf16)
    high = [jnp.concatenate([a, a], axis=0).astype(bf16) for a in products(upper, lower, 4, 4)]
    return low, high


def code_chunk(low, high, first, count):
    return jnp.concatenate(
        [high[a] * low[16 * j : 16 * (j + 1)] for a in range(first, first + count) for j in range(8)],
        axis=0,
    )


def pull_back(rows, planes_t, inv, upper, sums):
    total = sums[BITS * SETS :][:SETS]
    grad_proj = sums[: BITS * SETS] - upper * jnp.concatenate([total] * BITS, axis=0)
    head = grad_proj.astype(bf16)
    tail = (grad_proj - head.astype(f32)).astype(bf16)
    grad_unit = dot(planes_t, jnp.concatenate([head, tail], axis=0), NN) * (3.0 * inv)
    x = rows.astype(f32)
    return grad_unit - x * (inv * inv * jnp.sum(x * grad_unit, axis=0, keepdims=True))


def both(*refs):
    return jnp.concatenate([ref[...] for ref in refs], axis=1)


def key_kernel(planes, *refs, chunk, blocks):
    keys, vals, out = refs[:blocks], refs[blocks : 2 * blocks], refs[-1]
    start = refs[2 * blocks] if len(refs) > 2 * blocks + 1 else None
    _, upper, lower = sides(both(*keys), planes[...])
    low, high = half_codes(upper, lower)
    values = both(*vals)
    for c in range(0, 16, chunk):
        at = slice(128 * c, 128 * (c + chunk))
        part = dot(code_chunk(low, high, c, chunk), values, NT)
        if start is not None:
            part = part + start[0, at, :]
        out[0, at, :] = part.astype(out.dtype)


def query_kernel(planes, tables, *refs, chunk):
    rows, out = both(*refs[:-1]), refs[-1]
    _, upper, lower = sides(rows, planes[...])
    low, high = half_codes(upper, lower)
    acc = jnp.zeros((HEAD_DIM, rows.shape[1]), f32)
    for c in range(0, 16, chunk):
        acc += dot(tables[0, 128 * c : 128 * (c + chunk), :], code_chunk(low, high, c, chunk), TN)
    out[...] = (acc * (1.0 / HASHES)).astype(out.dtype)


def query_back_kernel(planes, planes_t, bits, tables, *refs, chunk, blocks, last):
    queries, grads = refs[: 2 * blocks], refs[2 * blocks : 3 * blocks]
    start = refs[3 * blocks] if len(refs) > 4 * blocks + 1 else None
    out, back_out = refs[-1 - blocks], refs[-blocks:]
    rows = both(*queries)
    inv, upper, lower = sides(rows, planes[...])
    low, high = half_codes(upper, lower)
    grad = both(*grads)
    sums = jnp.zeros((bits.shape[0], rows.shape[1]), f32)
    for c in range(0, 16, chunk):
        at = slice(128 * c, 128 * (c + chunk))
        codes = code_chunk(low, high, c, chunk)
        part = dot(codes, grad, NT)
        if start is not None:
            part = part + start[0, at, :]
        if last:
            part = part * (1.0 / HASHES)
        out[0, at, :] = part.astype(out.dtype)
        weighted = dot(tables[0, at, :], grad, NN).astype(bf16) * codes
        sums += dot(bits[:, at], weighted, NN)
    back = pull_back(rows, planes_t[...], inv, upper, sums * (1.0 / HASHES))
    width = back_out[0].shape[1]
    for i in range(blocks):
        back_out[i][...] = back[:, i * width : (i + 1) * width].astype(back_out[i].dtype)


def key_back_kernel(planes, planes_t, bits, ka, kb, va, vb, grad_tables, out, *, chunk):
    rows = both(ka, kb)
    inv, upper, lower = sides(rows, planes[...])
    low, high = half_codes(upper, lower)
    values = both(va, vb)
    width = rows.shape[1]
    sums = jnp.zeros((bits.shape[0], width), f32)
    grad_values = jnp.zeros((HEAD_DIM, width), f32)
    for c in range(0, 16, chunk):
        at = slice(128 * c, 128 * (c + chunk))
        codes = code_chunk(low, high, c, chunk)
        grad_values += dot(grad_tables[0, at, :], codes, TN)
        weighted = dot(grad_tables[0, at, :], values, NN).astype(bf16) * codes
        sums += dot(bits[:, at], weighted, NN)
    out[0] = pull_back(rows, planes_t[...], inv, upper, sums).astype(out.dtype)
    out[1] = grad_values.astype(out.dtype)


def bit_rows():
    out = np.zeros((80, BUCKETS, SETS), np.float32)
    for t in range(SETS):
        for i in range(BITS):
            out[i * SETS + t, :, t] = (np.arange(BUCKETS) >> i) & 1
        out[BITS * SETS + t, :, t] = 1
    return jnp.asarray(out.reshape(80, ROWS), bf16)


def whole(*shape):
    return pl.BlockSpec(shape, lambda h: (0,) * len(shape))


def head_rows(array, heads, which):
    width = array.shape[1]
    offset = (which - 3) * heads + array.shape[0] // HEAD_DIM
    return pl.BlockSpec((HEAD_DIM, width), lambda h: (h + offset, 0))


def per_head(width):
    return pl.BlockSpec((HEAD_DIM, width), lambda h: (h, 0))


def table_spec():
    return pl.BlockSpec((1, ROWS, HEAD_DIM), lambda h: (h, 0, 0))


def call(kernel, heads, micros, name, in_specs, out_specs, out_shape):
    return pl.pallas_call(
        kernel,
        grid=(heads,),
        in_specs=in_specs,
        out_specs=out_specs,
        out_shape=out_shape,
        compiler_params=pltpu.CompilerParams(vmem_limit_bytes=48 << 20),
        cost_estimate=pl.CostEstimate(
            flops=int(micros * 1.1e9), bytes_accessed=1 << 20, transcendentals=0
        ),
        name=name,
    )


def key_tables(planes, heads, blocks, start, kind):
    args = [planes, *blocks, *blocks]
    specs = [whole(64, 64)] + [head_rows(x, heads, w) for w in (1, 2) for x in blocks]
    if start is not None:
        specs.append(table_spec())
        args.append(start)
    return call(
        partial(key_kernel, chunk=2, blocks=len(blocks)),
        heads,
        30 if len(blocks) > 1 and start is not None else 1,
        "key_tables",
        specs,
        table_spec(),
        shape((heads, ROWS, HEAD_DIM), kind),
    )(*args)


def query_estimates(planes, heads, near, far, tables, kind):
    width = near.shape[1] + far.shape[1]
    return call(
        partial(query_kernel, chunk=2),
        heads,
        1,
        "query_estimates",
        [whole(64, 64), table_spec(), head_rows(near, heads, 0), per_head(far.shape[1])],
        per_head(width),
        shape((heads * HEAD_DIM, width), kind),
    )(planes, tables, near, far)


def query_backward(planes, planes_t, bits, heads, tables, queries, grads, start, last, kinds):
    width = grads[0].shape[1]
    blocks = len(grads)
    specs = [whole(64, 64), whole(64, 128), whole(80, ROWS), table_spec()]
    args = [planes, planes_t, bits, tables]
    for near, far in queries:
        specs += [head_rows(near, heads, 0), per_head(far.shape[1])]
        args += [near, far]
    specs += [per_head(width)] * blocks
    args += grads
    if start is not None:
        specs.append(table_spec())
        args.append(start)
    return call(
        partial(query_back_kernel, chunk=4, blocks=blocks, last=last),
        heads,
        25 * blocks,
        "query_backward",
        specs,
        [table_spec()] + [per_head(width)] * blocks,
        [shape((heads, ROWS, HEAD_DIM), bf16 if last else f32)]
        + [shape(grads[0].shape, kind) for kind in kinds],
    )(*args)


def key_backward(planes, planes_t, bits, heads, near, far, grad_tables, kind, micros=25):
    width = near.shape[1] + far.shape[1]
    return call(
        partial(key_back_kernel, chunk=4),
        heads,
        micros,
        "key_backward",
        [whole(64, 64), whole(64, 128), whole(80, ROWS)]
        + [head_rows(x, heads, w) for w in (1, 2) for x in (near, far)]
        + [table_spec()],
        pl.BlockSpec((2, HEAD_DIM, width), lambda h: (0, h, 0)),
        shape((2, heads * HEAD_DIM, width), kind),
    )(planes, planes_t, bits, near, far, near, far, grad_tables)


def norm(x):
    center = x - jnp.mean(x, axis=-1, keepdims=True)
    inv = lax.rsqrt(jnp.mean(center * center, axis=-1, keepdims=True) + 1e-5)
    return center * inv, inv


def norm_back(grad, unit, inv):
    return inv * (
        grad
        - jnp.mean(grad, axis=-1, keepdims=True)
        - unit * jnp.mean(grad * unit, axis=-1, keepdims=True)
    )


def column_sum(x):
    return jnp.sum(x, axis=0, keepdims=True)


def core_rows(core, ref, which):
    half = ref.shape[0] // 2
    at = core[0] if which == 0 else 1 - core[0]
    return ref[pl.ds(pl.multiple_of(at * half, 16), half), :]


def share_rows(keep, give, at, rows):
    part = keep.shape[2]
    for out in (keep, give):
        out[at] = rows[:, :part]
        out[at + 1] = rows[:, part:]


def dense_kernel(core, x_in, grad_out, gain, bias, *refs):
    attn, weights = refs[0:4], refs[4:6]
    layer_out, first_out, grad_second_out, slope, keep, give, heads_give, small = refs[6:14]
    owner = [core[1] ^ (b // 2) for b in range(8)]
    for j in range(4):
        heads_give[j] = core_rows(core, attn[j], 1)
    part = slope.shape[2]
    blocks = range(8)
    heads = jnp.concatenate([core_rows(core, attn[b // 2], b % 2) for b in blocks], axis=0)
    out_w = jnp.concatenate([weights[b % 2][owner[b], 2 * part :, :] for b in blocks], axis=0)
    attn_out = dot(heads, out_w, TN)
    resid = x_in[...].astype(f32)
    first = resid + attn_out
    first_out[...] = first
    small[0:1, :] = column_sum(resid * resid)
    small[1:2, :] = column_sum(attn_out * attn_out)
    small[2:3, :] = column_sum(first * first)
    unit_1, _ = norm(first)
    normed = (unit_1 * gain[0:1, :] + bias[0:1, :]).astype(bf16)
    share_rows(keep, give, 4, normed)
    second = normed.astype(f32)
    for b in blocks:
        pre = dot(normed, weights[b % 2][owner[b], 0:part, :], NT)
        below = 0.5 * (1.0 + lax.erf(pre * 0.7071067811865476))
        rows = (pre * below).astype(bf16)
        (keep, give)[b % 2][b // 2] = rows
        slope[b] = below + pre * (0.3989422804014327 * jnp.exp(-0.5 * pre * pre))
        second = second + dot(rows, weights[b % 2][owner[b], part : 2 * part, :], NN)
    unit_2, inv_2 = norm(second)
    layer_out[...] = (unit_2 * gain[1:2, :] + bias[1:2, :]).astype(layer_out.dtype)
    grad = grad_out[...]
    small[3:4, :] = column_sum(grad * unit_2)
    small[4:5, :] = column_sum(grad)
    small[5:8, :] = jnp.zeros_like(small[5:8, :])
    grad_second = norm_back(grad * gain[1:2, :], unit_2, inv_2)
    grad_second_out[...] = grad_second
    share_rows(keep, give, 6, grad_second.astype(bf16))


def dense_back_kernel(core, first, grad_second, slope, gain, *refs):
    weights = refs[0:2]
    grad_first_out, keep, give = refs[2:5]
    estimates, small = refs[5:9], refs[9]
    owner = [core[1] ^ (b // 2) for b in range(8)]
    part = slope.shape[2]
    blocks = range(8)
    grad_normed = grad_second[...]
    grad_ffn = grad_normed.astype(bf16)
    for b in blocks:
        rows = dot(grad_ffn, weights[b % 2][owner[b], part : 2 * part, :], NT)
        rows = (rows * slope[b]).astype(bf16)
        (keep, give)[b % 2][b // 2] = rows
        grad_normed = grad_normed + dot(rows, weights[b % 2][owner[b], 0:part, :], NN)
    unit, inv = norm(first[...])
    small[0:1, :] = column_sum(grad_normed * unit)
    small[1:2, :] = column_sum(grad_normed)
    small[2:8, :] = jnp.zeros_like(small[2:8, :])
    grad_first = norm_back(grad_normed * gain[0:1, :], unit, inv)
    grad_first_out[...] = grad_first
    grad_attn = grad_first.astype(bf16)
    share_rows(keep, give, 4, grad_attn)
    for b in blocks:
        half = estimates[0].shape[0] // 2
        at = core[0] if b % 2 == 0 else 1 - core[0]
        estimates[b // 2][pl.ds(pl.multiple_of(at * half, 16), half), :] = dot(
            weights[b % 2][owner[b], 2 * part :, :], grad_attn, NT
        ).astype(bf16)


def weight_grad_kernel(core, small_a, small_b, *refs):
    near, far, near_back, far_back = refs[0:4]
    attn, attn_far, out = refs[4:8], refs[8], refs[9]
    part = near.shape[2]
    sums = jnp.concatenate([small_a[...], small_b[...]], axis=0).astype(bf16)

    def wide(ref, at):
        return jnp.concatenate([ref[at], ref[at + 1]], axis=1)

    def rows(ref, other, at):
        return jnp.concatenate([wide(ref, at), wide(other, at)], axis=0)

    normed, grad_ffn = rows(near, far, 4), rows(near, far, 6)
    grad_attn = rows(near_back, far_back, 4)
    for j in range(4):
        owner = core[1] ^ j
        hidden = jnp.concatenate([near[j], far[j]], axis=0)
        grad_pre = jnp.concatenate([near_back[j], far_back[j]], axis=0)
        out[owner, 0:part, :] = dot(grad_pre, normed, TN).astype(bf16)
        out[owner, part : 2 * part, :] = dot(hidden, grad_ffn, TN).astype(bf16)
        heads = jnp.concatenate([core_rows(core, attn[j], 0), attn_far[j]], axis=1)
        at = 2 * part + heads.shape[0]
        out[owner, 2 * part : at, :] = dot(heads, grad_attn, NN).astype(bf16)
        out[owner, at : at + 16, :] = sums
        out[owner, at + 16 :, :] = jnp.zeros_like(sums)


def input_grad_kernel(core, grad_first, *refs):
    blocks, near, far, out = refs[0:4], refs[4], refs[5], refs[6]
    half = near.shape[2]
    total = grad_first[...]
    for which, halves in enumerate((near, far)):
        at = core[0] if which == 0 else 1 - core[0]
        at = pl.ds(pl.multiple_of(at * half, 16), half)
        for j in range(4):
            rows = jnp.concatenate([blocks[j][c, at, :] for c in range(3)], axis=0)
            weights = jnp.concatenate([halves[core[1] ^ j, c] for c in range(3)], axis=0)
            total = total + dot(rows, weights, TN)
    out[...] = total.astype(out.dtype)


def cut_points(width, near, owners):
    a, b = near // owners, (width - near) // owners
    return [(j * a, near + j * b) for j in range(owners)], a, b


def join_kernel(*refs, near):
    out = refs[-1]
    points, a, b = cut_points(out.shape[1], near, len(refs) - 1)
    for ref, (p, q) in zip(refs, points):
        out[:, p : p + a] = ref[:, 0:a]
        out[:, q : q + b] = ref[:, a:]


def cut_kernel(a, b, c, *outs, near):
    total = (a[...] + b[...].astype(f32) + c[...].astype(f32)).astype(bf16)
    points, a, b = cut_points(total.shape[1], near, len(outs))
    for out, (p, q) in zip(outs, points):
        out[:, 0:a] = total[:, p : p + a]
        out[:, a:] = total[:, q : q + b]


def cut_back_kernel(grad_q, a, b, c, whole_out, *outs, near):
    total = (a[...] + b[...].astype(f32) + c[...].astype(f32)).astype(bf16)
    points, wa, wb = cut_points(total.shape[2], near, len(outs))
    for i in range(3):
        rows = grad_q[...] if i == 0 else total[i - 1]
        whole_out[i] = rows
        for out, (p, q) in zip(outs, points):
            out[i, :, 0:wa] = rows[:, p : p + wa]
            out[i, :, wa:] = rows[:, q : q + wb]


def vmem(count):
    return [pl.BlockSpec(memory_space=pltpu.VMEM)] * count


def single(kernel, core, args, out_shape, micros, name, scratch=()):
    return pl.pallas_call(
        kernel,
        in_specs=[pl.BlockSpec(memory_space=pltpu.SMEM)] + vmem(len(args)),
        out_specs=vmem(len(out_shape)),
        out_shape=out_shape,
        scratch_shapes=scratch,
        compiler_params=pltpu.CompilerParams(vmem_limit_bytes=56 << 20),
        cost_estimate=pl.CostEstimate(
            flops=int(micros * 1.1e9), bytes_accessed=1 << 20, transcendentals=0
        ),
        name=name,
    )(core, *args)


def small_call(kernel, args, out_shape, name):
    return pl.pallas_call(
        kernel,
        in_specs=vmem(len(args)),
        out_specs=vmem(len(out_shape)),
        out_shape=out_shape,
        cost_estimate=pl.CostEstimate(flops=1 << 20, bytes_accessed=1 << 20, transcendentals=0),
        name=name,
    )(*args)


def dense(core, x_in, grad_out, gain, bias, attn, weights):
    rows, width = x_in.shape
    part = (weights[0].shape[1] - attn[0].shape[0] // 2) // 2
    out_shape = [
        shape((rows, width), bf16),
        shape((rows, width), f32),
        shape((rows, width), f32),
        shape((8, rows, part), f32),
        shape((8, rows, part), bf16),
        shape((8, rows, part), bf16),
        shape((4, attn[0].shape[0] // 2, rows), bf16),
        shape((8, width), f32),
    ]
    args = [x_in, grad_out, gain, bias, *attn, *weights]
    return single(dense_kernel, core, args, out_shape, 14, "dense")


def dense_back(core, first, grad_second, slope, gain, attn, weights):
    rows, width = first.shape
    part = (weights[0].shape[1] - attn[0].shape[0] // 2) // 2
    out_shape = [
        shape((rows, width), f32),
        shape((6, rows, part), bf16),
        shape((6, rows, part), bf16),
        *[shape(attn[0].shape, bf16)] * 4,
        shape((8, width), f32),
    ]
    args = [first, grad_second, slope, gain, *weights]
    return single(dense_back_kernel, core, args, out_shape, 8, "dense_back")


def weight_grads(core, small_a, small_b, shared, attn, attn_far):
    part, width = shared[0].shape[2], small_a.shape[1]
    out_shape = [shape((4, 2 * part + attn[0].shape[0] // 2 + 32, width), bf16)]
    args = [small_a, small_b, *shared, *attn, attn_far]
    return single(weight_grad_kernel, core, args, out_shape, 7, "weight_grads")[0]


def weight_results_kernel(core, near, far, up, down, out):
    part, rows = up.shape[1] // 2, out.shape[0] // 2
    for which, ref in enumerate((near, far)):
        at = core[0] if which == 0 else 1 - core[0]
        at_part = pl.ds(pl.multiple_of(at * part, 128), part)
        up[:, at_part] = ref[0:part, :].astype(f32).T
        down[at_part, :] = ref[part : 2 * part, :].astype(f32)
        at_rows = pl.ds(pl.multiple_of(at * rows, 16), rows)
        out[at_rows, :] = ref[2 * part : 2 * part + rows, :].astype(f32)


def weight_results(core, near, far, head_width):
    width = near.shape[1]
    part = (near.shape[0] - 32 - head_width // 2) // 2
    out_shape = [
        shape((width, 2 * part), f32), shape((2 * part, width), f32), shape((head_width, width), f32)
    ]
    return single(weight_results_kernel, core, [near, far], out_shape, 3, "weight_results")


def input_grad(core, grad_first, blocks, near, far):
    out_shape = [shape(grad_first.shape, bf16)]
    args = [grad_first, *blocks, near, far]
    return single(input_grad_kernel, core, args, out_shape, 40, "input_grad")[0]


def after(x, *others):
    return lax.optimization_barrier((x, *others))[0]


def add(a, *others):
    return sum([b.astype(f32) for b in others], a.astype(f32))


def shards(
    inputs,
    w_qkv,
    w_out,
    up_weight,
    down_weight,
    norm_gain,
    norm_bias,
    planes,
    mask_pos,
    cot_rows,
):
    own = inputs[0]
    piece, seqs, width = own.shape
    hash_count, head_count = lax.axis_size("hash"), lax.axis_size("head")
    groups, places = seqs, hash_count // seqs
    assert places == 2 and lax.axis_size("seq") == 2 and head_count == 4
    assert planes.shape[0] * hash_count == 4 * SETS
    quarter = piece // head_count
    rows = groups * quarter
    half_len = piece * hash_count
    head_width = w_out.shape[0]
    hidden_own = down_weight.shape[0]
    n_tokens = head_count * rows
    hash_id, d, s = lax.axis_index("hash"), lax.axis_index("head"), lax.axis_index("seq")
    g, r = hash_id // places, hash_id % places

    def over_seq(x):
        return lax.ppermute(x, "seq", [(0, 1), (1, 0)])

    def over_place(x):
        return lax.ppermute(x, "hash", [(h, h ^ 1) for h in range(hash_count)])

    def over_group(x, k):
        moves = [(h, ((h // places + k) % groups) * places + h % places) for h in range(hash_count)]
        return lax.ppermute(x, "hash", moves)

    def over_head(x, j):
        return lax.ppermute(x, "head", [(h, h ^ j) for h in range(head_count)])

    def seq_rows(block, index):
        return lax.dynamic_index_in_dim(block, index % seqs, 1, keepdims=False)

    here = [
        seq_rows(lax.dynamic_slice_in_dim(own, (d ^ j) * quarter, quarter, 0), g)
        for j in range(head_count)
    ]
    near_tokens = jnp.concatenate(here)
    my_quarter = lax.dynamic_slice_in_dim(own, d * quarter, quarter, 0)
    sent = [seq_rows(my_quarter, g + k) for k in range(1, groups)]
    arrived = [over_group(x, k + 1) for k, x in enumerate(sent)]

    signed = (2 * planes - 1).astype(bf16)
    if planes.shape[0] == SETS and groups == 2:
        moves = [
            ((2 * rr + ss) * 2 + gg, (gg * places + rr) * 2 + ss)
            for gg in range(2)
            for rr in range(2)
            for ss in range(2)
        ]
        signed = lax.ppermute(signed, ("hash", "seq"), moves)
    else:
        signed = lax.all_gather(signed, "hash", axis=0, tiled=True)
        signed = lax.dynamic_slice_in_dim(signed, (r * 2 + s) * SETS, SETS, 0)
    signed = signed.transpose(1, 0, 2).reshape(BITS * SETS, HEAD_DIM)
    signed_t = jnp.concatenate([signed.T, signed.T], axis=1)
    bits = bit_rows()

    cut, out_cut = hidden_own // 2, head_width // 2
    weights = jnp.concatenate(
        [
            lax.dynamic_slice_in_dim(after(up_weight, *sent), s * cut, cut, 1).T,
            lax.dynamic_slice_in_dim(down_weight, s * cut, cut, 0),
            lax.dynamic_slice_in_dim(w_out, s * out_cut, out_cut, 0),
        ]
    )
    weights = lax.all_gather(weights, "head", axis=0)
    w_qkv_t = lax.dynamic_slice_in_dim(w_qkv.transpose(0, 2, 1), s * out_cut, out_cut, 1)

    head_n = head_width // HEAD_DIM

    def project(w, rows_in):
        out = jnp.einsum("cde,ld->cel", w, rows_in, preferred_element_type=f32)
        return out.astype(bf16).reshape(-1, rows_in.shape[0])

    near_tokens = after(near_tokens, *arrived)
    near = project(w_qkv, near_tokens)
    near_z, near_o = over_place(near), over_seq(near)
    far_quarter = jnp.stack(arrived)
    moved = [over_head(far_quarter, j) for j in range(1, head_count)]
    tables = key_tables(signed, head_n, [near, near_o], None, f32)
    moved = [after(x, tables) for x in moved]

    near_z = after(near_z, tables)
    near_zo = over_seq(near_z)

    mask_pos = after(mask_pos, tables)
    slot = jnp.arange(groups, dtype=jnp.int32)[:, None]
    place_of = ((g - slot) % groups) * places + r
    position = s * half_len + place_of * piece + d * quarter + jnp.arange(quarter, dtype=jnp.int32)[None]
    mask_row = lax.dynamic_index_in_dim(mask_pos, g, 0, keepdims=False)
    cot = lax.dynamic_index_in_dim(cot_rows, g, 0, keepdims=False)
    pick = (position.reshape(rows)[:, None] == mask_row[None]).astype(bf16)
    grad_out = jnp.dot(pick, cot, preferred_element_type=f32)
    ready = after(signed, grad_out)
    tables = key_tables(ready, head_n, [near_z, near_zo], tables, f32)

    far_tokens = jnp.stack([far_quarter, *moved]).reshape(-1, width)
    kv = project(w_qkv[1:], far_tokens)
    q = project(after(w_qkv[:1], kv), far_tokens)
    tokens = jnp.concatenate([near_tokens, far_tokens])
    dense_in = jnp.concatenate([here[0], *arrived])
    kv_z, kv_o = over_place(kv), over_seq(kv)
    q_o, q_z = over_seq(q), over_place(q)
    n_near = near.shape[1]

    tables = key_tables(after(signed, q), head_n, [kv, kv_o], tables, f32)

    kv_z = after(kv_z, tables)
    kv_zo = over_seq(kv_z)
    ready = after(signed, tokens, dense_in)
    tables = key_tables(ready, head_n, [kv_z], tables, f32)

    q_z = after(q_z, tables)
    q_zo = over_seq(q_z)
    kv_zo = after(kv_zo, tables)
    tables = key_tables(after(signed, q_z), head_n, [kv_zo], tables, bf16)

    q_zo = after(q_zo, tables)
    e_zo = query_estimates(signed, head_n, near_zo, q_zo, tables, bf16)
    e_zo_moved = over_seq(e_zo)
    e_z = query_estimates(signed, head_n, near_z, after(q_z, e_zo), tables, bf16)
    e_far = add(e_z, after(e_zo_moved, e_z)).astype(bf16)
    ready = after(q_o, e_far)
    e_o = query_estimates(signed, head_n, near_o, ready, tables, bf16)
    e_far = over_place(e_far)
    e_o_moved = over_seq(e_o)
    e = query_estimates(signed, head_n, near, after(q, e_o), tables, f32)
    e_far = after(e_far, e)
    weights = after(weights, e_o)
    weights = [weights, over_seq(weights)]
    w_qkv_t = lax.all_gather(after(w_qkv_t, weights[0]), "head", axis=0)
    pieces = [shape((head_width, rows), bf16)] * head_count
    parts = small_call(
        partial(cut_kernel, near=n_near), [e, after(e_o_moved, e), e_far], pieces, "cut_estimates"
    )

    def to_owners(parts):
        moved = [over_head(parts[j], j) for j in range(1, head_count)]
        return [parts[0], *lax.optimization_barrier(moved)]

    attn_parts = to_owners(parts)

    def away(dense_rows):
        dense_rows = dense_rows.reshape(groups, quarter, width)
        return [dense_rows[0]] + [over_group(dense_rows[k], groups - k) for k in range(1, groups)]

    core = jnp.stack([s, d]).astype(jnp.int32)
    layer_rows, first, grad_second, slope, keep, give, heads_give, small_a = dense(
        core, dense_in, grad_out, norm_gain, norm_bias, attn_parts, weights
    )
    taken, heads_far = over_seq(give), over_seq(heads_give)
    grad_first, keep_back, give_back, *est_parts, small_b = dense_back(
        core, first, grad_second, slope, norm_gain, attn_parts, weights
    )
    taken_back = over_seq(give_back)
    est_moved = [over_head(est_parts[j], j) for j in range(1, head_count)]
    est_parts = [est_parts[0], *lax.optimization_barrier(est_moved)]
    grad = small_call(
        partial(join_kernel, near=n_near), est_parts, [shape((head_width, n_tokens), bf16)], "join"
    )[0]
    layer_moved = away(layer_rows)
    weight_parts = weight_grads(
        core, after(small_a, grad, w_qkv_t), small_b, [keep, taken, keep_back, taken_back], attn_parts, heads_far
    )

    weight_sum = lax.psum_scatter(weight_parts, "head", scatter_dimension=0, tiled=True)[0]
    grad_z = over_place(grad)
    grad_o = after(over_seq(grad), weight_parts)
    layer_moved = jnp.stack([after(x, weight_parts) for x in layer_moved])
    part, dq, dq_o = query_backward(
        signed, signed_t, bits, head_n, tables, [(near, after(q, layer_moved)), (near_o, q_o)], [grad, grad_o],
        None, False, [f32, bf16],
    )

    grad_z = after(grad_z, part)
    grad_zo = over_seq(grad_z)
    dq_o = over_seq(dq_o)
    part, dq_z = query_backward(
        signed, signed_t, bits, head_n, tables, [(near_z, q_z)], [grad_z], part, False, [f32]
    )

    dq_own = add(dq, after(dq_o, dq_z))
    grad_zo = after(grad_zo, dq_z)
    grad_tables, dq_zo = query_backward(
        signed, signed_t, bits, head_n, tables, [(near_zo, after(q_zo, dq_own))], [grad_zo], part, True, [bf16]
    )

    dq_zo = over_seq(dq_zo)
    w_qkv_t = after(w_qkv_t, grad_tables)
    w_qkv_far = over_seq(w_qkv_t)
    dkv_zo = key_backward(signed, signed_t, bits, head_n, near_zo, kv_zo, grad_tables, bf16)

    dkv_zo_moved = over_seq(dkv_zo)
    dq_far = add(dq_z, after(dq_zo, dkv_zo)).astype(bf16)
    layer_moved = [layer_moved] + [over_head(layer_moved, j) for j in range(1, head_count)]
    dkv_z = key_backward(signed, signed_t, bits, head_n, near_z, after(kv_z, dq_far), grad_tables, bf16)
    dq_far = over_place(dq_far)

    dkv_far = add(dkv_z, after(dkv_zo_moved, dkv_z)).astype(bf16)
    grad_q = add(dq_own, after(dq_far, dkv_z)).astype(bf16)
    weight_sum = after(weight_sum, dkv_z)
    layer_moved = [after(x, dkv_z) for x in layer_moved]
    dkv_o = key_backward(
        signed, signed_t, bits, head_n, near_o, after(kv_o, dkv_far, grad_q, weight_sum, *layer_moved),
        grad_tables, bf16, 25,
    )
    weight_sum = lax.psum(weight_sum, "hash")
    dkv_far = over_place(dkv_far)
    dkv_o_moved = over_seq(dkv_o)
    dkv = key_backward(
        signed, signed_t, bits, head_n, near, kv, grad_tables, f32, 25
    )

    dkv_o_moved = after(dkv_o_moved, dkv)
    out_shape = [shape((3, head_width, n_tokens), bf16)] + [shape((3, head_width, rows), bf16)] * head_count
    grad_qkv, *parts = small_call(
        partial(cut_back_kernel, near=n_near),
        [grad_q, dkv, dkv_o_moved, after(dkv_far, dkv)],
        out_shape,
        "cut_gradients",
    )
    qkv_parts = to_owners(parts)

    grad_in = input_grad(core, grad_first, qkv_parts, w_qkv_t, after(w_qkv_far, dkv))

    def in_halves(index, mine, other):
        first = jnp.where(index == 0, mine, other)
        second = jnp.where(index == 0, other, mine)
        return jnp.concatenate([first, second], axis=0)

    def split(x, index):
        half = x.shape[0] // 2
        return [lax.dynamic_slice_in_dim(x, at * half, half, 0) for at in (index, 1 - index)]

    w_grad = dot(grad_qkv.reshape(3 * head_width, n_tokens), tokens, NN).astype(bf16)
    w_keep, w_send = split(w_grad, s)
    w_keep, w_send = split(add(w_keep, over_seq(w_send)).astype(bf16), r)
    grad_moved = away(grad_in)
    w_keep = add(w_keep, over_place(w_send))
    w_send = w_keep.astype(bf16)
    grad_moved = after(jnp.stack(grad_moved), w_send)
    w_keep = add(w_keep, *[over_group(w_send, k) for k in range(1, groups)]).astype(bf16)
    grad_moved = [grad_moved] + [over_head(grad_moved, j) for j in range(1, head_count)]

    def home(blocks):
        table = jnp.stack(blocks)
        columns = []
        for q_at in range(head_count):
            block = lax.dynamic_index_in_dim(table, q_at ^ d, 0, keepdims=False)
            columns.append(
                jnp.stack(
                    [
                        lax.dynamic_index_in_dim(block, (at - g) % groups, 0, keepdims=False)
                        for at in range(seqs)
                    ],
                    axis=1,
                )
            )
        return jnp.concatenate(columns, axis=0)

    layer_out = home([after(x, grad_moved[0]) for x in layer_moved])
    grad_inputs = home(grad_moved).astype(f32)

    w_grad = in_halves(r, w_keep, over_place(w_keep))
    w_grad = in_halves(s, w_grad, over_seq(w_grad)).reshape(3, head_width, width)
    grad_w_qkv = w_grad.transpose(0, 2, 1).astype(f32)
    weight_sum = after(weight_sum, *grad_moved)
    weight_far = over_seq(weight_sum)
    grad_w_up, grad_w_down, grad_w_out = weight_results(core, weight_sum, weight_far, head_width)
    at = slice(2 * cut + out_cut, 2 * cut + out_cut + 16)
    small = add(weight_sum[at], weight_far[at])

    count = piece * seqs * width * hash_count * 2
    stream_rms = jnp.sqrt(jnp.sum(small[0:3], axis=1) / count)
    share = width // head_count
    norm_grads = lax.dynamic_slice_in_dim(small, d * share, share, 1)
    return (
        layer_out[None],
        grad_inputs[None],
        grad_w_qkv,
        grad_w_out,
        grad_w_up,
        grad_w_down,
        jnp.stack([norm_grads[8], norm_grads[3]]),
        jnp.stack([norm_grads[9], norm_grads[4]]),
        stream_rms,
    )


def solution(mesh):
    placed = (
        P("seq", "hash", None, None),
        P(None, None, "head"),
        P("head", None),
        P(None, "head"),
        P("head", None),
        P(),
        P(),
        P("hash", None, None),
        P(),
        P(),
    )
    return jax.shard_map(
        shards,
        mesh=mesh,
        in_specs=placed,
        out_specs=(
            P("seq", "hash", None, None),
            P("seq", "hash", None, None),
            P(None, None, "head"),
            P("head", None),
            P(None, "head"),
            P("head", None),
            P(None, "head"),
            P(None, "head"),
            P(),
        ),
        check_vma=False,
    )
```

```python
from functools import partial

import jax
import jax.numpy as jnp
import numpy as np
from jax import lax
from jax.experimental import pallas as pl
from jax.experimental.pallas import tpu as pltpu
from jax.sharding import PartitionSpec as P

HEAD_DIM = 64
HASHES = 32
BITS = 8
SETS = 8
BUCKETS = 1 << BITS
ROWS = BUCKETS * SETS

bf16 = jnp.bfloat16
f32 = jnp.float32
NN = (((1,), (0,)), ((), ()))
NT = (((1,), (1,)), ((), ()))
TN = (((0,), (0,)), ((), ()))


shape = jax.ShapeDtypeStruct


def dot(a, b, dims):
    return lax.dot_general(a, b, dims, preferred_element_type=f32)


def sides(rows, planes):
    x = rows.astype(f32)
    inv = lax.rsqrt(jnp.sum(x * x, axis=0, keepdims=True) + 1e-6)
    proj = dot(planes, rows, NN) * (3.0 * inv)
    small = jnp.exp(-proj)
    upper = 1.0 / (1.0 + small)
    return inv, upper, small * upper


def products(upper, lower, first, count):
    out = None
    for i in range(first, first + count):
        lo, up = lower[SETS * i : SETS * (i + 1)], upper[SETS * i : SETS * (i + 1)]
        out = [lo, up] if out is None else [c * lo for c in out] + [c * up for c in out]
    return out


def half_codes(upper, lower):
    low = jnp.concatenate(products(upper, lower, 0, 4), axis=0).astype(bf16)
    high = [jnp.concatenate([a, a], axis=0).astype(bf16) for a in products(upper, lower, 4, 4)]
    return low, high


def code_chunk(low, high, first, count):
    return jnp.concatenate(
        [high[a] * low[16 * j : 16 * (j + 1)] for a in range(first, first + count) for j in range(8)],
        axis=0,
    )


def pull_back(rows, planes_t, inv, upper, sums):
    total = sums[BITS * SETS :][:SETS]
    grad_proj = sums[: BITS * SETS] - upper * jnp.concatenate([total] * BITS, axis=0)
    head = grad_proj.astype(bf16)
    tail = (grad_proj - head.astype(f32)).astype(bf16)
    grad_unit = dot(planes_t, jnp.concatenate([head, tail], axis=0), NN) * (3.0 * inv)
    x = rows.astype(f32)
    return grad_unit - x * (inv * inv * jnp.sum(x * grad_unit, axis=0, keepdims=True))


def both(*refs):
    return jnp.concatenate([ref[...] for ref in refs], axis=1)


def key_kernel(planes, *refs, chunk, blocks):
    keys, vals, out = refs[:blocks], refs[blocks : 2 * blocks], refs[-1]
    start = refs[2 * blocks] if len(refs) > 2 * blocks + 1 else None
    _, upper, lower = sides(both(*keys), planes[...])
    low, high = half_codes(upper, lower)
    values = both(*vals)
    for c in range(0, 16, chunk):
        at = slice(128 * c, 128 * (c + chunk))
        part = dot(code_chunk(low, high, c, chunk), values, NT)
        if start is not None:
            part = part + start[0, at, :]
        out[0, at, :] = part.astype(out.dtype)


def query_kernel(planes, tables, *refs, chunk):
    rows, out = both(*refs[:-1]), refs[-1]
    _, upper, lower = sides(rows, planes[...])
    low, high = half_codes(upper, lower)
    acc = jnp.zeros((HEAD_DIM, rows.shape[1]), f32)
    for c in range(0, 16, chunk):
        acc += dot(tables[0, 128 * c : 128 * (c + chunk), :], code_chunk(low, high, c, chunk), TN)
    out[...] = (acc * (1.0 / HASHES)).astype(out.dtype)


def query_back_kernel(planes, planes_t, bits, tables, *refs, chunk, blocks, last):
    queries, grads = refs[: 2 * blocks], refs[2 * blocks : 3 * blocks]
    start = refs[3 * blocks] if len(refs) > 4 * blocks + 1 else None
    out, back_out = refs[-1 - blocks], refs[-blocks:]
    rows = both(*queries)
    inv, upper, lower = sides(rows, planes[...])
    low, high = half_codes(upper, lower)
    grad = both(*grads)
    sums = jnp.zeros((bits.shape[0], rows.shape[1]), f32)
    for c in range(0, 16, chunk):
        at = slice(128 * c, 128 * (c + chunk))
        codes = code_chunk(low, high, c, chunk)
        part = dot(codes, grad, NT)
        if start is not None:
            part = part + start[0, at, :]
        if last:
            part = part * (1.0 / HASHES)
        out[0, at, :] = part.astype(out.dtype)
        weighted = dot(tables[0, at, :], grad, NN).astype(bf16) * codes
        sums += dot(bits[:, at], weighted, NN)
    back = pull_back(rows, planes_t[...], inv, upper, sums * (1.0 / HASHES))
    width = back_out[0].shape[1]
    for i in range(blocks):
        back_out[i][...] = back[:, i * width : (i + 1) * width].astype(back_out[i].dtype)


def key_back_kernel(planes, planes_t, bits, ka, kb, va, vb, grad_tables, out, *, chunk):
    rows = both(ka, kb)
    inv, upper, lower = sides(rows, planes[...])
    low, high = half_codes(upper, lower)
    values = both(va, vb)
    width = rows.shape[1]
    sums = jnp.zeros((bits.shape[0], width), f32)
    grad_values = jnp.zeros((HEAD_DIM, width), f32)
    for c in range(0, 16, chunk):
        at = slice(128 * c, 128 * (c + chunk))
        codes = code_chunk(low, high, c, chunk)
        grad_values += dot(grad_tables[0, at, :], codes, TN)
        weighted = dot(grad_tables[0, at, :], values, NN).astype(bf16) * codes
        sums += dot(bits[:, at], weighted, NN)
    out[0] = pull_back(rows, planes_t[...], inv, upper, sums).astype(out.dtype)
    out[1] = grad_values.astype(out.dtype)


def bit_rows():
    out = np.zeros((80, BUCKETS, SETS), np.float32)
    for t in range(SETS):
        for i in range(BITS):
            out[i * SETS + t, :, t] = (np.arange(BUCKETS) >> i) & 1
        out[BITS * SETS + t, :, t] = 1
    return jnp.asarray(out.reshape(80, ROWS), bf16)


def whole(*shape):
    return pl.BlockSpec(shape, lambda h: (0,) * len(shape))


def head_rows(array, heads, which):
    width = array.shape[1]
    offset = (which - 3) * heads + array.shape[0] // HEAD_DIM
    return pl.BlockSpec((HEAD_DIM, width), lambda h: (h + offset, 0))


def per_head(width):
    return pl.BlockSpec((HEAD_DIM, width), lambda h: (h, 0))


def table_spec():
    return pl.BlockSpec((1, ROWS, HEAD_DIM), lambda h: (h, 0, 0))


def call(kernel, heads, micros, name, in_specs, out_specs, out_shape):
    return pl.pallas_call(
        kernel,
        grid=(heads,),
        in_specs=in_specs,
        out_specs=out_specs,
        out_shape=out_shape,
        compiler_params=pltpu.CompilerParams(vmem_limit_bytes=48 << 20),
        cost_estimate=pl.CostEstimate(
            flops=int(micros * 1.1e9), bytes_accessed=1 << 20, transcendentals=0
        ),
        name=name,
    )


def key_tables(planes, heads, blocks, start, kind):
    args = [planes, *blocks, *blocks]
    specs = [whole(64, 64)] + [head_rows(x, heads, w) for w in (1, 2) for x in blocks]
    if start is not None:
        specs.append(table_spec())
        args.append(start)
    return call(
        partial(key_kernel, chunk=2, blocks=len(blocks)),
        heads,
        30 if len(blocks) > 1 and start is not None else 1,
        "key_tables",
        specs,
        table_spec(),
        shape((heads, ROWS, HEAD_DIM), kind),
    )(*args)


def query_estimates(planes, heads, near, far, tables, kind):
    width = near.shape[1] + far.shape[1]
    return call(
        partial(query_kernel, chunk=2),
        heads,
        1,
        "query_estimates",
        [whole(64, 64), table_spec(), head_rows(near, heads, 0), head_rows(far, heads, 0)],
        per_head(width),
        shape((heads * HEAD_DIM, width), kind),
    )(planes, tables, near, far)


def query_backward(planes, planes_t, bits, heads, tables, queries, grads, start, last, kinds):
    width = grads[0].shape[1]
    blocks = len(grads)
    specs = [whole(64, 64), whole(64, 128), whole(80, ROWS), table_spec()]
    args = [planes, planes_t, bits, tables]
    for near, far in queries:
        specs += [head_rows(near, heads, 0), head_rows(far, heads, 0)]
        args += [near, far]
    specs += [per_head(width)] * blocks
    args += grads
    if start is not None:
        specs.append(table_spec())
        args.append(start)
    return call(
        partial(query_back_kernel, chunk=4 * blocks, blocks=blocks, last=last),
        heads,
        25 * blocks,
        "query_backward",
        specs,
        [table_spec()] + [per_head(width)] * blocks,
        [shape((heads, ROWS, HEAD_DIM), bf16 if last else f32)]
        + [shape(grads[0].shape, kind) for kind in kinds],
    )(*args)


def key_backward(planes, planes_t, bits, heads, near, far, grad_tables, kind, micros=25):
    width = near.shape[1] + far.shape[1]
    return call(
        partial(key_back_kernel, chunk=4),
        heads,
        micros,
        "key_backward",
        [whole(64, 64), whole(64, 128), whole(80, ROWS)]
        + [head_rows(x, heads, w) for w in (1, 2) for x in (near, far)]
        + [table_spec()],
        pl.BlockSpec((2, HEAD_DIM, width), lambda h: (0, h, 0)),
        shape((2, heads * HEAD_DIM, width), kind),
    )(planes, planes_t, bits, near, far, near, far, grad_tables)


def norm(x):
    center = x - jnp.mean(x, axis=-1, keepdims=True)
    inv = lax.rsqrt(jnp.mean(center * center, axis=-1, keepdims=True) + 1e-5)
    return center * inv, inv


def norm_back(grad, unit, inv):
    return inv * (
        grad
        - jnp.mean(grad, axis=-1, keepdims=True)
        - unit * jnp.mean(grad * unit, axis=-1, keepdims=True)
    )


def column_sum(x):
    return jnp.sum(x, axis=0, keepdims=True)


def core_rows(core, ref, which):
    half = ref.shape[0] // 2
    at = core[0] if which == 0 else 1 - core[0]
    return ref[pl.ds(pl.multiple_of(at * half, 16), half), :]


def share_rows(keep, give, at, rows):
    part = keep.shape[2]
    for out in (keep, give):
        out[at] = rows[:, :part]
        out[at + 1] = rows[:, part:]


def dense_kernel(core, x_in, grad_out, gain, bias, *refs):
    attn, weights = refs[0:4], refs[4:6]
    layer_out, first_out, grad_second_out, slope, keep, give, heads_give, small = refs[6:14]
    owner = [core[1] ^ (b // 2) for b in range(8)]
    for j in range(4):
        heads_give[j] = core_rows(core, attn[j], 1)
    part = slope.shape[2]
    blocks = range(8)
    heads = jnp.concatenate([core_rows(core, attn[b // 2], b % 2) for b in blocks], axis=0)
    out_w = jnp.concatenate([weights[b % 2][owner[b], 2 * part :, :] for b in blocks], axis=0)
    attn_out = dot(heads, out_w, TN)
    resid = x_in[...].astype(f32)
    first = resid + attn_out
    first_out[...] = first
    small[0:1, :] = column_sum(resid * resid)
    small[1:2, :] = column_sum(attn_out * attn_out)
    small[2:3, :] = column_sum(first * first)
    unit_1, _ = norm(first)
    normed = (unit_1 * gain[0:1, :] + bias[0:1, :]).astype(bf16)
    share_rows(keep, give, 4, normed)
    second = normed.astype(f32)
    for b in blocks:
        pre = dot(normed, weights[b % 2][owner[b], 0:part, :], NT)
        below = 0.5 * (1.0 + lax.erf(pre * 0.7071067811865476))
        rows = (pre * below).astype(bf16)
        (keep, give)[b % 2][b // 2] = rows
        slope[b] = below + pre * (0.3989422804014327 * jnp.exp(-0.5 * pre * pre))
        second = second + dot(rows, weights[b % 2][owner[b], part : 2 * part, :], NN)
    unit_2, inv_2 = norm(second)
    layer_out[...] = (unit_2 * gain[1:2, :] + bias[1:2, :]).astype(layer_out.dtype)
    grad = grad_out[...]
    small[3:4, :] = column_sum(grad * unit_2)
    small[4:5, :] = column_sum(grad)
    small[5:8, :] = jnp.zeros_like(small[5:8, :])
    grad_second = norm_back(grad * gain[1:2, :], unit_2, inv_2)
    grad_second_out[...] = grad_second
    share_rows(keep, give, 6, grad_second.astype(bf16))


def dense_back_kernel(core, first, grad_second, slope, gain, *refs):
    weights = refs[0:2]
    grad_first_out, keep, give = refs[2:5]
    estimates, small = refs[5:9], refs[9]
    owner = [core[1] ^ (b // 2) for b in range(8)]
    part = slope.shape[2]
    blocks = range(8)
    grad_normed = grad_second[...]
    grad_ffn = grad_normed.astype(bf16)
    for b in blocks:
        rows = dot(grad_ffn, weights[b % 2][owner[b], part : 2 * part, :], NT)
        rows = (rows * slope[b]).astype(bf16)
        (keep, give)[b % 2][b // 2] = rows
        grad_normed = grad_normed + dot(rows, weights[b % 2][owner[b], 0:part, :], NN)
    unit, inv = norm(first[...])
    small[0:1, :] = column_sum(grad_normed * unit)
    small[1:2, :] = column_sum(grad_normed)
    small[2:8, :] = jnp.zeros_like(small[2:8, :])
    grad_first = norm_back(grad_normed * gain[0:1, :], unit, inv)
    grad_first_out[...] = grad_first
    grad_attn = grad_first.astype(bf16)
    share_rows(keep, give, 4, grad_attn)
    for b in blocks:
        half = estimates[0].shape[0] // 2
        at = core[0] if b % 2 == 0 else 1 - core[0]
        estimates[b // 2][pl.ds(pl.multiple_of(at * half, 16), half), :] = dot(
            weights[b % 2][owner[b], 2 * part :, :], grad_attn, NT
        ).astype(bf16)


def weight_grad_kernel(core, small_a, small_b, *refs):
    near, far, near_back, far_back = refs[0:4]
    attn, attn_far, out = refs[4:8], refs[8], refs[9]
    part = near.shape[2]
    sums = jnp.concatenate([small_a[...], small_b[...]], axis=0).astype(bf16)

    def wide(ref, at):
        return jnp.concatenate([ref[at], ref[at + 1]], axis=1)

    def rows(ref, other, at):
        return jnp.concatenate([wide(ref, at), wide(other, at)], axis=0)

    normed, grad_ffn = rows(near, far, 4), rows(near, far, 6)
    grad_attn = rows(near_back, far_back, 4)
    for j in range(4):
        owner = core[1] ^ j
        hidden = jnp.concatenate([near[j], far[j]], axis=0)
        grad_pre = jnp.concatenate([near_back[j], far_back[j]], axis=0)
        out[owner, 0:part, :] = dot(grad_pre, normed, TN).astype(bf16)
        out[owner, part : 2 * part, :] = dot(hidden, grad_ffn, TN).astype(bf16)
        heads = jnp.concatenate([core_rows(core, attn[j], 0), attn_far[j]], axis=1)
        at = 2 * part + heads.shape[0]
        out[owner, 2 * part : at, :] = dot(heads, grad_attn, NN).astype(bf16)
        out[owner, at : at + 16, :] = sums
        out[owner, at + 16 :, :] = jnp.zeros_like(sums)


def input_grad_kernel(core, grad_first, *refs):
    blocks, near, far, out = refs[0:4], refs[4], refs[5], refs[6]
    half = near.shape[2]
    total = grad_first[...]
    for which, halves in enumerate((near, far)):
        at = core[0] if which == 0 else 1 - core[0]
        at = pl.ds(pl.multiple_of(at * half, 16), half)
        for j in range(4):
            rows = jnp.concatenate([blocks[j][c, at, :] for c in range(3)], axis=0)
            weights = jnp.concatenate([halves[core[1] ^ j, c] for c in range(3)], axis=0)
            total = total + dot(rows, weights, TN)
    out[...] = total.astype(out.dtype)


def vmem(count):
    return [pl.BlockSpec(memory_space=pltpu.VMEM)] * count


def single(kernel, core, args, out_shape, micros, name, scratch=()):
    return pl.pallas_call(
        kernel,
        in_specs=[pl.BlockSpec(memory_space=pltpu.SMEM)] + vmem(len(args)),
        out_specs=vmem(len(out_shape)),
        out_shape=out_shape,
        scratch_shapes=scratch,
        compiler_params=pltpu.CompilerParams(vmem_limit_bytes=56 << 20),
        cost_estimate=pl.CostEstimate(
            flops=int(micros * 1.1e9), bytes_accessed=1 << 20, transcendentals=0
        ),
        name=name,
    )(core, *args)


def dense(core, x_in, grad_out, gain, bias, attn, weights):
    rows, width = x_in.shape
    part = (weights[0].shape[1] - attn[0].shape[0] // 2) // 2
    out_shape = [
        shape((rows, width), bf16),
        shape((rows, width), f32),
        shape((rows, width), f32),
        shape((8, rows, part), f32),
        shape((8, rows, part), bf16),
        shape((8, rows, part), bf16),
        shape((4, attn[0].shape[0] // 2, rows), bf16),
        shape((8, width), f32),
    ]
    args = [x_in, grad_out, gain, bias, *attn, *weights]
    return single(dense_kernel, core, args, out_shape, 14, "dense")


def dense_back(core, first, grad_second, slope, gain, attn, weights):
    rows, width = first.shape
    part = (weights[0].shape[1] - attn[0].shape[0] // 2) // 2
    out_shape = [
        shape((rows, width), f32),
        shape((6, rows, part), bf16),
        shape((6, rows, part), bf16),
        *[shape(attn[0].shape, bf16)] * 4,
        shape((8, width), f32),
    ]
    args = [first, grad_second, slope, gain, *weights]
    return single(dense_back_kernel, core, args, out_shape, 8, "dense_back")


def weight_grads(core, small_a, small_b, shared, attn, attn_far):
    part, width = shared[0].shape[2], small_a.shape[1]
    out_shape = [shape((4, 2 * part + attn[0].shape[0] // 2 + 32, width), bf16)]
    args = [small_a, small_b, *shared, *attn, attn_far]
    return single(weight_grad_kernel, core, args, out_shape, 7, "weight_grads")[0]


def weight_results_kernel(core, near, far, up, down, out):
    part, rows = up.shape[1] // 2, out.shape[0] // 2
    for which, ref in enumerate((near, far)):
        at = core[0] if which == 0 else 1 - core[0]
        at_part = pl.ds(pl.multiple_of(at * part, 128), part)
        up[:, at_part] = ref[0:part, :].astype(f32).T
        down[at_part, :] = ref[part : 2 * part, :].astype(f32)
        at_rows = pl.ds(pl.multiple_of(at * rows, 16), rows)
        out[at_rows, :] = ref[2 * part : 2 * part + rows, :].astype(f32)


def weight_results(core, near, far, head_width):
    width = near.shape[1]
    part = (near.shape[0] - 32 - head_width // 2) // 2
    out_shape = [
        shape((width, 2 * part), f32), shape((2 * part, width), f32), shape((head_width, width), f32)
    ]
    return single(weight_results_kernel, core, [near, far], out_shape, 3, "weight_results")


def input_grad(core, grad_first, blocks, near, far):
    out_shape = [shape(grad_first.shape, bf16)]
    args = [grad_first, *blocks, near, far]
    return single(input_grad_kernel, core, args, out_shape, 40, "input_grad")[0]


def after(x, *others):
    return lax.optimization_barrier((x, *others))[0]


def add(a, *others):
    return sum([b.astype(f32) for b in others], a.astype(f32))


def shards(
    inputs,
    w_qkv,
    w_out,
    up_weight,
    down_weight,
    norm_gain,
    norm_bias,
    planes,
    mask_pos,
    cot_rows,
):
    own = inputs[0]
    piece, seqs, width = own.shape
    hash_count, head_count = lax.axis_size("hash"), lax.axis_size("head")
    groups, places = seqs, hash_count // seqs
    assert places == 2 and lax.axis_size("seq") == 2 and head_count == 4
    assert planes.shape[0] * hash_count == 4 * SETS
    quarter = piece // head_count
    rows = groups * quarter
    half_len = piece * hash_count
    head_width = w_out.shape[0]
    hidden_own = down_weight.shape[0]
    n_tokens = head_count * rows
    hash_id, d, s = lax.axis_index("hash"), lax.axis_index("head"), lax.axis_index("seq")
    g, r = hash_id // places, hash_id % places

    def over_seq(x):
        return lax.ppermute(x, "seq", [(0, 1), (1, 0)])

    def over_place(x):
        return lax.ppermute(x, "hash", [(h, h ^ 1) for h in range(hash_count)])

    def over_group(x, k):
        moves = [(h, ((h // places + k) % groups) * places + h % places) for h in range(hash_count)]
        return lax.ppermute(x, "hash", moves)

    def over_head(x, j):
        return lax.ppermute(x, "head", [(h, h ^ j) for h in range(head_count)])

    def seq_rows(block, index):
        return lax.dynamic_index_in_dim(block, index % seqs, 1, keepdims=False)

    here = [
        seq_rows(lax.dynamic_slice_in_dim(own, (d ^ j) * quarter, quarter, 0), g)
        for j in range(head_count)
    ]
    near_tokens = jnp.concatenate(here)
    my_quarter = lax.dynamic_slice_in_dim(own, d * quarter, quarter, 0)
    sent = [seq_rows(my_quarter, g + k) for k in range(1, groups)]
    arrived = [over_group(x, k + 1) for k, x in enumerate(sent)]

    signed = (2 * planes - 1).astype(bf16)
    if planes.shape[0] == SETS and groups == 2:
        moves = [
            ((2 * rr + ss) * 2 + gg, (gg * places + rr) * 2 + ss)
            for gg in range(2)
            for rr in range(2)
            for ss in range(2)
        ]
        signed = lax.ppermute(signed, ("hash", "seq"), moves)
    else:
        signed = lax.all_gather(signed, "hash", axis=0, tiled=True)
        signed = lax.dynamic_slice_in_dim(signed, (r * 2 + s) * SETS, SETS, 0)
    signed = signed.transpose(1, 0, 2).reshape(BITS * SETS, HEAD_DIM)
    signed_t = jnp.concatenate([signed.T, signed.T], axis=1)
    bits = bit_rows()

    cut, out_cut = hidden_own // 2, head_width // 2
    weights = jnp.concatenate(
        [
            lax.dynamic_slice_in_dim(after(up_weight, *sent), s * cut, cut, 1).T,
            lax.dynamic_slice_in_dim(down_weight, s * cut, cut, 0),
            lax.dynamic_slice_in_dim(w_out, s * out_cut, out_cut, 0),
        ]
    )
    weights = lax.all_gather(weights, "head", axis=0)
    w_qkv_t = lax.dynamic_slice_in_dim(w_qkv.transpose(0, 2, 1), s * out_cut, out_cut, 1)

    head_n = head_width // HEAD_DIM

    def project(w, rows_in):
        out = jnp.einsum("cde,ld->cel", w, rows_in, preferred_element_type=f32)
        return out.astype(bf16).reshape(-1, rows_in.shape[0])

    near_tokens = after(near_tokens, *arrived)
    near = project(w_qkv, near_tokens)
    near_z, near_o = over_place(near), over_seq(near)
    far_quarter = jnp.stack(arrived)
    moved = [over_head(far_quarter, j) for j in range(1, head_count)]
    dense_in = jnp.concatenate([here[0], *arrived])
    tables = key_tables(after(signed, dense_in), head_n, [near, near_o], None, f32)
    moved = [after(x, tables) for x in moved]

    near_z = after(near_z, tables)
    near_zo = over_seq(near_z)

    mask_pos = after(mask_pos, tables)
    slot = jnp.arange(groups, dtype=jnp.int32)[:, None]
    place_of = ((g - slot) % groups) * places + r
    position = s * half_len + place_of * piece + d * quarter + jnp.arange(quarter, dtype=jnp.int32)[None]
    mask_row = lax.dynamic_index_in_dim(mask_pos, g, 0, keepdims=False)
    cot = lax.dynamic_index_in_dim(cot_rows, g, 0, keepdims=False)
    pick = (position.reshape(rows)[:, None] == mask_row[None]).astype(bf16)
    grad_out = jnp.dot(pick, cot, preferred_element_type=f32)
    ready = after(signed, grad_out)
    tables = key_tables(ready, head_n, [near_z, near_zo], tables, f32)

    far_tokens = jnp.stack([far_quarter, *moved]).reshape(-1, width)
    far = project(w_qkv, far_tokens)
    tokens = jnp.concatenate([near_tokens, far_tokens])
    far_z, far_o = over_place(far), over_seq(far)
    n_near = near.shape[1]

    tables = key_tables(signed, head_n, [far, far_o], tables, f32)

    far_z = after(far_z, tables)
    far_zo = over_seq(far_z)
    tables = key_tables(after(signed, tokens), head_n, [far_z], tables, f32)

    far_zo = after(far_zo, tables)
    tables = key_tables(signed, head_n, [far_zo], tables, bf16)

    e_zo = query_estimates(signed, head_n, near_zo, far_zo, tables, bf16)
    e_zo_moved = over_seq(e_zo)
    e_z = query_estimates(signed, head_n, near_z, after(far_z, e_zo), tables, bf16)
    e_far = add(e_z, after(e_zo_moved, e_z)).astype(bf16)
    ready = after(far_o, e_far)
    e_o = query_estimates(signed, head_n, near_o, ready, tables, bf16)
    e_far = over_place(e_far)
    e_o_moved = over_seq(e_o)
    e = query_estimates(signed, head_n, near, after(far, e_o), tables, f32)
    e_far = after(e_far, e)
    weights = after(weights, e_far)
    weights = [weights, over_seq(weights)]
    w_qkv_t = lax.all_gather(after(w_qkv_t, weights[0]), "head", axis=0)
    attn = add(e, after(e_o_moved, e), e_far).astype(bf16)

    def to_dense(block):
        parts = []
        for j in range(head_count):
            a, b = j * quarter, n_near + j * (rows - quarter)
            cut = [block[..., a : a + quarter], block[..., b : b + rows - quarter]]
            parts.append(jnp.concatenate(cut, axis=-1))
        moved = [over_head(parts[j], j) for j in range(1, head_count)]
        return [parts[0], *lax.optimization_barrier(moved)]

    attn_parts = to_dense(attn)

    def away(dense_rows):
        dense_rows = dense_rows.reshape(groups, quarter, width)
        return [dense_rows[0]] + [over_group(dense_rows[k], groups - k) for k in range(1, groups)]

    core = jnp.stack([s, d]).astype(jnp.int32)
    layer_rows, first, grad_second, slope, keep, give, heads_give, small_a = dense(
        core, dense_in, grad_out, norm_gain, norm_bias, attn_parts, weights
    )
    taken, heads_far = over_seq(give), over_seq(heads_give)
    grad_first, keep_back, give_back, *est_parts, small_b = dense_back(
        core, first, grad_second, slope, norm_gain, attn_parts, weights
    )
    taken_back = over_seq(give_back)
    est_moved = [over_head(est_parts[j], j) for j in range(1, head_count)]
    est_parts = [est_parts[0], *lax.optimization_barrier(est_moved)]
    grad = jnp.concatenate(
        [x[:, :quarter] for x in est_parts] + [x[:, quarter:] for x in est_parts], axis=1
    )
    layer_moved = away(layer_rows)
    weight_parts = weight_grads(
        core, after(small_a, grad, w_qkv_t), small_b, [keep, taken, keep_back, taken_back], attn_parts, heads_far
    )

    weight_sum = lax.psum_scatter(weight_parts, "head", scatter_dimension=0, tiled=True)[0]
    grad_z = over_place(grad)
    grad_o = after(over_seq(grad), weight_parts)
    layer_moved = jnp.stack([after(x, weight_parts) for x in layer_moved])
    part, dq, dq_o = query_backward(
        signed, signed_t, bits, head_n, tables, [(near, after(far, layer_moved)), (near_o, far_o)], [grad, grad_o],
        None, False, [f32, bf16],
    )

    grad_z = after(grad_z, part)
    grad_zo = over_seq(grad_z)
    dq_o = over_seq(dq_o)
    part, dq_z = query_backward(
        signed, signed_t, bits, head_n, tables, [(near_z, far_z)], [grad_z], part, False, [f32]
    )

    dq_own = add(dq, after(dq_o, dq_z))
    grad_zo = after(grad_zo, dq_z)
    grad_tables, dq_zo = query_backward(
        signed, signed_t, bits, head_n, tables, [(near_zo, after(far_zo, dq_own))], [grad_zo], part, True, [bf16]
    )

    dq_zo = over_seq(dq_zo)
    w_qkv_t = after(w_qkv_t, grad_tables)
    w_qkv_far = over_seq(w_qkv_t)
    dkv_zo = key_backward(signed, signed_t, bits, head_n, near_zo, far_zo, grad_tables, bf16)

    dkv_zo_moved = over_seq(dkv_zo)
    dq_far = add(dq_z, after(dq_zo, dkv_zo)).astype(bf16)
    layer_moved = [layer_moved] + [over_head(layer_moved, j) for j in range(1, head_count)]
    dkv_z = key_backward(signed, signed_t, bits, head_n, near_z, after(far_z, dq_far), grad_tables, bf16)
    dq_far = over_place(dq_far)

    dkv_far = add(dkv_z, after(dkv_zo_moved, dkv_z)).astype(bf16)
    grad_q = add(dq_own, after(dq_far, dkv_z)).astype(bf16)
    weight_sum = after(weight_sum, dkv_z)
    layer_moved = [after(x, dkv_z) for x in layer_moved]
    dkv_o = key_backward(
        signed, signed_t, bits, head_n, near_o, after(far_o, dkv_far, grad_q, weight_sum, *layer_moved),
        grad_tables, bf16, 25,
    )
    weight_sum = lax.psum(weight_sum, "hash")
    dkv_far = over_place(dkv_far)
    dkv_o_moved = over_seq(dkv_o)
    dkv = key_backward(
        signed, signed_t, bits, head_n, near, far, grad_tables, f32, 25
    )

    dkv_o_moved = after(dkv_o_moved, dkv)
    grad_kv = add(dkv, dkv_o_moved, after(dkv_far, dkv)).astype(bf16)
    grad_qkv = jnp.concatenate([grad_q[None], grad_kv])
    qkv_parts = to_dense(grad_qkv)

    grad_in = input_grad(core, grad_first, qkv_parts, w_qkv_t, after(w_qkv_far, dkv))

    def in_halves(index, mine, other):
        first = jnp.where(index == 0, mine, other)
        second = jnp.where(index == 0, other, mine)
        return jnp.concatenate([first, second], axis=0)

    def split(x, index):
        half = x.shape[0] // 2
        return [lax.dynamic_slice_in_dim(x, at * half, half, 0) for at in (index, 1 - index)]

    w_grad = dot(grad_qkv.reshape(3 * head_width, n_tokens), tokens, NN).astype(bf16)
    w_keep, w_send = split(w_grad, s)
    w_keep, w_send = split(add(w_keep, over_seq(w_send)).astype(bf16), r)
    grad_moved = away(grad_in)
    w_keep = add(w_keep, over_place(w_send))
    w_send = w_keep.astype(bf16)
    grad_moved = after(jnp.stack(grad_moved), w_send)
    w_keep = add(w_keep, *[over_group(w_send, k) for k in range(1, groups)]).astype(bf16)
    grad_moved = [grad_moved] + [over_head(grad_moved, j) for j in range(1, head_count)]

    def home(blocks):
        table = jnp.stack(blocks)
        columns = []
        for q_at in range(head_count):
            block = lax.dynamic_index_in_dim(table, q_at ^ d, 0, keepdims=False)
            columns.append(
                jnp.stack(
                    [
                        lax.dynamic_index_in_dim(block, (at - g) % groups, 0, keepdims=False)
                        for at in range(seqs)
                    ],
                    axis=1,
                )
            )
        return jnp.concatenate(columns, axis=0)

    layer_out = home([after(x, grad_moved[0]) for x in layer_moved])
    grad_inputs = home(grad_moved).astype(f32)

    w_grad = in_halves(r, w_keep, over_place(w_keep))
    w_grad = in_halves(s, w_grad, over_seq(w_grad)).reshape(3, head_width, width)
    grad_w_qkv = w_grad.transpose(0, 2, 1).astype(f32)
    weight_sum = after(weight_sum, *grad_moved)
    weight_far = over_seq(weight_sum)
    grad_w_up, grad_w_down, grad_w_out = weight_results(core, weight_sum, weight_far, head_width)
    at = slice(2 * cut + out_cut, 2 * cut + out_cut + 16)
    small = add(weight_sum[at], weight_far[at])

    count = piece * seqs * width * hash_count * 2
    stream_rms = jnp.sqrt(jnp.sum(small[0:3], axis=1) / count)
    share = width // head_count
    norm_grads = lax.dynamic_slice_in_dim(small, d * share, share, 1)
    return (
        layer_out[None],
        grad_inputs[None],
        grad_w_qkv,
        grad_w_out,
        grad_w_up,
        grad_w_down,
        jnp.stack([norm_grads[8], norm_grads[3]]),
        jnp.stack([norm_grads[9], norm_grads[4]]),
        stream_rms,
    )


def solution(mesh):
    placed = (
        P("seq", "hash", None, None),
        P(None, None, "head"),
        P("head", None),
        P(None, "head"),
        P("head", None),
        P(),
        P(),
        P("hash", None, None),
        P(),
        P(),
    )
    return jax.shard_map(
        shards,
        mesh=mesh,
        in_specs=placed,
        out_specs=(
            P("seq", "hash", None, None),
            P("seq", "hash", None, None),
            P(None, None, "head"),
            P("head", None),
            P(None, "head"),
            P("head", None),
            P(None, "head"),
            P(None, "head"),
            P(),
        ),
        check_vma=False,
    )
```

```python
from functools import partial

import jax
import jax.numpy as jnp
import numpy as np
from jax import lax
from jax.experimental import pallas as pl
from jax.experimental.pallas import tpu as pltpu
from jax.sharding import PartitionSpec as P

HEAD_DIM = 64
HASHES = 32
BITS = 8
SETS = 8
BUCKETS = 1 << BITS
ROWS = BUCKETS * SETS

bf16 = jnp.bfloat16
f32 = jnp.float32
NN = (((1,), (0,)), ((), ()))
NT = (((1,), (1,)), ((), ()))
TN = (((0,), (0,)), ((), ()))


shape = jax.ShapeDtypeStruct


def dot(a, b, dims):
    return lax.dot_general(a, b, dims, preferred_element_type=f32)


def sides(rows, planes):
    x = rows.astype(f32)
    inv = lax.rsqrt(jnp.sum(x * x, axis=0, keepdims=True) + 1e-6)
    proj = dot(planes, rows, NN) * (3.0 * inv)
    small = jnp.exp(-proj)
    upper = 1.0 / (1.0 + small)
    return inv, upper, small * upper


def products(upper, lower, first, count):
    out = None
    for i in range(first, first + count):
        lo, up = lower[SETS * i : SETS * (i + 1)], upper[SETS * i : SETS * (i + 1)]
        out = [lo, up] if out is None else [c * lo for c in out] + [c * up for c in out]
    return out


def half_codes(upper, lower):
    low = jnp.concatenate(products(upper, lower, 0, 4), axis=0).astype(bf16)
    high = [jnp.concatenate([a, a], axis=0).astype(bf16) for a in products(upper, lower, 4, 4)]
    return low, high


def code_chunk(low, high, first, count):
    return jnp.concatenate(
        [high[a] * low[16 * j : 16 * (j + 1)] for a in range(first, first + count) for j in range(8)],
        axis=0,
    )


def pull_back(rows, planes_t, inv, upper, sums):
    total = sums[BITS * SETS :][:SETS]
    grad_proj = sums[: BITS * SETS] - upper * jnp.concatenate([total] * BITS, axis=0)
    head = grad_proj.astype(bf16)
    tail = (grad_proj - head.astype(f32)).astype(bf16)
    grad_unit = dot(planes_t, jnp.concatenate([head, tail], axis=0), NN) * (3.0 * inv)
    x = rows.astype(f32)
    return grad_unit - x * (inv * inv * jnp.sum(x * grad_unit, axis=0, keepdims=True))


def both(*refs):
    return jnp.concatenate([ref[...] for ref in refs], axis=1)


def key_kernel(planes, *refs, chunk, blocks):
    keys, vals, out = refs[:blocks], refs[blocks : 2 * blocks], refs[-1]
    start = refs[2 * blocks] if len(refs) > 2 * blocks + 1 else None
    _, upper, lower = sides(both(*keys), planes[...])
    low, high = half_codes(upper, lower)
    values = both(*vals)
    for c in range(0, 16, chunk):
        at = slice(128 * c, 128 * (c + chunk))
        part = dot(code_chunk(low, high, c, chunk), values, NT)
        if start is not None:
            part = part + start[0, at, :]
        out[0, at, :] = part.astype(out.dtype)


def query_kernel(planes, tables, *refs, chunk):
    rows, out = both(*refs[:-1]), refs[-1]
    _, upper, lower = sides(rows, planes[...])
    low, high = half_codes(upper, lower)
    acc = jnp.zeros((HEAD_DIM, rows.shape[1]), f32)
    for c in range(0, 16, chunk):
        acc += dot(tables[0, 128 * c : 128 * (c + chunk), :], code_chunk(low, high, c, chunk), TN)
    out[...] = (acc * (1.0 / HASHES)).astype(out.dtype)


def query_back_kernel(planes, planes_t, bits, tables, *refs, chunk, blocks, last):
    queries, grads = refs[: 2 * blocks], refs[2 * blocks : 3 * blocks]
    start = refs[3 * blocks] if len(refs) > 4 * blocks + 1 else None
    out, back_out = refs[-1 - blocks], refs[-blocks:]
    rows = both(*queries)
    inv, upper, lower = sides(rows, planes[...])
    low, high = half_codes(upper, lower)
    grad = both(*grads)
    sums = jnp.zeros((bits.shape[0], rows.shape[1]), f32)
    for c in range(0, 16, chunk):
        at = slice(128 * c, 128 * (c + chunk))
        codes = code_chunk(low, high, c, chunk)
        part = dot(codes, grad, NT)
        if start is not None:
            part = part + start[0, at, :]
        if last:
            part = part * (1.0 / HASHES)
        out[0, at, :] = part.astype(out.dtype)
        weighted = dot(tables[0, at, :], grad, NN).astype(bf16) * codes
        sums += dot(bits[:, at], weighted, NN)
    back = pull_back(rows, planes_t[...], inv, upper, sums * (1.0 / HASHES))
    width = back_out[0].shape[1]
    for i in range(blocks):
        back_out[i][...] = back[:, i * width : (i + 1) * width].astype(back_out[i].dtype)


def key_back_kernel(planes, planes_t, bits, ka, kb, va, vb, grad_tables, out, *, chunk):
    rows = both(ka, kb)
    inv, upper, lower = sides(rows, planes[...])
    low, high = half_codes(upper, lower)
    values = both(va, vb)
    width = rows.shape[1]
    sums = jnp.zeros((bits.shape[0], width), f32)
    grad_values = jnp.zeros((HEAD_DIM, width), f32)
    for c in range(0, 16, chunk):
        at = slice(128 * c, 128 * (c + chunk))
        codes = code_chunk(low, high, c, chunk)
        grad_values += dot(grad_tables[0, at, :], codes, TN)
        weighted = dot(grad_tables[0, at, :], values, NN).astype(bf16) * codes
        sums += dot(bits[:, at], weighted, NN)
    out[0] = pull_back(rows, planes_t[...], inv, upper, sums).astype(out.dtype)
    out[1] = grad_values.astype(out.dtype)


def bit_rows():
    out = np.zeros((80, BUCKETS, SETS), np.float32)
    for t in range(SETS):
        for i in range(BITS):
            out[i * SETS + t, :, t] = (np.arange(BUCKETS) >> i) & 1
        out[BITS * SETS + t, :, t] = 1
    return jnp.asarray(out.reshape(80, ROWS), bf16)


def whole(*shape):
    return pl.BlockSpec(shape, lambda h: (0,) * len(shape))


def head_rows(array, heads, which):
    width = array.shape[1]
    offset = (which - 3) * heads + array.shape[0] // HEAD_DIM
    return pl.BlockSpec((HEAD_DIM, width), lambda h: (h + offset, 0))


def per_head(width):
    return pl.BlockSpec((HEAD_DIM, width), lambda h: (h, 0))


def table_spec():
    return pl.BlockSpec((1, ROWS, HEAD_DIM), lambda h: (h, 0, 0))


def call(kernel, heads, micros, name, in_specs, out_specs, out_shape):
    return pl.pallas_call(
        kernel,
        grid=(heads,),
        in_specs=in_specs,
        out_specs=out_specs,
        out_shape=out_shape,
        compiler_params=pltpu.CompilerParams(vmem_limit_bytes=48 << 20),
        cost_estimate=pl.CostEstimate(
            flops=int(micros * 1.1e9), bytes_accessed=1 << 20, transcendentals=0
        ),
        name=name,
    )


def key_tables(planes, heads, blocks, start, kind):
    args = [planes, *blocks, *blocks]
    specs = [whole(64, 64)] + [head_rows(x, heads, w) for w in (1, 2) for x in blocks]
    if start is not None:
        specs.append(table_spec())
        args.append(start)
    return call(
        partial(key_kernel, chunk=2, blocks=len(blocks)),
        heads,
        30 if len(blocks) > 1 and start is not None else 1,
        "key_tables",
        specs,
        table_spec(),
        shape((heads, ROWS, HEAD_DIM), kind),
    )(*args)


def query_estimates(planes, heads, near, far, tables, kind):
    width = near.shape[1] + far.shape[1]
    return call(
        partial(query_kernel, chunk=2),
        heads,
        1,
        "query_estimates",
        [whole(64, 64), table_spec(), head_rows(near, heads, 0), head_rows(far, heads, 0)],
        per_head(width),
        shape((heads * HEAD_DIM, width), kind),
    )(planes, tables, near, far)


def query_backward(planes, planes_t, bits, heads, tables, queries, grads, start, last, kinds):
    width = grads[0].shape[1]
    blocks = len(grads)
    specs = [whole(64, 64), whole(64, 128), whole(80, ROWS), table_spec()]
    args = [planes, planes_t, bits, tables]
    for near, far in queries:
        specs += [head_rows(near, heads, 0), head_rows(far, heads, 0)]
        args += [near, far]
    specs += [per_head(width)] * blocks
    args += grads
    if start is not None:
        specs.append(table_spec())
        args.append(start)
    return call(
        partial(query_back_kernel, chunk=4 * blocks, blocks=blocks, last=last),
        heads,
        25 * blocks,
        "query_backward",
        specs,
        [table_spec()] + [per_head(width)] * blocks,
        [shape((heads, ROWS, HEAD_DIM), bf16 if last else f32)]
        + [shape(grads[0].shape, kind) for kind in kinds],
    )(*args)


def key_backward(planes, planes_t, bits, heads, near, far, grad_tables, kind, micros=25):
    width = near.shape[1] + far.shape[1]
    return call(
        partial(key_back_kernel, chunk=4),
        heads,
        micros,
        "key_backward",
        [whole(64, 64), whole(64, 128), whole(80, ROWS)]
        + [head_rows(x, heads, w) for w in (1, 2) for x in (near, far)]
        + [table_spec()],
        pl.BlockSpec((2, HEAD_DIM, width), lambda h: (0, h, 0)),
        shape((2, heads * HEAD_DIM, width), kind),
    )(planes, planes_t, bits, near, far, near, far, grad_tables)


def norm(x):
    center = x - jnp.mean(x, axis=-1, keepdims=True)
    inv = lax.rsqrt(jnp.mean(center * center, axis=-1, keepdims=True) + 1e-5)
    return center * inv, inv


def norm_back(grad, unit, inv):
    return inv * (
        grad
        - jnp.mean(grad, axis=-1, keepdims=True)
        - unit * jnp.mean(grad * unit, axis=-1, keepdims=True)
    )


def column_sum(x):
    return jnp.sum(x, axis=0, keepdims=True)


def core_rows(core, ref, which):
    half = ref.shape[0] // 2
    at = core[0] if which == 0 else 1 - core[0]
    return ref[pl.ds(pl.multiple_of(at * half, 16), half), :]


def share_rows(keep, give, at, rows):
    part = keep.shape[2]
    for out in (keep, give):
        out[at] = rows[:, :part]
        out[at + 1] = rows[:, part:]


def dense_kernel(core, x_in, grad_out, gain, bias, *refs):
    attn, weights = refs[0:4], refs[4:6]
    layer_out, first_out, grad_second_out, slope, keep, give, heads_give, small = refs[6:14]
    owner = [core[1] ^ (b // 2) for b in range(8)]
    for j in range(4):
        heads_give[j] = core_rows(core, attn[j], 1)
    part = slope.shape[2]
    blocks = range(8)
    heads = jnp.concatenate([core_rows(core, attn[b // 2], b % 2) for b in blocks], axis=0)
    out_w = jnp.concatenate([weights[b % 2][owner[b], 2 * part :, :] for b in blocks], axis=0)
    attn_out = dot(heads, out_w, TN)
    resid = x_in[...].astype(f32)
    first = resid + attn_out
    first_out[...] = first
    small[0:1, :] = column_sum(resid * resid)
    small[1:2, :] = column_sum(attn_out * attn_out)
    small[2:3, :] = column_sum(first * first)
    unit_1, _ = norm(first)
    normed = (unit_1 * gain[0:1, :] + bias[0:1, :]).astype(bf16)
    share_rows(keep, give, 4, normed)
    second = normed.astype(f32)
    for b in blocks:
        pre = dot(normed, weights[b % 2][owner[b], 0:part, :], NT)
        below = 0.5 * (1.0 + lax.erf(pre * 0.7071067811865476))
        rows = (pre * below).astype(bf16)
        (keep, give)[b % 2][b // 2] = rows
        slope[b] = below + pre * (0.3989422804014327 * jnp.exp(-0.5 * pre * pre))
        second = second + dot(rows, weights[b % 2][owner[b], part : 2 * part, :], NN)
    unit_2, inv_2 = norm(second)
    layer_out[...] = (unit_2 * gain[1:2, :] + bias[1:2, :]).astype(layer_out.dtype)
    grad = grad_out[...]
    small[3:4, :] = column_sum(grad * unit_2)
    small[4:5, :] = column_sum(grad)
    small[5:8, :] = jnp.zeros_like(small[5:8, :])
    grad_second = norm_back(grad * gain[1:2, :], unit_2, inv_2)
    grad_second_out[...] = grad_second
    share_rows(keep, give, 6, grad_second.astype(bf16))


def dense_back_kernel(core, first, grad_second, slope, gain, *refs):
    weights = refs[0:2]
    grad_first_out, keep, give = refs[2:5]
    estimates, small = refs[5:9], refs[9]
    owner = [core[1] ^ (b // 2) for b in range(8)]
    part = slope.shape[2]
    blocks = range(8)
    grad_normed = grad_second[...]
    grad_ffn = grad_normed.astype(bf16)
    for b in blocks:
        rows = dot(grad_ffn, weights[b % 2][owner[b], part : 2 * part, :], NT)
        rows = (rows * slope[b]).astype(bf16)
        (keep, give)[b % 2][b // 2] = rows
        grad_normed = grad_normed + dot(rows, weights[b % 2][owner[b], 0:part, :], NN)
    unit, inv = norm(first[...])
    small[0:1, :] = column_sum(grad_normed * unit)
    small[1:2, :] = column_sum(grad_normed)
    small[2:8, :] = jnp.zeros_like(small[2:8, :])
    grad_first = norm_back(grad_normed * gain[0:1, :], unit, inv)
    grad_first_out[...] = grad_first
    grad_attn = grad_first.astype(bf16)
    share_rows(keep, give, 4, grad_attn)
    for b in blocks:
        half = estimates[0].shape[0] // 2
        at = core[0] if b % 2 == 0 else 1 - core[0]
        estimates[b // 2][pl.ds(pl.multiple_of(at * half, 16), half), :] = dot(
            weights[b % 2][owner[b], 2 * part :, :], grad_attn, NT
        ).astype(bf16)


def weight_grad_kernel(core, small_a, small_b, *refs):
    near, far, near_back, far_back = refs[0:4]
    attn, attn_far, out = refs[4:8], refs[8], refs[9]
    part = near.shape[2]
    sums = jnp.concatenate([small_a[...], small_b[...]], axis=0).astype(bf16)

    def wide(ref, at):
        return jnp.concatenate([ref[at], ref[at + 1]], axis=1)

    def rows(ref, other, at):
        return jnp.concatenate([wide(ref, at), wide(other, at)], axis=0)

    normed, grad_ffn = rows(near, far, 4), rows(near, far, 6)
    grad_attn = rows(near_back, far_back, 4)
    for j in range(4):
        owner = core[1] ^ j
        hidden = jnp.concatenate([near[j], far[j]], axis=0)
        grad_pre = jnp.concatenate([near_back[j], far_back[j]], axis=0)
        out[owner, 0:part, :] = dot(grad_pre, normed, TN).astype(bf16)
        out[owner, part : 2 * part, :] = dot(hidden, grad_ffn, TN).astype(bf16)
        heads = jnp.concatenate([core_rows(core, attn[j], 0), attn_far[j]], axis=1)
        at = 2 * part + heads.shape[0]
        out[owner, 2 * part : at, :] = dot(heads, grad_attn, NN).astype(bf16)
        out[owner, at : at + 16, :] = sums
        out[owner, at + 16 :, :] = jnp.zeros_like(sums)


def input_grad_kernel(core, grad_first, *refs):
    blocks, near, far, out = refs[0:4], refs[4], refs[5], refs[6]
    half = near.shape[2]
    total = grad_first[...]
    for which, halves in enumerate((near, far)):
        at = core[0] if which == 0 else 1 - core[0]
        at = pl.ds(pl.multiple_of(at * half, 16), half)
        for j in range(4):
            rows = jnp.concatenate([blocks[j][c, at, :] for c in range(3)], axis=0)
            weights = jnp.concatenate([halves[core[1] ^ j, c] for c in range(3)], axis=0)
            total = total + dot(rows, weights, TN)
    out[...] = total.astype(out.dtype)


def vmem(count):
    return [pl.BlockSpec(memory_space=pltpu.VMEM)] * count


def single(kernel, core, args, out_shape, micros, name, scratch=()):
    return pl.pallas_call(
        kernel,
        in_specs=[pl.BlockSpec(memory_space=pltpu.SMEM)] + vmem(len(args)),
        out_specs=vmem(len(out_shape)),
        out_shape=out_shape,
        scratch_shapes=scratch,
        compiler_params=pltpu.CompilerParams(vmem_limit_bytes=56 << 20),
        cost_estimate=pl.CostEstimate(
            flops=int(micros * 1.1e9), bytes_accessed=1 << 20, transcendentals=0
        ),
        name=name,
    )(core, *args)


def dense(core, x_in, grad_out, gain, bias, attn, weights):
    rows, width = x_in.shape
    part = (weights[0].shape[1] - attn[0].shape[0] // 2) // 2
    out_shape = [
        shape((rows, width), bf16),
        shape((rows, width), f32),
        shape((rows, width), f32),
        shape((8, rows, part), f32),
        shape((8, rows, part), bf16),
        shape((8, rows, part), bf16),
        shape((4, attn[0].shape[0] // 2, rows), bf16),
        shape((8, width), f32),
    ]
    args = [x_in, grad_out, gain, bias, *attn, *weights]
    return single(dense_kernel, core, args, out_shape, 14, "dense")


def dense_back(core, first, grad_second, slope, gain, attn, weights):
    rows, width = first.shape
    part = (weights[0].shape[1] - attn[0].shape[0] // 2) // 2
    out_shape = [
        shape((rows, width), f32),
        shape((6, rows, part), bf16),
        shape((6, rows, part), bf16),
        *[shape(attn[0].shape, bf16)] * 4,
        shape((8, width), f32),
    ]
    args = [first, grad_second, slope, gain, *weights]
    return single(dense_back_kernel, core, args, out_shape, 8, "dense_back")


def weight_grads(core, small_a, small_b, shared, attn, attn_far):
    part, width = shared[0].shape[2], small_a.shape[1]
    out_shape = [shape((4, 2 * part + attn[0].shape[0] // 2 + 32, width), bf16)]
    args = [small_a, small_b, *shared, *attn, attn_far]
    return single(weight_grad_kernel, core, args, out_shape, 7, "weight_grads")[0]


def weight_results_kernel(core, near, far, up, down, out):
    part, rows = up.shape[1] // 2, out.shape[0] // 2
    for which, ref in enumerate((near, far)):
        at = core[0] if which == 0 else 1 - core[0]
        at_part = pl.ds(pl.multiple_of(at * part, 128), part)
        up[:, at_part] = ref[0:part, :].astype(f32).T
        down[at_part, :] = ref[part : 2 * part, :].astype(f32)
        at_rows = pl.ds(pl.multiple_of(at * rows, 16), rows)
        out[at_rows, :] = ref[2 * part : 2 * part + rows, :].astype(f32)


def weight_results(core, near, far, head_width):
    width = near.shape[1]
    part = (near.shape[0] - 32 - head_width // 2) // 2
    out_shape = [
        shape((width, 2 * part), f32), shape((2 * part, width), f32), shape((head_width, width), f32)
    ]
    return single(weight_results_kernel, core, [near, far], out_shape, 3, "weight_results")


def input_grad(core, grad_first, blocks, near, far):
    out_shape = [shape(grad_first.shape, bf16)]
    args = [grad_first, *blocks, near, far]
    return single(input_grad_kernel, core, args, out_shape, 40, "input_grad")[0]


def after(x, *others):
    return lax.optimization_barrier((x, *others))[0]


def add(a, *others):
    return sum([b.astype(f32) for b in others], a.astype(f32))


def shards(
    inputs,
    w_qkv,
    w_out,
    up_weight,
    down_weight,
    norm_gain,
    norm_bias,
    planes,
    mask_pos,
    cot_rows,
):
    own = inputs[0]
    piece, seqs, width = own.shape
    hash_count, head_count = lax.axis_size("hash"), lax.axis_size("head")
    groups, places = seqs, hash_count // seqs
    assert places == 2 and lax.axis_size("seq") == 2 and head_count == 4
    assert planes.shape[0] * hash_count == 4 * SETS
    quarter = piece // head_count
    rows = groups * quarter
    half_len = piece * hash_count
    head_width = w_out.shape[0]
    hidden_own = down_weight.shape[0]
    n_tokens = head_count * rows
    hash_id, d, s = lax.axis_index("hash"), lax.axis_index("head"), lax.axis_index("seq")
    g, r = hash_id // places, hash_id % places

    def over_seq(x):
        return lax.ppermute(x, "seq", [(0, 1), (1, 0)])

    def over_place(x):
        return lax.ppermute(x, "hash", [(h, h ^ 1) for h in range(hash_count)])

    def over_group(x, k):
        moves = [(h, ((h // places + k) % groups) * places + h % places) for h in range(hash_count)]
        return lax.ppermute(x, "hash", moves)

    def over_head(x, j):
        return lax.ppermute(x, "head", [(h, h ^ j) for h in range(head_count)])

    def seq_rows(block, index):
        return lax.dynamic_index_in_dim(block, index % seqs, 1, keepdims=False)

    here = [
        seq_rows(lax.dynamic_slice_in_dim(own, (d ^ j) * quarter, quarter, 0), g)
        for j in range(head_count)
    ]
    near_tokens = jnp.concatenate(here)
    my_quarter = lax.dynamic_slice_in_dim(own, d * quarter, quarter, 0)
    sent = [seq_rows(my_quarter, g + k) for k in range(1, groups)]
    arrived = [over_group(x, k + 1) for k, x in enumerate(sent)]

    signed = (2 * planes - 1).astype(bf16)
    if planes.shape[0] == SETS and groups == 2:
        moves = [
            ((2 * rr + ss) * 2 + gg, (gg * places + rr) * 2 + ss)
            for gg in range(2)
            for rr in range(2)
            for ss in range(2)
        ]
        signed = lax.ppermute(signed, ("hash", "seq"), moves)
    else:
        signed = lax.all_gather(signed, "hash", axis=0, tiled=True)
        signed = lax.dynamic_slice_in_dim(signed, (r * 2 + s) * SETS, SETS, 0)
    signed = signed.transpose(1, 0, 2).reshape(BITS * SETS, HEAD_DIM)
    signed_t = jnp.concatenate([signed.T, signed.T], axis=1)
    bits = bit_rows()

    cut, out_cut = hidden_own // 2, head_width // 2
    weights = jnp.concatenate(
        [
            lax.dynamic_slice_in_dim(after(up_weight, *sent), s * cut, cut, 1).T,
            lax.dynamic_slice_in_dim(down_weight, s * cut, cut, 0),
            lax.dynamic_slice_in_dim(w_out, s * out_cut, out_cut, 0),
        ]
    )
    weights = lax.all_gather(weights, "head", axis=0)
    w_qkv_t = lax.dynamic_slice_in_dim(w_qkv.transpose(0, 2, 1), s * out_cut, out_cut, 1)

    head_n = head_width // HEAD_DIM

    def project(w, rows_in):
        out = jnp.einsum("cde,ld->cel", w, rows_in, preferred_element_type=f32)
        return out.astype(bf16).reshape(-1, rows_in.shape[0])

    near_tokens = after(near_tokens, *arrived)
    near = project(w_qkv, near_tokens)
    near_z, near_o = over_place(near), over_seq(near)
    far_quarter = jnp.stack(arrived)
    moved = [over_head(far_quarter, j) for j in range(1, head_count)]
    dense_in = jnp.concatenate([here[0], *arrived])
    tables = key_tables(after(signed, dense_in), head_n, [near, near_o], None, f32)
    moved = [after(x, tables) for x in moved]

    near_z = after(near_z, tables)
    near_zo = over_seq(near_z)

    mask_pos = after(mask_pos, tables)
    slot = jnp.arange(groups, dtype=jnp.int32)[:, None]
    place_of = ((g - slot) % groups) * places + r
    position = s * half_len + place_of * piece + d * quarter + jnp.arange(quarter, dtype=jnp.int32)[None]
    mask_row = lax.dynamic_index_in_dim(mask_pos, g, 0, keepdims=False)
    cot = lax.dynamic_index_in_dim(cot_rows, g, 0, keepdims=False)
    pick = (position.reshape(rows)[:, None] == mask_row[None]).astype(bf16)
    grad_out = jnp.dot(pick, cot, preferred_element_type=f32)
    ready = after(signed, grad_out)
    tables = key_tables(ready, head_n, [near_z, near_zo], tables, f32)

    far_tokens = jnp.stack([far_quarter, *moved]).reshape(-1, width)
    far = project(w_qkv, far_tokens)
    tokens = jnp.concatenate([near_tokens, far_tokens])
    far_z, far_o = over_place(far), over_seq(far)
    n_near = near.shape[1]

    tables = key_tables(signed, head_n, [far, far_o], tables, f32)

    far_z = after(far_z, tables)
    far_zo = over_seq(far_z)
    tables = key_tables(after(signed, tokens, w_qkv_t), head_n, [far_z], tables, f32)

    far_zo = after(far_zo, tables)
    tables = key_tables(signed, head_n, [far_zo], tables, bf16)

    e_zo = query_estimates(signed, head_n, near_zo, far_zo, tables, bf16)
    e_zo_moved = over_seq(e_zo)
    e_z = query_estimates(signed, head_n, near_z, after(far_z, e_zo), tables, bf16)
    e_far = add(e_z, after(e_zo_moved, e_z)).astype(bf16)
    ready = after(far_o, e_far)
    e_o = query_estimates(signed, head_n, near_o, ready, tables, bf16)
    e_far = over_place(e_far)
    e_o_moved = over_seq(e_o)
    e = query_estimates(signed, head_n, near, after(far, e_o), tables, f32)
    e_far = after(e_far, e)
    e_o_moved = after(e_o_moved, e)
    weights = after(weights, e_far, e_o_moved)
    weights = [weights, over_seq(weights)]
    w_qkv_t = lax.all_gather(after(w_qkv_t, weights[0]), "head", axis=0)
    attn = add(e, e_o_moved, e_far).astype(bf16)

    def to_dense(block):
        parts = []
        for j in range(head_count):
            a, b = j * quarter, n_near + j * (rows - quarter)
            cut = [block[..., a : a + quarter], block[..., b : b + rows - quarter]]
            parts.append(jnp.concatenate(cut, axis=-1))
        moved = [over_head(parts[j], j) for j in range(1, head_count)]
        return [parts[0], *lax.optimization_barrier(moved)]

    attn_parts = to_dense(attn)

    def away(dense_rows):
        dense_rows = dense_rows.reshape(groups, quarter, width)
        return [dense_rows[0]] + [over_group(dense_rows[k], groups - k) for k in range(1, groups)]

    core = jnp.stack([s, d]).astype(jnp.int32)
    layer_rows, first, grad_second, slope, keep, give, heads_give, small_a = dense(
        core, dense_in, grad_out, norm_gain, norm_bias, attn_parts, weights
    )
    taken, heads_far = over_seq(give), over_seq(heads_give)
    grad_first, keep_back, give_back, *est_parts, small_b = dense_back(
        core, first, grad_second, slope, norm_gain, attn_parts, weights
    )
    taken_back = over_seq(give_back)
    est_moved = [over_head(est_parts[j], j) for j in range(1, head_count)]
    est_parts = [est_parts[0], *lax.optimization_barrier(est_moved)]
    grad = jnp.concatenate(
        [x[:, :quarter] for x in est_parts] + [x[:, quarter:] for x in est_parts], axis=1
    )
    layer_moved = away(layer_rows)
    weight_parts = weight_grads(
        core, after(small_a, grad, w_qkv_t), small_b, [keep, taken, keep_back, taken_back], attn_parts, heads_far
    )

    weight_sum = lax.psum_scatter(weight_parts, "head", scatter_dimension=0, tiled=True)[0]
    grad_z = over_place(grad)
    grad_o = after(over_seq(grad), weight_parts)
    layer_moved = [after(x, weight_parts) for x in layer_moved]
    part, dq, dq_o = query_backward(
        signed, signed_t, bits, head_n, tables, [(near, after(far, *layer_moved)), (near_o, far_o)], [grad, grad_o],
        None, False, [f32, bf16],
    )

    layer_moved = jnp.stack([after(x, part) for x in layer_moved])
    grad_z = after(grad_z, part)
    grad_zo = over_seq(grad_z)
    dq_o = over_seq(dq_o)
    part, dq_z = query_backward(
        signed, signed_t, bits, head_n, tables, [(near_z, far_z)], [grad_z], part, False, [f32]
    )

    dq_own = add(dq, after(dq_o, dq_z))
    grad_zo = after(grad_zo, dq_z)
    grad_tables, dq_zo = query_backward(
        signed, signed_t, bits, head_n, tables, [(near_zo, after(far_zo, dq_own))], [grad_zo], part, True, [bf16]
    )

    dq_zo = over_seq(dq_zo)
    w_qkv_t = after(w_qkv_t, grad_tables)
    w_qkv_far = over_seq(w_qkv_t)
    dkv_zo = key_backward(signed, signed_t, bits, head_n, near_zo, far_zo, grad_tables, bf16)

    dkv_zo_moved = over_seq(dkv_zo)
    dq_far = add(dq_z, after(dq_zo, dkv_zo)).astype(bf16)
    layer_moved = [layer_moved] + [over_head(layer_moved, j) for j in range(1, head_count)]
    dkv_z = key_backward(signed, signed_t, bits, head_n, near_z, after(far_z, dq_far), grad_tables, bf16)
    dq_far = over_place(dq_far)

    dkv_far = add(dkv_z, after(dkv_zo_moved, dkv_z)).astype(bf16)
    grad_q = add(dq_own, after(dq_far, dkv_z)).astype(bf16)
    weight_sum = after(weight_sum, dkv_z)
    layer_moved = [after(x, dkv_z) for x in layer_moved]
    dkv_o = key_backward(
        signed, signed_t, bits, head_n, near_o, after(far_o, dkv_far, grad_q, weight_sum, *layer_moved),
        grad_tables, bf16, 25,
    )
    weight_sum = lax.psum(weight_sum, "hash")
    dkv_far = over_place(dkv_far)
    dkv_o_moved = over_seq(dkv_o)
    dkv = key_backward(
        signed, signed_t, bits, head_n, near, far, grad_tables, f32, 25
    )

    dkv_o_moved = after(dkv_o_moved, dkv)
    grad_kv = add(dkv, dkv_o_moved, after(dkv_far, dkv)).astype(bf16)
    grad_qkv = jnp.concatenate([grad_q[None], grad_kv])
    qkv_parts = to_dense(grad_qkv)

    grad_in = input_grad(core, grad_first, qkv_parts, w_qkv_t, after(w_qkv_far, dkv))

    def in_halves(index, mine, other):
        first = jnp.where(index == 0, mine, other)
        second = jnp.where(index == 0, other, mine)
        return jnp.concatenate([first, second], axis=0)

    def split(x, index):
        half = x.shape[0] // 2
        return [lax.dynamic_slice_in_dim(x, at * half, half, 0) for at in (index, 1 - index)]

    w_grad = dot(grad_qkv.reshape(3 * head_width, n_tokens), tokens, NN).astype(bf16)
    w_keep, w_send = split(w_grad, s)
    w_keep, w_send = split(add(w_keep, over_seq(w_send)).astype(bf16), r)
    grad_moved = away(grad_in)
    w_keep = add(w_keep, over_place(w_send))
    w_send = w_keep.astype(bf16)
    grad_moved = after(jnp.stack(grad_moved), w_send)
    w_keep = add(w_keep, *[over_group(w_send, k) for k in range(1, groups)]).astype(bf16)
    grad_moved = [grad_moved] + [over_head(grad_moved, j) for j in range(1, head_count)]

    def home(blocks):
        table = jnp.stack(blocks)
        columns = []
        for q_at in range(head_count):
            block = lax.dynamic_index_in_dim(table, q_at ^ d, 0, keepdims=False)
            columns.append(
                jnp.stack(
                    [
                        lax.dynamic_index_in_dim(block, (at - g) % groups, 0, keepdims=False)
                        for at in range(seqs)
                    ],
                    axis=1,
                )
            )
        return jnp.concatenate(columns, axis=0)

    layer_out = home([after(x, grad_moved[0]) for x in layer_moved])
    grad_inputs = home(grad_moved).astype(f32)

    w_grad = in_halves(r, w_keep, over_place(w_keep))
    w_grad = in_halves(s, w_grad, over_seq(w_grad)).reshape(3, head_width, width)
    grad_w_qkv = w_grad.transpose(0, 2, 1).astype(f32)
    weight_sum = after(weight_sum, *grad_moved)
    weight_far = over_seq(weight_sum)
    grad_w_up, grad_w_down, grad_w_out = weight_results(core, weight_sum, weight_far, head_width)
    at = slice(2 * cut + out_cut, 2 * cut + out_cut + 16)
    small = add(weight_sum[at], weight_far[at])

    count = piece * seqs * width * hash_count * 2
    stream_rms = jnp.sqrt(jnp.sum(small[0:3], axis=1) / count)
    share = width // head_count
    norm_grads = lax.dynamic_slice_in_dim(small, d * share, share, 1)
    return (
        layer_out[None],
        grad_inputs[None],
        grad_w_qkv,
        grad_w_out,
        grad_w_up,
        grad_w_down,
        jnp.stack([norm_grads[8], norm_grads[3]]),
        jnp.stack([norm_grads[9], norm_grads[4]]),
        stream_rms,
    )


def solution(mesh):
    placed = (
        P("seq", "hash", None, None),
        P(None, None, "head"),
        P("head", None),
        P(None, "head"),
        P("head", None),
        P(),
        P(),
        P("hash", None, None),
        P(),
        P(),
    )
    return jax.shard_map(
        shards,
        mesh=mesh,
        in_specs=placed,
        out_specs=(
            P("seq", "hash", None, None),
            P("seq", "hash", None, None),
            P(None, None, "head"),
            P("head", None),
            P(None, "head"),
            P("head", None),
            P(None, "head"),
            P(None, "head"),
            P(),
        ),
        check_vma=False,
    )
```

```python
from functools import partial

import jax
import jax.numpy as jnp
import numpy as np
from jax import lax
from jax.experimental import pallas as pl
from jax.experimental.pallas import tpu as pltpu
from jax.sharding import PartitionSpec as P

HEAD_DIM = 64
HASHES = 32
BITS = 8
SETS = 8
BUCKETS = 1 << BITS
ROWS = BUCKETS * SETS

bf16 = jnp.bfloat16
f32 = jnp.float32
NN = (((1,), (0,)), ((), ()))
NT = (((1,), (1,)), ((), ()))
TN = (((0,), (0,)), ((), ()))


shape = jax.ShapeDtypeStruct


def dot(a, b, dims):
    return lax.dot_general(a, b, dims, preferred_element_type=f32)


def sides(rows, planes):
    x = rows.astype(f32)
    inv = lax.rsqrt(jnp.sum(x * x, axis=0, keepdims=True) + 1e-6)
    proj = dot(planes, rows, NN) * (3.0 * inv)
    small = jnp.exp(-proj)
    upper = 1.0 / (1.0 + small)
    return inv, upper, small * upper


def products(upper, lower, first, count):
    out = None
    for i in range(first, first + count):
        lo, up = lower[SETS * i : SETS * (i + 1)], upper[SETS * i : SETS * (i + 1)]
        out = [lo, up] if out is None else [c * lo for c in out] + [c * up for c in out]
    return out


def half_codes(upper, lower):
    low = jnp.concatenate(products(upper, lower, 0, 4), axis=0).astype(bf16)
    high = [jnp.concatenate([a, a], axis=0).astype(bf16) for a in products(upper, lower, 4, 4)]
    return low, high


def code_chunk(low, high, first, count):
    return jnp.concatenate(
        [high[a] * low[16 * j : 16 * (j + 1)] for a in range(first, first + count) for j in range(8)],
        axis=0,
    )


def pull_back(rows, planes_t, inv, upper, sums):
    total = sums[BITS * SETS :][:SETS]
    grad_proj = sums[: BITS * SETS] - upper * jnp.concatenate([total] * BITS, axis=0)
    head = grad_proj.astype(bf16)
    tail = (grad_proj - head.astype(f32)).astype(bf16)
    grad_unit = dot(planes_t, jnp.concatenate([head, tail], axis=0), NN) * (3.0 * inv)
    x = rows.astype(f32)
    return grad_unit - x * (inv * inv * jnp.sum(x * grad_unit, axis=0, keepdims=True))


def both(*refs):
    return jnp.concatenate([ref[...] for ref in refs], axis=1)


def key_kernel(planes, *refs, chunk, blocks):
    keys, vals, out = refs[:blocks], refs[blocks : 2 * blocks], refs[-1]
    start = refs[2 * blocks] if len(refs) > 2 * blocks + 1 else None
    _, upper, lower = sides(both(*keys), planes[...])
    low, high = half_codes(upper, lower)
    values = both(*vals)
    for c in range(0, 16, chunk):
        at = slice(128 * c, 128 * (c + chunk))
        part = dot(code_chunk(low, high, c, chunk), values, NT)
        if start is not None:
            part = part + start[0, at, :]
        out[0, at, :] = part.astype(out.dtype)


def query_kernel(planes, tables, *refs, chunk):
    rows, out = both(*refs[:-1]), refs[-1]
    _, upper, lower = sides(rows, planes[...])
    low, high = half_codes(upper, lower)
    acc = jnp.zeros((HEAD_DIM, rows.shape[1]), f32)
    for c in range(0, 16, chunk):
        acc += dot(tables[0, 128 * c : 128 * (c + chunk), :], code_chunk(low, high, c, chunk), TN)
    out[...] = (acc * (1.0 / HASHES)).astype(out.dtype)


def query_back_kernel(planes, planes_t, bits, tables, *refs, chunk, blocks, last):
    queries, grads = refs[: 2 * blocks], refs[2 * blocks : 3 * blocks]
    start = refs[3 * blocks] if len(refs) > 4 * blocks + 1 else None
    out, back_out = refs[-1 - blocks], refs[-blocks:]
    rows = both(*queries)
    inv, upper, lower = sides(rows, planes[...])
    low, high = half_codes(upper, lower)
    grad = both(*grads)
    sums = jnp.zeros((bits.shape[0], rows.shape[1]), f32)
    for c in range(0, 16, chunk):
        at = slice(128 * c, 128 * (c + chunk))
        codes = code_chunk(low, high, c, chunk)
        part = dot(codes, grad, NT)
        if start is not None:
            part = part + start[0, at, :]
        if last:
            part = part * (1.0 / HASHES)
        out[0, at, :] = part.astype(out.dtype)
        weighted = dot(tables[0, at, :], grad, NN).astype(bf16) * codes
        sums += dot(bits[:, at], weighted, NN)
    back = pull_back(rows, planes_t[...], inv, upper, sums * (1.0 / HASHES))
    width = back_out[0].shape[1]
    for i in range(blocks):
        back_out[i][...] = back[:, i * width : (i + 1) * width].astype(back_out[i].dtype)


def key_back_kernel(planes, planes_t, bits, ka, kb, va, vb, grad_tables, out, *, chunk):
    rows = both(ka, kb)
    inv, upper, lower = sides(rows, planes[...])
    low, high = half_codes(upper, lower)
    values = both(va, vb)
    width = rows.shape[1]
    sums = jnp.zeros((bits.shape[0], width), f32)
    grad_values = jnp.zeros((HEAD_DIM, width), f32)
    for c in range(0, 16, chunk):
        at = slice(128 * c, 128 * (c + chunk))
        codes = code_chunk(low, high, c, chunk)
        grad_values += dot(grad_tables[0, at, :], codes, TN)
        weighted = dot(grad_tables[0, at, :], values, NN).astype(bf16) * codes
        sums += dot(bits[:, at], weighted, NN)
    out[0] = pull_back(rows, planes_t[...], inv, upper, sums).astype(out.dtype)
    out[1] = grad_values.astype(out.dtype)


def bit_rows():
    out = np.zeros((80, BUCKETS, SETS), np.float32)
    for t in range(SETS):
        for i in range(BITS):
            out[i * SETS + t, :, t] = (np.arange(BUCKETS) >> i) & 1
        out[BITS * SETS + t, :, t] = 1
    return jnp.asarray(out.reshape(80, ROWS), bf16)


def whole(*shape):
    return pl.BlockSpec(shape, lambda h: (0,) * len(shape))


def head_rows(array, heads, which):
    width = array.shape[1]
    offset = (which - 3) * heads + array.shape[0] // HEAD_DIM
    return pl.BlockSpec((HEAD_DIM, width), lambda h: (h + offset, 0))


def per_head(width):
    return pl.BlockSpec((HEAD_DIM, width), lambda h: (h, 0))


def table_spec():
    return pl.BlockSpec((1, ROWS, HEAD_DIM), lambda h: (h, 0, 0))


def call(kernel, heads, micros, name, in_specs, out_specs, out_shape):
    return pl.pallas_call(
        kernel,
        grid=(heads,),
        in_specs=in_specs,
        out_specs=out_specs,
        out_shape=out_shape,
        compiler_params=pltpu.CompilerParams(vmem_limit_bytes=48 << 20),
        cost_estimate=pl.CostEstimate(
            flops=int(micros * 1.1e9), bytes_accessed=1 << 20, transcendentals=0
        ),
        name=name,
    )


def key_tables(planes, heads, blocks, start, kind):
    args = [planes, *blocks, *blocks]
    specs = [whole(64, 64)] + [head_rows(x, heads, w) for w in (1, 2) for x in blocks]
    if start is not None:
        specs.append(table_spec())
        args.append(start)
    return call(
        partial(key_kernel, chunk=2, blocks=len(blocks)),
        heads,
        30 if len(blocks) > 1 and start is not None else 1,
        "key_tables",
        specs,
        table_spec(),
        shape((heads, ROWS, HEAD_DIM), kind),
    )(*args)


def query_estimates(planes, heads, near, far, tables, kind):
    width = near.shape[1] + far.shape[1]
    return call(
        partial(query_kernel, chunk=2),
        heads,
        1,
        "query_estimates",
        [whole(64, 64), table_spec(), head_rows(near, heads, 0), head_rows(far, heads, 0)],
        per_head(width),
        shape((heads * HEAD_DIM, width), kind),
    )(planes, tables, near, far)


def query_backward(planes, planes_t, bits, heads, tables, queries, grads, start, last, kinds):
    width = grads[0].shape[1]
    blocks = len(grads)
    specs = [whole(64, 64), whole(64, 128), whole(80, ROWS), table_spec()]
    args = [planes, planes_t, bits, tables]
    for near, far in queries:
        specs += [head_rows(near, heads, 0), head_rows(far, heads, 0)]
        args += [near, far]
    specs += [per_head(width)] * blocks
    args += grads
    if start is not None:
        specs.append(table_spec())
        args.append(start)
    return call(
        partial(query_back_kernel, chunk=4 * blocks, blocks=blocks, last=last),
        heads,
        25 * blocks,
        "query_backward",
        specs,
        [table_spec()] + [per_head(width)] * blocks,
        [shape((heads, ROWS, HEAD_DIM), bf16 if last else f32)]
        + [shape(grads[0].shape, kind) for kind in kinds],
    )(*args)


def key_backward(planes, planes_t, bits, heads, near, far, grad_tables, kind, micros=25):
    width = near.shape[1] + far.shape[1]
    return call(
        partial(key_back_kernel, chunk=4),
        heads,
        micros,
        "key_backward",
        [whole(64, 64), whole(64, 128), whole(80, ROWS)]
        + [head_rows(x, heads, w) for w in (1, 2) for x in (near, far)]
        + [table_spec()],
        pl.BlockSpec((2, HEAD_DIM, width), lambda h: (0, h, 0)),
        shape((2, heads * HEAD_DIM, width), kind),
    )(planes, planes_t, bits, near, far, near, far, grad_tables)


def norm(x):
    center = x - jnp.mean(x, axis=-1, keepdims=True)
    inv = lax.rsqrt(jnp.mean(center * center, axis=-1, keepdims=True) + 1e-5)
    return center * inv, inv


def norm_back(grad, unit, inv):
    return inv * (
        grad
        - jnp.mean(grad, axis=-1, keepdims=True)
        - unit * jnp.mean(grad * unit, axis=-1, keepdims=True)
    )


def column_sum(x):
    return jnp.sum(x, axis=0, keepdims=True)


def core_rows(core, ref, which):
    half = ref.shape[0] // 2
    at = core[0] if which == 0 else 1 - core[0]
    return ref[pl.ds(pl.multiple_of(at * half, 16), half), :]


def share_rows(keep, give, at, rows):
    part = keep.shape[2]
    for out in (keep, give):
        out[at] = rows[:, :part]
        out[at + 1] = rows[:, part:]


def dense_kernel(core, x_in, grad_out, gain, bias, *refs):
    attn, weights = refs[0:4], refs[4:6]
    layer_out, first_out, grad_second_out, slope, keep, give, heads_give, small = refs[6:14]
    owner = [core[1] ^ (b // 2) for b in range(8)]
    for j in range(4):
        heads_give[j] = core_rows(core, attn[j], 1)
    part = slope.shape[2]
    blocks = range(8)
    heads = jnp.concatenate([core_rows(core, attn[b // 2], b % 2) for b in blocks], axis=0)
    out_w = jnp.concatenate([weights[b % 2][owner[b], 2 * part :, :] for b in blocks], axis=0)
    attn_out = dot(heads, out_w, TN)
    resid = x_in[...].astype(f32)
    first = resid + attn_out
    first_out[...] = first
    small[0:1, :] = column_sum(resid * resid)
    small[1:2, :] = column_sum(attn_out * attn_out)
    small[2:3, :] = column_sum(first * first)
    unit_1, _ = norm(first)
    normed = (unit_1 * gain[0:1, :] + bias[0:1, :]).astype(bf16)
    share_rows(keep, give, 4, normed)
    second = normed.astype(f32)
    for b in blocks:
        pre = dot(normed, weights[b % 2][owner[b], 0:part, :], NT)
        below = 0.5 * (1.0 + lax.erf(pre * 0.7071067811865476))
        rows = (pre * below).astype(bf16)
        (keep, give)[b % 2][b // 2] = rows
        slope[b] = below + pre * (0.3989422804014327 * jnp.exp(-0.5 * pre * pre))
        second = second + dot(rows, weights[b % 2][owner[b], part : 2 * part, :], NN)
    unit_2, inv_2 = norm(second)
    layer_out[...] = (unit_2 * gain[1:2, :] + bias[1:2, :]).astype(layer_out.dtype)
    grad = grad_out[...]
    small[3:4, :] = column_sum(grad * unit_2)
    small[4:5, :] = column_sum(grad)
    small[5:8, :] = jnp.zeros_like(small[5:8, :])
    grad_second = norm_back(grad * gain[1:2, :], unit_2, inv_2)
    grad_second_out[...] = grad_second
    share_rows(keep, give, 6, grad_second.astype(bf16))


def dense_back_kernel(core, first, grad_second, slope, gain, *refs):
    weights = refs[0:2]
    grad_first_out, keep, give = refs[2:5]
    estimates, small = refs[5:9], refs[9]
    owner = [core[1] ^ (b // 2) for b in range(8)]
    part = slope.shape[2]
    blocks = range(8)
    grad_normed = grad_second[...]
    grad_ffn = grad_normed.astype(bf16)
    for b in blocks:
        rows = dot(grad_ffn, weights[b % 2][owner[b], part : 2 * part, :], NT)
        rows = (rows * slope[b]).astype(bf16)
        (keep, give)[b % 2][b // 2] = rows
        grad_normed = grad_normed + dot(rows, weights[b % 2][owner[b], 0:part, :], NN)
    unit, inv = norm(first[...])
    small[0:1, :] = column_sum(grad_normed * unit)
    small[1:2, :] = column_sum(grad_normed)
    small[2:8, :] = jnp.zeros_like(small[2:8, :])
    grad_first = norm_back(grad_normed * gain[0:1, :], unit, inv)
    grad_first_out[...] = grad_first
    grad_attn = grad_first.astype(bf16)
    share_rows(keep, give, 4, grad_attn)
    for b in blocks:
        half = estimates[0].shape[0] // 2
        at = core[0] if b % 2 == 0 else 1 - core[0]
        estimates[b // 2][pl.ds(pl.multiple_of(at * half, 16), half), :] = dot(
            weights[b % 2][owner[b], 2 * part :, :], grad_attn, NT
        ).astype(bf16)


def weight_grad_kernel(core, small_a, small_b, *refs):
    near, far, near_back, far_back = refs[0:4]
    attn, attn_far, out = refs[4:8], refs[8], refs[9]
    part = near.shape[2]
    sums = jnp.concatenate([small_a[...], small_b[...]], axis=0).astype(bf16)

    def wide(ref, at):
        return jnp.concatenate([ref[at], ref[at + 1]], axis=1)

    def rows(ref, other, at):
        return jnp.concatenate([wide(ref, at), wide(other, at)], axis=0)

    normed, grad_ffn = rows(near, far, 4), rows(near, far, 6)
    grad_attn = rows(near_back, far_back, 4)
    for j in range(4):
        owner = core[1] ^ j
        hidden = jnp.concatenate([near[j], far[j]], axis=0)
        grad_pre = jnp.concatenate([near_back[j], far_back[j]], axis=0)
        out[owner, 0:part, :] = dot(grad_pre, normed, TN).astype(bf16)
        out[owner, part : 2 * part, :] = dot(hidden, grad_ffn, TN).astype(bf16)
        heads = jnp.concatenate([core_rows(core, attn[j], 0), attn_far[j]], axis=1)
        at = 2 * part + heads.shape[0]
        out[owner, 2 * part : at, :] = dot(heads, grad_attn, NN).astype(bf16)
        out[owner, at : at + 16, :] = sums
        out[owner, at + 16 :, :] = jnp.zeros_like(sums)


def input_grad_kernel(core, grad_first, *refs):
    blocks, near, far, out = refs[0:4], refs[4], refs[5], refs[6]
    half = near.shape[2]
    total = grad_first[...]
    for which, halves in enumerate((near, far)):
        at = core[0] if which == 0 else 1 - core[0]
        at = pl.ds(pl.multiple_of(at * half, 16), half)
        for j in range(4):
            rows = jnp.concatenate([blocks[j][c, at, :] for c in range(3)], axis=0)
            weights = jnp.concatenate([halves[core[1] ^ j, c] for c in range(3)], axis=0)
            total = total + dot(rows, weights, TN)
    out[...] = total.astype(out.dtype)


def vmem(count):
    return [pl.BlockSpec(memory_space=pltpu.VMEM)] * count


def single(kernel, core, args, out_shape, micros, name, scratch=()):
    return pl.pallas_call(
        kernel,
        in_specs=[pl.BlockSpec(memory_space=pltpu.SMEM)] + vmem(len(args)),
        out_specs=vmem(len(out_shape)),
        out_shape=out_shape,
        scratch_shapes=scratch,
        compiler_params=pltpu.CompilerParams(vmem_limit_bytes=56 << 20),
        cost_estimate=pl.CostEstimate(
            flops=int(micros * 1.1e9), bytes_accessed=1 << 20, transcendentals=0
        ),
        name=name,
    )(core, *args)


def dense(core, x_in, grad_out, gain, bias, attn, weights):
    rows, width = x_in.shape
    part = (weights[0].shape[1] - attn[0].shape[0] // 2) // 2
    out_shape = [
        shape((rows, width), bf16),
        shape((rows, width), f32),
        shape((rows, width), f32),
        shape((8, rows, part), f32),
        shape((8, rows, part), bf16),
        shape((8, rows, part), bf16),
        shape((4, attn[0].shape[0] // 2, rows), bf16),
        shape((8, width), f32),
    ]
    args = [x_in, grad_out, gain, bias, *attn, *weights]
    return single(dense_kernel, core, args, out_shape, 14, "dense")


def dense_back(core, first, grad_second, slope, gain, attn, weights):
    rows, width = first.shape
    part = (weights[0].shape[1] - attn[0].shape[0] // 2) // 2
    out_shape = [
        shape((rows, width), f32),
        shape((6, rows, part), bf16),
        shape((6, rows, part), bf16),
        *[shape(attn[0].shape, bf16)] * 4,
        shape((8, width), f32),
    ]
    args = [first, grad_second, slope, gain, *weights]
    return single(dense_back_kernel, core, args, out_shape, 8, "dense_back")


def weight_grads(core, small_a, small_b, shared, attn, attn_far):
    part, width = shared[0].shape[2], small_a.shape[1]
    out_shape = [shape((4, 2 * part + attn[0].shape[0] // 2 + 32, width), bf16)]
    args = [small_a, small_b, *shared, *attn, attn_far]
    return single(weight_grad_kernel, core, args, out_shape, 7, "weight_grads")[0]


def weight_results_kernel(core, near, far, up, down, out):
    part, rows = up.shape[1] // 2, out.shape[0] // 2
    for which, ref in enumerate((near, far)):
        at = core[0] if which == 0 else 1 - core[0]
        at_part = pl.ds(pl.multiple_of(at * part, 128), part)
        up[:, at_part] = ref[0:part, :].astype(f32).T
        down[at_part, :] = ref[part : 2 * part, :].astype(f32)
        at_rows = pl.ds(pl.multiple_of(at * rows, 16), rows)
        out[at_rows, :] = ref[2 * part : 2 * part + rows, :].astype(f32)


def weight_results(core, near, far, head_width):
    width = near.shape[1]
    part = (near.shape[0] - 32 - head_width // 2) // 2
    out_shape = [
        shape((width, 2 * part), f32), shape((2 * part, width), f32), shape((head_width, width), f32)
    ]
    return single(weight_results_kernel, core, [near, far], out_shape, 3, "weight_results")


def input_grad(core, grad_first, blocks, near, far):
    out_shape = [shape(grad_first.shape, bf16)]
    args = [grad_first, *blocks, near, far]
    return single(input_grad_kernel, core, args, out_shape, 40, "input_grad")[0]


def after(x, *others):
    return lax.optimization_barrier((x, *others))[0]


def add(a, *others):
    return sum([b.astype(f32) for b in others], a.astype(f32))


def shards(
    inputs,
    w_qkv,
    w_out,
    up_weight,
    down_weight,
    norm_gain,
    norm_bias,
    planes,
    mask_pos,
    cot_rows,
):
    own = inputs[0]
    piece, seqs, width = own.shape
    hash_count, head_count = lax.axis_size("hash"), lax.axis_size("head")
    groups, places = seqs, hash_count // seqs
    assert places == 2 and lax.axis_size("seq") == 2 and head_count == 4
    assert planes.shape[0] * hash_count == 4 * SETS
    quarter = piece // head_count
    rows = groups * quarter
    half_len = piece * hash_count
    head_width = w_out.shape[0]
    hidden_own = down_weight.shape[0]
    n_tokens = head_count * rows
    hash_id, d, s = lax.axis_index("hash"), lax.axis_index("head"), lax.axis_index("seq")
    g, r = hash_id // places, hash_id % places

    def over_seq(x):
        return lax.ppermute(x, "seq", [(0, 1), (1, 0)])

    def over_place(x):
        return lax.ppermute(x, "hash", [(h, h ^ 1) for h in range(hash_count)])

    def over_group(x, k):
        moves = [(h, ((h // places + k) % groups) * places + h % places) for h in range(hash_count)]
        return lax.ppermute(x, "hash", moves)

    def over_head(x, j):
        return lax.ppermute(x, "head", [(h, h ^ j) for h in range(head_count)])

    def seq_rows(block, index):
        return lax.dynamic_index_in_dim(block, index % seqs, 1, keepdims=False)

    here = [
        seq_rows(lax.dynamic_slice_in_dim(own, (d ^ j) * quarter, quarter, 0), g)
        for j in range(head_count)
    ]
    near_tokens = jnp.concatenate(here)
    my_quarter = lax.dynamic_slice_in_dim(own, d * quarter, quarter, 0)
    sent = [seq_rows(my_quarter, g + k) for k in range(1, groups)]
    arrived = [over_group(x, k + 1) for k, x in enumerate(sent)]

    signed = (2 * planes - 1).astype(bf16)
    if planes.shape[0] == SETS and groups == 2:
        moves = [
            ((2 * rr + ss) * 2 + gg, (gg * places + rr) * 2 + ss)
            for gg in range(2)
            for rr in range(2)
            for ss in range(2)
        ]
        signed = lax.ppermute(signed, ("hash", "seq"), moves)
    else:
        signed = lax.all_gather(signed, "hash", axis=0, tiled=True)
        signed = lax.dynamic_slice_in_dim(signed, (r * 2 + s) * SETS, SETS, 0)
    signed = signed.transpose(1, 0, 2).reshape(BITS * SETS, HEAD_DIM)
    signed_t = jnp.concatenate([signed.T, signed.T], axis=1)
    bits = bit_rows()

    cut, out_cut = hidden_own // 2, head_width // 2
    weights = jnp.concatenate(
        [
            lax.dynamic_slice_in_dim(after(up_weight, *sent), s * cut, cut, 1).T,
            lax.dynamic_slice_in_dim(down_weight, s * cut, cut, 0),
            lax.dynamic_slice_in_dim(w_out, s * out_cut, out_cut, 0),
        ]
    )
    weights = lax.all_gather(weights, "head", axis=0)
    w_qkv_t = lax.dynamic_slice_in_dim(w_qkv.transpose(0, 2, 1), s * out_cut, out_cut, 1)

    head_n = head_width // HEAD_DIM

    def project(w, rows_in):
        out = jnp.einsum("cde,ld->cel", w, rows_in, preferred_element_type=f32)
        return out.astype(bf16).reshape(-1, rows_in.shape[0])

    near_tokens = after(near_tokens, *arrived)
    near = project(w_qkv, near_tokens)
    near_z, near_o = over_place(near), over_seq(near)
    far_quarter = jnp.stack(arrived)
    moved = [over_head(far_quarter, j) for j in range(1, head_count)]
    dense_in = jnp.concatenate([here[0], *arrived])
    tables = key_tables(after(signed, dense_in), head_n, [near, near_o], None, f32)
    moved = [after(x, tables) for x in moved]

    near_z = after(near_z, tables)
    near_zo = over_seq(near_z)

    mask_pos = after(mask_pos, tables)
    slot = jnp.arange(groups, dtype=jnp.int32)[:, None]
    place_of = ((g - slot) % groups) * places + r
    position = s * half_len + place_of * piece + d * quarter + jnp.arange(quarter, dtype=jnp.int32)[None]
    mask_row = lax.dynamic_index_in_dim(mask_pos, g, 0, keepdims=False)
    cot = lax.dynamic_index_in_dim(cot_rows, g, 0, keepdims=False)
    pick = (position.reshape(rows)[:, None] == mask_row[None]).astype(bf16)
    grad_out = jnp.dot(pick, cot, preferred_element_type=f32)
    ready = after(signed, grad_out)
    tables = key_tables(ready, head_n, [near_z, near_zo], tables, f32)

    far_tokens = jnp.stack([far_quarter, *moved]).reshape(-1, width)
    far = project(w_qkv, far_tokens)
    tokens = jnp.concatenate([near_tokens, far_tokens])
    far_z, far_o = over_place(far), over_seq(far)
    n_near = near.shape[1]

    tables = key_tables(signed, head_n, [far, far_o], tables, f32)

    far_z = after(far_z, tables)
    far_zo = over_seq(far_z)
    tables = key_tables(after(signed, tokens, w_qkv_t), head_n, [far_z], tables, f32)

    far_zo = after(far_zo, tables)
    tables = key_tables(signed, head_n, [far_zo], tables, bf16)

    e_zo = query_estimates(signed, head_n, near_zo, far_zo, tables, bf16)
    e_zo_moved = over_seq(e_zo)
    e_z = query_estimates(signed, head_n, near_z, after(far_z, e_zo), tables, bf16)
    e_far = add(e_z, after(e_zo_moved, e_z)).astype(bf16)
    ready = after(far_o, e_far)
    e_o = query_estimates(signed, head_n, near_o, ready, tables, bf16)
    e_far = over_place(e_far)
    e_o_moved = over_seq(e_o)
    e = query_estimates(signed, head_n, near, after(far, e_o), tables, f32)
    e_far = after(e_far, e)
    e_o_moved = after(e_o_moved, e)
    weights = after(weights, e_far, e_o_moved)
    weights = [weights, over_seq(weights)]
    w_qkv_t = lax.all_gather(after(w_qkv_t, weights[0]), "head", axis=0)
    attn = add(e, e_o_moved, e_far).astype(bf16)

    def to_dense(block):
        parts = []
        for j in range(head_count):
            a, b = j * quarter, n_near + j * (rows - quarter)
            cut = [block[..., a : a + quarter], block[..., b : b + rows - quarter]]
            parts.append(jnp.concatenate(cut, axis=-1))
        moved = [over_head(parts[j], j) for j in range(1, head_count)]
        return [parts[0], *lax.optimization_barrier(moved)]

    attn_parts = to_dense(attn)

    def away(dense_rows):
        dense_rows = dense_rows.reshape(groups, quarter, width)
        return [dense_rows[0]] + [over_group(dense_rows[k], groups - k) for k in range(1, groups)]

    core = jnp.stack([s, d]).astype(jnp.int32)
    layer_rows, first, grad_second, slope, keep, give, heads_give, small_a = dense(
        core, dense_in, grad_out, norm_gain, norm_bias, attn_parts, weights
    )
    taken, heads_far = over_seq(give), over_seq(heads_give)
    grad_first, keep_back, give_back, *est_parts, small_b = dense_back(
        core, first, grad_second, slope, norm_gain, attn_parts, weights
    )
    taken_back = over_seq(give_back)
    est_moved = [over_head(est_parts[j], j) for j in range(1, head_count)]
    est_parts = [est_parts[0], *lax.optimization_barrier(est_moved)]
    grad = jnp.concatenate(
        [x[:, :quarter] for x in est_parts] + [x[:, quarter:] for x in est_parts], axis=1
    )
    layer_moved = away(layer_rows)
    weight_parts = weight_grads(
        core, after(small_a, grad, w_qkv_t), small_b, [keep, taken, keep_back, taken_back], attn_parts, heads_far
    )

    weight_sum = lax.psum_scatter(weight_parts, "head", scatter_dimension=0, tiled=True)[0]
    grad_z = over_place(grad)
    grad_o = after(over_seq(grad), weight_parts)
    layer_moved = [after(x, weight_parts) for x in layer_moved]
    part, dq, dq_o = query_backward(
        signed, signed_t, bits, head_n, tables, [(near, after(far, *layer_moved)), (near_o, far_o)], [grad, grad_o],
        None, False, [f32, bf16],
    )

    layer_moved = jnp.stack([after(x, part) for x in layer_moved])
    grad_z = after(grad_z, part)
    grad_zo = over_seq(grad_z)
    dq_o = over_seq(dq_o)
    part, dq_z = query_backward(
        signed, signed_t, bits, head_n, tables, [(near_z, far_z)], [grad_z], part, False, [f32]
    )

    dq_own = add(dq, after(dq_o, dq_z))
    grad_zo = after(grad_zo, dq_z)
    grad_tables, dq_zo = query_backward(
        signed, signed_t, bits, head_n, tables, [(near_zo, after(far_zo, dq_own))], [grad_zo], part, True, [bf16]
    )

    dq_zo = over_seq(dq_zo)
    w_qkv_t = after(w_qkv_t, grad_tables)
    w_qkv_far = over_seq(w_qkv_t)
    dkv_zo = key_backward(signed, signed_t, bits, head_n, near_zo, far_zo, grad_tables, bf16)

    dkv_zo_moved = over_seq(dkv_zo)
    dq_far = add(dq_z, after(dq_zo, dkv_zo)).astype(bf16)
    layer_moved = [layer_moved] + [over_head(layer_moved, j) for j in range(1, head_count)]
    dkv_z = key_backward(signed, signed_t, bits, head_n, near_z, after(far_z, dq_far), grad_tables, bf16)
    dq_far = over_place(dq_far)

    dkv_far = add(dkv_z, after(dkv_zo_moved, dkv_z)).astype(bf16)
    grad_q = add(dq_own, after(dq_far, dkv_z)).astype(bf16)
    weight_sum = after(weight_sum, dkv_z)
    layer_moved = [after(x, dkv_z) for x in layer_moved]
    dkv_o = key_backward(
        signed, signed_t, bits, head_n, near_o, after(far_o, dkv_far, grad_q, weight_sum, *layer_moved),
        grad_tables, bf16, 25,
    )
    weight_sum = lax.psum(weight_sum, "hash")
    dkv_far = over_place(dkv_far)
    dkv_o_moved = over_seq(dkv_o)
    dkv = key_backward(
        signed, signed_t, bits, head_n, near, after(far, dkv_o), grad_tables, f32, 25
    )

    dkv_o_moved = after(dkv_o_moved, dkv)
    grad_kv = add(dkv, dkv_o_moved, after(dkv_far, dkv)).astype(bf16)
    grad_qkv = jnp.concatenate([grad_q[None], grad_kv])
    qkv_parts = to_dense(grad_qkv)

    grad_in = input_grad(core, grad_first, qkv_parts, w_qkv_t, after(w_qkv_far, dkv))

    def in_halves(index, mine, other):
        first = jnp.where(index == 0, mine, other)
        second = jnp.where(index == 0, other, mine)
        return jnp.concatenate([first, second], axis=0)

    def split(x, index):
        half = x.shape[0] // 2
        return [lax.dynamic_slice_in_dim(x, at * half, half, 0) for at in (index, 1 - index)]

    w_grad = dot(grad_qkv.reshape(3 * head_width, n_tokens), tokens, NN).astype(bf16)
    w_keep, w_send = split(w_grad, s)
    w_keep, w_send = split(add(w_keep, over_seq(w_send)).astype(bf16), r)
    grad_moved = away(grad_in)
    w_keep = add(w_keep, over_place(w_send))
    w_send = w_keep.astype(bf16)
    grad_moved = after(jnp.stack(grad_moved), w_send)
    w_keep = add(w_keep, *[over_group(w_send, k) for k in range(1, groups)]).astype(bf16)
    grad_moved = [grad_moved] + [over_head(grad_moved, j) for j in range(1, head_count)]

    def home(blocks):
        table = jnp.stack(blocks)
        columns = []
        for q_at in range(head_count):
            block = lax.dynamic_index_in_dim(table, q_at ^ d, 0, keepdims=False)
            columns.append(
                jnp.stack(
                    [
                        lax.dynamic_index_in_dim(block, (at - g) % groups, 0, keepdims=False)
                        for at in range(seqs)
                    ],
                    axis=1,
                )
            )
        return jnp.concatenate(columns, axis=0)

    layer_out = home([after(x, grad_moved[0]) for x in layer_moved])
    grad_inputs = home(grad_moved).astype(f32)

    w_grad = in_halves(r, w_keep, over_place(w_keep))
    w_grad = in_halves(s, w_grad, over_seq(w_grad)).reshape(3, head_width, width)
    grad_w_qkv = w_grad.transpose(0, 2, 1).astype(f32)
    weight_sum = after(weight_sum, *grad_moved)
    weight_far = over_seq(weight_sum)
    grad_w_up, grad_w_down, grad_w_out = weight_results(core, weight_sum, weight_far, head_width)
    at = slice(2 * cut + out_cut, 2 * cut + out_cut + 16)
    small = add(weight_sum[at], weight_far[at])

    count = piece * seqs * width * hash_count * 2
    stream_rms = jnp.sqrt(jnp.sum(small[0:3], axis=1) / count)
    share = width // head_count
    norm_grads = lax.dynamic_slice_in_dim(small, d * share, share, 1)
    return (
        layer_out[None],
        grad_inputs[None],
        grad_w_qkv,
        grad_w_out,
        grad_w_up,
        grad_w_down,
        jnp.stack([norm_grads[8], norm_grads[3]]),
        jnp.stack([norm_grads[9], norm_grads[4]]),
        stream_rms,
    )


def solution(mesh):
    placed = (
        P("seq", "hash", None, None),
        P(None, None, "head"),
        P("head", None),
        P(None, "head"),
        P("head", None),
        P(),
        P(),
        P("hash", None, None),
        P(),
        P(),
    )
    return jax.shard_map(
        shards,
        mesh=mesh,
        in_specs=placed,
        out_specs=(
            P("seq", "hash", None, None),
            P("seq", "hash", None, None),
            P(None, None, "head"),
            P("head", None),
            P(None, "head"),
            P("head", None),
            P(None, "head"),
            P(None, "head"),
            P(),
        ),
        check_vma=False,
    )
```

```python
from functools import partial

import jax
import jax.numpy as jnp
import numpy as np
from jax import lax
from jax.experimental import pallas as pl
from jax.experimental.pallas import tpu as pltpu
from jax.sharding import PartitionSpec as P

HEAD_DIM = 64
HASHES = 32
BITS = 8
SETS = 8
BUCKETS = 1 << BITS
ROWS = BUCKETS * SETS

bf16 = jnp.bfloat16
f32 = jnp.float32
NN = (((1,), (0,)), ((), ()))
NT = (((1,), (1,)), ((), ()))
TN = (((0,), (0,)), ((), ()))


shape = jax.ShapeDtypeStruct


def dot(a, b, dims):
    return lax.dot_general(a, b, dims, preferred_element_type=f32)


def sides(rows, planes):
    x = rows.astype(f32)
    inv = lax.rsqrt(jnp.sum(x * x, axis=0, keepdims=True) + 1e-6)
    proj = dot(planes, rows, NN) * (3.0 * inv)
    small = jnp.exp(-proj)
    upper = 1.0 / (1.0 + small)
    return inv, upper, small * upper


def products(upper, lower, first, count):
    out = None
    for i in range(first, first + count):
        lo, up = lower[SETS * i : SETS * (i + 1)], upper[SETS * i : SETS * (i + 1)]
        out = [lo, up] if out is None else [c * lo for c in out] + [c * up for c in out]
    return out


def half_codes(upper, lower):
    low = jnp.concatenate(products(upper, lower, 0, 4), axis=0).astype(bf16)
    high = [jnp.concatenate([a, a], axis=0).astype(bf16) for a in products(upper, lower, 4, 4)]
    return low, high


def code_chunk(low, high, first, count):
    return jnp.concatenate(
        [high[a] * low[16 * j : 16 * (j + 1)] for a in range(first, first + count) for j in range(8)],
        axis=0,
    )


def pull_back(rows, planes_t, inv, upper, sums):
    total = sums[BITS * SETS :][:SETS]
    grad_proj = sums[: BITS * SETS] - upper * jnp.concatenate([total] * BITS, axis=0)
    head = grad_proj.astype(bf16)
    tail = (grad_proj - head.astype(f32)).astype(bf16)
    grad_unit = dot(planes_t, jnp.concatenate([head, tail], axis=0), NN) * (3.0 * inv)
    x = rows.astype(f32)
    return grad_unit - x * (inv * inv * jnp.sum(x * grad_unit, axis=0, keepdims=True))


def both(*refs):
    return jnp.concatenate([ref[...] for ref in refs], axis=1)


def key_kernel(planes, *refs, chunk, blocks):
    keys, vals, out = refs[:blocks], refs[blocks : 2 * blocks], refs[-1]
    start = refs[2 * blocks] if len(refs) > 2 * blocks + 1 else None
    _, upper, lower = sides(both(*keys), planes[...])
    low, high = half_codes(upper, lower)
    values = both(*vals)
    for c in range(0, 16, chunk):
        at = slice(128 * c, 128 * (c + chunk))
        part = dot(code_chunk(low, high, c, chunk), values, NT)
        if start is not None:
            part = part + start[0, at, :]
        out[0, at, :] = part.astype(out.dtype)


def query_kernel(planes, tables, *refs, chunk):
    rows, out = both(*refs[:-1]), refs[-1]
    _, upper, lower = sides(rows, planes[...])
    low, high = half_codes(upper, lower)
    acc = jnp.zeros((HEAD_DIM, rows.shape[1]), f32)
    for c in range(0, 16, chunk):
        acc += dot(tables[0, 128 * c : 128 * (c + chunk), :], code_chunk(low, high, c, chunk), TN)
    out[...] = (acc * (1.0 / HASHES)).astype(out.dtype)


def query_back_kernel(planes, planes_t, bits, tables, *refs, chunk, blocks, last):
    queries, grads = refs[: 2 * blocks], refs[2 * blocks : 3 * blocks]
    start = refs[3 * blocks] if len(refs) > 4 * blocks + 1 else None
    out, back_out = refs[-1 - blocks], refs[-blocks:]
    rows = both(*queries)
    inv, upper, lower = sides(rows, planes[...])
    low, high = half_codes(upper, lower)
    grad = both(*grads)
    sums = jnp.zeros((bits.shape[0], rows.shape[1]), f32)
    for c in range(0, 16, chunk):
        at = slice(128 * c, 128 * (c + chunk))
        codes = code_chunk(low, high, c, chunk)
        part = dot(codes, grad, NT)
        if start is not None:
            part = part + start[0, at, :]
        if last:
            part = part * (1.0 / HASHES)
        out[0, at, :] = part.astype(out.dtype)
        weighted = dot(tables[0, at, :], grad, NN).astype(bf16) * codes
        sums += dot(bits[:, at], weighted, NN)
    back = pull_back(rows, planes_t[...], inv, upper, sums * (1.0 / HASHES))
    width = back_out[0].shape[1]
    for i in range(blocks):
        back_out[i][...] = back[:, i * width : (i + 1) * width].astype(back_out[i].dtype)


def key_back_kernel(planes, planes_t, bits, ka, kb, va, vb, grad_tables, out, *, chunk):
    rows = both(ka, kb)
    inv, upper, lower = sides(rows, planes[...])
    low, high = half_codes(upper, lower)
    values = both(va, vb)
    width = rows.shape[1]
    sums = jnp.zeros((bits.shape[0], width), f32)
    grad_values = jnp.zeros((HEAD_DIM, width), f32)
    for c in range(0, 16, chunk):
        at = slice(128 * c, 128 * (c + chunk))
        codes = code_chunk(low, high, c, chunk)
        grad_values += dot(grad_tables[0, at, :], codes, TN)
        weighted = dot(grad_tables[0, at, :], values, NN).astype(bf16) * codes
        sums += dot(bits[:, at], weighted, NN)
    out[0] = pull_back(rows, planes_t[...], inv, upper, sums).astype(out.dtype)
    out[1] = grad_values.astype(out.dtype)


def bit_rows():
    out = np.zeros((80, BUCKETS, SETS), np.float32)
    for t in range(SETS):
        for i in range(BITS):
            out[i * SETS + t, :, t] = (np.arange(BUCKETS) >> i) & 1
        out[BITS * SETS + t, :, t] = 1
    return jnp.asarray(out.reshape(80, ROWS), bf16)


def whole(*shape):
    return pl.BlockSpec(shape, lambda h: (0,) * len(shape))


def head_rows(array, heads, which):
    width = array.shape[1]
    offset = (which - 3) * heads + array.shape[0] // HEAD_DIM
    return pl.BlockSpec((HEAD_DIM, width), lambda h: (h + offset, 0))


def per_head(width):
    return pl.BlockSpec((HEAD_DIM, width), lambda h: (h, 0))


def table_spec():
    return pl.BlockSpec((1, ROWS, HEAD_DIM), lambda h: (h, 0, 0))


def call(kernel, heads, micros, name, in_specs, out_specs, out_shape):
    return pl.pallas_call(
        kernel,
        grid=(heads,),
        in_specs=in_specs,
        out_specs=out_specs,
        out_shape=out_shape,
        compiler_params=pltpu.CompilerParams(vmem_limit_bytes=48 << 20),
        cost_estimate=pl.CostEstimate(
            flops=int(micros * 1.1e9), bytes_accessed=1 << 20, transcendentals=0
        ),
        name=name,
    )


def key_tables(planes, heads, blocks, start, kind):
    args = [planes, *blocks, *blocks]
    specs = [whole(64, 64)] + [head_rows(x, heads, w) for w in (1, 2) for x in blocks]
    if start is not None:
        specs.append(table_spec())
        args.append(start)
    return call(
        partial(key_kernel, chunk=2, blocks=len(blocks)),
        heads,
        30 if len(blocks) > 1 and start is not None else 1,
        "key_tables",
        specs,
        table_spec(),
        shape((heads, ROWS, HEAD_DIM), kind),
    )(*args)


def query_estimates(planes, heads, near, far, tables, kind):
    width = near.shape[1] + far.shape[1]
    return call(
        partial(query_kernel, chunk=2),
        heads,
        1,
        "query_estimates",
        [whole(64, 64), table_spec(), head_rows(near, heads, 0), head_rows(far, heads, 0)],
        per_head(width),
        shape((heads * HEAD_DIM, width), kind),
    )(planes, tables, near, far)


def query_backward(planes, planes_t, bits, heads, tables, queries, grads, start, last, kinds):
    width = grads[0].shape[1]
    blocks = len(grads)
    specs = [whole(64, 64), whole(64, 128), whole(80, ROWS), table_spec()]
    args = [planes, planes_t, bits, tables]
    for near, far in queries:
        specs += [head_rows(near, heads, 0), head_rows(far, heads, 0)]
        args += [near, far]
    specs += [per_head(width)] * blocks
    args += grads
    if start is not None:
        specs.append(table_spec())
        args.append(start)
    return call(
        partial(query_back_kernel, chunk=4 * blocks, blocks=blocks, last=last),
        heads,
        25 * blocks,
        "query_backward",
        specs,
        [table_spec()] + [per_head(width)] * blocks,
        [shape((heads, ROWS, HEAD_DIM), bf16 if last else f32)]
        + [shape(grads[0].shape, kind) for kind in kinds],
    )(*args)


def key_backward(planes, planes_t, bits, heads, near, far, grad_tables, kind, micros=25):
    width = near.shape[1] + far.shape[1]
    return call(
        partial(key_back_kernel, chunk=4),
        heads,
        micros,
        "key_backward",
        [whole(64, 64), whole(64, 128), whole(80, ROWS)]
        + [head_rows(x, heads, w) for w in (1, 2) for x in (near, far)]
        + [table_spec()],
        pl.BlockSpec((2, HEAD_DIM, width), lambda h: (0, h, 0)),
        shape((2, heads * HEAD_DIM, width), kind),
    )(planes, planes_t, bits, near, far, near, far, grad_tables)


def norm(x):
    center = x - jnp.mean(x, axis=-1, keepdims=True)
    inv = lax.rsqrt(jnp.mean(center * center, axis=-1, keepdims=True) + 1e-5)
    return center * inv, inv


def norm_back(grad, unit, inv):
    return inv * (
        grad
        - jnp.mean(grad, axis=-1, keepdims=True)
        - unit * jnp.mean(grad * unit, axis=-1, keepdims=True)
    )


def column_sum(x):
    return jnp.sum(x, axis=0, keepdims=True)


def core_rows(core, ref, which):
    half = ref.shape[0] // 2
    at = core[0] if which == 0 else 1 - core[0]
    return ref[pl.ds(pl.multiple_of(at * half, 16), half), :]


def share_rows(keep, give, at, rows):
    part = keep.shape[2]
    for out in (keep, give):
        out[at] = rows[:, :part]
        out[at + 1] = rows[:, part:]


def dense_kernel(core, x_in, grad_out, gain, bias, *refs):
    attn, weights = refs[0:4], refs[4:6]
    layer_out, grad_first_out, keep, give, keep_back, give_back, heads_give = refs[6:13]
    estimates, small, slope = refs[13:17], refs[17], refs[18]
    owner = [core[1] ^ (b // 2) for b in range(8)]
    for j in range(4):
        heads_give[j] = core_rows(core, attn[j], 1)
    part = slope.shape[2]
    blocks = range(8)
    heads = jnp.concatenate([core_rows(core, attn[b // 2], b % 2) for b in blocks], axis=0)
    out_w = jnp.concatenate([weights[b % 2][owner[b], 2 * part :, :] for b in blocks], axis=0)
    attn_out = dot(heads, out_w, TN)
    resid = x_in[...].astype(f32)
    first = resid + attn_out
    small[0:1, :] = column_sum(resid * resid)
    small[1:2, :] = column_sum(attn_out * attn_out)
    small[2:3, :] = column_sum(first * first)
    unit_1, inv_1 = norm(first)
    normed = (unit_1 * gain[0:1, :] + bias[0:1, :]).astype(bf16)
    share_rows(keep, give, 4, normed)
    second = normed.astype(f32)
    for b in blocks:
        pre = dot(normed, weights[b % 2][owner[b], 0:part, :], NT)
        below = 0.5 * (1.0 + lax.erf(pre * 0.7071067811865476))
        rows = (pre * below).astype(bf16)
        (keep, give)[b % 2][b // 2] = rows
        slope[b] = below + pre * (0.3989422804014327 * jnp.exp(-0.5 * pre * pre))
        second = second + dot(rows, weights[b % 2][owner[b], part : 2 * part, :], NN)
    unit_2, inv_2 = norm(second)
    layer_out[...] = (unit_2 * gain[1:2, :] + bias[1:2, :]).astype(layer_out.dtype)
    grad = grad_out[...]
    small[3:4, :] = column_sum(grad * unit_2)
    small[4:5, :] = column_sum(grad)
    grad_second = norm_back(grad * gain[1:2, :], unit_2, inv_2)
    grad_ffn = grad_second.astype(bf16)
    share_rows(keep, give, 6, grad_ffn)
    grad_normed = grad_second
    for b in blocks:
        rows = dot(grad_ffn, weights[b % 2][owner[b], part : 2 * part, :], NT)
        rows = (rows * slope[b]).astype(bf16)
        (keep_back, give_back)[b % 2][b // 2] = rows
        grad_normed = grad_normed + dot(rows, weights[b % 2][owner[b], 0:part, :], NN)
    small[5:6, :] = column_sum(grad_normed * unit_1)
    small[6:7, :] = column_sum(grad_normed)
    small[7:16, :] = jnp.zeros_like(small[7:16, :])
    grad_first = norm_back(grad_normed * gain[0:1, :], unit_1, inv_1)
    grad_first_out[...] = grad_first
    grad_attn = grad_first.astype(bf16)
    share_rows(keep_back, give_back, 4, grad_attn)
    for b in blocks:
        half = estimates[0].shape[0] // 2
        at = core[0] if b % 2 == 0 else 1 - core[0]
        estimates[b // 2][pl.ds(pl.multiple_of(at * half, 16), half), :] = dot(
            weights[b % 2][owner[b], 2 * part :, :], grad_attn, NT
        ).astype(bf16)


def weight_grad_kernel(core, small, *refs):
    near, far, near_back, far_back = refs[0:4]
    attn, attn_far, out = refs[4:8], refs[8], refs[9]
    part = near.shape[2]
    sums = small[...].astype(bf16)

    def wide(ref, at):
        return jnp.concatenate([ref[at], ref[at + 1]], axis=1)

    def rows(ref, other, at):
        return jnp.concatenate([wide(ref, at), wide(other, at)], axis=0)

    normed, grad_ffn = rows(near, far, 4), rows(near, far, 6)
    grad_attn = rows(near_back, far_back, 4)
    for j in range(4):
        owner = core[1] ^ j
        hidden = jnp.concatenate([near[j], far[j]], axis=0)
        grad_pre = jnp.concatenate([near_back[j], far_back[j]], axis=0)
        out[owner, 0:part, :] = dot(grad_pre, normed, TN).astype(bf16)
        out[owner, part : 2 * part, :] = dot(hidden, grad_ffn, TN).astype(bf16)
        heads = jnp.concatenate([core_rows(core, attn[j], 0), attn_far[j]], axis=1)
        at = 2 * part + heads.shape[0]
        out[owner, 2 * part : at, :] = dot(heads, grad_attn, NN).astype(bf16)
        out[owner, at : at + 16, :] = sums
        out[owner, at + 16 :, :] = jnp.zeros_like(sums)


def input_grad_kernel(core, grad_first, *refs):
    blocks, near, far, out = refs[0:4], refs[4], refs[5], refs[6]
    half = near.shape[2]
    total = grad_first[...]
    for which, halves in enumerate((near, far)):
        at = core[0] if which == 0 else 1 - core[0]
        at = pl.ds(pl.multiple_of(at * half, 16), half)
        for j in range(4):
            rows = jnp.concatenate([blocks[j][c, at, :] for c in range(3)], axis=0)
            weights = jnp.concatenate([halves[core[1] ^ j, c] for c in range(3)], axis=0)
            total = total + dot(rows, weights, TN)
    out[...] = total.astype(out.dtype)


def vmem(count):
    return [pl.BlockSpec(memory_space=pltpu.VMEM)] * count


def single(kernel, core, args, out_shape, micros, name, scratch=()):
    return pl.pallas_call(
        kernel,
        in_specs=[pl.BlockSpec(memory_space=pltpu.SMEM)] + vmem(len(args)),
        out_specs=vmem(len(out_shape)),
        out_shape=out_shape,
        scratch_shapes=scratch,
        compiler_params=pltpu.CompilerParams(vmem_limit_bytes=56 << 20),
        cost_estimate=pl.CostEstimate(
            flops=int(micros * 1.1e9), bytes_accessed=1 << 20, transcendentals=0
        ),
        name=name,
    )(core, *args)


def dense(core, x_in, grad_out, gain, bias, attn, weights):
    rows, width = x_in.shape
    part = (weights[0].shape[1] - attn[0].shape[0] // 2) // 2
    out_shape = [
        shape((rows, width), bf16),
        shape((rows, width), f32),
        *[shape((8, rows, part), bf16)] * 2,
        *[shape((6, rows, part), bf16)] * 2,
        shape((4, attn[0].shape[0] // 2, rows), bf16),
        *[shape(attn[0].shape, bf16)] * 4,
        shape((16, width), f32),
    ]
    args = [x_in, grad_out, gain, bias, *attn, *weights]
    scratch = [pltpu.VMEM((8, rows, part), f32)]
    return single(dense_kernel, core, args, out_shape, 22, "dense", scratch)


def weight_grads(core, small, shared, attn, attn_far):
    part, width = shared[0].shape[2], small.shape[1]
    out_shape = [shape((4, 2 * part + attn[0].shape[0] // 2 + 32, width), bf16)]
    args = [small, *shared, *attn, attn_far]
    return single(weight_grad_kernel, core, args, out_shape, 7, "weight_grads")[0]


def weight_results_kernel(core, near, far, up, down, out):
    part, rows = up.shape[1] // 2, out.shape[0] // 2
    for which, ref in enumerate((near, far)):
        at = core[0] if which == 0 else 1 - core[0]
        at_part = pl.ds(pl.multiple_of(at * part, 128), part)
        up[:, at_part] = ref[0:part, :].astype(f32).T
        down[at_part, :] = ref[part : 2 * part, :].astype(f32)
        at_rows = pl.ds(pl.multiple_of(at * rows, 16), rows)
        out[at_rows, :] = ref[2 * part : 2 * part + rows, :].astype(f32)


def weight_results(core, near, far, head_width):
    width = near.shape[1]
    part = (near.shape[0] - 32 - head_width // 2) // 2
    out_shape = [
        shape((width, 2 * part), f32), shape((2 * part, width), f32), shape((head_width, width), f32)
    ]
    return single(weight_results_kernel, core, [near, far], out_shape, 3, "weight_results")


def input_grad(core, grad_first, blocks, near, far):
    out_shape = [shape(grad_first.shape, bf16)]
    args = [grad_first, *blocks, near, far]
    return single(input_grad_kernel, core, args, out_shape, 40, "input_grad")[0]


def after(x, *others):
    return lax.optimization_barrier((x, *others))[0]


def add(a, *others):
    return sum([b.astype(f32) for b in others], a.astype(f32))


def shards(
    inputs,
    w_qkv,
    w_out,
    up_weight,
    down_weight,
    norm_gain,
    norm_bias,
    planes,
    mask_pos,
    cot_rows,
):
    own = inputs[0]
    piece, seqs, width = own.shape
    hash_count, head_count = lax.axis_size("hash"), lax.axis_size("head")
    groups, places = seqs, hash_count // seqs
    assert places == 2 and lax.axis_size("seq") == 2 and head_count == 4
    assert planes.shape[0] * hash_count == 4 * SETS
    quarter = piece // head_count
    rows = groups * quarter
    half_len = piece * hash_count
    head_width = w_out.shape[0]
    hidden_own = down_weight.shape[0]
    n_tokens = head_count * rows
    hash_id, d, s = lax.axis_index("hash"), lax.axis_index("head"), lax.axis_index("seq")
    g, r = hash_id // places, hash_id % places

    def over_seq(x):
        return lax.ppermute(x, "seq", [(0, 1), (1, 0)])

    def over_place(x):
        return lax.ppermute(x, "hash", [(h, h ^ 1) for h in range(hash_count)])

    def over_group(x, k):
        moves = [(h, ((h // places + k) % groups) * places + h % places) for h in range(hash_count)]
        return lax.ppermute(x, "hash", moves)

    def over_head(x, j):
        return lax.ppermute(x, "head", [(h, h ^ j) for h in range(head_count)])

    def seq_rows(block, index):
        return lax.dynamic_index_in_dim(block, index % seqs, 1, keepdims=False)

    here = [
        seq_rows(lax.dynamic_slice_in_dim(own, (d ^ j) * quarter, quarter, 0), g)
        for j in range(head_count)
    ]
    near_tokens = jnp.concatenate(here)
    my_quarter = lax.dynamic_slice_in_dim(own, d * quarter, quarter, 0)
    sent = [seq_rows(my_quarter, g + k) for k in range(1, groups)]
    arrived = [over_group(x, k + 1) for k, x in enumerate(sent)]

    signed = (2 * planes - 1).astype(bf16)
    if planes.shape[0] == SETS and groups == 2:
        moves = [
            ((2 * rr + ss) * 2 + gg, (gg * places + rr) * 2 + ss)
            for gg in range(2)
            for rr in range(2)
            for ss in range(2)
        ]
        signed = lax.ppermute(signed, ("hash", "seq"), moves)
    else:
        signed = lax.all_gather(signed, "hash", axis=0, tiled=True)
        signed = lax.dynamic_slice_in_dim(signed, (r * 2 + s) * SETS, SETS, 0)
    signed = signed.transpose(1, 0, 2).reshape(BITS * SETS, HEAD_DIM)
    signed_t = jnp.concatenate([signed.T, signed.T], axis=1)
    bits = bit_rows()

    cut, out_cut = hidden_own // 2, head_width // 2
    weights = jnp.concatenate(
        [
            lax.dynamic_slice_in_dim(after(up_weight, *sent), s * cut, cut, 1).T,
            lax.dynamic_slice_in_dim(down_weight, s * cut, cut, 0),
            lax.dynamic_slice_in_dim(w_out, s * out_cut, out_cut, 0),
        ]
    )
    weights = lax.all_gather(weights, "head", axis=0)
    w_qkv_t = lax.dynamic_slice_in_dim(w_qkv.transpose(0, 2, 1), s * out_cut, out_cut, 1)

    head_n = head_width // HEAD_DIM

    def project(w, rows_in):
        out = jnp.einsum("cde,ld->cel", w, rows_in, preferred_element_type=f32)
        return out.astype(bf16).reshape(-1, rows_in.shape[0])

    near_tokens = after(near_tokens, *arrived)
    near = project(w_qkv, near_tokens)
    near_z, near_o = over_place(near), over_seq(near)
    far_quarter = jnp.stack(arrived)
    moved = [over_head(far_quarter, j) for j in range(1, head_count)]
    dense_in = jnp.concatenate([here[0], *arrived])
    tables = key_tables(after(signed, dense_in), head_n, [near, near_o], None, f32)
    moved = [after(x, tables) for x in moved]

    near_z = after(near_z, tables)
    near_zo = over_seq(near_z)

    mask_pos = after(mask_pos, tables)
    slot = jnp.arange(groups, dtype=jnp.int32)[:, None]
    place_of = ((g - slot) % groups) * places + r
    position = s * half_len + place_of * piece + d * quarter + jnp.arange(quarter, dtype=jnp.int32)[None]
    mask_row = lax.dynamic_index_in_dim(mask_pos, g, 0, keepdims=False)
    cot = lax.dynamic_index_in_dim(cot_rows, g, 0, keepdims=False)
    pick = (position.reshape(rows)[:, None] == mask_row[None]).astype(bf16)
    grad_out = jnp.dot(pick, cot, preferred_element_type=f32)
    ready = after(signed, grad_out)
    tables = key_tables(ready, head_n, [near_z, near_zo], tables, f32)

    far_tokens = jnp.stack([far_quarter, *moved]).reshape(-1, width)
    far = project(w_qkv, far_tokens)
    tokens = jnp.concatenate([near_tokens, far_tokens])
    far_z, far_o = over_place(far), over_seq(far)
    n_near = near.shape[1]

    tables = key_tables(signed, head_n, [far, far_o], tables, f32)

    far_z = after(far_z, tables)
    far_zo = over_seq(far_z)
    tables = key_tables(after(signed, tokens, w_qkv_t), head_n, [far_z], tables, f32)

    far_zo = after(far_zo, tables)
    tables = key_tables(signed, head_n, [far_zo], tables, bf16)

    e_zo = query_estimates(signed, head_n, near_zo, far_zo, tables, bf16)
    e_zo_moved = over_seq(e_zo)
    e_z = query_estimates(signed, head_n, near_z, after(far_z, e_zo), tables, bf16)
    e_far = add(e_z, after(e_zo_moved, e_z)).astype(bf16)
    ready = after(far_o, e_far)
    e_o = query_estimates(signed, head_n, near_o, ready, tables, bf16)
    e_far = over_place(e_far)
    e_o_moved = over_seq(e_o)
    e = query_estimates(signed, head_n, near, after(far, e_o), tables, f32)
    e_far = after(e_far, e)
    e_o_moved = after(e_o_moved, e)
    weights = after(weights, e_far, e_o_moved)
    weights = [weights, over_seq(weights)]
    w_qkv_t = lax.all_gather(after(w_qkv_t, weights[0]), "head", axis=0)
    attn = add(e, e_o_moved, e_far).astype(bf16)

    def to_dense(block):
        parts = []
        for j in range(head_count):
            a, b = j * quarter, n_near + j * (rows - quarter)
            cut = [block[..., a : a + quarter], block[..., b : b + rows - quarter]]
            parts.append(jnp.concatenate(cut, axis=-1))
        moved = [over_head(parts[j], j) for j in range(1, head_count)]
        return [parts[0], *lax.optimization_barrier(moved)]

    attn_parts = to_dense(attn)

    def away(dense_rows):
        dense_rows = dense_rows.reshape(groups, quarter, width)
        return [dense_rows[0]] + [over_group(dense_rows[k], groups - k) for k in range(1, groups)]

    core = jnp.stack([s, d]).astype(jnp.int32)
    layer_rows, grad_first, keep, give, keep_back, give_back, heads_give, *est_parts, small = dense(
        core, dense_in, grad_out, norm_gain, norm_bias, attn_parts, weights
    )
    taken, taken_back, heads_far = over_seq(give), over_seq(give_back), over_seq(heads_give)
    est_moved = [over_head(est_parts[j], j) for j in range(1, head_count)]
    est_parts = [est_parts[0], *lax.optimization_barrier(est_moved)]
    grad = jnp.concatenate(
        [x[:, :quarter] for x in est_parts] + [x[:, quarter:] for x in est_parts], axis=1
    )
    layer_moved = away(layer_rows)
    weight_parts = weight_grads(
        core, after(small, grad, w_qkv_t), [keep, taken, keep_back, taken_back], attn_parts, heads_far
    )

    weight_sum = lax.psum_scatter(weight_parts, "head", scatter_dimension=0, tiled=True)[0]
    grad_z = over_place(grad)
    grad_o = after(over_seq(grad), weight_parts)
    layer_moved = [after(x, weight_parts) for x in layer_moved]
    part, dq, dq_o = query_backward(
        signed, signed_t, bits, head_n, tables, [(near, after(far, *layer_moved)), (near_o, far_o)], [grad, grad_o],
        None, False, [f32, bf16],
    )

    layer_moved = jnp.stack([after(x, part) for x in layer_moved])
    grad_z = after(grad_z, part)
    grad_zo = over_seq(grad_z)
    dq_o = over_seq(dq_o)
    part, dq_z = query_backward(
        signed, signed_t, bits, head_n, tables, [(near_z, far_z)], [grad_z], part, False, [f32]
    )

    dq_own = add(dq, after(dq_o, dq_z))
    grad_zo = after(grad_zo, dq_z)
    grad_tables, dq_zo = query_backward(
        signed, signed_t, bits, head_n, tables, [(near_zo, after(far_zo, dq_own))], [grad_zo], part, True, [bf16]
    )

    dq_zo = over_seq(dq_zo)
    w_qkv_t = after(w_qkv_t, grad_tables)
    w_qkv_far = over_seq(w_qkv_t)
    dkv_zo = key_backward(signed, signed_t, bits, head_n, near_zo, far_zo, grad_tables, bf16)

    dkv_zo_moved = over_seq(dkv_zo)
    dq_far = add(dq_z, after(dq_zo, dkv_zo)).astype(bf16)
    layer_moved = [layer_moved] + [over_head(layer_moved, j) for j in range(1, head_count)]
    dkv_z = key_backward(signed, signed_t, bits, head_n, near_z, after(far_z, dq_far), grad_tables, bf16)
    dq_far = over_place(dq_far)

    dkv_far = add(dkv_z, after(dkv_zo_moved, dkv_z)).astype(bf16)
    grad_q = add(dq_own, after(dq_far, dkv_z)).astype(bf16)
    weight_sum = after(weight_sum, dkv_z)
    layer_moved = [after(x, dkv_z) for x in layer_moved]
    dkv_o = key_backward(
        signed, signed_t, bits, head_n, near_o, after(far_o, dkv_far, grad_q, weight_sum, *layer_moved),
        grad_tables, bf16, 25,
    )
    weight_sum = lax.psum(weight_sum, "hash")
    dkv_far = over_place(dkv_far)
    dkv_o_moved = over_seq(dkv_o)
    dkv = key_backward(
        signed, signed_t, bits, head_n, near, after(far, dkv_o), grad_tables, f32, 25
    )

    dkv_o_moved = after(dkv_o_moved, dkv)
    grad_kv = add(dkv, dkv_o_moved, after(dkv_far, dkv)).astype(bf16)
    grad_qkv = jnp.concatenate([grad_q[None], grad_kv])
    qkv_parts = to_dense(grad_qkv)

    grad_in = input_grad(core, grad_first, qkv_parts, w_qkv_t, after(w_qkv_far, dkv))

    def in_halves(index, mine, other):
        first = jnp.where(index == 0, mine, other)
        second = jnp.where(index == 0, other, mine)
        return jnp.concatenate([first, second], axis=0)

    def split(x, index):
        half = x.shape[0] // 2
        return [lax.dynamic_slice_in_dim(x, at * half, half, 0) for at in (index, 1 - index)]

    w_grad = dot(grad_qkv.reshape(3 * head_width, n_tokens), tokens, NN).astype(bf16)
    w_keep, w_send = split(w_grad, s)
    w_keep, w_send = split(add(w_keep, over_seq(w_send)).astype(bf16), r)
    grad_moved = away(grad_in)
    w_keep = add(w_keep, over_place(w_send))
    w_send = w_keep.astype(bf16)
    grad_moved = after(jnp.stack(grad_moved), w_send)
    w_keep = add(w_keep, *[over_group(w_send, k) for k in range(1, groups)]).astype(bf16)
    grad_moved = [grad_moved] + [over_head(grad_moved, j) for j in range(1, head_count)]

    def home(blocks):
        table = jnp.stack(blocks)
        columns = []
        for q_at in range(head_count):
            block = lax.dynamic_index_in_dim(table, q_at ^ d, 0, keepdims=False)
            columns.append(
                jnp.stack(
                    [
                        lax.dynamic_index_in_dim(block, (at - g) % groups, 0, keepdims=False)
                        for at in range(seqs)
                    ],
                    axis=1,
                )
            )
        return jnp.concatenate(columns, axis=0)

    layer_out = home([after(x, grad_moved[0]) for x in layer_moved])
    grad_inputs = home(grad_moved).astype(f32)

    w_grad = in_halves(r, w_keep, over_place(w_keep))
    w_grad = in_halves(s, w_grad, over_seq(w_grad)).reshape(3, head_width, width)
    grad_w_qkv = w_grad.transpose(0, 2, 1).astype(f32)
    weight_sum = after(weight_sum, *grad_moved)
    weight_far = over_seq(weight_sum)
    grad_w_up, grad_w_down, grad_w_out = weight_results(core, weight_sum, weight_far, head_width)
    at = slice(2 * cut + out_cut, 2 * cut + out_cut + 16)
    small = add(weight_sum[at], weight_far[at])

    count = piece * seqs * width * hash_count * 2
    stream_rms = jnp.sqrt(jnp.sum(small[0:3], axis=1) / count)
    share = width // head_count
    norm_grads = lax.dynamic_slice_in_dim(small, d * share, share, 1)
    return (
        layer_out[None],
        grad_inputs[None],
        grad_w_qkv,
        grad_w_out,
        grad_w_up,
        grad_w_down,
        jnp.stack([norm_grads[5], norm_grads[3]]),
        jnp.stack([norm_grads[6], norm_grads[4]]),
        stream_rms,
    )


def solution(mesh):
    placed = (
        P("seq", "hash", None, None),
        P(None, None, "head"),
        P("head", None),
        P(None, "head"),
        P("head", None),
        P(),
        P(),
        P("hash", None, None),
        P(),
        P(),
    )
    return jax.shard_map(
        shards,
        mesh=mesh,
        in_specs=placed,
        out_specs=(
            P("seq", "hash", None, None),
            P("seq", "hash", None, None),
            P(None, None, "head"),
            P("head", None),
            P(None, "head"),
            P("head", None),
            P(None, "head"),
            P(None, "head"),
            P(),
        ),
        check_vma=False,
    )
```

```python
from functools import partial

import jax
import jax.numpy as jnp
import numpy as np
from jax import lax
from jax.experimental import pallas as pl
from jax.experimental.pallas import tpu as pltpu
from jax.sharding import PartitionSpec as P

HEAD_DIM = 64
HASHES = 32
BITS = 8
SETS = 8
BUCKETS = 1 << BITS
ROWS = BUCKETS * SETS

bf16 = jnp.bfloat16
f32 = jnp.float32
NN = (((1,), (0,)), ((), ()))
NT = (((1,), (1,)), ((), ()))
TN = (((0,), (0,)), ((), ()))


shape = jax.ShapeDtypeStruct


def dot(a, b, dims):
    return lax.dot_general(a, b, dims, preferred_element_type=f32)


def sides(rows, planes):
    x = rows.astype(f32)
    inv = lax.rsqrt(jnp.sum(x * x, axis=0, keepdims=True) + 1e-6)
    proj = dot(planes, rows, NN) * (3.0 * inv)
    small = jnp.exp(-proj)
    upper = 1.0 / (1.0 + small)
    return inv, upper, small * upper


def products(upper, lower, first, count):
    out = None
    for i in range(first, first + count):
        lo, up = lower[SETS * i : SETS * (i + 1)], upper[SETS * i : SETS * (i + 1)]
        out = [lo, up] if out is None else [c * lo for c in out] + [c * up for c in out]
    return out


def half_codes(upper, lower):
    low = jnp.concatenate(products(upper, lower, 0, 4), axis=0).astype(bf16)
    high = [jnp.concatenate([a, a], axis=0).astype(bf16) for a in products(upper, lower, 4, 4)]
    return low, high


def code_chunk(low, high, first, count):
    return jnp.concatenate(
        [high[a] * low[16 * j : 16 * (j + 1)] for a in range(first, first + count) for j in range(8)],
        axis=0,
    )


def pull_back(rows, planes_t, inv, upper, sums):
    total = sums[BITS * SETS :][:SETS]
    grad_proj = sums[: BITS * SETS] - upper * jnp.concatenate([total] * BITS, axis=0)
    head = grad_proj.astype(bf16)
    tail = (grad_proj - head.astype(f32)).astype(bf16)
    grad_unit = dot(planes_t, jnp.concatenate([head, tail], axis=0), NN) * (3.0 * inv)
    x = rows.astype(f32)
    return grad_unit - x * (inv * inv * jnp.sum(x * grad_unit, axis=0, keepdims=True))


def both(*refs):
    return jnp.concatenate([ref[...] for ref in refs], axis=1)


def key_kernel(planes, *refs, chunk, blocks):
    keys, vals, out = refs[:blocks], refs[blocks : 2 * blocks], refs[-1]
    start = refs[2 * blocks] if len(refs) > 2 * blocks + 1 else None
    _, upper, lower = sides(both(*keys), planes[...])
    low, high = half_codes(upper, lower)
    values = both(*vals)
    for c in range(0, 16, chunk):
        at = slice(128 * c, 128 * (c + chunk))
        part = dot(code_chunk(low, high, c, chunk), values, NT)
        if start is not None:
            part = part + start[0, at, :]
        out[0, at, :] = part.astype(out.dtype)


def query_kernel(planes, tables, *refs, chunk):
    rows, out = both(*refs[:-1]), refs[-1]
    _, upper, lower = sides(rows, planes[...])
    low, high = half_codes(upper, lower)
    acc = jnp.zeros((HEAD_DIM, rows.shape[1]), f32)
    for c in range(0, 16, chunk):
        acc += dot(tables[0, 128 * c : 128 * (c + chunk), :], code_chunk(low, high, c, chunk), TN)
    out[...] = (acc * (1.0 / HASHES)).astype(out.dtype)


def query_back_kernel(planes, planes_t, bits, tables, *refs, chunk, blocks, last):
    queries, grads = refs[: 2 * blocks], refs[2 * blocks : 3 * blocks]
    start = refs[3 * blocks] if len(refs) > 4 * blocks + 1 else None
    out, back_out = refs[-1 - blocks], refs[-blocks:]
    rows = both(*queries)
    inv, upper, lower = sides(rows, planes[...])
    low, high = half_codes(upper, lower)
    grad = both(*grads)
    sums = jnp.zeros((bits.shape[0], rows.shape[1]), f32)
    for c in range(0, 16, chunk):
        at = slice(128 * c, 128 * (c + chunk))
        codes = code_chunk(low, high, c, chunk)
        part = dot(codes, grad, NT)
        if start is not None:
            part = part + start[0, at, :]
        if last:
            part = part * (1.0 / HASHES)
        out[0, at, :] = part.astype(out.dtype)
        weighted = dot(tables[0, at, :], grad, NN).astype(bf16) * codes
        sums += dot(bits[:, at], weighted, NN)
    back = pull_back(rows, planes_t[...], inv, upper, sums * (1.0 / HASHES))
    width = back_out[0].shape[1]
    for i in range(blocks):
        back_out[i][...] = back[:, i * width : (i + 1) * width].astype(back_out[i].dtype)


def key_back_kernel(planes, planes_t, bits, ka, kb, va, vb, grad_tables, out, *, chunk):
    rows = both(ka, kb)
    inv, upper, lower = sides(rows, planes[...])
    low, high = half_codes(upper, lower)
    values = both(va, vb)
    width = rows.shape[1]
    sums = jnp.zeros((bits.shape[0], width), f32)
    grad_values = jnp.zeros((HEAD_DIM, width), f32)
    for c in range(0, 16, chunk):
        at = slice(128 * c, 128 * (c + chunk))
        codes = code_chunk(low, high, c, chunk)
        grad_values += dot(grad_tables[0, at, :], codes, TN)
        weighted = dot(grad_tables[0, at, :], values, NN).astype(bf16) * codes
        sums += dot(bits[:, at], weighted, NN)
    out[0] = pull_back(rows, planes_t[...], inv, upper, sums).astype(out.dtype)
    out[1] = grad_values.astype(out.dtype)


def bit_rows():
    out = np.zeros((80, BUCKETS, SETS), np.float32)
    for t in range(SETS):
        for i in range(BITS):
            out[i * SETS + t, :, t] = (np.arange(BUCKETS) >> i) & 1
        out[BITS * SETS + t, :, t] = 1
    return jnp.asarray(out.reshape(80, ROWS), bf16)


def whole(*shape):
    return pl.BlockSpec(shape, lambda h: (0,) * len(shape))


def head_rows(array, heads, which):
    width = array.shape[1]
    offset = (which - 3) * heads + array.shape[0] // HEAD_DIM
    return pl.BlockSpec((HEAD_DIM, width), lambda h: (h + offset, 0))


def per_head(width):
    return pl.BlockSpec((HEAD_DIM, width), lambda h: (h, 0))


def table_spec():
    return pl.BlockSpec((1, ROWS, HEAD_DIM), lambda h: (h, 0, 0))


def call(kernel, heads, micros, name, in_specs, out_specs, out_shape):
    return pl.pallas_call(
        kernel,
        grid=(heads,),
        in_specs=in_specs,
        out_specs=out_specs,
        out_shape=out_shape,
        compiler_params=pltpu.CompilerParams(vmem_limit_bytes=48 << 20),
        cost_estimate=pl.CostEstimate(
            flops=int(micros * 1.1e9), bytes_accessed=1 << 20, transcendentals=0
        ),
        name=name,
    )


def key_tables(planes, heads, blocks, start, kind):
    args = [planes, *blocks, *blocks]
    specs = [whole(64, 64)] + [head_rows(x, heads, w) for w in (1, 2) for x in blocks]
    if start is not None:
        specs.append(table_spec())
        args.append(start)
    return call(
        partial(key_kernel, chunk=2, blocks=len(blocks)),
        heads,
        30 if len(blocks) > 1 and start is not None else 1,
        "key_tables",
        specs,
        table_spec(),
        shape((heads, ROWS, HEAD_DIM), kind),
    )(*args)


def query_estimates(planes, heads, near, far, tables, kind):
    width = near.shape[1] + far.shape[1]
    return call(
        partial(query_kernel, chunk=2),
        heads,
        1,
        "query_estimates",
        [whole(64, 64), table_spec(), head_rows(near, heads, 0), head_rows(far, heads, 0)],
        per_head(width),
        shape((heads * HEAD_DIM, width), kind),
    )(planes, tables, near, far)


def query_backward(planes, planes_t, bits, heads, tables, queries, grads, start, last, kinds):
    width = grads[0].shape[1]
    blocks = len(grads)
    specs = [whole(64, 64), whole(64, 128), whole(80, ROWS), table_spec()]
    args = [planes, planes_t, bits, tables]
    for near, far in queries:
        specs += [head_rows(near, heads, 0), head_rows(far, heads, 0)]
        args += [near, far]
    specs += [per_head(width)] * blocks
    args += grads
    if start is not None:
        specs.append(table_spec())
        args.append(start)
    return call(
        partial(query_back_kernel, chunk=4 * blocks, blocks=blocks, last=last),
        heads,
        25 * blocks,
        "query_backward",
        specs,
        [table_spec()] + [per_head(width)] * blocks,
        [shape((heads, ROWS, HEAD_DIM), bf16 if last else f32)]
        + [shape(grads[0].shape, kind) for kind in kinds],
    )(*args)


def key_backward(planes, planes_t, bits, heads, near, far, grad_tables, kind, micros=25):
    width = near.shape[1] + far.shape[1]
    return call(
        partial(key_back_kernel, chunk=4),
        heads,
        micros,
        "key_backward",
        [whole(64, 64), whole(64, 128), whole(80, ROWS)]
        + [head_rows(x, heads, w) for w in (1, 2) for x in (near, far)]
        + [table_spec()],
        pl.BlockSpec((2, HEAD_DIM, width), lambda h: (0, h, 0)),
        shape((2, heads * HEAD_DIM, width), kind),
    )(planes, planes_t, bits, near, far, near, far, grad_tables)


def norm(x):
    center = x - jnp.mean(x, axis=-1, keepdims=True)
    inv = lax.rsqrt(jnp.mean(center * center, axis=-1, keepdims=True) + 1e-5)
    return center * inv, inv


def norm_back(grad, unit, inv):
    return inv * (
        grad
        - jnp.mean(grad, axis=-1, keepdims=True)
        - unit * jnp.mean(grad * unit, axis=-1, keepdims=True)
    )


def column_sum(x):
    return jnp.sum(x, axis=0, keepdims=True)


def core_rows(core, ref, which):
    half = ref.shape[0] // 2
    at = core[0] if which == 0 else 1 - core[0]
    return ref[pl.ds(pl.multiple_of(at * half, 16), half), :]


def share_rows(keep, give, at, rows):
    part = keep.shape[2]
    for out in (keep, give):
        out[at] = rows[:, :part]
        out[at + 1] = rows[:, part:]


def dense_kernel(core, x_in, grad_out, gain, bias, *refs):
    attn, weights = refs[0:4], refs[4:6]
    layer_out, grad_first_out, keep, give, keep_back, give_back, heads_give = refs[6:13]
    estimates, small, slope = refs[13:17], refs[17], refs[18]
    owner = [core[1] ^ (b // 2) for b in range(8)]
    for j in range(4):
        heads_give[j] = core_rows(core, attn[j], 1)
    part = slope.shape[2]
    blocks = range(8)
    heads = jnp.concatenate([core_rows(core, attn[b // 2], b % 2) for b in blocks], axis=0)
    out_w = jnp.concatenate([weights[b % 2][owner[b], 2 * part :, :] for b in blocks], axis=0)
    attn_out = dot(heads, out_w, TN)
    resid = x_in[...].astype(f32)
    first = resid + attn_out
    small[0:1, :] = column_sum(resid * resid)
    small[1:2, :] = column_sum(attn_out * attn_out)
    small[2:3, :] = column_sum(first * first)
    unit_1, inv_1 = norm(first)
    normed = (unit_1 * gain[0:1, :] + bias[0:1, :]).astype(bf16)
    share_rows(keep, give, 4, normed)
    second = normed.astype(f32)
    for b in blocks:
        pre = dot(normed, weights[b % 2][owner[b], 0:part, :], NT)
        below = 0.5 * (1.0 + lax.erf(pre * 0.7071067811865476))
        rows = (pre * below).astype(bf16)
        (keep, give)[b % 2][b // 2] = rows
        slope[b] = below + pre * (0.3989422804014327 * jnp.exp(-0.5 * pre * pre))
        second = second + dot(rows, weights[b % 2][owner[b], part : 2 * part, :], NN)
    unit_2, inv_2 = norm(second)
    layer_out[...] = (unit_2 * gain[1:2, :] + bias[1:2, :]).astype(layer_out.dtype)
    grad = grad_out[...]
    small[3:4, :] = column_sum(grad * unit_2)
    small[4:5, :] = column_sum(grad)
    grad_second = norm_back(grad * gain[1:2, :], unit_2, inv_2)
    grad_ffn = grad_second.astype(bf16)
    share_rows(keep, give, 6, grad_ffn)
    grad_normed = grad_second
    for b in blocks:
        rows = dot(grad_ffn, weights[b % 2][owner[b], part : 2 * part, :], NT)
        rows = (rows * slope[b]).astype(bf16)
        (keep_back, give_back)[b % 2][b // 2] = rows
        grad_normed = grad_normed + dot(rows, weights[b % 2][owner[b], 0:part, :], NN)
    small[5:6, :] = column_sum(grad_normed * unit_1)
    small[6:7, :] = column_sum(grad_normed)
    small[7:16, :] = jnp.zeros_like(small[7:16, :])
    grad_first = norm_back(grad_normed * gain[0:1, :], unit_1, inv_1)
    grad_first_out[...] = grad_first
    grad_attn = grad_first.astype(bf16)
    share_rows(keep_back, give_back, 4, grad_attn)
    for b in blocks:
        half = estimates[0].shape[0] // 2
        at = core[0] if b % 2 == 0 else 1 - core[0]
        estimates[b // 2][pl.ds(pl.multiple_of(at * half, 16), half), :] = dot(
            weights[b % 2][owner[b], 2 * part :, :], grad_attn, NT
        ).astype(bf16)


def weight_grad_kernel(core, small, *refs):
    near, far, near_back, far_back = refs[0:4]
    attn, attn_far, out = refs[4:8], refs[8], refs[9]
    part = near.shape[2]
    sums = small[...].astype(bf16)

    def wide(ref, at):
        return jnp.concatenate([ref[at], ref[at + 1]], axis=1)

    def rows(ref, other, at):
        return jnp.concatenate([wide(ref, at), wide(other, at)], axis=0)

    normed, grad_ffn = rows(near, far, 4), rows(near, far, 6)
    grad_attn = rows(near_back, far_back, 4)
    for j in range(4):
        owner = core[1] ^ j
        hidden = jnp.concatenate([near[j], far[j]], axis=0)
        grad_pre = jnp.concatenate([near_back[j], far_back[j]], axis=0)
        out[owner, 0:part, :] = dot(grad_pre, normed, TN).astype(bf16)
        out[owner, part : 2 * part, :] = dot(hidden, grad_ffn, TN).astype(bf16)
        heads = jnp.concatenate([core_rows(core, attn[j], 0), attn_far[j]], axis=1)
        at = 2 * part + heads.shape[0]
        out[owner, 2 * part : at, :] = dot(heads, grad_attn, NN).astype(bf16)
        out[owner, at : at + 16, :] = sums
        out[owner, at + 16 :, :] = jnp.zeros_like(sums)


def input_grad_kernel(core, grad_first, *refs):
    blocks, near, far, out = refs[0:4], refs[4], refs[5], refs[6]
    half = near.shape[2]
    total = grad_first[...]
    for which, halves in enumerate((near, far)):
        at = core[0] if which == 0 else 1 - core[0]
        at = pl.ds(pl.multiple_of(at * half, 16), half)
        for j in range(4):
            rows = jnp.concatenate([blocks[j][c, at, :] for c in range(3)], axis=0)
            weights = jnp.concatenate([halves[core[1] ^ j, c] for c in range(3)], axis=0)
            total = total + dot(rows, weights, TN)
    out[...] = total.astype(out.dtype)


def vmem(count):
    return [pl.BlockSpec(memory_space=pltpu.VMEM)] * count


def single(kernel, core, args, out_shape, micros, name, scratch=()):
    return pl.pallas_call(
        kernel,
        in_specs=[pl.BlockSpec(memory_space=pltpu.SMEM)] + vmem(len(args)),
        out_specs=vmem(len(out_shape)),
        out_shape=out_shape,
        scratch_shapes=scratch,
        compiler_params=pltpu.CompilerParams(vmem_limit_bytes=56 << 20),
        cost_estimate=pl.CostEstimate(
            flops=int(micros * 1.1e9), bytes_accessed=1 << 20, transcendentals=0
        ),
        name=name,
    )(core, *args)


def dense(core, x_in, grad_out, gain, bias, attn, weights):
    rows, width = x_in.shape
    part = (weights[0].shape[1] - attn[0].shape[0] // 2) // 2
    out_shape = [
        shape((rows, width), bf16),
        shape((rows, width), f32),
        *[shape((8, rows, part), bf16)] * 2,
        *[shape((6, rows, part), bf16)] * 2,
        shape((4, attn[0].shape[0] // 2, rows), bf16),
        *[shape(attn[0].shape, bf16)] * 4,
        shape((16, width), f32),
    ]
    args = [x_in, grad_out, gain, bias, *attn, *weights]
    scratch = [pltpu.VMEM((8, rows, part), f32)]
    return single(dense_kernel, core, args, out_shape, 22, "dense", scratch)


def weight_grads(core, small, shared, attn, attn_far):
    part, width = shared[0].shape[2], small.shape[1]
    out_shape = [shape((4, 2 * part + attn[0].shape[0] // 2 + 32, width), bf16)]
    args = [small, *shared, *attn, attn_far]
    return single(weight_grad_kernel, core, args, out_shape, 7, "weight_grads")[0]


def weight_results_kernel(core, near, far, up, down, out):
    part, rows = up.shape[1] // 2, out.shape[0] // 2
    for which, ref in enumerate((near, far)):
        at = core[0] if which == 0 else 1 - core[0]
        at_part = pl.ds(pl.multiple_of(at * part, 128), part)
        up[:, at_part] = ref[0:part, :].astype(f32).T
        down[at_part, :] = ref[part : 2 * part, :].astype(f32)
        at_rows = pl.ds(pl.multiple_of(at * rows, 16), rows)
        out[at_rows, :] = ref[2 * part : 2 * part + rows, :].astype(f32)


def weight_results(core, near, far, head_width):
    width = near.shape[1]
    part = (near.shape[0] - 32 - head_width // 2) // 2
    out_shape = [
        shape((width, 2 * part), f32), shape((2 * part, width), f32), shape((head_width, width), f32)
    ]
    return single(weight_results_kernel, core, [near, far], out_shape, 3, "weight_results")


def input_grad(core, grad_first, blocks, near, far):
    out_shape = [shape(grad_first.shape, bf16)]
    args = [grad_first, *blocks, near, far]
    return single(input_grad_kernel, core, args, out_shape, 40, "input_grad")[0]


def after(x, *others):
    return lax.optimization_barrier((x, *others))[0]


def add(a, *others):
    return sum([b.astype(f32) for b in others], a.astype(f32))


def shards(
    inputs,
    w_qkv,
    w_out,
    up_weight,
    down_weight,
    norm_gain,
    norm_bias,
    planes,
    mask_pos,
    cot_rows,
):
    own = inputs[0]
    piece, seqs, width = own.shape
    hash_count, head_count = lax.axis_size("hash"), lax.axis_size("head")
    groups, places = seqs, hash_count // seqs
    assert places == 2 and lax.axis_size("seq") == 2 and head_count == 4
    assert planes.shape[0] * hash_count == 4 * SETS
    quarter = piece // head_count
    rows = groups * quarter
    half_len = piece * hash_count
    head_width = w_out.shape[0]
    hidden_own = down_weight.shape[0]
    n_tokens = head_count * rows
    hash_id, d, s = lax.axis_index("hash"), lax.axis_index("head"), lax.axis_index("seq")
    g, r = hash_id // places, hash_id % places

    def over_seq(x):
        return lax.ppermute(x, "seq", [(0, 1), (1, 0)])

    def over_place(x):
        return lax.ppermute(x, "hash", [(h, h ^ 1) for h in range(hash_count)])

    def over_group(x, k):
        moves = [(h, ((h // places + k) % groups) * places + h % places) for h in range(hash_count)]
        return lax.ppermute(x, "hash", moves)

    def over_head(x, j):
        return lax.ppermute(x, "head", [(h, h ^ j) for h in range(head_count)])

    def seq_rows(block, index):
        return lax.dynamic_index_in_dim(block, index % seqs, 1, keepdims=False)

    here = [
        seq_rows(lax.dynamic_slice_in_dim(own, (d ^ j) * quarter, quarter, 0), g)
        for j in range(head_count)
    ]
    near_tokens = jnp.concatenate(here)
    my_quarter = lax.dynamic_slice_in_dim(own, d * quarter, quarter, 0)
    sent = [seq_rows(my_quarter, g + k) for k in range(1, groups)]
    arrived = [over_group(x, k + 1) for k, x in enumerate(sent)]

    signed = (2 * planes - 1).astype(bf16)
    if planes.shape[0] == SETS and groups == 2:
        moves = [
            ((2 * rr + ss) * 2 + gg, (gg * places + rr) * 2 + ss)
            for gg in range(2)
            for rr in range(2)
            for ss in range(2)
        ]
        signed = lax.ppermute(signed, ("hash", "seq"), moves)
    else:
        signed = lax.all_gather(signed, "hash", axis=0, tiled=True)
        signed = lax.dynamic_slice_in_dim(signed, (r * 2 + s) * SETS, SETS, 0)
    signed = signed.transpose(1, 0, 2).reshape(BITS * SETS, HEAD_DIM)
    signed_t = jnp.concatenate([signed.T, signed.T], axis=1)
    bits = bit_rows()

    cut, out_cut = hidden_own // 2, head_width // 2
    weights = jnp.concatenate(
        [
            lax.dynamic_slice_in_dim(after(up_weight, *sent), s * cut, cut, 1).T,
            lax.dynamic_slice_in_dim(down_weight, s * cut, cut, 0),
            lax.dynamic_slice_in_dim(w_out, s * out_cut, out_cut, 0),
        ]
    )
    weights = lax.all_gather(weights, "head", axis=0)
    w_qkv_t = lax.dynamic_slice_in_dim(w_qkv.transpose(0, 2, 1), s * out_cut, out_cut, 1)

    head_n = head_width // HEAD_DIM

    def project(w, rows_in):
        out = jnp.einsum("cde,ld->cel", w, rows_in, preferred_element_type=f32)
        return out.astype(bf16).reshape(-1, rows_in.shape[0])

    near_tokens = after(near_tokens, *arrived)
    near = project(w_qkv, near_tokens)
    near_z, near_o = over_place(near), over_seq(near)
    far_quarter = jnp.stack(arrived)
    moved = [over_head(far_quarter, j) for j in range(1, head_count)]
    dense_in = jnp.concatenate([here[0], *arrived])
    tables = key_tables(after(signed, dense_in), head_n, [near, near_o], None, f32)
    moved = [after(x, tables) for x in moved]

    near_z = after(near_z, tables)
    near_zo = over_seq(near_z)

    mask_pos = after(mask_pos, tables)
    slot = jnp.arange(groups, dtype=jnp.int32)[:, None]
    place_of = ((g - slot) % groups) * places + r
    position = s * half_len + place_of * piece + d * quarter + jnp.arange(quarter, dtype=jnp.int32)[None]
    mask_row = lax.dynamic_index_in_dim(mask_pos, g, 0, keepdims=False)
    cot = lax.dynamic_index_in_dim(cot_rows, g, 0, keepdims=False)
    pick = (position.reshape(rows)[:, None] == mask_row[None]).astype(bf16)
    grad_out = jnp.dot(pick, cot, preferred_element_type=f32)
    ready = after(signed, grad_out)
    tables = key_tables(ready, head_n, [near_z, near_zo], tables, f32)

    far_tokens = jnp.stack([far_quarter, *moved]).reshape(-1, width)
    far = project(w_qkv, far_tokens)
    tokens = jnp.concatenate([near_tokens, far_tokens])
    far_z, far_o = over_place(far), over_seq(far)
    n_near = near.shape[1]

    tables = key_tables(signed, head_n, [far, far_o], tables, f32)

    far_z = after(far_z, tables)
    far_zo = over_seq(far_z)
    tables = key_tables(after(signed, tokens, w_qkv_t), head_n, [far_z], tables, f32)

    far_zo = after(far_zo, tables)
    tables = key_tables(signed, head_n, [far_zo], tables, bf16)

    e_zo = query_estimates(signed, head_n, near_zo, far_zo, tables, bf16)
    e_zo_moved = over_seq(e_zo)
    e_z = query_estimates(signed, head_n, near_z, after(far_z, e_zo), tables, bf16)
    e_far = add(e_z, after(e_zo_moved, e_z)).astype(bf16)
    ready = after(far_o, e_far)
    e_o = query_estimates(signed, head_n, near_o, ready, tables, bf16)
    e_far = over_place(e_far)
    e_o_moved = over_seq(e_o)
    e = query_estimates(signed, head_n, near, after(far, e_o), tables, f32)
    e_far = after(e_far, e)
    e_o_moved = after(e_o_moved, e)
    weights = after(weights, e_far, e_o_moved)
    weights = [weights, over_seq(weights)]
    w_qkv_t = lax.all_gather(after(w_qkv_t, weights[0]), "head", axis=0)
    attn = add(e, e_o_moved, e_far).astype(bf16)

    def to_dense(block):
        parts = []
        for j in range(head_count):
            a, b = j * quarter, n_near + j * (rows - quarter)
            cut = [block[..., a : a + quarter], block[..., b : b + rows - quarter]]
            parts.append(jnp.concatenate(cut, axis=-1))
        moved = [over_head(parts[j], j) for j in range(1, head_count)]
        return [parts[0], *lax.optimization_barrier(moved)]

    attn_parts = to_dense(attn)

    def away(dense_rows):
        dense_rows = dense_rows.reshape(groups, quarter, width)
        return [dense_rows[0]] + [over_group(dense_rows[k], groups - k) for k in range(1, groups)]

    core = jnp.stack([s, d]).astype(jnp.int32)
    layer_rows, grad_first, keep, give, keep_back, give_back, heads_give, *est_parts, small = dense(
        core, dense_in, grad_out, norm_gain, norm_bias, attn_parts, weights
    )
    taken, taken_back, heads_far = over_seq(give), over_seq(give_back), over_seq(heads_give)
    est_moved = [over_head(est_parts[j], j) for j in range(1, head_count)]
    est_parts = [est_parts[0], *lax.optimization_barrier(est_moved)]
    grad = jnp.concatenate(
        [x[:, :quarter] for x in est_parts] + [x[:, quarter:] for x in est_parts], axis=1
    )
    layer_moved = away(layer_rows)
    weight_parts = weight_grads(
        core, after(small, grad), [keep, taken, keep_back, taken_back], attn_parts, heads_far
    )

    weight_sum = lax.psum_scatter(weight_parts, "head", scatter_dimension=0, tiled=True)[0]
    grad_z = over_place(grad)
    grad_o = after(over_seq(grad), weight_parts)
    layer_moved = [after(x, weight_parts) for x in layer_moved]
    part, dq, dq_o = query_backward(
        signed, signed_t, bits, head_n, tables, [(near, after(far, w_qkv_t, *layer_moved)), (near_o, far_o)], [grad, grad_o],
        None, False, [f32, bf16],
    )

    layer_moved = jnp.stack([after(x, part) for x in layer_moved])
    grad_z = after(grad_z, part)
    grad_zo = over_seq(grad_z)
    dq_o = over_seq(dq_o)
    part, dq_z = query_backward(
        signed, signed_t, bits, head_n, tables, [(near_z, far_z)], [grad_z], part, False, [f32]
    )

    dq_own = add(dq, after(dq_o, dq_z))
    grad_zo = after(grad_zo, dq_z)
    grad_tables, dq_zo = query_backward(
        signed, signed_t, bits, head_n, tables, [(near_zo, after(far_zo, dq_own))], [grad_zo], part, True, [bf16]
    )

    dq_zo = over_seq(dq_zo)
    w_qkv_t = after(w_qkv_t, grad_tables)
    w_qkv_far = over_seq(w_qkv_t)
    dkv_zo = key_backward(signed, signed_t, bits, head_n, near_zo, far_zo, grad_tables, bf16)

    dkv_zo_moved = over_seq(dkv_zo)
    dq_far = add(dq_z, after(dq_zo, dkv_zo)).astype(bf16)
    layer_moved = [layer_moved] + [over_head(layer_moved, j) for j in range(1, head_count)]
    dkv_z = key_backward(signed, signed_t, bits, head_n, near_z, after(far_z, dq_far), grad_tables, bf16)
    dq_far = over_place(dq_far)

    dkv_far = add(dkv_z, after(dkv_zo_moved, dkv_z)).astype(bf16)
    grad_q = add(dq_own, after(dq_far, dkv_z)).astype(bf16)
    weight_sum = after(weight_sum, dkv_z)
    layer_moved = [after(x, dkv_z) for x in layer_moved]
    dkv_o = key_backward(
        signed, signed_t, bits, head_n, near_o, after(far_o, dkv_far, grad_q, weight_sum, *layer_moved),
        grad_tables, bf16, 25,
    )
    weight_sum = lax.psum(weight_sum, "hash")
    dkv_far = over_place(dkv_far)
    dkv_o_moved = over_seq(dkv_o)
    dkv = key_backward(
        signed, signed_t, bits, head_n, near, after(far, dkv_o), grad_tables, f32, 25
    )

    dkv_o_moved = after(dkv_o_moved, dkv)
    grad_kv = add(dkv, dkv_o_moved, after(dkv_far, dkv)).astype(bf16)
    grad_qkv = jnp.concatenate([grad_q[None], grad_kv])
    qkv_parts = to_dense(grad_qkv)

    grad_in = input_grad(core, grad_first, qkv_parts, w_qkv_t, after(w_qkv_far, dkv))

    def in_halves(index, mine, other):
        first = jnp.where(index == 0, mine, other)
        second = jnp.where(index == 0, other, mine)
        return jnp.concatenate([first, second], axis=0)

    def split(x, index):
        half = x.shape[0] // 2
        return [lax.dynamic_slice_in_dim(x, at * half, half, 0) for at in (index, 1 - index)]

    w_grad = dot(grad_qkv.reshape(3 * head_width, n_tokens), tokens, NN).astype(bf16)
    w_keep, w_send = split(w_grad, s)
    w_keep, w_send = split(add(w_keep, over_seq(w_send)).astype(bf16), r)
    grad_moved = away(grad_in)
    w_keep = add(w_keep, over_place(w_send))
    w_send = w_keep.astype(bf16)
    grad_moved = after(jnp.stack(grad_moved), w_send)
    w_keep = add(w_keep, *[over_group(w_send, k) for k in range(1, groups)]).astype(bf16)
    grad_moved = [grad_moved] + [over_head(grad_moved, j) for j in range(1, head_count)]

    def home(blocks):
        table = jnp.stack(blocks)
        columns = []
        for q_at in range(head_count):
            block = lax.dynamic_index_in_dim(table, q_at ^ d, 0, keepdims=False)
            columns.append(
                jnp.stack(
                    [
                        lax.dynamic_index_in_dim(block, (at - g) % groups, 0, keepdims=False)
                        for at in range(seqs)
                    ],
                    axis=1,
                )
            )
        return jnp.concatenate(columns, axis=0)

    layer_out = home([after(x, grad_moved[0]) for x in layer_moved])
    grad_inputs = home(grad_moved).astype(f32)

    w_grad = in_halves(r, w_keep, over_place(w_keep))
    w_grad = in_halves(s, w_grad, over_seq(w_grad)).reshape(3, head_width, width)
    grad_w_qkv = w_grad.transpose(0, 2, 1).astype(f32)
    weight_sum = after(weight_sum, *grad_moved)
    weight_far = over_seq(weight_sum)
    grad_w_up, grad_w_down, grad_w_out = weight_results(core, weight_sum, weight_far, head_width)
    at = slice(2 * cut + out_cut, 2 * cut + out_cut + 16)
    small = add(weight_sum[at], weight_far[at])

    count = piece * seqs * width * hash_count * 2
    stream_rms = jnp.sqrt(jnp.sum(small[0:3], axis=1) / count)
    share = width // head_count
    norm_grads = lax.dynamic_slice_in_dim(small, d * share, share, 1)
    return (
        layer_out[None],
        grad_inputs[None],
        grad_w_qkv,
        grad_w_out,
        grad_w_up,
        grad_w_down,
        jnp.stack([norm_grads[5], norm_grads[3]]),
        jnp.stack([norm_grads[6], norm_grads[4]]),
        stream_rms,
    )


def solution(mesh):
    placed = (
        P("seq", "hash", None, None),
        P(None, None, "head"),
        P("head", None),
        P(None, "head"),
        P("head", None),
        P(),
        P(),
        P("hash", None, None),
        P(),
        P(),
    )
    return jax.shard_map(
        shards,
        mesh=mesh,
        in_specs=placed,
        out_specs=(
            P("seq", "hash", None, None),
            P("seq", "hash", None, None),
            P(None, None, "head"),
            P("head", None),
            P(None, "head"),
            P("head", None),
            P(None, "head"),
            P(None, "head"),
            P(),
        ),
        check_vma=False,
    )
```

```python
from functools import partial

import jax
import jax.numpy as jnp
import numpy as np
from jax import lax
from jax.experimental import pallas as pl
from jax.experimental.pallas import tpu as pltpu
from jax.sharding import PartitionSpec as P

HEAD_DIM = 64
HASHES = 32
BITS = 8
SETS = 8
BUCKETS = 1 << BITS
ROWS = BUCKETS * SETS

bf16 = jnp.bfloat16
f32 = jnp.float32
NN = (((1,), (0,)), ((), ()))
NT = (((1,), (1,)), ((), ()))
TN = (((0,), (0,)), ((), ()))


shape = jax.ShapeDtypeStruct


def dot(a, b, dims):
    return lax.dot_general(a, b, dims, preferred_element_type=f32)


def sides(rows, planes):
    x = rows.astype(f32)
    inv = lax.rsqrt(jnp.sum(x * x, axis=0, keepdims=True) + 1e-6)
    proj = dot(planes, rows, NN) * (3.0 * inv)
    small = jnp.exp(-proj)
    upper = 1.0 / (1.0 + small)
    return inv, upper, small * upper


def products(upper, lower, first, count):
    out = None
    for i in range(first, first + count):
        lo, up = lower[SETS * i : SETS * (i + 1)], upper[SETS * i : SETS * (i + 1)]
        out = [lo, up] if out is None else [c * lo for c in out] + [c * up for c in out]
    return out


def half_codes(upper, lower):
    low = jnp.concatenate(products(upper, lower, 0, 4), axis=0).astype(bf16)
    high = [jnp.concatenate([a, a], axis=0).astype(bf16) for a in products(upper, lower, 4, 4)]
    return low, high


def code_chunk(low, high, first, count):
    return jnp.concatenate(
        [high[a] * low[16 * j : 16 * (j + 1)] for a in range(first, first + count) for j in range(8)],
        axis=0,
    )


def pull_back(rows, planes_t, inv, upper, sums):
    total = sums[BITS * SETS :][:SETS]
    grad_proj = sums[: BITS * SETS] - upper * jnp.concatenate([total] * BITS, axis=0)
    head = grad_proj.astype(bf16)
    tail = (grad_proj - head.astype(f32)).astype(bf16)
    grad_unit = dot(planes_t, jnp.concatenate([head, tail], axis=0), NN) * (3.0 * inv)
    x = rows.astype(f32)
    return grad_unit - x * (inv * inv * jnp.sum(x * grad_unit, axis=0, keepdims=True))


def both(*refs):
    return jnp.concatenate([ref[...] for ref in refs], axis=1)


def key_kernel(planes, *refs, chunk, blocks):
    keys, vals, out = refs[:blocks], refs[blocks : 2 * blocks], refs[-1]
    start = refs[2 * blocks] if len(refs) > 2 * blocks + 1 else None
    _, upper, lower = sides(both(*keys), planes[...])
    low, high = half_codes(upper, lower)
    values = both(*vals)
    for c in range(0, 16, chunk):
        at = slice(128 * c, 128 * (c + chunk))
        part = dot(code_chunk(low, high, c, chunk), values, NT)
        if start is not None:
            part = part + start[0, at, :]
        out[0, at, :] = part.astype(out.dtype)


def query_kernel(planes, tables, *refs, chunk):
    blocks = len(refs) // 3
    rows, outs = both(*refs[: 2 * blocks]), refs[2 * blocks :]
    _, upper, lower = sides(rows, planes[...])
    low, high = half_codes(upper, lower)
    acc = jnp.zeros((HEAD_DIM, rows.shape[1]), f32)
    for c in range(0, 16, chunk):
        acc += dot(tables[0, 128 * c : 128 * (c + chunk), :], code_chunk(low, high, c, chunk), TN)
    width = outs[0].shape[1]
    for i, out in enumerate(outs):
        out[...] = (acc[:, i * width : (i + 1) * width] * (1.0 / HASHES)).astype(out.dtype)


def query_back_kernel(planes, planes_t, bits, tables, *refs, chunk, blocks, last):
    queries, grads = refs[: 2 * blocks], refs[2 * blocks : 3 * blocks]
    start = refs[3 * blocks] if len(refs) > 4 * blocks + 1 else None
    out, back_out = refs[-1 - blocks], refs[-blocks:]
    rows = both(*queries)
    inv, upper, lower = sides(rows, planes[...])
    low, high = half_codes(upper, lower)
    grad = both(*grads)
    sums = jnp.zeros((bits.shape[0], rows.shape[1]), f32)
    for c in range(0, 16, chunk):
        at = slice(128 * c, 128 * (c + chunk))
        codes = code_chunk(low, high, c, chunk)
        part = dot(codes, grad, NT)
        if start is not None:
            part = part + start[0, at, :]
        if last:
            part = part * (1.0 / HASHES)
        out[0, at, :] = part.astype(out.dtype)
        weighted = dot(tables[0, at, :], grad, NN).astype(bf16) * codes
        sums += dot(bits[:, at], weighted, NN)
    back = pull_back(rows, planes_t[...], inv, upper, sums * (1.0 / HASHES))
    width = back_out[0].shape[1]
    for i in range(blocks):
        back_out[i][...] = back[:, i * width : (i + 1) * width].astype(back_out[i].dtype)


def key_back_kernel(planes, planes_t, bits, ka, kb, va, vb, grad_tables, out, *, chunk):
    rows = both(ka, kb)
    inv, upper, lower = sides(rows, planes[...])
    low, high = half_codes(upper, lower)
    values = both(va, vb)
    width = rows.shape[1]
    sums = jnp.zeros((bits.shape[0], width), f32)
    grad_values = jnp.zeros((HEAD_DIM, width), f32)
    for c in range(0, 16, chunk):
        at = slice(128 * c, 128 * (c + chunk))
        codes = code_chunk(low, high, c, chunk)
        grad_values += dot(grad_tables[0, at, :], codes, TN)
        weighted = dot(grad_tables[0, at, :], values, NN).astype(bf16) * codes
        sums += dot(bits[:, at], weighted, NN)
    out[0] = pull_back(rows, planes_t[...], inv, upper, sums).astype(out.dtype)
    out[1] = grad_values.astype(out.dtype)


def bit_rows():
    out = np.zeros((80, BUCKETS, SETS), np.float32)
    for t in range(SETS):
        for i in range(BITS):
            out[i * SETS + t, :, t] = (np.arange(BUCKETS) >> i) & 1
        out[BITS * SETS + t, :, t] = 1
    return jnp.asarray(out.reshape(80, ROWS), bf16)


def whole(*shape):
    return pl.BlockSpec(shape, lambda h: (0,) * len(shape))


def head_rows(array, heads, which):
    width = array.shape[1]
    offset = (which - 3) * heads + array.shape[0] // HEAD_DIM
    return pl.BlockSpec((HEAD_DIM, width), lambda h: (h + offset, 0))


def per_head(width):
    return pl.BlockSpec((HEAD_DIM, width), lambda h: (h, 0))


def table_spec():
    return pl.BlockSpec((1, ROWS, HEAD_DIM), lambda h: (h, 0, 0))


def call(kernel, heads, micros, name, in_specs, out_specs, out_shape):
    return pl.pallas_call(
        kernel,
        grid=(heads,),
        in_specs=in_specs,
        out_specs=out_specs,
        out_shape=out_shape,
        compiler_params=pltpu.CompilerParams(vmem_limit_bytes=48 << 20),
        cost_estimate=pl.CostEstimate(
            flops=int(micros * 1.1e9), bytes_accessed=1 << 20, transcendentals=0
        ),
        name=name,
    )


def key_tables(planes, heads, blocks, start, kind):
    args = [planes, *blocks, *blocks]
    specs = [whole(64, 64)] + [head_rows(x, heads, w) for w in (1, 2) for x in blocks]
    if start is not None:
        specs.append(table_spec())
        args.append(start)
    return call(
        partial(key_kernel, chunk=2, blocks=len(blocks)),
        heads,
        30 if len(blocks) > 1 and start is not None else 1,
        "key_tables",
        specs,
        table_spec(),
        shape((heads, ROWS, HEAD_DIM), kind),
    )(*args)


def query_estimates(planes, heads, blocks, tables, kinds):
    width = blocks[0][0].shape[1] + blocks[0][1].shape[1]
    arrays = [x for pair in blocks for x in pair]
    return call(
        partial(query_kernel, chunk=2),
        heads,
        1 if len(blocks) == 1 else 20,
        "query_estimates",
        [whole(64, 64), table_spec()] + [head_rows(x, heads, 0) for x in arrays],
        [per_head(width)] * len(blocks),
        [shape((heads * HEAD_DIM, width), kind) for kind in kinds],
    )(planes, tables, *arrays)


def query_backward(planes, planes_t, bits, heads, tables, queries, grads, start, last, kinds):
    width = grads[0].shape[1]
    blocks = len(grads)
    specs = [whole(64, 64), whole(64, 128), whole(80, ROWS), table_spec()]
    args = [planes, planes_t, bits, tables]
    for near, far in queries:
        specs += [head_rows(near, heads, 0), head_rows(far, heads, 0)]
        args += [near, far]
    specs += [per_head(width)] * blocks
    args += grads
    if start is not None:
        specs.append(table_spec())
        args.append(start)
    return call(
        partial(query_back_kernel, chunk=4 * blocks, blocks=blocks, last=last),
        heads,
        25 * blocks,
        "query_backward",
        specs,
        [table_spec()] + [per_head(width)] * blocks,
        [shape((heads, ROWS, HEAD_DIM), bf16 if last else f32)]
        + [shape(grads[0].shape, kind) for kind in kinds],
    )(*args)


def key_backward(planes, planes_t, bits, heads, near, far, grad_tables, kind, micros=25):
    width = near.shape[1] + far.shape[1]
    return call(
        partial(key_back_kernel, chunk=4),
        heads,
        micros,
        "key_backward",
        [whole(64, 64), whole(64, 128), whole(80, ROWS)]
        + [head_rows(x, heads, w) for w in (1, 2) for x in (near, far)]
        + [table_spec()],
        pl.BlockSpec((2, HEAD_DIM, width), lambda h: (0, h, 0)),
        shape((2, heads * HEAD_DIM, width), kind),
    )(planes, planes_t, bits, near, far, near, far, grad_tables)


def norm(x):
    center = x - jnp.mean(x, axis=-1, keepdims=True)
    inv = lax.rsqrt(jnp.mean(center * center, axis=-1, keepdims=True) + 1e-5)
    return center * inv, inv


def norm_back(grad, unit, inv):
    return inv * (
        grad
        - jnp.mean(grad, axis=-1, keepdims=True)
        - unit * jnp.mean(grad * unit, axis=-1, keepdims=True)
    )


def column_sum(x):
    return jnp.sum(x, axis=0, keepdims=True)


def core_rows(core, ref, which):
    half = ref.shape[0] // 2
    at = core[0] if which == 0 else 1 - core[0]
    return ref[pl.ds(pl.multiple_of(at * half, 16), half), :]


def share_rows(keep, give, at, rows):
    part = keep.shape[2]
    for out in (keep, give):
        out[at] = rows[:, :part]
        out[at + 1] = rows[:, part:]


def dense_kernel(core, x_in, grad_out, gain, bias, *refs):
    attn, weights = refs[0:4], refs[4:6]
    layer_out, grad_first_out, keep, give, keep_back, give_back, heads_give = refs[6:13]
    estimates, small, slope = refs[13:17], refs[17], refs[18]
    owner = [core[1] ^ (b // 2) for b in range(8)]
    for j in range(4):
        heads_give[j] = core_rows(core, attn[j], 1)
    part = slope.shape[2]
    blocks = range(8)
    heads = jnp.concatenate([core_rows(core, attn[b // 2], b % 2) for b in blocks], axis=0)
    out_w = jnp.concatenate([weights[b % 2][owner[b], 2 * part :, :] for b in blocks], axis=0)
    attn_out = dot(heads, out_w, TN)
    resid = x_in[...].astype(f32)
    first = resid + attn_out
    small[0:1, :] = column_sum(resid * resid)
    small[1:2, :] = column_sum(attn_out * attn_out)
    small[2:3, :] = column_sum(first * first)
    unit_1, inv_1 = norm(first)
    normed = (unit_1 * gain[0:1, :] + bias[0:1, :]).astype(bf16)
    share_rows(keep, give, 4, normed)
    second = normed.astype(f32)
    for b in blocks:
        pre = dot(normed, weights[b % 2][owner[b], 0:part, :], NT)
        below = 0.5 * (1.0 + lax.erf(pre * 0.7071067811865476))
        rows = (pre * below).astype(bf16)
        (keep, give)[b % 2][b // 2] = rows
        slope[b] = below + pre * (0.3989422804014327 * jnp.exp(-0.5 * pre * pre))
        second = second + dot(rows, weights[b % 2][owner[b], part : 2 * part, :], NN)
    unit_2, inv_2 = norm(second)
    layer_out[...] = (unit_2 * gain[1:2, :] + bias[1:2, :]).astype(layer_out.dtype)
    grad = grad_out[...]
    small[3:4, :] = column_sum(grad * unit_2)
    small[4:5, :] = column_sum(grad)
    grad_second = norm_back(grad * gain[1:2, :], unit_2, inv_2)
    grad_ffn = grad_second.astype(bf16)
    share_rows(keep, give, 6, grad_ffn)
    grad_normed = grad_second
    for b in blocks:
        rows = dot(grad_ffn, weights[b % 2][owner[b], part : 2 * part, :], NT)
        rows = (rows * slope[b]).astype(bf16)
        (keep_back, give_back)[b % 2][b // 2] = rows
        grad_normed = grad_normed + dot(rows, weights[b % 2][owner[b], 0:part, :], NN)
    small[5:6, :] = column_sum(grad_normed * unit_1)
    small[6:7, :] = column_sum(grad_normed)
    small[7:16, :] = jnp.zeros_like(small[7:16, :])
    grad_first = norm_back(grad_normed * gain[0:1, :], unit_1, inv_1)
    grad_first_out[...] = grad_first
    grad_attn = grad_first.astype(bf16)
    share_rows(keep_back, give_back, 4, grad_attn)
    for b in blocks:
        half = estimates[0].shape[0] // 2
        at = core[0] if b % 2 == 0 else 1 - core[0]
        estimates[b // 2][pl.ds(pl.multiple_of(at * half, 16), half), :] = dot(
            weights[b % 2][owner[b], 2 * part :, :], grad_attn, NT
        ).astype(bf16)


def weight_grad_kernel(core, small, *refs):
    near, far, near_back, far_back = refs[0:4]
    attn, attn_far, out = refs[4:8], refs[8], refs[9]
    part = near.shape[2]
    sums = small[...].astype(bf16)

    def wide(ref, at):
        return jnp.concatenate([ref[at], ref[at + 1]], axis=1)

    def rows(ref, other, at):
        return jnp.concatenate([wide(ref, at), wide(other, at)], axis=0)

    normed, grad_ffn = rows(near, far, 4), rows(near, far, 6)
    grad_attn = rows(near_back, far_back, 4)
    for j in range(4):
        owner = core[1] ^ j
        hidden = jnp.concatenate([near[j], far[j]], axis=0)
        grad_pre = jnp.concatenate([near_back[j], far_back[j]], axis=0)
        out[owner, 0:part, :] = dot(grad_pre, normed, TN).astype(bf16)
        out[owner, part : 2 * part, :] = dot(hidden, grad_ffn, TN).astype(bf16)
        heads = jnp.concatenate([core_rows(core, attn[j], 0), attn_far[j]], axis=1)
        at = 2 * part + heads.shape[0]
        out[owner, 2 * part : at, :] = dot(heads, grad_attn, NN).astype(bf16)
        out[owner, at : at + 16, :] = sums
        out[owner, at + 16 :, :] = jnp.zeros_like(sums)


def input_grad_kernel(core, grad_first, *refs):
    blocks, near, far, out = refs[0:4], refs[4], refs[5], refs[6]
    half = near.shape[2]
    total = grad_first[...]
    for which, halves in enumerate((near, far)):
        at = core[0] if which == 0 else 1 - core[0]
        at = pl.ds(pl.multiple_of(at * half, 16), half)
        for j in range(4):
            rows = jnp.concatenate([blocks[j][c, at, :] for c in range(3)], axis=0)
            weights = jnp.concatenate([halves[core[1] ^ j, c] for c in range(3)], axis=0)
            total = total + dot(rows, weights, TN)
    out[...] = total.astype(out.dtype)


def vmem(count):
    return [pl.BlockSpec(memory_space=pltpu.VMEM)] * count


def single(kernel, core, args, out_shape, micros, name, scratch=()):
    return pl.pallas_call(
        kernel,
        in_specs=[pl.BlockSpec(memory_space=pltpu.SMEM)] + vmem(len(args)),
        out_specs=vmem(len(out_shape)),
        out_shape=out_shape,
        scratch_shapes=scratch,
        compiler_params=pltpu.CompilerParams(vmem_limit_bytes=56 << 20),
        cost_estimate=pl.CostEstimate(
            flops=int(micros * 1.1e9), bytes_accessed=1 << 20, transcendentals=0
        ),
        name=name,
    )(core, *args)


def dense(core, x_in, grad_out, gain, bias, attn, weights):
    rows, width = x_in.shape
    part = (weights[0].shape[1] - attn[0].shape[0] // 2) // 2
    out_shape = [
        shape((rows, width), bf16),
        shape((rows, width), f32),
        *[shape((8, rows, part), bf16)] * 2,
        *[shape((6, rows, part), bf16)] * 2,
        shape((4, attn[0].shape[0] // 2, rows), bf16),
        *[shape(attn[0].shape, bf16)] * 4,
        shape((16, width), f32),
    ]
    args = [x_in, grad_out, gain, bias, *attn, *weights]
    scratch = [pltpu.VMEM((8, rows, part), f32)]
    return single(dense_kernel, core, args, out_shape, 22, "dense", scratch)


def weight_grads(core, small, shared, attn, attn_far):
    part, width = shared[0].shape[2], small.shape[1]
    out_shape = [shape((4, 2 * part + attn[0].shape[0] // 2 + 32, width), bf16)]
    args = [small, *shared, *attn, attn_far]
    return single(weight_grad_kernel, core, args, out_shape, 7, "weight_grads")[0]


def weight_results_kernel(core, near, far, up, down, out):
    part, rows = up.shape[1] // 2, out.shape[0] // 2
    for which, ref in enumerate((near, far)):
        at = core[0] if which == 0 else 1 - core[0]
        at_part = pl.ds(pl.multiple_of(at * part, 128), part)
        up[:, at_part] = ref[0:part, :].astype(f32).T
        down[at_part, :] = ref[part : 2 * part, :].astype(f32)
        at_rows = pl.ds(pl.multiple_of(at * rows, 16), rows)
        out[at_rows, :] = ref[2 * part : 2 * part + rows, :].astype(f32)


def weight_results(core, near, far, head_width):
    width = near.shape[1]
    part = (near.shape[0] - 32 - head_width // 2) // 2
    out_shape = [
        shape((width, 2 * part), f32), shape((2 * part, width), f32), shape((head_width, width), f32)
    ]
    return single(weight_results_kernel, core, [near, far], out_shape, 3, "weight_results")


def input_grad(core, grad_first, blocks, near, far):
    out_shape = [shape(grad_first.shape, bf16)]
    args = [grad_first, *blocks, near, far]
    return single(input_grad_kernel, core, args, out_shape, 40, "input_grad")[0]


def after(x, *others):
    return lax.optimization_barrier((x, *others))[0]


def add(a, *others):
    return sum([b.astype(f32) for b in others], a.astype(f32))


def shards(
    inputs,
    w_qkv,
    w_out,
    up_weight,
    down_weight,
    norm_gain,
    norm_bias,
    planes,
    mask_pos,
    cot_rows,
):
    own = inputs[0]
    piece, seqs, width = own.shape
    hash_count, head_count = lax.axis_size("hash"), lax.axis_size("head")
    groups, places = seqs, hash_count // seqs
    assert places == 2 and lax.axis_size("seq") == 2 and head_count == 4
    assert planes.shape[0] * hash_count == 4 * SETS
    quarter = piece // head_count
    rows = groups * quarter
    half_len = piece * hash_count
    head_width = w_out.shape[0]
    hidden_own = down_weight.shape[0]
    n_tokens = head_count * rows
    hash_id, d, s = lax.axis_index("hash"), lax.axis_index("head"), lax.axis_index("seq")
    g, r = hash_id // places, hash_id % places

    def over_seq(x):
        return lax.ppermute(x, "seq", [(0, 1), (1, 0)])

    def over_place(x):
        return lax.ppermute(x, "hash", [(h, h ^ 1) for h in range(hash_count)])

    def over_group(x, k):
        moves = [(h, ((h // places + k) % groups) * places + h % places) for h in range(hash_count)]
        return lax.ppermute(x, "hash", moves)

    def over_head(x, j):
        return lax.ppermute(x, "head", [(h, h ^ j) for h in range(head_count)])

    def seq_rows(block, index):
        return lax.dynamic_index_in_dim(block, index % seqs, 1, keepdims=False)

    here = [
        seq_rows(lax.dynamic_slice_in_dim(own, (d ^ j) * quarter, quarter, 0), g)
        for j in range(head_count)
    ]
    near_tokens = jnp.concatenate(here)
    my_quarter = lax.dynamic_slice_in_dim(own, d * quarter, quarter, 0)
    sent = [seq_rows(my_quarter, g + k) for k in range(1, groups)]
    arrived = [over_group(x, k + 1) for k, x in enumerate(sent)]

    signed = (2 * planes - 1).astype(bf16)
    if planes.shape[0] == SETS and groups == 2:
        moves = [
            ((2 * rr + ss) * 2 + gg, (gg * places + rr) * 2 + ss)
            for gg in range(2)
            for rr in range(2)
            for ss in range(2)
        ]
        signed = lax.ppermute(signed, ("hash", "seq"), moves)
    else:
        signed = lax.all_gather(signed, "hash", axis=0, tiled=True)
        signed = lax.dynamic_slice_in_dim(signed, (r * 2 + s) * SETS, SETS, 0)
    signed = signed.transpose(1, 0, 2).reshape(BITS * SETS, HEAD_DIM)
    signed_t = jnp.concatenate([signed.T, signed.T], axis=1)
    bits = bit_rows()

    cut, out_cut = hidden_own // 2, head_width // 2
    weights = jnp.concatenate(
        [
            lax.dynamic_slice_in_dim(after(up_weight, *sent), s * cut, cut, 1).T,
            lax.dynamic_slice_in_dim(down_weight, s * cut, cut, 0),
            lax.dynamic_slice_in_dim(w_out, s * out_cut, out_cut, 0),
        ]
    )
    weights = lax.all_gather(weights, "head", axis=0)
    w_qkv_t = lax.dynamic_slice_in_dim(w_qkv.transpose(0, 2, 1), s * out_cut, out_cut, 1)

    head_n = head_width // HEAD_DIM

    def project(w, rows_in):
        out = jnp.einsum("cde,ld->cel", w, rows_in, preferred_element_type=f32)
        return out.astype(bf16).reshape(-1, rows_in.shape[0])

    near_tokens = after(near_tokens, *arrived)
    near = project(w_qkv, near_tokens)
    near_z, near_o = over_place(near), over_seq(near)
    far_quarter = jnp.stack(arrived)
    moved = [over_head(far_quarter, j) for j in range(1, head_count)]
    dense_in = jnp.concatenate([here[0], *arrived])
    tables = key_tables(after(signed, dense_in), head_n, [near, near_o], None, f32)
    moved = [after(x, tables) for x in moved]

    near_z = after(near_z, tables)
    near_zo = over_seq(near_z)

    mask_pos = after(mask_pos, tables)
    slot = jnp.arange(groups, dtype=jnp.int32)[:, None]
    place_of = ((g - slot) % groups) * places + r
    position = s * half_len + place_of * piece + d * quarter + jnp.arange(quarter, dtype=jnp.int32)[None]
    mask_row = lax.dynamic_index_in_dim(mask_pos, g, 0, keepdims=False)
    cot = lax.dynamic_index_in_dim(cot_rows, g, 0, keepdims=False)
    pick = (position.reshape(rows)[:, None] == mask_row[None]).astype(bf16)
    grad_out = jnp.dot(pick, cot, preferred_element_type=f32)
    ready = after(signed, grad_out)
    tables = key_tables(ready, head_n, [near_z, near_zo], tables, f32)

    far_tokens = jnp.stack([far_quarter, *moved]).reshape(-1, width)
    far = project(w_qkv, far_tokens)
    tokens = jnp.concatenate([near_tokens, far_tokens])
    far_z, far_o = over_place(far), over_seq(far)
    n_near = near.shape[1]

    tables = key_tables(signed, head_n, [far, far_o], tables, f32)

    far_z = after(far_z, tables)
    far_zo = over_seq(far_z)
    tables = key_tables(after(signed, tokens, w_qkv_t), head_n, [far_z], tables, f32)

    far_zo = after(far_zo, tables)
    tables = key_tables(signed, head_n, [far_zo], tables, bf16)

    e_zo = query_estimates(signed, head_n, [(near_zo, far_zo)], tables, [bf16])[0]
    e_zo_moved = over_seq(e_zo)
    e_z = query_estimates(signed, head_n, [(near_z, after(far_z, e_zo))], tables, [bf16])[0]
    e_far = add(e_z, after(e_zo_moved, e_z)).astype(bf16)
    ready = after(far_o, e_far)
    e, e_o = query_estimates(signed, head_n, [(near, far), (near_o, ready)], tables, [f32, bf16])
    e_far = after(over_place(e_far), e)
    e_o_moved = over_seq(after(e_o, e_far))
    e_o_moved = after(e_o_moved, e)
    weights = after(weights, e_far, e_o_moved)
    weights = [weights, over_seq(weights)]
    w_qkv_t = lax.all_gather(after(w_qkv_t, weights[0]), "head", axis=0)
    attn = add(e, e_o_moved, e_far).astype(bf16)

    def to_dense(block):
        parts = []
        for j in range(head_count):
            a, b = j * quarter, n_near + j * (rows - quarter)
            cut = [block[..., a : a + quarter], block[..., b : b + rows - quarter]]
            parts.append(jnp.concatenate(cut, axis=-1))
        moved = [over_head(parts[j], j) for j in range(1, head_count)]
        return [parts[0], *lax.optimization_barrier(moved)]

    attn_parts = to_dense(attn)

    def away(dense_rows):
        dense_rows = dense_rows.reshape(groups, quarter, width)
        return [dense_rows[0]] + [over_group(dense_rows[k], groups - k) for k in range(1, groups)]

    core = jnp.stack([s, d]).astype(jnp.int32)
    layer_rows, grad_first, keep, give, keep_back, give_back, heads_give, *est_parts, small = dense(
        core, dense_in, grad_out, norm_gain, norm_bias, attn_parts, weights
    )
    taken, taken_back, heads_far = over_seq(give), over_seq(give_back), over_seq(heads_give)
    est_moved = [over_head(est_parts[j], j) for j in range(1, head_count)]
    est_parts = [est_parts[0], *lax.optimization_barrier(est_moved)]
    grad = jnp.concatenate(
        [x[:, :quarter] for x in est_parts] + [x[:, quarter:] for x in est_parts], axis=1
    )
    layer_moved = away(layer_rows)
    weight_parts = weight_grads(
        core, after(small, grad), [keep, taken, keep_back, taken_back], attn_parts, heads_far
    )

    weight_sum = lax.psum_scatter(weight_parts, "head", scatter_dimension=0, tiled=True)[0]
    grad_z = over_place(grad)
    grad_o = after(over_seq(grad), weight_parts)
    layer_moved = [after(x, weight_parts) for x in layer_moved]
    part, dq, dq_o = query_backward(
        signed, signed_t, bits, head_n, tables, [(near, after(far, w_qkv_t, *layer_moved)), (near_o, far_o)], [grad, grad_o],
        None, False, [f32, bf16],
    )

    layer_moved = jnp.stack([after(x, part) for x in layer_moved])
    grad_z = after(grad_z, part)
    grad_zo = over_seq(grad_z)
    dq_o = over_seq(dq_o)
    part, dq_z = query_backward(
        signed, signed_t, bits, head_n, tables, [(near_z, far_z)], [grad_z], part, False, [f32]
    )

    dq_own = add(dq, after(dq_o, dq_z))
    grad_zo = after(grad_zo, dq_z)
    grad_tables, dq_zo = query_backward(
        signed, signed_t, bits, head_n, tables, [(near_zo, after(far_zo, dq_own))], [grad_zo], part, True, [bf16]
    )

    dq_zo = over_seq(dq_zo)
    w_qkv_t = after(w_qkv_t, grad_tables)
    w_qkv_far = over_seq(w_qkv_t)
    dkv_zo = key_backward(signed, signed_t, bits, head_n, near_zo, far_zo, grad_tables, bf16)

    dkv_zo_moved = over_seq(dkv_zo)
    dq_far = add(dq_z, after(dq_zo, dkv_zo)).astype(bf16)
    layer_moved = [layer_moved] + [over_head(layer_moved, j) for j in range(1, head_count)]
    dkv_z = key_backward(signed, signed_t, bits, head_n, near_z, after(far_z, dq_far), grad_tables, bf16)
    dq_far = over_place(dq_far)

    dkv_far = add(dkv_z, after(dkv_zo_moved, dkv_z)).astype(bf16)
    grad_q = add(dq_own, after(dq_far, dkv_z)).astype(bf16)
    weight_sum = after(weight_sum, dkv_z)
    layer_moved = [after(x, dkv_z) for x in layer_moved]
    dkv_o = key_backward(
        signed, signed_t, bits, head_n, near_o, after(far_o, dkv_far, grad_q, weight_sum, *layer_moved),
        grad_tables, bf16, 25,
    )
    weight_sum = lax.psum(weight_sum, "hash")
    dkv_far = over_place(dkv_far)
    dkv_o_moved = over_seq(dkv_o)
    dkv = key_backward(
        signed, signed_t, bits, head_n, near, after(far, dkv_o), grad_tables, f32, 25
    )

    dkv_o_moved = after(dkv_o_moved, dkv)
    grad_kv = add(dkv, dkv_o_moved, after(dkv_far, dkv)).astype(bf16)
    grad_qkv = jnp.concatenate([grad_q[None], grad_kv])
    qkv_parts = to_dense(grad_qkv)

    grad_in = input_grad(core, grad_first, qkv_parts, w_qkv_t, after(w_qkv_far, dkv))

    def in_halves(index, mine, other):
        first = jnp.where(index == 0, mine, other)
        second = jnp.where(index == 0, other, mine)
        return jnp.concatenate([first, second], axis=0)

    def split(x, index):
        half = x.shape[0] // 2
        return [lax.dynamic_slice_in_dim(x, at * half, half, 0) for at in (index, 1 - index)]

    w_grad = dot(grad_qkv.reshape(3 * head_width, n_tokens), tokens, NN).astype(bf16)
    w_keep, w_send = split(w_grad, s)
    w_keep, w_send = split(add(w_keep, over_seq(w_send)).astype(bf16), r)
    grad_moved = away(grad_in)
    w_keep = add(w_keep, over_place(w_send))
    w_send = w_keep.astype(bf16)
    grad_moved = after(jnp.stack(grad_moved), w_send)
    w_keep = add(w_keep, *[over_group(w_send, k) for k in range(1, groups)]).astype(bf16)
    grad_moved = [grad_moved] + [over_head(grad_moved, j) for j in range(1, head_count)]

    def home(blocks):
        table = jnp.stack(blocks)
        columns = []
        for q_at in range(head_count):
            block = lax.dynamic_index_in_dim(table, q_at ^ d, 0, keepdims=False)
            columns.append(
                jnp.stack(
                    [
                        lax.dynamic_index_in_dim(block, (at - g) % groups, 0, keepdims=False)
                        for at in range(seqs)
                    ],
                    axis=1,
                )
            )
        return jnp.concatenate(columns, axis=0)

    layer_out = home([after(x, grad_moved[0]) for x in layer_moved])
    grad_inputs = home(grad_moved).astype(f32)

    w_grad = in_halves(r, w_keep, over_place(w_keep))
    w_grad = in_halves(s, w_grad, over_seq(w_grad)).reshape(3, head_width, width)
    grad_w_qkv = w_grad.transpose(0, 2, 1).astype(f32)
    weight_sum = after(weight_sum, *grad_moved)
    weight_far = over_seq(weight_sum)
    grad_w_up, grad_w_down, grad_w_out = weight_results(core, weight_sum, weight_far, head_width)
    at = slice(2 * cut + out_cut, 2 * cut + out_cut + 16)
    small = add(weight_sum[at], weight_far[at])

    count = piece * seqs * width * hash_count * 2
    stream_rms = jnp.sqrt(jnp.sum(small[0:3], axis=1) / count)
    share = width // head_count
    norm_grads = lax.dynamic_slice_in_dim(small, d * share, share, 1)
    return (
        layer_out[None],
        grad_inputs[None],
        grad_w_qkv,
        grad_w_out,
        grad_w_up,
        grad_w_down,
        jnp.stack([norm_grads[5], norm_grads[3]]),
        jnp.stack([norm_grads[6], norm_grads[4]]),
        stream_rms,
    )


def solution(mesh):
    placed = (
        P("seq", "hash", None, None),
        P(None, None, "head"),
        P("head", None),
        P(None, "head"),
        P("head", None),
        P(),
        P(),
        P("hash", None, None),
        P(),
        P(),
    )
    return jax.shard_map(
        shards,
        mesh=mesh,
        in_specs=placed,
        out_specs=(
            P("seq", "hash", None, None),
            P("seq", "hash", None, None),
            P(None, None, "head"),
            P("head", None),
            P(None, "head"),
            P("head", None),
            P(None, "head"),
            P(None, "head"),
            P(),
        ),
        check_vma=False,
    )
```
